32 devices in a mesh: wide: 8 (over y, x, core), narrow: 4 (over z).
Axes of the slice: x: 2, y: 2, z: 4, core: 2. Of those that a mesh axis runs over, the one named last changes fastest.
Arguments:
- inputs: bfloat16 [32, 258, 1152], P(('wide', 'narrow')), may hold values from -6 to 6
- skip_tokens: bfloat16 [32, 258, 1152], P(('wide', 'narrow')), may hold values from -6 to 6
- cotangent: bfloat16 [32, 258, 1152], P(('wide', 'narrow')), may hold values from -12 to 12
- merge_weight: float32 [2304, 1152], P('wide', 'narrow'), may hold values from -0.125 to 0.125
- merge_moment: float32 [2304, 1152], P('wide', 'narrow'), may hold values from -1536 to 1536
- merge_square: float32 [2304, 1152], P('wide', 'narrow'), may hold values from 74304 to 297216
- attend_weight: float32 [1152, 3456], P('wide', 'narrow'), may hold values from -0.25 to 0.25
- attend_moment: float32 [1152, 3456], P('wide', 'narrow'), may hold values from -1024 to 1024
- attend_square: float32 [1152, 3456], P('wide', 'narrow'), may hold values from 33024 to 132096
- output_weight: float32 [1152, 1152], P('wide', 'narrow'), may hold values from -2 to 2
- output_moment: float32 [1152, 1152], P('wide', 'narrow'), may hold values from -128 to 128
- output_square: float32 [1152, 1152], P('wide', 'narrow'), may hold values from 516 to 2064
- expand_weight: float32 [1152, 4608], P('wide', 'narrow'), may hold values from -0.1875 to 0.1875
- expand_moment: float32 [1152, 4608], P('wide', 'narrow'), may hold values from -160 to 160
- expand_square: float32 [1152, 4608], P('wide', 'narrow'), may hold values from 743.04 to 2972.16
- shrink_weight: float32 [4608, 1152], P('wide', 'narrow'), may hold values from -0.09375 to 0.09375
- shrink_moment: float32 [4608, 1152], P('wide', 'narrow'), may hold values from -320 to 320
- shrink_square: float32 [4608, 1152], P('wide', 'narrow'), may hold values from 2972.16 to 11888.64
- vectors: float32 [12672], P('narrow'), may hold values from -1.2 to 1.5
- vector_moment: float32 [12672], P('narrow'), may hold values from -1024 to 1024
- vector_square: float32 [12672], P('narrow'), may hold values from 33024 to 132096
Outputs:
- outputs: bfloat16 [32, 258, 1152], P(('wide', 'narrow'))
- input_gradient: bfloat16 [32, 258, 1152], P(('wide', 'narrow'))
- skip_gradient: bfloat16 [32, 258, 1152], P(('wide', 'narrow'))
- renewed_merge: float32 [2304, 1152], P('wide', 'narrow')
- moment_merge: float32 [2304, 1152], P('wide', 'narrow')
- square_merge: float32 [2304, 1152], P('wide', 'narrow')
- renewed_attend: float32 [1152, 3456], P('wide', 'narrow')
- moment_attend: float32 [1152, 3456], P('wide', 'narrow')
- square_attend: float32 [1152, 3456], P('wide', 'narrow')
- renewed_output: float32 [1152, 1152], P('wide', 'narrow')
- moment_output: float32 [1152, 1152], P('wide', 'narrow')
- square_output: float32 [1152, 1152], P('wide', 'narrow')
- renewed_expand: float32 [1152, 4608], P('wide', 'narrow')
- moment_expand: float32 [1152, 4608], P('wide', 'narrow')
- square_expand: float32 [1152, 4608], P('wide', 'narrow')
- renewed_shrink: float32 [4608, 1152], P('wide', 'narrow')
- moment_shrink: float32 [4608, 1152], P('wide', 'narrow')
- square_shrink: float32 [4608, 1152], P('wide', 'narrow')
- renewed_vector: float32 [12672], P('narrow')
- moment_vector: float32 [12672], P('narrow')
- square_vector: float32 [12672], P('narrow')
The draws below stay inside these ranges and needn't reach their ends.
All inputs are finite; a program needn't handle non-finite values.
Results may differ from the reference program's by a relative error of at most 0.017.
The reference program's roundings to bfloat16 on the way count: a program that leaves them out, or rounds other values in their place, can miss the bound.
Values may be sent and summed in bfloat16 or wider, within the bound.
No kernel may reach another device: no remote copies, remote signals or barrier semaphores. Data moves between devices by JAX's collectives and lax.ppermute only.
A program may use at most 256 MiB of HBM per device.

```python
import math
import jax
import jax.numpy as jnp
from jax import lax

D = 1152
FF = 4608
H = 16
HD = 72
L = 258
STEP = 5
B = 32
TOKENS = 8256
VEC = 12672


def draw_vectors(key, part):
    key = jax.random.fold_in(key, 17)
    noise_key, gain_key = jax.random.split(key)
    entries = 7 * D + FF
    normal_part = jnp.clip(jax.random.normal(noise_key, (entries,), jnp.float32), -4.0, 4.0)
    gain_part = jax.random.uniform(gain_key, (entries,), jnp.float32, 0.5, 1.5)
    position = jnp.arange(entries)
    is_gain = (position >= D) & (position < 2 * D) | (position >= 4 * D) & (position < 5 * D)
    return jnp.where(is_gain, gain_part, 0.3 * normal_part)


def with_spikes(values, stream_key, source, target, blocks, factor):
    owner, partner = [(jnp.arange(values.shape[dim]) // (values.shape[dim] // blocks)).reshape([-1 if axis == dim else 1 for axis in range(values.ndim)]) for dim in (source, target)]
    chosen = jax.random.permutation(stream_key, blocks)[partner]
    strong = (owner == chosen) | (owner == (partner + blocks // 2) % blocks)
    return jnp.where(strong, factor * values, values)


def levels(key, extent, shards, low, largest):
    loudness = 1.0
    for dim, shards_of in shards:
        heights = jax.random.uniform(jax.random.fold_in(jax.random.fold_in(key, 6), dim), (shards_of,), jnp.float32, low / len(shards), largest / len(shards))
        loudness = loudness * jnp.repeat(jnp.exp(heights), extent[dim] // shards_of).reshape((-1,) + (1,) * (len(extent) - 1 - dim))
    return loudness


def gaussian(stream_key, shape, scale, most, shards=(), dtype=jnp.bfloat16):
    drawn = jax.random.normal(stream_key, shape, jnp.float32) * scale
    if len(shards) > 0:
        drawn = levels(stream_key, shape, shards, -0.22, 0.18) * drawn
    return jnp.clip(drawn, min=-most, max=most).astype(dtype)


def gaussian_with(rng, extent, deviation, reach, shards, heavy, dtype=jnp.bfloat16):
    drawn = deviation * jax.random.normal(rng, extent, jnp.float32)
    if shards:
        drawn = drawn * levels(rng, extent, shards, -0.22, 0.18)
    return jnp.clip(with_spikes(drawn, jax.random.fold_in(rng, 3), *heavy), -reach, reach).astype(dtype)


def setup_inputs(seed: int = 0) -> dict:
    key_list = jax.random.split(jax.random.key(seed), 22)
    return {
        "inputs": gaussian(key_list[0], (B, L, D), 1.0, 6.0, ((0, 32),)),
        "skip_tokens": gaussian(key_list[1], (B, L, D), 1.0, 6.0, ((0, 32),)),
        "cotangent": gaussian_with(key_list[2], (B, L, D), 1.0, 12.0, ((0, 32),), (0, 2, 32, 2.75)),
        "merge_weight": gaussian(key_list[3], (2 * D, D), (2 * D) ** -0.5, 0.125, ((0, 8), (1, 4)), jnp.float32),
        "merge_moment": gaussian(key_list[4], (2 * D, D), (3 * TOKENS ** 0.5), 1536.0, ((0, 8), (1, 4)), jnp.float32),
        "merge_square": jnp.clip(jnp.exp(math.log(297216.0) - 1.3862944 * jax.random.uniform(key_list[5], (2 * D, D), jnp.float32) ** levels(key_list[5], (2 * D, D), ((0, 8), (1, 4)), -0.2, 0.2)), 74304.0, 297216.0),
        "attend_weight": gaussian(key_list[6], (D, 3 * D), (D / 2) ** -0.5, 0.25, ((0, 8), (1, 4)), jnp.float32),
        "attend_moment": gaussian(key_list[7], (D, 3 * D), (2 * TOKENS ** 0.5), 1024.0, ((0, 8), (1, 4)), jnp.float32),
        "attend_square": jnp.clip(jnp.exp(math.log(132096.0) - 1.3862944 * jax.random.uniform(key_list[8], (D, 3 * D), jnp.float32) ** levels(key_list[8], (D, 3 * D), ((0, 8), (1, 4)), -0.2, 0.2)), 33024.0, 132096.0),
        "output_weight": gaussian(key_list[9], (D, D), (max(D // 128, 1)) ** -0.5, 2.0, ((0, 8), (1, 4)), jnp.float32),
        "output_moment": gaussian(key_list[10], (D, D), (0.25 * TOKENS ** 0.5), 128.0, ((0, 8), (1, 4)), jnp.float32),
        "output_square": jnp.clip(jnp.exp(math.log(2064.0) - 1.3862944 * jax.random.uniform(key_list[11], (D, D), jnp.float32) ** levels(key_list[11], (D, D), ((0, 8), (1, 4)), -0.2, 0.2)), 516.0, 2064.0),
        "expand_weight": gaussian(key_list[12], (D, FF), D ** -0.5, 0.1875, ((0, 8), (1, 4)), jnp.float32),
        "expand_moment": gaussian(key_list[13], (D, FF), (0.3 * TOKENS ** 0.5), 160.0, ((0, 8), (1, 4)), jnp.float32),
        "expand_square": jnp.clip(jnp.exp(math.log(2972.16) - 1.3862944 * jax.random.uniform(key_list[14], (D, FF), jnp.float32) ** levels(key_list[14], (D, FF), ((0, 8), (1, 4)), -0.2, 0.2)), 743.04, 2972.16),
        "shrink_weight": gaussian(key_list[15], (FF, D), FF ** -0.5, 0.09375, ((0, 8), (1, 4)), jnp.float32),
        "shrink_moment": gaussian(key_list[16], (FF, D), (0.6 * TOKENS ** 0.5), 320.0, ((0, 8), (1, 4)), jnp.float32),
        "shrink_square": jnp.clip(jnp.exp(math.log(11888.64) - 1.3862944 * jax.random.uniform(key_list[17], (FF, D), jnp.float32) ** levels(key_list[17], (FF, D), ((0, 8), (1, 4)), -0.2, 0.2)), 2972.16, 11888.64),
        "vectors": draw_vectors(jax.random.fold_in(key_list[21], 71), 0),
        "vector_moment": gaussian(key_list[19], (VEC,), (2 * TOKENS ** 0.5), 1024.0, ((0, 4),), jnp.float32),
        "vector_square": jnp.clip(jnp.exp(math.log(132096.0) - 1.3862944 * jax.random.uniform(key_list[20], (VEC,), jnp.float32) ** levels(key_list[20], (VEC,), ((0, 4),), -0.2, 0.2)), 33024.0, 132096.0),
    }


norm_epsilon = 1e-05
adam_epsilon = 1e-08
beta_moment = 0.5
weight_decay = 0.01
rate_merge = 0.04
rate_attend = 0.08
rate_output = 0.6
rate_expand = 0.06
rate_shrink = 0.03
rate_vector = 0.6

@jax.custom_vjp
def low(v):
    return lax.optimization_barrier(v.astype(jnp.bfloat16)).astype(jnp.float32)

@jax.custom_vjp
def low_back(v):
    return v

def low_keep(v):
    return (low(v), None)

def low_pass(kept, grad):
    return (grad,)

def back_keep(v):
    return (v, None)

def back_low(kept, grad):
    return (low(grad),)
low.defvjp(low_keep, low_pass)
low_back.defvjp(back_keep, back_low)

def product(left_side, right_side):
    return jnp.dot(left_side, right_side, precision=lax.Precision.HIGHEST, preferred_element_type=jnp.float32)

def normalize(values):
    centered = values - lax.optimization_barrier(jnp.mean(values, axis=-1, keepdims=True))
    spread = lax.optimization_barrier(jnp.mean(centered * centered, axis=-1, keepdims=True))
    return centered * lax.rsqrt(spread + norm_epsilon)

def forward(inputs, skip_tokens, merge_weight, attend_weight, output_weight, expand_weight, shrink_weight, vectors):
    packed = low(vectors)
    skip_bias = packed[0:D]
    gain_one = packed[D:2 * D]
    bias_one = packed[2 * D:3 * D]
    output_bias = packed[3 * D:4 * D]
    gain_two = packed[4 * D:5 * D]
    bias_two = packed[5 * D:6 * D]
    shrink_bias = packed[6 * D:7 * D]
    expand_bias = packed[7 * D:7 * D + FF]
    groups = inputs.shape[0]
    length = inputs.shape[1]
    joined = jnp.concatenate([inputs, skip_tokens], axis=-1)
    stream = low_back(product(joined, low(merge_weight))) + skip_bias
    normed = low(normalize(stream) * gain_one + bias_one)
    mixed_heads = low(low_back(product(normed, low(attend_weight))))
    query_heads = mixed_heads[..., 0:D].reshape(groups, length, H, HD)
    key_heads = mixed_heads[..., D:2 * D].reshape(groups, length, H, HD)
    value_heads = mixed_heads[..., 2 * D:3 * D].reshape(groups, length, H, HD)
    raw_scores = low_back(jnp.einsum('glhe,gmhe->ghlm', query_heads, key_heads, precision=lax.Precision.HIGHEST))
    softmax_out = jax.nn.softmax(raw_scores * HD ** (-0.5), axis=-1)
    mixture = low(low_back(jnp.einsum('ghlm,gmhe->glhe', low(softmax_out), value_heads, precision=lax.Precision.HIGHEST)))
    mixture = mixture.reshape(groups, length, D)
    stream = stream + low_back(product(mixture, low(output_weight))) + output_bias
    normed_two = low(normalize(stream) * gain_two + bias_two)
    hidden = low_back(product(normed_two, low(expand_weight))) + expand_bias
    active = low(jax.nn.gelu(hidden, approximate=False))
    return stream + low_back(product(active, low(shrink_weight))) + shrink_bias

def adamw_update(weight, moment, square, gradient, step_rate):
    moment_new = beta_moment * moment + (1.0 - beta_moment) * gradient
    square_new = beta_moment * square + (1.0 - beta_moment) * gradient * gradient
    correct = 1.0 - beta_moment ** STEP
    direction = moment_new / correct / (jnp.sqrt(square_new / correct) + adam_epsilon)
    return (weight - step_rate * (direction + weight_decay * weight), moment_new, square_new)

def reference(inputs, skip_tokens, cotangent, merge_weight, merge_moment, merge_square, attend_weight, attend_moment, attend_square, output_weight, output_moment, output_square, expand_weight, expand_moment, expand_square, shrink_weight, shrink_moment, shrink_square, vectors, vector_moment, vector_square):
    weights = (merge_weight, attend_weight, output_weight, expand_weight, shrink_weight, vectors)
    images = inputs.shape[0]
    per_group = 8 if images % 8 == 0 else 1

    def regroup(array):
        return array.astype(jnp.float32).reshape(images // per_group, per_group, array.shape[1], array.shape[2])

    def one_group(totals, pieces):
        first_in, second_in, pulled = pieces
        result, pullback = jax.vjp(forward, first_in, second_in, *weights)
        gradients = pullback(pulled)
        totals = tuple((running + fresh for running, fresh in zip(totals, gradients[2:])))
        return (totals, (result.astype(jnp.bfloat16), gradients[0].astype(jnp.bfloat16), gradients[1].astype(jnp.bfloat16)))
    starts = tuple((jnp.zeros(matrix.shape, jnp.float32) for matrix in weights))
    totals, stacked = lax.scan(one_group, starts, (regroup(inputs), regroup(skip_tokens), regroup(cotangent)))
    outputs = stacked[0].reshape(inputs.shape)
    input_gradient = stacked[1].reshape(inputs.shape)
    skip_gradient = stacked[2].reshape(inputs.shape)
    merge_new = adamw_update(merge_weight, merge_moment, merge_square, totals[0], rate_merge)
    attend_new = adamw_update(attend_weight, attend_moment, attend_square, totals[1], rate_attend)
    output_new = adamw_update(output_weight, output_moment, output_square, totals[2], rate_output)
    expand_new = adamw_update(expand_weight, expand_moment, expand_square, totals[3], rate_expand)
    shrink_new = adamw_update(shrink_weight, shrink_moment, shrink_square, totals[4], rate_shrink)
    vector_new = adamw_update(vectors, vector_moment, vector_square, totals[5], rate_vector)
    return (outputs, input_gradient, skip_gradient, merge_new[0], merge_new[1], merge_new[2], attend_new[0], attend_new[1], attend_new[2], output_new[0], output_new[1], output_new[2], expand_new[0], expand_new[1], expand_new[2], shrink_new[0], shrink_new[1], shrink_new[2], vector_new[0], vector_new[1], vector_new[2])
```

```python
import jax
import jax.numpy as jnp
from jax import lax
from jax.experimental import pallas as pl
from jax.experimental.pallas import tpu as pltpu
from jax.sharding import PartitionSpec as P

D = 1152
FF = 4608
H = 16
HD = 72
STEP = 5


norm_epsilon = 1e-05
adam_epsilon = 1e-08
beta_moment = 0.5
weight_decay = 0.01
rate_merge = 0.04
rate_attend = 0.08
rate_output = 0.6
rate_expand = 0.06
rate_shrink = 0.03
rate_vector = 0.6


def product(left_side, right_side):
    return jnp.dot(left_side, right_side, preferred_element_type=jnp.float32)


def transposed(gradient, matrix):
    return lax.dot_general(
        gradient,
        matrix,
        (((gradient.ndim - 1,), (1,)), ((), ())),
        preferred_element_type=jnp.float32,
    )


def weight_gradient(activations, gradient):
    flat_left = activations.reshape(-1, activations.shape[-1])
    flat_right = gradient.reshape(-1, gradient.shape[-1])
    return lax.dot_general(
        flat_left, flat_right, (((0,), (0,)), ((), ())), preferred_element_type=jnp.float32
    )


def normalize(values):
    centered = values - jnp.mean(values, axis=-1, keepdims=True)
    spread = jnp.mean(centered * centered, axis=-1, keepdims=True)
    inverse = lax.rsqrt(spread + norm_epsilon)
    return (centered * inverse, inverse)


def norm_back(gradient, normed, inverse):
    return inverse * (
        gradient
        - jnp.mean(gradient, axis=-1, keepdims=True)
        - normed * jnp.mean(gradient * normed, axis=-1, keepdims=True)
    )


def row_sum(values):
    return jnp.sum(values, axis=(0, 1))


def unpack(packed):
    return tuple((packed[position * D : (position + 1) * D] for position in range(7))) + (
        packed[7 * D : 7 * D + FF],
    )


def gaussian_unit(values):
    return jax.nn.gelu(values, approximate=False)


def adamw_update(weight, moment, square, gradient, step_rate):
    moment_new = beta_moment * moment + (1.0 - beta_moment) * gradient
    square_new = beta_moment * square + (1.0 - beta_moment) * gradient * gradient
    correct = 1.0 - beta_moment**STEP
    direction = moment_new / correct / (jnp.sqrt(square_new / correct) + adam_epsilon)
    return (weight - step_rate * (direction + weight_decay * weight), moment_new, square_new)


def general_device(
    inputs,
    skip_tokens,
    cotangent,
    merge_weight,
    merge_moment,
    merge_square,
    attend_weight,
    attend_moment,
    attend_square,
    output_weight,
    output_moment,
    output_square,
    expand_weight,
    expand_moment,
    expand_square,
    shrink_weight,
    shrink_moment,
    shrink_square,
    vectors,
    vector_moment,
    vector_square,
):
    merge_low = merge_weight.astype(jnp.bfloat16)
    attend_low = attend_weight.astype(jnp.bfloat16)
    output_low = output_weight.astype(jnp.bfloat16)
    expand_low = expand_weight.astype(jnp.bfloat16)
    shrink_low = shrink_weight.astype(jnp.bfloat16)
    vector_low = vectors.astype(jnp.bfloat16)
    columns = (
        lax.all_gather(merge_low, "narrow", axis=1, tiled=True),
        lax.all_gather(attend_low, "narrow", axis=1, tiled=True),
        lax.all_gather(output_low, "narrow", axis=1, tiled=True),
        lax.all_gather(expand_low, "narrow", axis=1, tiled=True),
        lax.all_gather(shrink_low, "narrow", axis=1, tiled=True),
        lax.all_gather(vector_low, "narrow", axis=0, tiled=True),
    )
    matrices = (
        lax.all_gather(columns[0], "wide", axis=0, tiled=True),
        lax.all_gather(columns[1], "wide", axis=0, tiled=True),
        lax.all_gather(columns[2], "wide", axis=0, tiled=True),
        lax.all_gather(columns[3], "wide", axis=0, tiled=True),
        lax.all_gather(columns[4], "wide", axis=0, tiled=True),
    )
    skip_bias, gain_one, bias_one, output_bias, gain_two, bias_two, shrink_bias, expand_bias = (
        unpack(columns[5].astype(jnp.float32))
    )
    images = inputs.shape[0]
    length = inputs.shape[1]
    softmax_scale = HD ** (-0.5)
    joined = jnp.concatenate([inputs, skip_tokens], axis=-1)
    stream_zero = product(joined, matrices[0]) + skip_bias
    normed_one, inverse_one = normalize(stream_zero)
    attend_input = (normed_one * gain_one + bias_one).astype(jnp.bfloat16)
    mixed_heads = product(attend_input, matrices[1]).astype(jnp.bfloat16)
    query_heads = mixed_heads[..., 0:D].reshape(images, length, H, HD)
    key_heads = mixed_heads[..., D : 2 * D].reshape(images, length, H, HD)
    value_heads = mixed_heads[..., 2 * D : 3 * D].reshape(images, length, H, HD)
    logits = (
        jnp.einsum("blhe,bmhe->bhlm", query_heads, key_heads, preferred_element_type=jnp.float32)
        * softmax_scale
    )
    maxima = jnp.max(logits, axis=-1, keepdims=True)
    log_total = maxima + jnp.log(jnp.sum(jnp.exp(logits - maxima), axis=-1, keepdims=True))
    softmax_low = jnp.exp(logits - log_total).astype(jnp.bfloat16)
    mixture = jnp.einsum(
        "bhlm,bmhe->blhe", softmax_low, value_heads, preferred_element_type=jnp.float32
    )
    mixture = mixture.astype(jnp.bfloat16).reshape(images, length, D)
    stream_one = stream_zero + product(mixture, matrices[2]) + output_bias
    normed_two, inverse_two = normalize(stream_one)
    expand_input = (normed_two * gain_two + bias_two).astype(jnp.bfloat16)
    hidden = product(expand_input, matrices[3]) + expand_bias
    active, pullback = jax.vjp(gaussian_unit, hidden)
    active_low = active.astype(jnp.bfloat16)
    outputs = (stream_one + product(active_low, matrices[4]) + shrink_bias).astype(jnp.bfloat16)
    columns_back = (
        lax.all_gather(merge_low, "narrow", axis=1, tiled=True),
        lax.all_gather(attend_low, "narrow", axis=1, tiled=True),
        lax.all_gather(output_low, "narrow", axis=1, tiled=True),
        lax.all_gather(expand_low, "narrow", axis=1, tiled=True),
        lax.all_gather(shrink_low, "narrow", axis=1, tiled=True),
        lax.all_gather(vector_low, "narrow", axis=0, tiled=True),
    )
    matrices_back = (
        lax.all_gather(columns_back[0], "wide", axis=0, tiled=True),
        lax.all_gather(columns_back[1], "wide", axis=0, tiled=True),
        lax.all_gather(columns_back[2], "wide", axis=0, tiled=True),
        lax.all_gather(columns_back[3], "wide", axis=0, tiled=True),
        lax.all_gather(columns_back[4], "wide", axis=0, tiled=True),
    )
    packed_back = columns_back[5].astype(jnp.float32)
    unpacked = unpack(packed_back)
    gain_first = unpacked[1]
    gain_second = unpacked[4]
    upstream = cotangent.astype(jnp.float32)
    shrink_gradient = weight_gradient(active_low, cotangent)
    delta_active = transposed(cotangent, matrices_back[4])
    delta_hidden = pullback(delta_active)[0]
    hidden_low = delta_hidden.astype(jnp.bfloat16)
    expand_gradient = weight_gradient(expand_input, hidden_low)
    delta_expand = transposed(hidden_low, matrices_back[3])
    delta_one = upstream + norm_back(delta_expand * gain_second, normed_two, inverse_two)
    stream_low = delta_one.astype(jnp.bfloat16)
    output_gradient = weight_gradient(mixture, stream_low)
    delta_mixture = (
        transposed(stream_low, matrices_back[2]).astype(jnp.bfloat16).reshape(images, length, H, HD)
    )
    logits_again = (
        jnp.einsum("blhe,bmhe->bhlm", query_heads, key_heads, preferred_element_type=jnp.float32)
        * softmax_scale
    )
    softmax_again = jnp.exp(logits_again - log_total)
    delta_softmax = jnp.einsum(
        "blhe,bmhe->bhlm", delta_mixture, value_heads, preferred_element_type=jnp.float32
    )
    delta_values = jnp.einsum(
        "bhlm,blhe->bmhe",
        softmax_again.astype(jnp.bfloat16),
        delta_mixture,
        preferred_element_type=jnp.float32,
    )
    delta_logits = softmax_again * (
        delta_softmax - jnp.sum(softmax_again * delta_softmax, axis=-1, keepdims=True)
    )
    delta_scores = (softmax_scale * delta_logits).astype(jnp.bfloat16)
    delta_queries = jnp.einsum(
        "bhlm,bmhe->blhe", delta_scores, key_heads, preferred_element_type=jnp.float32
    )
    delta_keys = jnp.einsum(
        "bhlm,blhe->bmhe", delta_scores, query_heads, preferred_element_type=jnp.float32
    )
    delta_mixed = jnp.concatenate(
        [
            delta_queries.reshape(images, length, D),
            delta_keys.reshape(images, length, D),
            delta_values.reshape(images, length, D),
        ],
        axis=-1,
    ).astype(jnp.bfloat16)
    attend_gradient = weight_gradient(attend_input, delta_mixed)
    delta_attend = transposed(delta_mixed, matrices_back[1])
    delta_zero = delta_one + norm_back(delta_attend * gain_first, normed_one, inverse_one)
    zero_low = delta_zero.astype(jnp.bfloat16)
    merge_gradient = weight_gradient(joined, zero_low)
    delta_joined = transposed(zero_low, matrices_back[0])
    input_gradient = delta_joined[..., 0:D].astype(jnp.bfloat16)
    skip_gradient = delta_joined[..., D : 2 * D].astype(jnp.bfloat16)
    vector_gradient = jnp.concatenate(
        [
            row_sum(delta_zero),
            row_sum(delta_attend * normed_one),
            row_sum(delta_attend),
            row_sum(delta_one),
            row_sum(delta_expand * normed_two),
            row_sum(delta_expand),
            row_sum(upstream),
            row_sum(delta_hidden),
        ]
    )
    owned_rows = (
        lax.psum_scatter(merge_gradient, "wide", scatter_dimension=0, tiled=True),
        lax.psum_scatter(attend_gradient, "wide", scatter_dimension=0, tiled=True),
        lax.psum_scatter(output_gradient, "wide", scatter_dimension=0, tiled=True),
        lax.psum_scatter(expand_gradient, "wide", scatter_dimension=0, tiled=True),
        lax.psum_scatter(shrink_gradient, "wide", scatter_dimension=0, tiled=True),
    )
    vector_total = lax.psum(vector_gradient, "wide")
    parted = (
        lax.psum_scatter(owned_rows[0], "narrow", scatter_dimension=1, tiled=True),
        lax.psum_scatter(owned_rows[1], "narrow", scatter_dimension=1, tiled=True),
        lax.psum_scatter(owned_rows[2], "narrow", scatter_dimension=1, tiled=True),
        lax.psum_scatter(owned_rows[3], "narrow", scatter_dimension=1, tiled=True),
        lax.psum_scatter(owned_rows[4], "narrow", scatter_dimension=1, tiled=True),
        lax.psum_scatter(vector_total, "narrow", scatter_dimension=0, tiled=True),
    )
    merge_new = adamw_update(merge_weight, merge_moment, merge_square, parted[0], rate_merge)
    attend_new = adamw_update(attend_weight, attend_moment, attend_square, parted[1], rate_attend)
    output_new = adamw_update(output_weight, output_moment, output_square, parted[2], rate_output)
    expand_new = adamw_update(expand_weight, expand_moment, expand_square, parted[3], rate_expand)
    shrink_new = adamw_update(shrink_weight, shrink_moment, shrink_square, parted[4], rate_shrink)
    vector_new = adamw_update(vectors, vector_moment, vector_square, parted[5], rate_vector)
    return (
        outputs,
        input_gradient,
        skip_gradient,
        merge_new[0],
        merge_new[1],
        merge_new[2],
        attend_new[0],
        attend_new[1],
        attend_new[2],
        output_new[0],
        output_new[1],
        output_new[2],
        expand_new[0],
        expand_new[1],
        expand_new[2],
        shrink_new[0],
        shrink_new[1],
        shrink_new[2],
        vector_new[0],
        vector_new[1],
        vector_new[2],
    )


CORE = 1
ACROSS = 2
ALONG = 4
VMEM_BYTES = 56 * 1024 * 1024


def swap_wide(value, bit):
    return lax.ppermute(value, "wide", [(i, i ^ bit) for i in range(8)])


def swap_narrow(value, bit):
    return lax.ppermute(value, "narrow", [(i, i ^ bit) for i in range(4)])


def together(*values):
    return lax.optimization_barrier(values)


def spot():
    wide = lax.axis_index("wide")
    narrow = lax.axis_index("narrow")
    return (wide & 1, (wide >> 1) & 1, (wide >> 2) & 1, narrow & 1, narrow >> 1)


def split_rows(rows):
    return -(-rows // 32) * 16


def column_blocks(kind, quarter):
    if kind == "expand":
        width = quarter // 2
        order = [2 * n + p for p in range(2) for n in range(4)]
    elif kind == "attend":
        width = quarter // 6
        order = [8 * part + 2 * n + p for part in range(3) for p in range(2) for n in range(4)]
    else:
        width = quarter // 2
        order = [2 * n + p for p in range(2) for n in range(4)]
    per = quarter // width
    return width, [(block // per, (block % per) * width) for block in order]


def arrange(kind, shard, far, near):
    rows, quarter = shard.shape
    split = split_rows(rows)
    width, blocks = column_blocks(kind, quarter)

    def kernel(shard_ref, far_ref, near_ref, top_ref, bottom_ref, held):
        narrow = lax.axis_index("narrow")
        held[0] = shard_ref[...]
        held[2] = far_ref[...]
        held[1] = near_ref[0]
        held[3] = near_ref[1]
        for number in range(4):
            value = held[narrow ^ number]
            for position, (owner, offset) in enumerate(blocks):
                if owner == number:
                    column = position * width
                    piece = value[:, offset : offset + width]
                    top_ref[:, column : column + width] = piece[:split]
                    bottom_ref[:, column : column + width] = piece[split:]

    return pl.pallas_call(
        kernel,
        out_shape=(
            jax.ShapeDtypeStruct((split, 4 * quarter), jnp.bfloat16),
            jax.ShapeDtypeStruct((rows - split, 4 * quarter), jnp.bfloat16),
        ),
        scratch_shapes=[pltpu.VMEM((4, rows, quarter), jnp.bfloat16)],
        compiler_params=pltpu.CompilerParams(vmem_limit_bytes=VMEM_BYTES),
        cost_estimate=pl.CostEstimate(
            flops=0, bytes_accessed=16 * rows * quarter, transcendentals=0
        ),
    )(shard, far, near)


def place(pieces):
    split, columns = pieces[0].shape
    rows = split + pieces[1].shape[0]

    def kernel(*refs):
        full = refs[8]
        chip = lax.axis_index("wide") >> 1
        for relative in range(4):
            start = (chip ^ relative) * rows
            top, bottom = refs[2 * relative], refs[2 * relative + 1]
            full[pl.ds(pl.multiple_of(start, 16), split)] = top[...]
            full[pl.ds(pl.multiple_of(start + split, 16), rows - split)] = bottom[...]

    return pl.pallas_call(
        kernel,
        out_shape=jax.ShapeDtypeStruct((4 * rows, columns), jnp.bfloat16),
        compiler_params=pltpu.CompilerParams(vmem_limit_bytes=VMEM_BYTES),
        cost_estimate=pl.CostEstimate(
            flops=0, bytes_accessed=16 * rows * columns, transcendentals=0
        ),
    )(*pieces)


def unarrange(kind, kept_top, got_top, kept_bottom, got_bottom):
    split, columns = kept_top.shape
    rows = split + kept_bottom.shape[0]
    quarter = columns // 4
    width, blocks = column_blocks(kind, quarter)

    def kernel(kept_top_ref, got_top_ref, kept_bottom_ref, got_bottom_ref, keep_ref, send_ref, held):
        low_bit = lax.axis_index("narrow") & 1
        held[:split] = add_low(kept_top_ref[...], got_top_ref[...])
        held[split:] = add_low(kept_bottom_ref[...], got_bottom_ref[...])
        for position, (owner, offset) in enumerate(blocks):
            piece = held[:, position * width : (position + 1) * width]
            high = owner >> 1

            @pl.when(low_bit == (owner & 1))
            def _():
                keep_ref[high, :, offset : offset + width] = piece

            @pl.when(low_bit != (owner & 1))
            def _():
                send_ref[high, :, offset : offset + width] = piece

    shape = jax.ShapeDtypeStruct((2, rows, quarter), jnp.bfloat16)
    return pl.pallas_call(
        kernel,
        out_shape=(shape, shape),
        scratch_shapes=[pltpu.VMEM((rows, columns), jnp.bfloat16)],
        compiler_params=pltpu.CompilerParams(vmem_limit_bytes=VMEM_BYTES),
        cost_estimate=pl.CostEstimate(
            flops=0, bytes_accessed=8 * rows * columns, transcendentals=0
        ),
    )(kept_top, got_top, kept_bottom, got_bottom)


def add_low(left, right):
    return (left.astype(jnp.float32) + right.astype(jnp.float32)).astype(jnp.bfloat16)


def pick(value, index, dim):
    return lax.dynamic_index_in_dim(value, index, dim, keepdims=False)


def halves_of(value, core):
    middle = value.shape[-1] // 2
    first, second = value[..., :middle], value[..., middle:]
    return jnp.where(core == 0, first, second), jnp.where(core == 0, second, first)


def whole_of(mine, other, core):
    return jnp.concatenate(
        [jnp.where(core == 0, mine, other), jnp.where(core == 0, other, mine)], axis=-1
    )


def inner(value):
    width = value.shape[-1] // 8
    return jnp.concatenate(
        [
            value[..., (2 * n + p) * width : (2 * n + p + 1) * width]
            for p in range(2)
            for n in range(4)
        ],
        axis=-1,
    )


def outer(value):
    width = value.shape[-1] // 8
    return jnp.concatenate(
        [
            value[..., (4 * p + n) * width : (4 * p + n + 1) * width]
            for n in range(4)
            for p in range(2)
        ],
        axis=-1,
    )


def across_first(top, bottom):
    return swap_wide(top, ACROSS), swap_wide(bottom, ALONG)


def across_second(top, bottom, top_x, bottom_y):
    return (
        swap_wide(top, ALONG),
        swap_wide(bottom, ACROSS),
        swap_wide(top_x, ALONG),
        swap_wide(bottom_y, ACROSS),
    )


def placed(top, bottom, first, second):
    return place(
        [top, bottom, first[0], second[1], second[0], first[1], second[2], second[3]]
    )


def pair_gradient(left, left_sibling, right, right_sibling):
    both_left = jnp.concatenate([left, left_sibling], axis=0)
    both_right = jnp.concatenate([right, right_sibling], axis=0)
    total = lax.dot_general(
        both_left, both_right, (((0,), (0,)), ((), ())), preferred_element_type=jnp.float32
    )
    return total.astype(jnp.bfloat16).reshape(2, 2, left.shape[1] // 4, right.shape[1])


def scatter_first(blocks):
    _, across, along = spot()[:3]
    split = split_rows(blocks.shape[2])
    top, bottom = blocks[:, :, :split], blocks[:, :, split:]
    kept = (pick(top, across, 1), pick(bottom, along, 0))
    got = (
        swap_wide(pick(top, 1 - across, 1), ACROSS),
        swap_wide(pick(bottom, 1 - along, 0), ALONG),
    )
    return kept, got


def scatter_second(state):
    _, across, along = spot()[:3]
    kept, got = state
    top, bottom = add_low(kept[0], got[0]), add_low(kept[1], got[1])
    return (pick(top, along, 0), pick(bottom, across, 0)), (
        swap_wide(pick(top, 1 - along, 0), ALONG),
        swap_wide(pick(bottom, 1 - across, 0), ACROSS),
    )


def scatter_third(kind, state):
    kept, got = state
    keep, send = unarrange(kind, kept[0], got[0], kept[1], got[1])
    return keep, swap_narrow(send, 1)


def scatter_fourth(state):
    high_bit = spot()[4]
    kept, got = state
    part = add_low(kept, got)
    return pick(part, high_bit, 0), swap_narrow(pick(part, 1 - high_bit, 0), 2)


def scatter_last(state):
    return state[0].astype(jnp.float32) + state[1].astype(jnp.float32)


def gather_vector(far, near, vector):
    low_bit, high_bit = spot()[3:]
    own = jnp.stack([vector, far])
    own = jnp.where(high_bit == 0, own, own[::-1])
    near = jnp.where(high_bit == 0, near, near[::-1])
    even = jnp.where(low_bit == 0, own, near)
    odd = jnp.where(low_bit == 0, near, own)
    return jnp.concatenate([even[0], odd[0], even[1], odd[1]])


def scatter_vector(vector):
    low_bit, high_bit = spot()[3:]
    total = vector + swap_wide(vector, CORE)
    total = total + swap_wide(total, ACROSS)
    total = total + swap_wide(total, ALONG)
    halves = total.reshape(2, -1)
    total = pick(halves, high_bit, 0) + swap_narrow(pick(halves, 1 - high_bit, 0), 2)
    halves = total.reshape(2, -1)
    return pick(halves, low_bit, 0) + swap_narrow(pick(halves, 1 - low_bit, 0), 1)


def inner_dot(activations, mine, other, core):
    left, right = halves_of(activations, core)
    return product(left, mine) + product(right, other)


def inner_back(gradient, mine, other, core):
    return whole_of(transposed(gradient, mine), transposed(gradient, other), core)


def on_device(
    inputs,
    skip_tokens,
    cotangent,
    merge_weight,
    merge_moment,
    merge_square,
    attend_weight,
    attend_moment,
    attend_square,
    output_weight,
    output_moment,
    output_square,
    expand_weight,
    expand_moment,
    expand_square,
    shrink_weight,
    shrink_moment,
    shrink_square,
    vectors,
    vector_moment,
    vector_square,
):
    core = spot()[0]
    low = jnp.bfloat16
    merge_low = merge_weight.astype(low)
    attend_low = attend_weight.astype(low)
    output_low = output_weight.astype(low)
    expand_low = expand_weight.astype(low)
    shrink_low = shrink_weight.astype(low)
    vector_low = vectors.astype(low)
    length = inputs.shape[1]
    softmax_scale = HD ** (-0.5)

    merge_far = swap_narrow(merge_low, 2)
    vector_far = swap_narrow(vector_low, 2)
    joined = inner(jnp.concatenate([inputs[0], skip_tokens[0]], axis=-1))
    pulled = inner(cotangent[0])
    merge_far, vector_far, joined, pulled, attend_low, output_low = together(
        merge_far, vector_far, joined, pulled, attend_low, output_low
    )
    merge_near = swap_narrow(jnp.stack([merge_low, merge_far]), 1)
    vector_near = swap_narrow(jnp.stack([vector_low, vector_far]), 1)
    attend_far = swap_narrow(attend_low, 2)
    output_far = swap_narrow(output_low, 2)
    joined_mine, joined_other = halves_of(joined, core)
    joined_sibling = swap_wide(joined_other, CORE)
    pulled_sibling = swap_wide(pulled, CORE)
    (
        merge_near,
        vector_near,
        attend_far,
        output_far,
        joined_sibling,
        pulled_sibling,
        joined_mine,
        joined_other,
        expand_low,
    ) = together(
        merge_near,
        vector_near,
        attend_far,
        output_far,
        joined_sibling,
        pulled_sibling,
        joined_mine,
        joined_other,
        expand_low,
    )
    merge_top, merge_bottom = arrange("merge", merge_low, merge_far, merge_near)
    merge_first = across_first(merge_top, merge_bottom)
    attend_near = swap_narrow(jnp.stack([attend_low, attend_far]), 1)
    output_near = swap_narrow(jnp.stack([output_low, output_far]), 1)
    pieces = unpack(gather_vector(vector_far, vector_near, vector_low).astype(jnp.float32))
    pieces = tuple(inner(piece) for piece in pieces)
    merge_first, attend_near, output_near, pieces, expand_low = together(
        merge_first, attend_near, output_near, pieces, expand_low
    )
    skip_bias, gain_one, bias_one, output_bias, gain_two, bias_two, shrink_bias, expand_bias = pieces
    merge_second = across_second(merge_top, merge_bottom, *merge_first)
    expand_far = swap_narrow(expand_low, 2)
    attend_top, attend_bottom = arrange("attend", attend_low, attend_far, attend_near)
    output_top, output_bottom = arrange("output", output_low, output_far, output_near)
    merge_second, expand_far, attend_top, attend_bottom, output_top, output_bottom = together(
        merge_second, expand_far, attend_top, attend_bottom, output_top, output_bottom
    )
    attend_first = across_first(attend_top, attend_bottom)
    output_first = across_first(output_top, output_bottom)
    expand_near = swap_narrow(jnp.stack([expand_low, expand_far]), 1)
    merge_mine = placed(merge_top, merge_bottom, merge_first, merge_second)
    merge_other = swap_wide(merge_mine, CORE)
    attend_first, output_first, expand_near, merge_mine, merge_other, shrink_low = together(
        attend_first, output_first, expand_near, merge_mine, merge_other, shrink_low
    )
    attend_second = across_second(attend_top, attend_bottom, *attend_first)
    output_second = across_second(output_top, output_bottom, *output_first)
    shrink_far = swap_narrow(shrink_low, 2)
    expand_top, expand_bottom = arrange("expand", expand_low, expand_far, expand_near)
    stream_zero = product(joined_mine, merge_mine) + product(joined_other, merge_other) + skip_bias
    normed_one, inverse_one = normalize(stream_zero)
    attend_input = (normed_one * gain_one + bias_one).astype(low)
    (
        attend_second,
        output_second,
        shrink_far,
        expand_top,
        expand_bottom,
        stream_zero,
        normed_one,
        inverse_one,
        attend_input,
    ) = together(
        attend_second,
        output_second,
        shrink_far,
        expand_top,
        expand_bottom,
        stream_zero,
        normed_one,
        inverse_one,
        attend_input,
    )
    expand_first = across_first(expand_top, expand_bottom)
    shrink_near = swap_narrow(jnp.stack([shrink_low, shrink_far]), 1)
    attend_mine = placed(attend_top, attend_bottom, attend_first, attend_second)
    attend_other = swap_wide(attend_mine, CORE)
    output_mine = placed(output_top, output_bottom, output_first, output_second)
    output_other = swap_wide(output_mine, CORE)
    attend_input_mine, attend_input_other = halves_of(attend_input, core)
    attend_input_sibling = swap_wide(attend_input_other, CORE)
    (
        expand_first,
        shrink_near,
        attend_mine,
        attend_other,
        output_mine,
        output_other,
        attend_input_mine,
        attend_input_other,
        attend_input_sibling,
    ) = together(
        expand_first,
        shrink_near,
        attend_mine,
        attend_other,
        output_mine,
        output_other,
        attend_input_mine,
        attend_input_other,
        attend_input_sibling,
    )
    expand_second = across_second(expand_top, expand_bottom, *expand_first)
    shrink_top, shrink_bottom = arrange("shrink", shrink_low, shrink_far, shrink_near)
    mixed_heads = (
        product(attend_input_mine, attend_mine) + product(attend_input_other, attend_other)
    ).astype(low)
    query_heads = mixed_heads[..., 0:D].reshape(1, length, H, HD)
    key_heads = mixed_heads[..., D : 2 * D].reshape(1, length, H, HD)
    value_heads = mixed_heads[..., 2 * D : 3 * D].reshape(1, length, H, HD)
    logits = (
        jnp.einsum("blhe,bmhe->bhlm", query_heads, key_heads, preferred_element_type=jnp.float32)
        * softmax_scale
    )
    maxima = jnp.max(logits, axis=-1, keepdims=True)
    log_total = maxima + jnp.log(jnp.sum(jnp.exp(logits - maxima), axis=-1, keepdims=True))
    softmax_low = jnp.exp(logits - log_total).astype(low)
    mixture = jnp.einsum(
        "bhlm,bmhe->blhe", softmax_low, value_heads, preferred_element_type=jnp.float32
    )
    mixture = mixture.astype(low).reshape(length, D)
    mixture_mine, mixture_other = halves_of(mixture, core)
    stream_one = (
        stream_zero
        + (product(mixture_mine, output_mine) + product(mixture_other, output_other))
        + output_bias
    )
    normed_two, inverse_two = normalize(stream_one)
    expand_input = (normed_two * gain_two + bias_two).astype(low)
    (
        expand_second,
        shrink_top,
        shrink_bottom,
        stream_one,
        normed_two,
        inverse_two,
        expand_input,
        mixture_mine,
        mixture_other,
    ) = together(
        expand_second,
        shrink_top,
        shrink_bottom,
        stream_one,
        normed_two,
        inverse_two,
        expand_input,
        mixture_mine,
        mixture_other,
    )
    shrink_first = across_first(shrink_top, shrink_bottom)
    mixture_sibling = swap_wide(mixture_other, CORE)
    expand_input_mine, expand_input_other = halves_of(expand_input, core)
    expand_input_sibling = swap_wide(expand_input_other, CORE)
    expand_mine = placed(expand_top, expand_bottom, expand_first, expand_second)
    expand_other = swap_wide(expand_mine, CORE)
    expand_input_mine, expand_input_other, expand_mine, expand_other = together(
        expand_input_mine, expand_input_other, expand_mine, expand_other
    )
    hidden = (
        product(expand_input_mine, expand_mine) + product(expand_input_other, expand_other)
    ) + expand_bias
    active, pullback = jax.vjp(gaussian_unit, hidden)
    active_low = active.astype(low)
    slope = pullback(jnp.ones_like(hidden))[0]
    shrink_first, mixture_sibling, expand_input_sibling, active_low, slope = together(
        shrink_first, mixture_sibling, expand_input_sibling, active_low, slope
    )
    shrink_second = across_second(shrink_top, shrink_bottom, *shrink_first)
    active_mine, active_other = halves_of(active_low, core)
    active_sibling = swap_wide(active_other, CORE)
    active_mine, active_other, active_sibling = together(active_mine, active_other, active_sibling)
    shrink_gradient = pair_gradient(active_mine, active_sibling, pulled, pulled_sibling)
    shrink_second, shrink_gradient, active_mine, active_other, slope = together(
        shrink_second, shrink_gradient, active_mine, active_other, slope
    )
    shrink_mine = placed(shrink_top, shrink_bottom, shrink_first, shrink_second)
    shrink_other = swap_wide(shrink_mine, CORE)
    shrink_parts = scatter_first(shrink_gradient)
    delta_hidden = inner_back(pulled, shrink_mine, shrink_other, core) * slope
    hidden_low = delta_hidden.astype(low)
    hidden_sum = jnp.sum(delta_hidden, axis=0)
    hidden_low, hidden_sum = together(hidden_low, hidden_sum)
    hidden_sibling = swap_wide(hidden_low, CORE)
    delta_expand = inner_back(hidden_low, expand_mine, expand_other, core)
    hidden_sibling, delta_expand = together(hidden_sibling, delta_expand)
    expand_gradient = pair_gradient(
        expand_input_mine, expand_input_sibling, hidden_low, hidden_sibling
    )
    upstream = pulled.astype(jnp.float32)
    delta_one = upstream + norm_back(delta_expand * gain_two, normed_two, inverse_two)
    stream_low = delta_one.astype(low)
    sums_two = (
        jnp.sum(delta_one, axis=0),
        jnp.sum(delta_expand * normed_two, axis=0),
        jnp.sum(delta_expand, axis=0),
    )
    shrink_parts, expand_gradient, delta_one, stream_low, sums_two = together(
        shrink_parts, expand_gradient, delta_one, stream_low, sums_two
    )
    shrink_parts = scatter_second(shrink_parts)
    expand_parts = scatter_first(expand_gradient)
    stream_sibling = swap_wide(stream_low, CORE)
    delta_mixture = (
        inner_back(stream_low, output_mine, output_other, core)
        .astype(low)
        .reshape(1, length, H, HD)
    )
    logits_again = (
        jnp.einsum("blhe,bmhe->bhlm", query_heads, key_heads, preferred_element_type=jnp.float32)
        * softmax_scale
    )
    softmax_again = jnp.exp(logits_again - log_total)
    delta_softmax = jnp.einsum(
        "blhe,bmhe->bhlm", delta_mixture, value_heads, preferred_element_type=jnp.float32
    )
    delta_values = jnp.einsum(
        "bhlm,blhe->bmhe",
        softmax_again.astype(low),
        delta_mixture,
        preferred_element_type=jnp.float32,
    )
    delta_logits = softmax_again * (
        delta_softmax - jnp.sum(softmax_again * delta_softmax, axis=-1, keepdims=True)
    )
    delta_scores = (softmax_scale * delta_logits).astype(low)
    delta_queries = jnp.einsum(
        "bhlm,bmhe->blhe", delta_scores, key_heads, preferred_element_type=jnp.float32
    )
    delta_keys = jnp.einsum(
        "bhlm,blhe->bmhe", delta_scores, query_heads, preferred_element_type=jnp.float32
    )
    delta_mixed = jnp.concatenate(
        [
            delta_queries.reshape(length, D),
            delta_keys.reshape(length, D),
            delta_values.reshape(length, D),
        ],
        axis=-1,
    ).astype(low)
    shrink_parts, expand_parts, stream_sibling, delta_mixed = together(
        shrink_parts, expand_parts, stream_sibling, delta_mixed
    )
    shrink_parts = scatter_third("shrink", shrink_parts)
    expand_parts = scatter_second(expand_parts)
    mixed_sibling = swap_wide(delta_mixed, CORE)
    output_gradient = pair_gradient(mixture_mine, mixture_sibling, stream_low, stream_sibling)
    delta_attend = inner_back(delta_mixed, attend_mine, attend_other, core)
    mixed_sibling, delta_attend, output_gradient = together(
        mixed_sibling, delta_attend, output_gradient
    )
    attend_gradient = pair_gradient(
        attend_input_mine, attend_input_sibling, delta_mixed, mixed_sibling
    )
    shrink_parts, expand_parts, attend_gradient, output_gradient, delta_attend = together(
        shrink_parts, expand_parts, attend_gradient, output_gradient, delta_attend
    )
    shrink_parts = scatter_fourth(shrink_parts)
    expand_parts = scatter_third("expand", expand_parts)
    attend_parts = scatter_first(attend_gradient)
    output_parts = scatter_first(output_gradient)
    delta_zero = delta_one + norm_back(delta_attend * gain_one, normed_one, inverse_one)
    zero_low = delta_zero.astype(low)
    zero_sibling = swap_wide(zero_low, CORE)
    vector_gradient = jnp.concatenate(
        [
            outer(jnp.sum(delta_zero, axis=0)),
            outer(jnp.sum(delta_attend * normed_one, axis=0)),
            outer(jnp.sum(delta_attend, axis=0)),
            outer(sums_two[0]),
            outer(sums_two[1]),
            outer(sums_two[2]),
            outer(jnp.sum(upstream, axis=0)),
            outer(hidden_sum),
        ]
    )
    zero_low, zero_sibling = together(zero_low, zero_sibling)
    merge_gradient = pair_gradient(joined_mine, joined_sibling, zero_low, zero_sibling)
    shrink_parts, expand_parts, attend_parts, output_parts, merge_gradient, vector_gradient = (
        together(
            shrink_parts, expand_parts, attend_parts, output_parts, merge_gradient, vector_gradient
        )
    )
    merge_parts = scatter_first(merge_gradient)
    attend_parts = scatter_second(attend_parts)
    output_parts = scatter_second(output_parts)
    expand_parts = scatter_fourth(expand_parts)
    vector_total = scatter_vector(vector_gradient)
    shrink_new = adamw_update(
        shrink_weight, shrink_moment, shrink_square, scatter_last(shrink_parts), rate_shrink
    )
    outputs = outer(
        (
            stream_one
            + (product(active_mine, shrink_mine) + product(active_other, shrink_other))
            + shrink_bias
        ).astype(low)
    )[None]
    merge_parts, attend_parts, output_parts, expand_parts, shrink_new, outputs = together(
        merge_parts, attend_parts, output_parts, expand_parts, shrink_new, outputs
    )
    merge_parts = scatter_second(merge_parts)
    attend_parts = scatter_third("attend", attend_parts)
    output_parts = scatter_third("output", output_parts)
    delta_joined = outer(inner_back(zero_low, merge_mine, merge_other, core).astype(low))
    input_gradient = delta_joined[None, :, 0:D]
    skip_gradient = delta_joined[None, :, D : 2 * D]
    merge_parts, attend_parts, output_parts, input_gradient, skip_gradient = together(
        merge_parts, attend_parts, output_parts, input_gradient, skip_gradient
    )
    merge_parts = scatter_third("merge", merge_parts)
    attend_parts = scatter_fourth(attend_parts)
    output_parts = scatter_fourth(output_parts)
    expand_new = adamw_update(
        expand_weight, expand_moment, expand_square, scatter_last(expand_parts), rate_expand
    )
    merge_parts, attend_parts, output_parts, expand_new = together(
        merge_parts, attend_parts, output_parts, expand_new
    )
    merge_parts = scatter_fourth(merge_parts)
    attend_new = adamw_update(
        attend_weight, attend_moment, attend_square, scatter_last(attend_parts), rate_attend
    )
    output_new = adamw_update(
        output_weight, output_moment, output_square, scatter_last(output_parts), rate_output
    )
    merge_new = adamw_update(
        merge_weight, merge_moment, merge_square, scatter_last(merge_parts), rate_merge
    )
    vector_new = adamw_update(vectors, vector_moment, vector_square, vector_total, rate_vector)
    return (
        outputs,
        input_gradient,
        skip_gradient,
        *merge_new,
        *attend_new,
        *output_new,
        *expand_new,
        *shrink_new,
        *vector_new,
    )


def solution(mesh):
    in_specs = (
        P(("wide", "narrow"), None, None),
        P(("wide", "narrow"), None, None),
        P(("wide", "narrow"), None, None),
        P("wide", "narrow"),
        P("wide", "narrow"),
        P("wide", "narrow"),
        P("wide", "narrow"),
        P("wide", "narrow"),
        P("wide", "narrow"),
        P("wide", "narrow"),
        P("wide", "narrow"),
        P("wide", "narrow"),
        P("wide", "narrow"),
        P("wide", "narrow"),
        P("wide", "narrow"),
        P("wide", "narrow"),
        P("wide", "narrow"),
        P("wide", "narrow"),
        P("narrow"),
        P("narrow"),
        P("narrow"),
    )
    out_specs = (
        P(("wide", "narrow"), None, None),
        P(("wide", "narrow"), None, None),
        P(("wide", "narrow"), None, None),
        P("wide", "narrow"),
        P("wide", "narrow"),
        P("wide", "narrow"),
        P("wide", "narrow"),
        P("wide", "narrow"),
        P("wide", "narrow"),
        P("wide", "narrow"),
        P("wide", "narrow"),
        P("wide", "narrow"),
        P("wide", "narrow"),
        P("wide", "narrow"),
        P("wide", "narrow"),
        P("wide", "narrow"),
        P("wide", "narrow"),
        P("wide", "narrow"),
        P("narrow"),
        P("narrow"),
        P("narrow"),
    )
    tuned = mesh.shape["wide"] == 8 and mesh.shape["narrow"] == 4
    return jax.shard_map(
        on_device if tuned else general_device, mesh=mesh, in_specs=in_specs, out_specs=out_specs, check_vma=False
    )
```

```python
import jax
import jax.numpy as jnp
from jax import lax
from jax.experimental import pallas as pl
from jax.experimental.pallas import tpu as pltpu
from jax.sharding import PartitionSpec as P

D = 1152
FF = 4608
H = 16
HD = 72
STEP = 5


norm_epsilon = 1e-05
adam_epsilon = 1e-08
beta_moment = 0.5
weight_decay = 0.01
rate_merge = 0.04
rate_attend = 0.08
rate_output = 0.6
rate_expand = 0.06
rate_shrink = 0.03
rate_vector = 0.6


def product(left_side, right_side):
    return jnp.dot(left_side, right_side, preferred_element_type=jnp.float32)


def transposed(gradient, matrix):
    return lax.dot_general(
        gradient,
        matrix,
        (((gradient.ndim - 1,), (1,)), ((), ())),
        preferred_element_type=jnp.float32,
    )


def weight_gradient(activations, gradient):
    flat_left = activations.reshape(-1, activations.shape[-1])
    flat_right = gradient.reshape(-1, gradient.shape[-1])
    return lax.dot_general(
        flat_left, flat_right, (((0,), (0,)), ((), ())), preferred_element_type=jnp.float32
    )


def normalize(values):
    centered = values - jnp.mean(values, axis=-1, keepdims=True)
    spread = jnp.mean(centered * centered, axis=-1, keepdims=True)
    inverse = lax.rsqrt(spread + norm_epsilon)
    return (centered * inverse, inverse)


def norm_back(gradient, normed, inverse):
    return inverse * (
        gradient
        - jnp.mean(gradient, axis=-1, keepdims=True)
        - normed * jnp.mean(gradient * normed, axis=-1, keepdims=True)
    )


def row_sum(values):
    return jnp.sum(values, axis=(0, 1))


def unpack(packed):
    return tuple((packed[position * D : (position + 1) * D] for position in range(7))) + (
        packed[7 * D : 7 * D + FF],
    )


def gaussian_unit(values):
    return jax.nn.gelu(values, approximate=False)


def adamw_update(weight, moment, square, gradient, step_rate):
    moment_new = beta_moment * moment + (1.0 - beta_moment) * gradient
    square_new = beta_moment * square + (1.0 - beta_moment) * gradient * gradient
    correct = 1.0 - beta_moment**STEP
    direction = moment_new / correct / (jnp.sqrt(square_new / correct) + adam_epsilon)
    return (weight - step_rate * (direction + weight_decay * weight), moment_new, square_new)


def general_device(
    inputs,
    skip_tokens,
    cotangent,
    merge_weight,
    merge_moment,
    merge_square,
    attend_weight,
    attend_moment,
    attend_square,
    output_weight,
    output_moment,
    output_square,
    expand_weight,
    expand_moment,
    expand_square,
    shrink_weight,
    shrink_moment,
    shrink_square,
    vectors,
    vector_moment,
    vector_square,
):
    merge_low = merge_weight.astype(jnp.bfloat16)
    attend_low = attend_weight.astype(jnp.bfloat16)
    output_low = output_weight.astype(jnp.bfloat16)
    expand_low = expand_weight.astype(jnp.bfloat16)
    shrink_low = shrink_weight.astype(jnp.bfloat16)
    vector_low = vectors.astype(jnp.bfloat16)
    columns = (
        lax.all_gather(merge_low, "narrow", axis=1, tiled=True),
        lax.all_gather(attend_low, "narrow", axis=1, tiled=True),
        lax.all_gather(output_low, "narrow", axis=1, tiled=True),
        lax.all_gather(expand_low, "narrow", axis=1, tiled=True),
        lax.all_gather(shrink_low, "narrow", axis=1, tiled=True),
        lax.all_gather(vector_low, "narrow", axis=0, tiled=True),
    )
    matrices = (
        lax.all_gather(columns[0], "wide", axis=0, tiled=True),
        lax.all_gather(columns[1], "wide", axis=0, tiled=True),
        lax.all_gather(columns[2], "wide", axis=0, tiled=True),
        lax.all_gather(columns[3], "wide", axis=0, tiled=True),
        lax.all_gather(columns[4], "wide", axis=0, tiled=True),
    )
    skip_bias, gain_one, bias_one, output_bias, gain_two, bias_two, shrink_bias, expand_bias = (
        unpack(columns[5].astype(jnp.float32))
    )
    images = inputs.shape[0]
    length = inputs.shape[1]
    softmax_scale = HD ** (-0.5)
    joined = jnp.concatenate([inputs, skip_tokens], axis=-1)
    stream_zero = product(joined, matrices[0]) + skip_bias
    normed_one, inverse_one = normalize(stream_zero)
    attend_input = (normed_one * gain_one + bias_one).astype(jnp.bfloat16)
    mixed_heads = product(attend_input, matrices[1]).astype(jnp.bfloat16)
    query_heads = mixed_heads[..., 0:D].reshape(images, length, H, HD)
    key_heads = mixed_heads[..., D : 2 * D].reshape(images, length, H, HD)
    value_heads = mixed_heads[..., 2 * D : 3 * D].reshape(images, length, H, HD)
    logits = (
        jnp.einsum("blhe,bmhe->bhlm", query_heads, key_heads, preferred_element_type=jnp.float32)
        * softmax_scale
    )
    maxima = jnp.max(logits, axis=-1, keepdims=True)
    log_total = maxima + jnp.log(jnp.sum(jnp.exp(logits - maxima), axis=-1, keepdims=True))
    softmax_low = jnp.exp(logits - log_total).astype(jnp.bfloat16)
    mixture = jnp.einsum(
        "bhlm,bmhe->blhe", softmax_low, value_heads, preferred_element_type=jnp.float32
    )
    mixture = mixture.astype(jnp.bfloat16).reshape(images, length, D)
    stream_one = stream_zero + product(mixture, matrices[2]) + output_bias
    normed_two, inverse_two = normalize(stream_one)
    expand_input = (normed_two * gain_two + bias_two).astype(jnp.bfloat16)
    hidden = product(expand_input, matrices[3]) + expand_bias
    active, pullback = jax.vjp(gaussian_unit, hidden)
    active_low = active.astype(jnp.bfloat16)
    outputs = (stream_one + product(active_low, matrices[4]) + shrink_bias).astype(jnp.bfloat16)
    columns_back = (
        lax.all_gather(merge_low, "narrow", axis=1, tiled=True),
        lax.all_gather(attend_low, "narrow", axis=1, tiled=True),
        lax.all_gather(output_low, "narrow", axis=1, tiled=True),
        lax.all_gather(expand_low, "narrow", axis=1, tiled=True),
        lax.all_gather(shrink_low, "narrow", axis=1, tiled=True),
        lax.all_gather(vector_low, "narrow", axis=0, tiled=True),
    )
    matrices_back = (
        lax.all_gather(columns_back[0], "wide", axis=0, tiled=True),
        lax.all_gather(columns_back[1], "wide", axis=0, tiled=True),
        lax.all_gather(columns_back[2], "wide", axis=0, tiled=True),
        lax.all_gather(columns_back[3], "wide", axis=0, tiled=True),
        lax.all_gather(columns_back[4], "wide", axis=0, tiled=True),
    )
    packed_back = columns_back[5].astype(jnp.float32)
    unpacked = unpack(packed_back)
    gain_first = unpacked[1]
    gain_second = unpacked[4]
    upstream = cotangent.astype(jnp.float32)
    shrink_gradient = weight_gradient(active_low, cotangent)
    delta_active = transposed(cotangent, matrices_back[4])
    delta_hidden = pullback(delta_active)[0]
    hidden_low = delta_hidden.astype(jnp.bfloat16)
    expand_gradient = weight_gradient(expand_input, hidden_low)
    delta_expand = transposed(hidden_low, matrices_back[3])
    delta_one = upstream + norm_back(delta_expand * gain_second, normed_two, inverse_two)
    stream_low = delta_one.astype(jnp.bfloat16)
    output_gradient = weight_gradient(mixture, stream_low)
    delta_mixture = (
        transposed(stream_low, matrices_back[2]).astype(jnp.bfloat16).reshape(images, length, H, HD)
    )
    logits_again = (
        jnp.einsum("blhe,bmhe->bhlm", query_heads, key_heads, preferred_element_type=jnp.float32)
        * softmax_scale
    )
    softmax_again = jnp.exp(logits_again - log_total)
    delta_softmax = jnp.einsum(
        "blhe,bmhe->bhlm", delta_mixture, value_heads, preferred_element_type=jnp.float32
    )
    delta_values = jnp.einsum(
        "bhlm,blhe->bmhe",
        softmax_again.astype(jnp.bfloat16),
        delta_mixture,
        preferred_element_type=jnp.float32,
    )
    delta_logits = softmax_again * (
        delta_softmax - jnp.sum(softmax_again * delta_softmax, axis=-1, keepdims=True)
    )
    delta_scores = (softmax_scale * delta_logits).astype(jnp.bfloat16)
    delta_queries = jnp.einsum(
        "bhlm,bmhe->blhe", delta_scores, key_heads, preferred_element_type=jnp.float32
    )
    delta_keys = jnp.einsum(
        "bhlm,blhe->bmhe", delta_scores, query_heads, preferred_element_type=jnp.float32
    )
    delta_mixed = jnp.concatenate(
        [
            delta_queries.reshape(images, length, D),
            delta_keys.reshape(images, length, D),
            delta_values.reshape(images, length, D),
        ],
        axis=-1,
    ).astype(jnp.bfloat16)
    attend_gradient = weight_gradient(attend_input, delta_mixed)
    delta_attend = transposed(delta_mixed, matrices_back[1])
    delta_zero = delta_one + norm_back(delta_attend * gain_first, normed_one, inverse_one)
    zero_low = delta_zero.astype(jnp.bfloat16)
    merge_gradient = weight_gradient(joined, zero_low)
    delta_joined = transposed(zero_low, matrices_back[0])
    input_gradient = delta_joined[..., 0:D].astype(jnp.bfloat16)
    skip_gradient = delta_joined[..., D : 2 * D].astype(jnp.bfloat16)
    vector_gradient = jnp.concatenate(
        [
            row_sum(delta_zero),
            row_sum(delta_attend * normed_one),
            row_sum(delta_attend),
            row_sum(delta_one),
            row_sum(delta_expand * normed_two),
            row_sum(delta_expand),
            row_sum(upstream),
            row_sum(delta_hidden),
        ]
    )
    owned_rows = (
        lax.psum_scatter(merge_gradient, "wide", scatter_dimension=0, tiled=True),
        lax.psum_scatter(attend_gradient, "wide", scatter_dimension=0, tiled=True),
        lax.psum_scatter(output_gradient, "wide", scatter_dimension=0, tiled=True),
        lax.psum_scatter(expand_gradient, "wide", scatter_dimension=0, tiled=True),
        lax.psum_scatter(shrink_gradient, "wide", scatter_dimension=0, tiled=True),
    )
    vector_total = lax.psum(vector_gradient, "wide")
    parted = (
        lax.psum_scatter(owned_rows[0], "narrow", scatter_dimension=1, tiled=True),
        lax.psum_scatter(owned_rows[1], "narrow", scatter_dimension=1, tiled=True),
        lax.psum_scatter(owned_rows[2], "narrow", scatter_dimension=1, tiled=True),
        lax.psum_scatter(owned_rows[3], "narrow", scatter_dimension=1, tiled=True),
        lax.psum_scatter(owned_rows[4], "narrow", scatter_dimension=1, tiled=True),
        lax.psum_scatter(vector_total, "narrow", scatter_dimension=0, tiled=True),
    )
    merge_new = adamw_update(merge_weight, merge_moment, merge_square, parted[0], rate_merge)
    attend_new = adamw_update(attend_weight, attend_moment, attend_square, parted[1], rate_attend)
    output_new = adamw_update(output_weight, output_moment, output_square, parted[2], rate_output)
    expand_new = adamw_update(expand_weight, expand_moment, expand_square, parted[3], rate_expand)
    shrink_new = adamw_update(shrink_weight, shrink_moment, shrink_square, parted[4], rate_shrink)
    vector_new = adamw_update(vectors, vector_moment, vector_square, parted[5], rate_vector)
    return (
        outputs,
        input_gradient,
        skip_gradient,
        merge_new[0],
        merge_new[1],
        merge_new[2],
        attend_new[0],
        attend_new[1],
        attend_new[2],
        output_new[0],
        output_new[1],
        output_new[2],
        expand_new[0],
        expand_new[1],
        expand_new[2],
        shrink_new[0],
        shrink_new[1],
        shrink_new[2],
        vector_new[0],
        vector_new[1],
        vector_new[2],
    )


CORE = 1
ACROSS = 2
ALONG = 4
PAD = 384
VMEM_BYTES = 56 * 1024 * 1024
LIGHT = pl.CostEstimate(flops=0, bytes_accessed=1024, transcendentals=0)
PARAMS = pltpu.CompilerParams(vmem_limit_bytes=VMEM_BYTES)


def swap_wide(value, bit):
    return lax.ppermute(value, "wide", [(i, i ^ bit) for i in range(8)])


def swap_narrow(value, bit):
    return lax.ppermute(value, "narrow", [(i, i ^ bit) for i in range(4)])


def together(*values):
    return lax.optimization_barrier(values)


def spot():
    wide = lax.axis_index("wide")
    narrow = lax.axis_index("narrow")
    return (wide & 1, (wide >> 1) & 1, (wide >> 2) & 1, narrow & 1, narrow >> 1)


def split_rows(rows):
    return -(-rows // 32) * 16


def column_blocks(kind, quarter):
    if kind == "attend_output":
        width = quarter // 8
        order = [8 * part + 2 * n + p for part in range(3) for p in range(2) for n in range(4)]
        blocks = [(block // 6, (block % 6) * width) for block in order]
        return width, blocks + [(n, (6 + p) * width) for p in range(2) for n in range(4)]
    width = quarter // 2
    return width, [(n, p * width) for p in range(2) for n in range(4)]


def fold(shard):
    parts = max(1, shard.shape[0] // (D // 8))
    height = shard.shape[0] // parts
    return jnp.concatenate(
        [shard[part * height : (part + 1) * height] for part in range(parts)], axis=1
    )


def unfold(value, rows):
    parts = rows // value.shape[0]
    quarter = value.shape[1] // parts
    return jnp.concatenate(
        [value[:, part * quarter : (part + 1) * quarter] for part in range(parts)], axis=0
    )


def arrange(kind, parts, shard, far, near, near_far):
    height = shard.shape[0]
    rows, quarter = parts * height, shard.shape[1] // parts
    split = split_rows(rows)
    width, blocks = column_blocks(kind, quarter)

    def kernel(shard_ref, far_ref, near_ref, near_far_ref, top_ref, bottom_ref, held):
        narrow = lax.axis_index("narrow")
        held[0] = shard_ref[...]
        held[2] = far_ref[...]
        held[1] = near_ref[...]
        held[3] = near_far_ref[...]
        for number in range(4):
            value = held[narrow ^ number]
            for position, (owner, offset) in enumerate(blocks):
                if owner == number:
                    column = slice(position * width, (position + 1) * width)
                    if parts == 1:
                        piece = value[:, offset : offset + width]
                        top_ref[:, column] = piece[:split]
                        bottom_ref[:, column] = piece[split:]
                    for part in range(parts if parts > 1 else 0):
                        start = part * quarter + offset
                        piece = value[:, start : start + width]
                        row = part * height
                        if row < split:
                            top_ref[row : row + height, column] = piece
                        else:
                            bottom_ref[row - split : row - split + height, column] = piece

    return pl.pallas_call(
        kernel,
        out_shape=(
            jax.ShapeDtypeStruct((split, 4 * quarter), jnp.bfloat16),
            jax.ShapeDtypeStruct((rows - split, 4 * quarter), jnp.bfloat16),
        ),
        scratch_shapes=[pltpu.VMEM((4,) + shard.shape, jnp.bfloat16)],
        compiler_params=PARAMS,
        cost_estimate=LIGHT,
    )(shard, far, near, near_far)


def place(parts, first, second, third):
    split, columns = parts[0].shape
    rest = parts[1].shape[0]
    rows = split + rest

    def kernel(top, bottom, top_x, bottom_y, top_y, bottom_x, top_xy, bottom_xy, full):
        chip = lax.axis_index("wide") >> 1
        tops = (top, top_x, top_y, top_xy)
        bottoms = (bottom, bottom_x, bottom_y, bottom_xy)
        for relative in range(4):
            start = (chip ^ relative) * rows
            full[pl.ds(pl.multiple_of(start, 16), split)] = tops[relative][...]
            full[pl.ds(pl.multiple_of(start + split, 16), rest)] = bottoms[relative][...]

    return pl.pallas_call(
        kernel,
        out_shape=jax.ShapeDtypeStruct((4 * rows, columns), jnp.bfloat16),
        compiler_params=PARAMS,
        cost_estimate=LIGHT,
    )(*parts, *first, *second, *third)


def pair_gradient(lefts, rights):
    height = lefts[0][0].shape[0]
    rows = height // 4
    split = split_rows(rows)
    tokens = rights[0][0].shape[0]
    widths = [right[0].shape[1] for right in rights]
    tile = 384 if height > 576 else 1152
    steps = [width // tile for width in widths]
    starts = [sum(steps[:position]) for position in range(len(steps))]
    count = len(lefts)

    def kernel(*refs):
        left_refs = refs[: 2 * count]
        right_refs = refs[2 * count : 4 * count]
        outs, (joint, beside) = refs[4 * count : 4 * count + 8], refs[4 * count + 8 :]
        step = pl.program_id(0)
        wide = lax.axis_index("wide")
        across, along = (wide >> 1) & 1, (wide >> 2) & 1

        @pl.when(step == 0)
        def _():
            joint[...] = jnp.zeros_like(joint)

        for number in range(count):

            @pl.when(step == starts[number])
            def _():
                beside[:, :PAD] = left_refs[2 * number][...]
                beside[:, PAD:] = left_refs[2 * number + 1][...]

            @pl.when((step >= starts[number]) & (step < starts[number] + steps[number]))
            def _():
                joint[:tokens] = right_refs[2 * number][...]
                joint[PAD : PAD + tokens] = right_refs[2 * number + 1][...]
                for y in range(2):
                    for x in range(2):
                        first_row = (2 * y + x) * rows
                        total = jnp.dot(
                            beside[first_row : first_row + rows],
                            joint[...],
                            preferred_element_type=jnp.float32,
                        ).astype(jnp.bfloat16)

                        for kept_x in range(2):
                            for kept_y in range(2):

                                @pl.when(
                                    ((across == x) == (kept_x == 1))
                                    & ((along == y) == (kept_y == 1))
                                )
                                def _():
                                    outs[2 * (1 - kept_x) + (1 - kept_y)][...] = total[:split]
                                    outs[4 + 2 * (1 - kept_y) + (1 - kept_x)][...] = total[split:]

    def right_spec(number):
        return pl.BlockSpec(
            (tokens, tile),
            lambda i: (0, jnp.clip(i - starts[number], 0, steps[number] - 1)),
        )

    in_specs = [pl.BlockSpec((height, PAD), lambda i: (0, 0))] * (2 * count)
    operands = [left for pair in lefts for left in pair]
    for number in range(count):
        in_specs += [right_spec(number)] * 2
        operands += list(rights[number])
    top_spec = pl.BlockSpec((split, tile), lambda i: (0, i))
    bottom_spec = pl.BlockSpec((rows - split, tile), lambda i: (0, i))
    top_shape = jax.ShapeDtypeStruct((split, sum(widths)), jnp.bfloat16)
    bottom_shape = jax.ShapeDtypeStruct((rows - split, sum(widths)), jnp.bfloat16)
    outs = pl.pallas_call(
        kernel,
        grid=(sum(steps),),
        in_specs=in_specs,
        out_specs=(top_spec,) * 4 + (bottom_spec,) * 4,
        out_shape=(top_shape,) * 4 + (bottom_shape,) * 4,
        scratch_shapes=[
            pltpu.VMEM((2 * PAD, tile), jnp.bfloat16),
            pltpu.VMEM((height, 2 * PAD), jnp.bfloat16),
        ],
        compiler_params=PARAMS,
        cost_estimate=LIGHT,
    )(*operands)
    return outs[:4], outs[4:]


def unarrange(kind, parts, top, bottom):
    split, columns = top[0].shape
    rest = bottom[0].shape[0]
    rows = split + rest
    quarter = columns // 4
    height = rows // parts
    width, blocks = column_blocks(kind, quarter)

    def kernel(*refs):
        tops, bottoms = refs[:3], refs[3:6]
        keep_ref, keep_far_ref, send_ref, send_far_ref, held = refs[6:]
        narrow = lax.axis_index("narrow")
        low_bit, high_bit = narrow & 1, narrow >> 1
        held[:split] = add_low(*[ref[...] for ref in tops])
        held[split:] = add_low(*[ref[...] for ref in bottoms])
        for position, (owner, offset) in enumerate(blocks):
            piece = held[:, position * width : (position + 1) * width]
            for kept_low in range(2):
                for kept_high in range(2):
                    target = (keep_ref, keep_far_ref, send_ref, send_far_ref)[
                        2 * (1 - kept_low) + (1 - kept_high)
                    ]

                    @pl.when(
                        ((low_bit == (owner & 1)) == (kept_low == 1))
                        & ((high_bit == (owner >> 1)) == (kept_high == 1))
                    )
                    def _():
                        for part in range(parts):
                            start = part * quarter + offset
                            target[:, start : start + width] = piece[
                                part * height : (part + 1) * height
                            ]

    shape = jax.ShapeDtypeStruct((height, parts * quarter), jnp.bfloat16)
    return pl.pallas_call(
        kernel,
        out_shape=(shape,) * 4,
        scratch_shapes=[pltpu.VMEM((rows, columns), jnp.bfloat16)],
        compiler_params=PARAMS,
        cost_estimate=LIGHT,
    )(*top, *bottom)


def add_low(*terms):
    return sum(term.astype(jnp.float32) for term in terms).astype(jnp.bfloat16)


def pick(value, index, dim=0):
    return lax.dynamic_index_in_dim(value, index, dim, keepdims=False)


def halves_of(value, core):
    middle = value.shape[-1] // 2
    first, second = value[..., :middle], value[..., middle:]
    return jnp.where(core == 0, first, second), jnp.where(core == 0, second, first)


def inner(value):
    width = value.shape[-1] // 8
    return jnp.concatenate(
        [
            value[..., (2 * n + p) * width : (2 * n + p + 1) * width]
            for p in range(2)
            for n in range(4)
        ],
        axis=-1,
    )


def outer(value):
    width = value.shape[-1] // 8
    return jnp.concatenate(
        [
            value[..., (4 * p + n) * width : (4 * p + n + 1) * width]
            for n in range(4)
            for p in range(2)
        ],
        axis=-1,
    )


def upright(value):
    return jnp.pad(value, ((0, PAD - value.shape[0]), (0, 0))).T


def both(parts, order):
    if order == 0:
        return swap_wide(parts[0], ACROSS), swap_wide(parts[1], ALONG)
    return swap_wide(parts[0], ALONG), swap_wide(parts[1], ACROSS)


KEEP_NEAR, KEEP_FAR, SEND_NEAR, SEND_FAR = range(4)


def send(blocks, which):
    return both((blocks[0][which], blocks[1][which]), 0)


def forward(blocks, got):
    return both(tuple(add_low(blocks[i][KEEP_FAR], got[i]) for i in range(2)), 1)


def settle(kind, parts, blocks, got_near, got_last):
    return unarrange(
        kind, parts, *[(blocks[i][KEEP_NEAR], got_near[i], got_last[i]) for i in range(2)]
    )


def narrow_first(quarters):
    return swap_narrow(quarters[SEND_FAR], 1), swap_narrow(quarters[SEND_NEAR], 1)


def narrow_second(quarters, got):
    return swap_narrow(add_low(quarters[KEEP_FAR], got[0]), 2)


def finish(quarters, got, got_last):
    return (
        quarters[KEEP_NEAR].astype(jnp.float32)
        + got[1].astype(jnp.float32)
        + got_last.astype(jnp.float32)
    )


def gather_vector(far, near, vector):
    low_bit, high_bit = spot()[3:]
    own = jnp.stack([vector, far])
    own = jnp.where(high_bit == 0, own, own[::-1])
    near = jnp.where(high_bit == 0, near, near[::-1])
    even = jnp.where(low_bit == 0, own, near)
    odd = jnp.where(low_bit == 0, near, own)
    return jnp.concatenate([even[0], odd[0], even[1], odd[1]])


def heavy(kernel, outs, scratch, *operands):
    return pl.pallas_call(
        kernel,
        out_shape=tuple(jax.ShapeDtypeStruct(shape, dtype) for shape, dtype in outs),
        scratch_shapes=[pltpu.VMEM(shape, dtype) for shape, dtype in scratch],
        compiler_params=PARAMS,
        cost_estimate=LIGHT,
    )(*operands)


def dot_rows(left, right):
    return lax.dot_general(left, right, (((1,), (1,)), ((), ())), preferred_element_type=jnp.float32)


def dot_depth(left, right):
    return lax.dot_general(left, right, (((0,), (0,)), ((), ())), preferred_element_type=jnp.float32)


def in_order(mine, other, work):
    core = lax.axis_index("wide") & 1

    @pl.when(core == 0)
    def _():
        work(mine, other)

    @pl.when(core == 1)
    def _():
        work(other, mine)


def store_upright(value, padded, mine, other):
    features = value.shape[1]
    padded[: value.shape[0]] = value
    turned = padded[...].T.astype(jnp.bfloat16)

    def work(even, odd):
        even[...] = turned[: features // 2]
        odd[...] = turned[features // 2 :]

    in_order(mine, other, work)


def merge_forward(joined_mine, joined_other, merge_mine, merge_other, bias, gain, shift):
    length = joined_mine.shape[0]

    def kernel(
        left, right, mine, other, bias_ref, gain_ref, shift_ref, stream, entry, up_mine, up_other, padded
    ):
        padded[...] = jnp.zeros_like(padded)
        stream[...] = product(left[...], mine[...]) + product(right[...], other[...]) + bias_ref[...]
        normed = normalize(stream[...])[0]
        value = (normed * gain_ref[...] + shift_ref[...]).astype(jnp.bfloat16)
        entry[...] = value
        store_upright(value.astype(jnp.float32), padded, up_mine, up_other)

    return heavy(
        kernel,
        [
            ((length, D), jnp.float32),
            ((length, D), jnp.bfloat16),
            ((D // 2, PAD), jnp.bfloat16),
            ((D // 2, PAD), jnp.bfloat16),
        ],
        [((PAD, D), jnp.float32)],
        joined_mine,
        joined_other,
        merge_mine,
        merge_other,
        bias,
        gain,
        shift,
    )


def attend_head(heads, head, chances_ref, slot):
    at = head * HD
    queries = heads[:, at : at + HD]
    keys = heads[:, D + at : D + at + HD]
    values = heads[:, 2 * D + at : 2 * D + at + HD]
    logits = dot_rows(queries, keys) * HD ** (-0.5)
    powers = jnp.exp(logits - jnp.max(logits, axis=-1, keepdims=True))
    chances = powers / jnp.sum(powers, axis=-1, keepdims=True)
    chances_ref[slot] = chances
    return product(chances.astype(jnp.bfloat16), values).astype(jnp.bfloat16)


def attend_first(entry, mixed_mine, mixed_other):
    length = entry.shape[0]
    half = D // 2

    def kernel(entry_ref, mine, other, heads, chances_ref, mix_ref):
        def project(even, odd):
            for part in range(3):
                columns = slice(part * D, (part + 1) * D)
                heads[:, columns] = (
                    product(entry_ref[:, :half], even[:, columns])
                    + product(entry_ref[:, half:], odd[:, columns])
                ).astype(jnp.bfloat16)

        in_order(mine, other, project)
        for head in range(H // 2):
            mix_ref[:, head * HD : (head + 1) * HD] = attend_head(heads, head, chances_ref, head)

    return heavy(
        kernel,
        [
            ((length, 3 * D), jnp.bfloat16),
            ((H // 2, length, length), jnp.float32),
            ((length, half), jnp.bfloat16),
        ],
        [],
        entry,
        mixed_mine,
        mixed_other,
    )


def attend_second(heads, mix_first, mixed_mine, mixed_other, stream_zero, bias, gain, shift):
    length = heads.shape[0]
    half = D // 2

    def kernel(
        heads_ref,
        first_ref,
        mine,
        other,
        zero_ref,
        bias_ref,
        gain_ref,
        shift_ref,
        chances_ref,
        stream,
        value_ref,
        mix_mine,
        mix_other,
        up_mine,
        up_other,
        mixed,
        padded,
    ):
        padded[...] = jnp.zeros_like(padded)
        mixed[:, :half] = first_ref[...]
        for head in range(H // 2, H):
            mixed[:, head * HD : (head + 1) * HD] = attend_head(
                heads_ref, head, chances_ref, head - H // 2
            )

        def leave(even, odd):
            stream[...] = (
                zero_ref[...]
                + (product(mixed[:, :half], even[...]) + product(mixed[:, half:], odd[...]))
                + bias_ref[...]
            )

        in_order(mine, other, leave)
        store_upright(mixed[...].astype(jnp.float32), padded, mix_mine, mix_other)
        normed = normalize(stream[...])[0]
        value = (normed * gain_ref[...] + shift_ref[...]).astype(jnp.bfloat16)
        value_ref[...] = value
        store_upright(value.astype(jnp.float32), padded, up_mine, up_other)

    full = lambda shape: pl.BlockSpec(shape, lambda i: (0,) * len(shape))
    shapes = (
        ((H // 2, length, length), jnp.float32),
        ((length, D), jnp.float32),
        ((length, D), jnp.bfloat16),
        ((half, PAD), jnp.bfloat16),
        ((half, PAD), jnp.bfloat16),
        ((half, PAD), jnp.bfloat16),
        ((half, PAD), jnp.bfloat16),
    )
    return pl.pallas_call(
        kernel,
        grid=(1,),
        in_specs=[
            full((length, 3 * D)),
            full((length, half)),
            pl.BlockSpec((half, D), lambda i: (0, 3)),
            pl.BlockSpec((half, D), lambda i: (0, 3)),
            full((length, D)),
            full((1, D)),
            full((1, D)),
            full((1, D)),
        ],
        out_specs=tuple(full(shape) for shape, _ in shapes),
        out_shape=tuple(jax.ShapeDtypeStruct(shape, dtype) for shape, dtype in shapes),
        scratch_shapes=[pltpu.VMEM((length, D), jnp.bfloat16), pltpu.VMEM((PAD, D), jnp.float32)],
        compiler_params=PARAMS,
        cost_estimate=LIGHT,
    )(heads, mix_first, mixed_mine, mixed_other, stream_zero, bias, gain, shift)


def expand_forward(entry, expand_mine, expand_other, bias):
    length = entry.shape[0]
    half = D // 2
    tile = D
    per = FF // 2 // tile

    def kernel(
        entry_ref, mine, other, bias_ref, active_ref, slope_ref, up_mine, up_other, padded, hidden
    ):
        step = pl.program_id(0)

        @pl.when(step == 0)
        def _():
            padded[...] = jnp.zeros_like(padded)

        def work(even, odd):
            hidden[...] = (
                product(entry_ref[:, :half], even[...]) + product(entry_ref[:, half:], odd[...])
            ) + bias_ref[...]

        in_order(mine, other, work)
        value = hidden[...]
        inside = 0.5 * (1.0 + lax.erf(value * (0.5**0.5)))
        bell = jnp.exp(-0.5 * value * value) * (2.0 * jnp.pi) ** -0.5
        active = (value * inside).astype(jnp.bfloat16)
        slope_ref[...] = inside + value * bell
        active_ref[...] = active
        padded[:length] = active.astype(jnp.float32)
        turned = padded[...].T.astype(jnp.bfloat16)
        rows = pl.ds(pl.multiple_of(lax.rem(step, per) * tile, tile), tile)
        core = lax.axis_index("wide") & 1

        @pl.when(step // per == core)
        def _():
            up_mine[rows] = turned

        @pl.when(step // per != core)
        def _():
            up_other[rows] = turned

    whole = lambda i: (0, 0)
    across = lambda i: (0, i)
    return pl.pallas_call(
        kernel,
        grid=(FF // tile,),
        in_specs=[
            pl.BlockSpec((length, D), whole),
            pl.BlockSpec((half, tile), across),
            pl.BlockSpec((half, tile), across),
            pl.BlockSpec((1, tile), across),
        ],
        out_specs=(
            pl.BlockSpec((length, tile), across),
            pl.BlockSpec((length, tile), across),
            pl.BlockSpec((FF // 2, PAD), whole),
            pl.BlockSpec((FF // 2, PAD), whole),
        ),
        out_shape=(
            jax.ShapeDtypeStruct((length, FF), jnp.bfloat16),
            jax.ShapeDtypeStruct((length, FF), jnp.float32),
            jax.ShapeDtypeStruct((FF // 2, PAD), jnp.bfloat16),
            jax.ShapeDtypeStruct((FF // 2, PAD), jnp.bfloat16),
        ),
        scratch_shapes=[
            pltpu.VMEM((PAD, tile), jnp.float32),
            pltpu.VMEM((length, tile), jnp.float32),
        ],
        compiler_params=PARAMS,
        cost_estimate=LIGHT,
    )(entry, expand_mine, expand_other, bias)


def hidden_backward(pulled, shrink_mine, shrink_other, slope):
    length = pulled.shape[0]
    half = FF // 2

    def kernel(pulled_ref, mine, other, slope_ref, low_ref, sum_ref):
        core = lax.axis_index("wide") & 1
        for weight, parity in ((mine, core), (other, 1 - core)):
            for part in range(half // D):
                columns = pl.ds(pl.multiple_of(parity * half + part * D, 128), D)
                delta = (
                    dot_rows(pulled_ref[...], weight[part * D : (part + 1) * D])
                    * slope_ref[:, columns]
                )
                low_ref[:, columns] = delta.astype(jnp.bfloat16)
                sum_ref[:, columns] = jnp.sum(delta, axis=0, keepdims=True)

    return heavy(
        kernel,
        [((length, FF), jnp.bfloat16), ((1, FF), jnp.float32)],
        [],
        pulled,
        shrink_mine,
        shrink_other,
        slope,
    )


def expand_backward(
    hidden_low, expand_mine, expand_other, pulled, stream_one, gain, mixed_mine, mixed_other
):
    length = pulled.shape[0]
    half = D // 2

    def kernel(
        hidden_ref,
        mine,
        other,
        pulled_ref,
        stream_ref,
        gain_ref,
        out_mine,
        out_other,
        one_ref,
        low_ref,
        sums,
        mix_ref,
        delta,
    ):
        def work(even, odd):
            delta[:, :half] = dot_rows(hidden_ref[...], even[...])
            delta[:, half:] = dot_rows(hidden_ref[...], odd[...])

        in_order(mine, other, work)
        normed, inverse = normalize(stream_ref[...])
        value = delta[...]
        one = pulled_ref[...].astype(jnp.float32) + norm_back(value * gain_ref[...], normed, inverse)
        one_ref[...] = one
        low_value = one.astype(jnp.bfloat16)
        low_ref[...] = low_value
        sums[0:1] = jnp.sum(one, axis=0, keepdims=True)
        sums[1:2] = jnp.sum(value * normed, axis=0, keepdims=True)
        sums[2:3] = jnp.sum(value, axis=0, keepdims=True)
        sums[3:4] = jnp.sum(pulled_ref[...].astype(jnp.float32), axis=0, keepdims=True)

        def back(even, odd):
            mix_ref[:, :half] = dot_rows(low_value, even[...]).astype(jnp.bfloat16)
            mix_ref[:, half:] = dot_rows(low_value, odd[...]).astype(jnp.bfloat16)

        in_order(out_mine, out_other, back)

    whole = lambda i: (0, 0)
    last = lambda i: (0, 3)
    return pl.pallas_call(
        kernel,
        grid=(1,),
        in_specs=[
            pl.BlockSpec((length, FF), whole),
            pl.BlockSpec((half, FF), whole),
            pl.BlockSpec((half, FF), whole),
            pl.BlockSpec((length, D), whole),
            pl.BlockSpec((length, D), whole),
            pl.BlockSpec((1, D), whole),
            pl.BlockSpec((half, D), last),
            pl.BlockSpec((half, D), last),
        ],
        out_specs=(
            pl.BlockSpec((length, D), whole),
            pl.BlockSpec((length, D), whole),
            pl.BlockSpec((4, D), whole),
            pl.BlockSpec((length, D), whole),
        ),
        out_shape=(
            jax.ShapeDtypeStruct((length, D), jnp.float32),
            jax.ShapeDtypeStruct((length, D), jnp.bfloat16),
            jax.ShapeDtypeStruct((4, D), jnp.float32),
            jax.ShapeDtypeStruct((length, D), jnp.bfloat16),
        ),
        scratch_shapes=[pltpu.VMEM((length, D), jnp.float32)],
        compiler_params=PARAMS,
        cost_estimate=LIGHT,
    )(hidden_low, expand_mine, expand_other, pulled, stream_one, gain, mixed_mine, mixed_other)


def attend_backward(heads, chances_first, chances_second, delta_mixture):
    length = heads.shape[0]
    scale = HD ** (-0.5)

    def kernel(heads_ref, first_ref, second_ref, delta_ref, mixed):
        for head in range(H):
            at = head * HD
            queries = heads_ref[:, at : at + HD]
            keys = heads_ref[:, D + at : D + at + HD]
            values = heads_ref[:, 2 * D + at : 2 * D + at + HD]
            delta = delta_ref[:, at : at + HD]
            chances = (first_ref, second_ref)[head // (H // 2)][head % (H // 2)]
            pull = dot_rows(delta, values)
            inner_sum = jnp.sum(chances * pull, axis=-1, keepdims=True)
            scores = (scale * (chances * (pull - inner_sum))).astype(jnp.bfloat16)
            mixed[:, at : at + HD] = product(scores, keys).astype(jnp.bfloat16)
            mixed[:, D + at : D + at + HD] = dot_depth(scores, queries).astype(jnp.bfloat16)
            mixed[:, 2 * D + at : 2 * D + at + HD] = dot_depth(
                chances.astype(jnp.bfloat16), delta
            ).astype(jnp.bfloat16)

    return heavy(
        kernel,
        [((length, 3 * D), jnp.bfloat16)],
        [],
        heads,
        chances_first,
        chances_second,
        delta_mixture,
    )[0]


def entry_backward(delta_mixed, mixed_mine, mixed_other, delta_one, stream_zero, gain):
    length = delta_mixed.shape[0]
    half = D // 2

    def kernel(mixed_ref, mine, other, one_ref, stream_ref, gain_ref, low_ref, sums, delta):
        def work(even, odd):
            delta[:, :half] = dot_rows(mixed_ref[...], even[...])
            delta[:, half:] = dot_rows(mixed_ref[...], odd[...])

        in_order(mine, other, work)
        normed, inverse = normalize(stream_ref[...])
        value = delta[...]
        zero = one_ref[...] + norm_back(value * gain_ref[...], normed, inverse)
        low_ref[...] = zero.astype(jnp.bfloat16)
        sums[0:1] = jnp.sum(zero, axis=0, keepdims=True)
        sums[1:2] = jnp.sum(value * normed, axis=0, keepdims=True)
        sums[2:3] = jnp.sum(value, axis=0, keepdims=True)

    whole = lambda i: (0, 0)
    return pl.pallas_call(
        kernel,
        grid=(1,),
        in_specs=[
            pl.BlockSpec((length, 3 * D), whole),
            pl.BlockSpec((half, 3 * D), whole),
            pl.BlockSpec((half, 3 * D), whole),
            pl.BlockSpec((length, D), whole),
            pl.BlockSpec((length, D), whole),
            pl.BlockSpec((1, D), whole),
        ],
        out_specs=(pl.BlockSpec((length, D), whole), pl.BlockSpec((3, D), whole)),
        out_shape=(
            jax.ShapeDtypeStruct((length, D), jnp.bfloat16),
            jax.ShapeDtypeStruct((3, D), jnp.float32),
        ),
        scratch_shapes=[pltpu.VMEM((length, D), jnp.float32)],
        compiler_params=PARAMS,
        cost_estimate=LIGHT,
    )(delta_mixed, mixed_mine, mixed_other, delta_one, stream_zero, gain)


def joined_backward(zero_low, merge_mine, merge_other):
    length = zero_low.shape[0]
    width = 2 * D // 8

    def kernel(zero_ref, mine, other, first_ref, second_ref):
        def work(even, odd):
            for parity, weight in enumerate((even, odd)):
                delta = dot_rows(zero_ref[...], weight[...]).astype(jnp.bfloat16)
                for number in range(4):
                    target = (first_ref, second_ref)[number // 2]
                    column = (2 * (number % 2) + parity) * width
                    target[:, column : column + width] = delta[
                        :, number * width : (number + 1) * width
                    ]

        in_order(mine, other, work)

    out = ((length, D), jnp.bfloat16)
    return heavy(kernel, [out, out], [], zero_low, merge_mine, merge_other)


def shrink_forward(active, shrink_mine, shrink_other, stream_one, bias):
    length = active.shape[0]
    half = FF // 2
    width = D // 8

    def kernel(active_ref, mine, other, stream_ref, bias_ref, out_ref):
        def work(even, odd):
            total = (
                stream_ref[...]
                + (product(active_ref[:, :half], even[...]) + product(active_ref[:, half:], odd[...]))
                + bias_ref[...]
            ).astype(jnp.bfloat16)
            for parity in range(2):
                for number in range(4):
                    column = (2 * number + parity) * width
                    source = (4 * parity + number) * width
                    out_ref[:, column : column + width] = total[:, source : source + width]

        in_order(mine, other, work)

    return heavy(
        kernel,
        [((length, D), jnp.bfloat16)],
        [],
        active,
        shrink_mine,
        shrink_other,
        stream_one,
        bias,
    )[0]


def on_device(
    inputs,
    skip_tokens,
    cotangent,
    merge_weight,
    merge_moment,
    merge_square,
    attend_weight,
    attend_moment,
    attend_square,
    output_weight,
    output_moment,
    output_square,
    expand_weight,
    expand_moment,
    expand_square,
    shrink_weight,
    shrink_moment,
    shrink_square,
    vectors,
    vector_moment,
    vector_square,
):
    core, across, along, low_bit, high_bit = spot()
    low = jnp.bfloat16
    length = inputs.shape[1]
    columns = attend_weight.shape[1]

    merge_low = fold(merge_weight.astype(low))
    vector_low = vectors.astype(low)
    merge_far = swap_narrow(merge_low, 2)
    vector_far = swap_narrow(vector_low, 2)
    mixed_low = jnp.concatenate([attend_weight.astype(low), output_weight.astype(low)], axis=1)
    merge_far, vector_far, mixed_low = together(merge_far, vector_far, mixed_low)
    merge_near = swap_narrow(merge_low, 1), swap_narrow(merge_far, 1)
    vector_near = swap_narrow(jnp.stack([vector_low, vector_far]), 1)
    joined = inner(jnp.concatenate([inputs[0], skip_tokens[0]], axis=-1))
    joined_mine, joined_other = halves_of(joined, core)
    merge_near, vector_near, joined_mine, joined_other = together(
        merge_near, vector_near, joined_mine, joined_other
    )
    merge_parts = arrange("merge", 2, merge_low, merge_far, *merge_near)
    merge_first = both(merge_parts, 0)
    merge_second = both(merge_parts, 1)
    mixed_far = swap_narrow(mixed_low, 2)
    pulled = inner(cotangent[0])
    joined_up = upright(joined_mine)
    joined_up_other = upright(joined_other)
    merge_first, merge_second, mixed_far, joined_up, joined_up_other, pulled = together(
        merge_first, merge_second, mixed_far, joined_up, joined_up_other, pulled
    )
    merge_third = both(merge_first, 1)
    mixed_near = swap_narrow(mixed_low, 1), swap_narrow(mixed_far, 1)
    pieces = unpack(gather_vector(vector_far, vector_near, vector_low).astype(jnp.float32))
    pieces = tuple(inner(piece)[None] for piece in pieces)
    expand_low = expand_weight.astype(low)
    shrink_low = fold(shrink_weight.astype(low))
    merge_third, mixed_near, pieces, expand_low, shrink_low = together(
        merge_third, mixed_near, pieces, expand_low, shrink_low
    )
    skip_bias, gain_one, bias_one, output_bias, gain_two, bias_two, shrink_bias, expand_bias = pieces
    mixed_parts = arrange("attend_output", 1, mixed_low, mixed_far, *mixed_near)
    mixed_first = both(mixed_parts, 0)
    expand_far = swap_narrow(expand_low, 2)
    merge_mine = place(merge_parts, merge_first, merge_second, merge_third)
    mixed_first, expand_far, merge_mine = together(mixed_first, expand_far, merge_mine)
    mixed_second = both(mixed_parts, 1)
    expand_near = swap_narrow(expand_low, 1), swap_narrow(expand_far, 1)
    merge_other = swap_wide(merge_mine, CORE)
    mixed_second, expand_near, merge_other = together(mixed_second, expand_near, merge_other)
    mixed_third = both(mixed_first, 1)
    shrink_far = swap_narrow(shrink_low, 2)
    joined_sibling = swap_wide(joined_up_other, CORE)
    stream_zero, attend_input, attend_up, attend_up_other = merge_forward(
        joined_mine, joined_other, merge_mine, merge_other, skip_bias, gain_one, bias_one
    )
    expand_parts = arrange("expand", 1, expand_low, expand_far, *expand_near)
    mixed_third, shrink_far, joined_sibling, stream_zero, attend_input, attend_up_other, expand_parts = (
        together(
            mixed_third,
            shrink_far,
            joined_sibling,
            stream_zero,
            attend_input,
            attend_up_other,
            expand_parts,
        )
    )
    expand_first = both(expand_parts, 0)
    shrink_near = swap_narrow(shrink_low, 1), swap_narrow(shrink_far, 1)
    mixed_mine = place(mixed_parts, mixed_first, mixed_second, mixed_third)
    expand_first, mixed_mine, shrink_near = together(expand_first, mixed_mine, shrink_near)
    expand_second = both(expand_parts, 1)
    mixed_other = swap_wide(mixed_mine, CORE)
    attend_up_sibling = swap_wide(attend_up_other, CORE)
    shrink_parts = arrange("shrink", 4, shrink_low, shrink_far, *shrink_near)
    expand_second, mixed_other, attend_up_sibling, shrink_parts = together(
        expand_second, mixed_other, attend_up_sibling, shrink_parts
    )
    expand_third = both(expand_first, 1)
    heads, chances_first, mix_first = attend_first(attend_input, mixed_mine, mixed_other)
    expand_third, heads, mix_first = together(expand_third, heads, mix_first)
    shrink_first = both(shrink_parts, 0)
    expand_mine = place(expand_parts, expand_first, expand_second, expand_third)
    expand_other = swap_wide(expand_mine, CORE)
    (
        chances_second,
        stream_one,
        expand_input,
        mixture_up,
        mixture_up_other,
        expand_up,
        expand_up_other,
    ) = attend_second(
        heads, mix_first, mixed_mine, mixed_other, stream_zero, output_bias, gain_two, bias_two
    )
    shrink_first, expand_mine, expand_other, expand_input, mixture_up_other, expand_up_other = (
        together(
            shrink_first, expand_mine, expand_other, expand_input, mixture_up_other, expand_up_other
        )
    )
    shrink_second = both(shrink_parts, 1)
    pulled_sibling = swap_wide(pulled, CORE)
    mixture_up_sibling = swap_wide(mixture_up_other, CORE)
    active, slope, active_up, active_up_other = expand_forward(
        expand_input, expand_mine, expand_other, expand_bias
    )
    shrink_second, pulled_sibling, mixture_up_sibling, active, slope, active_up, active_up_other = (
        together(
            shrink_second,
            pulled_sibling,
            mixture_up_sibling,
            active,
            slope,
            active_up,
            active_up_other,
        )
    )
    shrink_third = both(shrink_first, 1)
    expand_up_sibling = swap_wide(expand_up_other, CORE)
    active_up_sibling = swap_wide(active_up_other, CORE)
    shrink_blocks = pair_gradient([(active_up, active_up_sibling)], [(pulled, pulled_sibling)])
    shrink_third, expand_up_sibling, shrink_blocks = together(
        shrink_third, expand_up_sibling, shrink_blocks
    )
    shrink_far_got = send(shrink_blocks, SEND_FAR)
    shrink_near_got = send(shrink_blocks, SEND_NEAR)
    shrink_mine = place(shrink_parts, shrink_first, shrink_second, shrink_third)
    shrink_other = swap_wide(shrink_mine, CORE)
    hidden_low, hidden_sum = hidden_backward(pulled, shrink_mine, shrink_other, slope)
    shrink_far_got, shrink_near_got, hidden_low, hidden_sum = together(
        shrink_far_got, shrink_near_got, hidden_low, hidden_sum
    )
    shrink_got_last = forward(shrink_blocks, shrink_far_got)
    hidden_sibling = swap_wide(hidden_low, CORE)
    expand_blocks = pair_gradient([(expand_up, expand_up_sibling)], [(hidden_low, hidden_sibling)])
    shrink_got_last, expand_blocks, hidden_low = together(shrink_got_last, expand_blocks, hidden_low)
    expand_far_got = send(expand_blocks, SEND_FAR)
    delta_one, stream_low, sums_two, delta_mixture = expand_backward(
        hidden_low,
        expand_mine,
        expand_other,
        pulled,
        stream_one,
        gain_two,
        mixed_mine,
        mixed_other,
    )
    expand_far_got, stream_low, delta_mixture = together(expand_far_got, stream_low, delta_mixture)
    expand_near_got = send(expand_blocks, SEND_NEAR)
    stream_sibling = swap_wide(stream_low, CORE)
    delta_mixed = attend_backward(heads, chances_first, chances_second, delta_mixture)
    expand_near_got, stream_sibling, delta_mixed = together(
        expand_near_got, stream_sibling, delta_mixed
    )
    expand_got_last = forward(expand_blocks, expand_far_got)
    mixed_sibling = swap_wide(delta_mixed, CORE)
    shrink_quarters = settle("shrink", 4, shrink_blocks, shrink_near_got, shrink_got_last)
    mixed_blocks = pair_gradient(
        [(attend_up, attend_up_sibling), (mixture_up, mixture_up_sibling)],
        [(delta_mixed, mixed_sibling), (stream_low, stream_sibling)],
    )
    expand_got_last, shrink_quarters, mixed_blocks, delta_mixed = together(
        expand_got_last, shrink_quarters, mixed_blocks, delta_mixed
    )
    mixed_far_got = send(mixed_blocks, SEND_FAR)
    shrink_got = narrow_first(shrink_quarters)
    zero_low, sums_one = entry_backward(
        delta_mixed, mixed_mine, mixed_other, delta_one, stream_zero, gain_one
    )
    mixed_far_got, shrink_got, zero_low, sums_one = together(
        mixed_far_got, shrink_got, zero_low, sums_one
    )
    mixed_near_got = send(mixed_blocks, SEND_NEAR)
    shrink_end = narrow_second(shrink_quarters, shrink_got)
    zero_sibling = swap_wide(zero_low, CORE)
    vector_total = jnp.concatenate(
        [
            outer(row)
            for row in (
                sums_one[0],
                sums_one[1],
                sums_one[2],
                sums_two[0],
                sums_two[1],
                sums_two[2],
                sums_two[3],
                hidden_sum[0],
            )
        ]
    )
    expand_quarters = settle("expand", 1, expand_blocks, expand_near_got, expand_got_last)
    mixed_near_got, shrink_end, zero_sibling, vector_total, expand_quarters = together(
        mixed_near_got, shrink_end, zero_sibling, vector_total, expand_quarters
    )
    mixed_got_last = forward(mixed_blocks, mixed_far_got)
    expand_got = narrow_first(expand_quarters)
    vector_total = vector_total + swap_wide(vector_total, CORE)
    merge_blocks = pair_gradient([(joined_up, joined_sibling)], [(zero_low, zero_sibling)])
    mixed_got_last, expand_got, vector_total, merge_blocks = together(
        mixed_got_last, expand_got, vector_total, merge_blocks
    )
    merge_far_got = send(merge_blocks, SEND_FAR)
    merge_near_got = send(merge_blocks, SEND_NEAR)
    expand_end = narrow_second(expand_quarters, expand_got)
    mixed_quarters = settle("attend_output", 1, mixed_blocks, mixed_near_got, mixed_got_last)
    outputs = shrink_forward(active, shrink_mine, shrink_other, stream_one, shrink_bias)[None]
    merge_far_got, merge_near_got, expand_end, mixed_quarters, outputs = together(
        merge_far_got, merge_near_got, expand_end, mixed_quarters, outputs
    )
    merge_got_last = forward(merge_blocks, merge_far_got)
    mixed_got = narrow_first(mixed_quarters)
    vector_total = vector_total + swap_wide(vector_total, ACROSS)
    input_gradient, skip_gradient = joined_backward(zero_low, merge_mine, merge_other)
    shrink_new = adamw_update(
        shrink_weight,
        shrink_moment,
        shrink_square,
        unfold(finish(shrink_quarters, shrink_got, shrink_end), shrink_weight.shape[0]),
        rate_shrink,
    )
    merge_got_last, mixed_got, vector_total, input_gradient, skip_gradient, shrink_new = together(
        merge_got_last, mixed_got, vector_total, input_gradient, skip_gradient, shrink_new
    )
    merge_quarters = settle("merge", 2, merge_blocks, merge_near_got, merge_got_last)
    merge_got = narrow_first(merge_quarters)
    mixed_end = narrow_second(mixed_quarters, mixed_got)
    vector_total = vector_total + swap_wide(vector_total, ALONG)
    expand_new = adamw_update(
        expand_weight,
        expand_moment,
        expand_square,
        finish(expand_quarters, expand_got, expand_end),
        rate_expand,
    )
    merge_got, mixed_end, vector_total, expand_new = together(
        merge_got, mixed_end, vector_total, expand_new
    )
    merge_end = narrow_second(merge_quarters, merge_got)
    halves = vector_total.reshape(2, -1)
    vector_total = pick(halves, high_bit) + swap_narrow(pick(halves, 1 - high_bit), 2)
    halves = vector_total.reshape(2, -1)
    vector_total = pick(halves, low_bit) + swap_narrow(pick(halves, 1 - low_bit), 1)
    mixed_total = finish(mixed_quarters, mixed_got, mixed_end)
    attend_new = adamw_update(
        attend_weight, attend_moment, attend_square, mixed_total[:, :columns], rate_attend
    )
    output_new = adamw_update(
        output_weight, output_moment, output_square, mixed_total[:, columns:], rate_output
    )
    merge_new = adamw_update(
        merge_weight,
        merge_moment,
        merge_square,
        unfold(finish(merge_quarters, merge_got, merge_end), merge_weight.shape[0]),
        rate_merge,
    )
    vector_new = adamw_update(vectors, vector_moment, vector_square, vector_total, rate_vector)
    return (
        outputs,
        input_gradient[None],
        skip_gradient[None],
        *merge_new,
        *attend_new,
        *output_new,
        *expand_new,
        *shrink_new,
        *vector_new,
    )


def solution(mesh):
    in_specs = (
        P(("wide", "narrow"), None, None),
        P(("wide", "narrow"), None, None),
        P(("wide", "narrow"), None, None),
        P("wide", "narrow"),
        P("wide", "narrow"),
        P("wide", "narrow"),
        P("wide", "narrow"),
        P("wide", "narrow"),
        P("wide", "narrow"),
        P("wide", "narrow"),
        P("wide", "narrow"),
        P("wide", "narrow"),
        P("wide", "narrow"),
        P("wide", "narrow"),
        P("wide", "narrow"),
        P("wide", "narrow"),
        P("wide", "narrow"),
        P("wide", "narrow"),
        P("narrow"),
        P("narrow"),
        P("narrow"),
    )
    out_specs = (
        P(("wide", "narrow"), None, None),
        P(("wide", "narrow"), None, None),
        P(("wide", "narrow"), None, None),
        P("wide", "narrow"),
        P("wide", "narrow"),
        P("wide", "narrow"),
        P("wide", "narrow"),
        P("wide", "narrow"),
        P("wide", "narrow"),
        P("wide", "narrow"),
        P("wide", "narrow"),
        P("wide", "narrow"),
        P("wide", "narrow"),
        P("wide", "narrow"),
        P("wide", "narrow"),
        P("wide", "narrow"),
        P("wide", "narrow"),
        P("wide", "narrow"),
        P("narrow"),
        P("narrow"),
        P("narrow"),
    )
    tuned = mesh.shape["wide"] == 8 and mesh.shape["narrow"] == 4
    return jax.shard_map(
        on_device if tuned else general_device, mesh=mesh, in_specs=in_specs, out_specs=out_specs, check_vma=False
    )
```

```python
import jax
import jax.numpy as jnp
from jax import lax
from jax.experimental import pallas as pl
from jax.experimental.pallas import tpu as pltpu
from jax.sharding import PartitionSpec as P

D = 1152
FF = 4608
H = 16
HD = 72
STEP = 5


norm_epsilon = 1e-05
adam_epsilon = 1e-08
beta_moment = 0.5
weight_decay = 0.01
rate_merge = 0.04
rate_attend = 0.08
rate_output = 0.6
rate_expand = 0.06
rate_shrink = 0.03
rate_vector = 0.6


def product(left_side, right_side):
    return jnp.dot(left_side, right_side, preferred_element_type=jnp.float32)


def transposed(gradient, matrix):
    return lax.dot_general(
        gradient,
        matrix,
        (((gradient.ndim - 1,), (1,)), ((), ())),
        preferred_element_type=jnp.float32,
    )


def weight_gradient(activations, gradient):
    flat_left = activations.reshape(-1, activations.shape[-1])
    flat_right = gradient.reshape(-1, gradient.shape[-1])
    return lax.dot_general(
        flat_left, flat_right, (((0,), (0,)), ((), ())), preferred_element_type=jnp.float32
    )


def normalize(values):
    centered = values - jnp.mean(values, axis=-1, keepdims=True)
    spread = jnp.mean(centered * centered, axis=-1, keepdims=True)
    inverse = lax.rsqrt(spread + norm_epsilon)
    return (centered * inverse, inverse)


def norm_back(gradient, normed, inverse):
    return inverse * (
        gradient
        - jnp.mean(gradient, axis=-1, keepdims=True)
        - normed * jnp.mean(gradient * normed, axis=-1, keepdims=True)
    )


def row_sum(values):
    return jnp.sum(values, axis=(0, 1))


def unpack(packed):
    return tuple((packed[position * D : (position + 1) * D] for position in range(7))) + (
        packed[7 * D : 7 * D + FF],
    )


def gaussian_unit(values):
    return jax.nn.gelu(values, approximate=False)


def adamw_update(weight, moment, square, gradient, step_rate):
    moment_new = beta_moment * moment + (1.0 - beta_moment) * gradient
    square_new = beta_moment * square + (1.0 - beta_moment) * gradient * gradient
    correct = 1.0 - beta_moment**STEP
    direction = moment_new / correct / (jnp.sqrt(square_new / correct) + adam_epsilon)
    return (weight - step_rate * (direction + weight_decay * weight), moment_new, square_new)


def general_device(
    inputs,
    skip_tokens,
    cotangent,
    merge_weight,
    merge_moment,
    merge_square,
    attend_weight,
    attend_moment,
    attend_square,
    output_weight,
    output_moment,
    output_square,
    expand_weight,
    expand_moment,
    expand_square,
    shrink_weight,
    shrink_moment,
    shrink_square,
    vectors,
    vector_moment,
    vector_square,
):
    merge_low = merge_weight.astype(jnp.bfloat16)
    attend_low = attend_weight.astype(jnp.bfloat16)
    output_low = output_weight.astype(jnp.bfloat16)
    expand_low = expand_weight.astype(jnp.bfloat16)
    shrink_low = shrink_weight.astype(jnp.bfloat16)
    vector_low = vectors.astype(jnp.bfloat16)
    columns = (
        lax.all_gather(merge_low, "narrow", axis=1, tiled=True),
        lax.all_gather(attend_low, "narrow", axis=1, tiled=True),
        lax.all_gather(output_low, "narrow", axis=1, tiled=True),
        lax.all_gather(expand_low, "narrow", axis=1, tiled=True),
        lax.all_gather(shrink_low, "narrow", axis=1, tiled=True),
        lax.all_gather(vector_low, "narrow", axis=0, tiled=True),
    )
    matrices = (
        lax.all_gather(columns[0], "wide", axis=0, tiled=True),
        lax.all_gather(columns[1], "wide", axis=0, tiled=True),
        lax.all_gather(columns[2], "wide", axis=0, tiled=True),
        lax.all_gather(columns[3], "wide", axis=0, tiled=True),
        lax.all_gather(columns[4], "wide", axis=0, tiled=True),
    )
    skip_bias, gain_one, bias_one, output_bias, gain_two, bias_two, shrink_bias, expand_bias = (
        unpack(columns[5].astype(jnp.float32))
    )
    images = inputs.shape[0]
    length = inputs.shape[1]
    softmax_scale = HD ** (-0.5)
    joined = jnp.concatenate([inputs, skip_tokens], axis=-1)
    stream_zero = product(joined, matrices[0]) + skip_bias
    normed_one, inverse_one = normalize(stream_zero)
    attend_input = (normed_one * gain_one + bias_one).astype(jnp.bfloat16)
    mixed_heads = product(attend_input, matrices[1]).astype(jnp.bfloat16)
    query_heads = mixed_heads[..., 0:D].reshape(images, length, H, HD)
    key_heads = mixed_heads[..., D : 2 * D].reshape(images, length, H, HD)
    value_heads = mixed_heads[..., 2 * D : 3 * D].reshape(images, length, H, HD)
    logits = (
        jnp.einsum("blhe,bmhe->bhlm", query_heads, key_heads, preferred_element_type=jnp.float32)
        * softmax_scale
    )
    maxima = jnp.max(logits, axis=-1, keepdims=True)
    log_total = maxima + jnp.log(jnp.sum(jnp.exp(logits - maxima), axis=-1, keepdims=True))
    softmax_low = jnp.exp(logits - log_total).astype(jnp.bfloat16)
    mixture = jnp.einsum(
        "bhlm,bmhe->blhe", softmax_low, value_heads, preferred_element_type=jnp.float32
    )
    mixture = mixture.astype(jnp.bfloat16).reshape(images, length, D)
    stream_one = stream_zero + product(mixture, matrices[2]) + output_bias
    normed_two, inverse_two = normalize(stream_one)
    expand_input = (normed_two * gain_two + bias_two).astype(jnp.bfloat16)
    hidden = product(expand_input, matrices[3]) + expand_bias
    active, pullback = jax.vjp(gaussian_unit, hidden)
    active_low = active.astype(jnp.bfloat16)
    outputs = (stream_one + product(active_low, matrices[4]) + shrink_bias).astype(jnp.bfloat16)
    columns_back = (
        lax.all_gather(merge_low, "narrow", axis=1, tiled=True),
        lax.all_gather(attend_low, "narrow", axis=1, tiled=True),
        lax.all_gather(output_low, "narrow", axis=1, tiled=True),
        lax.all_gather(expand_low, "narrow", axis=1, tiled=True),
        lax.all_gather(shrink_low, "narrow", axis=1, tiled=True),
        lax.all_gather(vector_low, "narrow", axis=0, tiled=True),
    )
    matrices_back = (
        lax.all_gather(columns_back[0], "wide", axis=0, tiled=True),
        lax.all_gather(columns_back[1], "wide", axis=0, tiled=True),
        lax.all_gather(columns_back[2], "wide", axis=0, tiled=True),
        lax.all_gather(columns_back[3], "wide", axis=0, tiled=True),
        lax.all_gather(columns_back[4], "wide", axis=0, tiled=True),
    )
    packed_back = columns_back[5].astype(jnp.float32)
    unpacked = unpack(packed_back)
    gain_first = unpacked[1]
    gain_second = unpacked[4]
    upstream = cotangent.astype(jnp.float32)
    shrink_gradient = weight_gradient(active_low, cotangent)
    delta_active = transposed(cotangent, matrices_back[4])
    delta_hidden = pullback(delta_active)[0]
    hidden_low = delta_hidden.astype(jnp.bfloat16)
    expand_gradient = weight_gradient(expand_input, hidden_low)
    delta_expand = transposed(hidden_low, matrices_back[3])
    delta_one = upstream + norm_back(delta_expand * gain_second, normed_two, inverse_two)
    stream_low = delta_one.astype(jnp.bfloat16)
    output_gradient = weight_gradient(mixture, stream_low)
    delta_mixture = (
        transposed(stream_low, matrices_back[2]).astype(jnp.bfloat16).reshape(images, length, H, HD)
    )
    logits_again = (
        jnp.einsum("blhe,bmhe->bhlm", query_heads, key_heads, preferred_element_type=jnp.float32)
        * softmax_scale
    )
    softmax_again = jnp.exp(logits_again - log_total)
    delta_softmax = jnp.einsum(
        "blhe,bmhe->bhlm", delta_mixture, value_heads, preferred_element_type=jnp.float32
    )
    delta_values = jnp.einsum(
        "bhlm,blhe->bmhe",
        softmax_again.astype(jnp.bfloat16),
        delta_mixture,
        preferred_element_type=jnp.float32,
    )
    delta_logits = softmax_again * (
        delta_softmax - jnp.sum(softmax_again * delta_softmax, axis=-1, keepdims=True)
    )
    delta_scores = (softmax_scale * delta_logits).astype(jnp.bfloat16)
    delta_queries = jnp.einsum(
        "bhlm,bmhe->blhe", delta_scores, key_heads, preferred_element_type=jnp.float32
    )
    delta_keys = jnp.einsum(
        "bhlm,blhe->bmhe", delta_scores, query_heads, preferred_element_type=jnp.float32
    )
    delta_mixed = jnp.concatenate(
        [
            delta_queries.reshape(images, length, D),
            delta_keys.reshape(images, length, D),
            delta_values.reshape(images, length, D),
        ],
        axis=-1,
    ).astype(jnp.bfloat16)
    attend_gradient = weight_gradient(attend_input, delta_mixed)
    delta_attend = transposed(delta_mixed, matrices_back[1])
    delta_zero = delta_one + norm_back(delta_attend * gain_first, normed_one, inverse_one)
    zero_low = delta_zero.astype(jnp.bfloat16)
    merge_gradient = weight_gradient(joined, zero_low)
    delta_joined = transposed(zero_low, matrices_back[0])
    input_gradient = delta_joined[..., 0:D].astype(jnp.bfloat16)
    skip_gradient = delta_joined[..., D : 2 * D].astype(jnp.bfloat16)
    vector_gradient = jnp.concatenate(
        [
            row_sum(delta_zero),
            row_sum(delta_attend * normed_one),
            row_sum(delta_attend),
            row_sum(delta_one),
            row_sum(delta_expand * normed_two),
            row_sum(delta_expand),
            row_sum(upstream),
            row_sum(delta_hidden),
        ]
    )
    owned_rows = (
        lax.psum_scatter(merge_gradient, "wide", scatter_dimension=0, tiled=True),
        lax.psum_scatter(attend_gradient, "wide", scatter_dimension=0, tiled=True),
        lax.psum_scatter(output_gradient, "wide", scatter_dimension=0, tiled=True),
        lax.psum_scatter(expand_gradient, "wide", scatter_dimension=0, tiled=True),
        lax.psum_scatter(shrink_gradient, "wide", scatter_dimension=0, tiled=True),
    )
    vector_total = lax.psum(vector_gradient, "wide")
    parted = (
        lax.psum_scatter(owned_rows[0], "narrow", scatter_dimension=1, tiled=True),
        lax.psum_scatter(owned_rows[1], "narrow", scatter_dimension=1, tiled=True),
        lax.psum_scatter(owned_rows[2], "narrow", scatter_dimension=1, tiled=True),
        lax.psum_scatter(owned_rows[3], "narrow", scatter_dimension=1, tiled=True),
        lax.psum_scatter(owned_rows[4], "narrow", scatter_dimension=1, tiled=True),
        lax.psum_scatter(vector_total, "narrow", scatter_dimension=0, tiled=True),
    )
    merge_new = adamw_update(merge_weight, merge_moment, merge_square, parted[0], rate_merge)
    attend_new = adamw_update(attend_weight, attend_moment, attend_square, parted[1], rate_attend)
    output_new = adamw_update(output_weight, output_moment, output_square, parted[2], rate_output)
    expand_new = adamw_update(expand_weight, expand_moment, expand_square, parted[3], rate_expand)
    shrink_new = adamw_update(shrink_weight, shrink_moment, shrink_square, parted[4], rate_shrink)
    vector_new = adamw_update(vectors, vector_moment, vector_square, parted[5], rate_vector)
    return (
        outputs,
        input_gradient,
        skip_gradient,
        merge_new[0],
        merge_new[1],
        merge_new[2],
        attend_new[0],
        attend_new[1],
        attend_new[2],
        output_new[0],
        output_new[1],
        output_new[2],
        expand_new[0],
        expand_new[1],
        expand_new[2],
        shrink_new[0],
        shrink_new[1],
        shrink_new[2],
        vector_new[0],
        vector_new[1],
        vector_new[2],
    )


CORE = 1
ACROSS = 2
ALONG = 4
PAD = 384
VMEM_BYTES = 56 * 1024 * 1024
LIGHT = pl.CostEstimate(flops=0, bytes_accessed=1024, transcendentals=0)
PARAMS = pltpu.CompilerParams(vmem_limit_bytes=VMEM_BYTES)


def swap_wide(value, bit):
    return lax.ppermute(value, "wide", [(i, i ^ bit) for i in range(8)])


def swap_narrow(value, bit):
    return lax.ppermute(value, "narrow", [(i, i ^ bit) for i in range(4)])


def together(*values):
    return lax.optimization_barrier(values)


def spot():
    wide = lax.axis_index("wide")
    narrow = lax.axis_index("narrow")
    return (wide & 1, (wide >> 1) & 1, (wide >> 2) & 1, narrow & 1, narrow >> 1)


def split_rows(rows):
    return -(-rows // 32) * 16


def column_blocks(kind, quarter):
    if kind == "attend_output":
        width = quarter // 8
        order = [8 * part + 2 * n + p for part in range(3) for p in range(2) for n in range(4)]
        blocks = [(block // 6, (block % 6) * width) for block in order]
        return width, blocks + [(n, (6 + p) * width) for p in range(2) for n in range(4)]
    width = quarter // 2
    return width, [(n, p * width) for p in range(2) for n in range(4)]


def fold(shard):
    parts = max(1, shard.shape[0] // (D // 8))
    height = shard.shape[0] // parts
    return jnp.concatenate(
        [shard[part * height : (part + 1) * height] for part in range(parts)], axis=1
    )


def unfold(value, rows):
    parts = rows // value.shape[0]
    quarter = value.shape[1] // parts
    return jnp.concatenate(
        [value[:, part * quarter : (part + 1) * quarter] for part in range(parts)], axis=0
    )


def arrange(kind, parts, shard, others, extra=0):
    height = shard.shape[0] - extra
    rows, quarter = parts * height, shard.shape[1] // parts
    width, blocks = column_blocks(kind, quarter)

    def kernel(*refs):
        full, apart, held = refs[4], refs[5], refs[-1]
        narrow = lax.axis_index("narrow")
        for relative in range(4):
            held[relative] = refs[relative][...]
        for number in range(4):
            value = held[narrow ^ number]
            if extra:
                apart[number] = value[height:]
            for position, (owner, offset) in enumerate(blocks):
                if owner == number:
                    column = slice(position * width, (position + 1) * width)
                    for part in range(parts):
                        start = part * quarter + offset
                        full[part * height : (part + 1) * height, column] = value[
                            :height, start : start + width
                        ]

    outs = [jax.ShapeDtypeStruct((rows, 4 * quarter), jnp.bfloat16)]
    if extra:
        outs.append(jax.ShapeDtypeStruct((4, extra, shard.shape[1]), jnp.bfloat16))
    return pl.pallas_call(
        kernel,
        out_shape=tuple(outs),
        scratch_shapes=[pltpu.VMEM((4,) + shard.shape, jnp.bfloat16)],
        compiler_params=PARAMS,
        cost_estimate=LIGHT,
    )(shard, *others)


def weight_scratch(rows, columns):
    return [pltpu.VMEM((rows, columns), jnp.bfloat16), pltpu.SemaphoreType.DMA((8,))]


def fetch(refs, full, sems, columns=None):
    wide = lax.axis_index("wide")
    core, chip = wide & 1, wide >> 1
    rows = full.shape[0] // 8
    copies = []
    for number, (ends, from_x, from_y) in enumerate((refs[:3], refs[3:])):
        parity = core if number == 0 else 1 - core
        own, far = ends.at[pl.ds(0, rows)], ends.at[pl.ds(rows, rows)]
        for relative, piece in enumerate((own, from_x, from_y, far)):
            if columns is not None:
                piece = piece.at[:, columns]
            start = pl.multiple_of((4 * parity + (chip ^ relative)) * rows, 16)
            copies.append(
                pltpu.make_async_copy(
                    piece, full.at[pl.ds(start, rows)], sems.at[4 * number + relative]
                )
            )
    for copy in copies:
        copy.start()
    for copy in copies:
        copy.wait()


def pair_gradient(lefts, rights):
    height = lefts[0][0].shape[0]
    rows = height // 4
    split = split_rows(rows)
    tokens = rights[0][0].shape[0]
    widths = [right[0].shape[1] for right in rights]
    tile = 384 if height > 576 else 1152
    steps = [width // tile for width in widths]
    starts = [sum(steps[:position]) for position in range(len(steps))]
    count = len(lefts)

    def kernel(*refs):
        left_refs = refs[: 2 * count]
        right_refs = refs[2 * count : 4 * count]
        outs, (joint, beside) = refs[4 * count : 4 * count + 8], refs[4 * count + 8 :]
        step = pl.program_id(0)
        wide = lax.axis_index("wide")
        across, along = (wide >> 1) & 1, (wide >> 2) & 1

        @pl.when(step == 0)
        def _():
            joint[...] = jnp.zeros_like(joint)

        for number in range(count):

            @pl.when(step == starts[number])
            def _():
                beside[:, :PAD] = left_refs[2 * number][...]
                beside[:, PAD:] = left_refs[2 * number + 1][...]

            @pl.when((step >= starts[number]) & (step < starts[number] + steps[number]))
            def _():
                joint[:tokens] = right_refs[2 * number][...]
                joint[PAD : PAD + tokens] = right_refs[2 * number + 1][...]
                for y in range(2):
                    for x in range(2):
                        first_row = (2 * y + x) * rows
                        total = jnp.dot(
                            beside[first_row : first_row + rows],
                            joint[...],
                            preferred_element_type=jnp.float32,
                        ).astype(jnp.bfloat16)

                        for kept_x in range(2):
                            for kept_y in range(2):

                                @pl.when(
                                    ((across == x) == (kept_x == 1))
                                    & ((along == y) == (kept_y == 1))
                                )
                                def _():
                                    outs[2 * (1 - kept_x) + (1 - kept_y)][...] = total[:split]
                                    outs[4 + 2 * (1 - kept_y) + (1 - kept_x)][...] = total[split:]

    def right_spec(number):
        return pl.BlockSpec(
            (tokens, tile),
            lambda i: (0, jnp.clip(i - starts[number], 0, steps[number] - 1)),
        )

    in_specs = [pl.BlockSpec((height, PAD), lambda i: (0, 0))] * (2 * count)
    operands = [left for pair in lefts for left in pair]
    for number in range(count):
        in_specs += [right_spec(number)] * 2
        operands += list(rights[number])
    top_spec = pl.BlockSpec((split, tile), lambda i: (0, i))
    bottom_spec = pl.BlockSpec((rows - split, tile), lambda i: (0, i))
    top_shape = jax.ShapeDtypeStruct((split, sum(widths)), jnp.bfloat16)
    bottom_shape = jax.ShapeDtypeStruct((rows - split, sum(widths)), jnp.bfloat16)
    outs = pl.pallas_call(
        kernel,
        grid=(sum(steps),),
        in_specs=in_specs,
        out_specs=(top_spec,) * 4 + (bottom_spec,) * 4,
        out_shape=(top_shape,) * 4 + (bottom_shape,) * 4,
        scratch_shapes=[
            pltpu.VMEM((2 * PAD, tile), jnp.bfloat16),
            pltpu.VMEM((height, 2 * PAD), jnp.bfloat16),
        ],
        compiler_params=PARAMS,
        cost_estimate=LIGHT,
    )(*operands)
    return outs[:4], outs[4:]


def unarrange(kind, parts, top, bottom):
    split, columns = top[0].shape
    rest = bottom[0].shape[0]
    rows = split + rest
    quarter = columns // 4
    height = rows // parts
    width, blocks = column_blocks(kind, quarter)

    def kernel(*refs):
        tops, bottoms = refs[:3], refs[3:6]
        keep_ref, keep_far_ref, send_ref, send_far_ref, held = refs[6:]
        narrow = lax.axis_index("narrow")
        low_bit, high_bit = narrow & 1, narrow >> 1
        held[:split] = add_low(*[ref[...] for ref in tops])
        held[split:] = add_low(*[ref[...] for ref in bottoms])
        for position, (owner, offset) in enumerate(blocks):
            piece = held[:, position * width : (position + 1) * width]
            for kept_low in range(2):
                for kept_high in range(2):
                    target = (keep_ref, keep_far_ref, send_ref, send_far_ref)[
                        2 * (1 - kept_low) + (1 - kept_high)
                    ]

                    @pl.when(
                        ((low_bit == (owner & 1)) == (kept_low == 1))
                        & ((high_bit == (owner >> 1)) == (kept_high == 1))
                    )
                    def _():
                        for part in range(parts):
                            start = part * quarter + offset
                            target[:, start : start + width] = piece[
                                part * height : (part + 1) * height
                            ]

    shape = jax.ShapeDtypeStruct((height, parts * quarter), jnp.bfloat16)
    return pl.pallas_call(
        kernel,
        out_shape=(shape,) * 4,
        scratch_shapes=[pltpu.VMEM((rows, columns), jnp.bfloat16)],
        compiler_params=PARAMS,
        cost_estimate=LIGHT,
    )(*top, *bottom)


def add_low(*terms):
    return sum(term.astype(jnp.float32) for term in terms).astype(jnp.bfloat16)


def pick(value, index, dim=0):
    return lax.dynamic_index_in_dim(value, index, dim, keepdims=False)


def halves_of(value, core):
    middle = value.shape[-1] // 2
    first, second = value[..., :middle], value[..., middle:]
    return jnp.where(core == 0, first, second), jnp.where(core == 0, second, first)


def inner(value):
    width = value.shape[-1] // 8
    return jnp.concatenate(
        [
            value[..., (2 * n + p) * width : (2 * n + p + 1) * width]
            for p in range(2)
            for n in range(4)
        ],
        axis=-1,
    )


def outer(value):
    width = value.shape[-1] // 8
    return jnp.concatenate(
        [
            value[..., (4 * p + n) * width : (4 * p + n + 1) * width]
            for n in range(4)
            for p in range(2)
        ],
        axis=-1,
    )


def upright(value):
    return jnp.pad(value, ((0, PAD - value.shape[0]), (0, 0))).T


def both(parts, order):
    if order == 0:
        return swap_wide(parts[0], ACROSS), swap_wide(parts[1], ALONG)
    return swap_wide(parts[0], ALONG), swap_wide(parts[1], ACROSS)


KEEP_NEAR, KEEP_FAR, SEND_NEAR, SEND_FAR = range(4)


def send(blocks, which):
    return both((blocks[0][which], blocks[1][which]), 0)


def forward(blocks, got):
    return both(tuple(add_low(blocks[i][KEEP_FAR], got[i]) for i in range(2)), 1)


def settle(kind, parts, blocks, got_near, got_last):
    return unarrange(
        kind, parts, *[(blocks[i][KEEP_NEAR], got_near[i], got_last[i]) for i in range(2)]
    )


def narrow_first(quarters):
    return swap_narrow(quarters[SEND_FAR], 1), swap_narrow(quarters[SEND_NEAR], 1)


def narrow_second(quarters, got):
    return swap_narrow(add_low(quarters[KEEP_FAR], got[0]), 2)


def finish(quarters, got, got_last):
    return (
        quarters[KEEP_NEAR].astype(jnp.float32)
        + got[1].astype(jnp.float32)
        + got_last.astype(jnp.float32)
    )


def across_narrow(shard):
    return tuple(swap_narrow(shard, bit) for bit in (1, 2, 3))


def gather_first(block):
    return swap_wide(block, ACROSS), swap_wide(block, ALONG)


def gather_second(first):
    split = split_rows(first[0].shape[0])
    return swap_wide(first[0][:split], ALONG), swap_wide(first[1][split:], ACROSS)


def swap_sides(first):
    return swap_wide(first[0], CORE), swap_wide(first[1], CORE)


def ends_of(block, second):
    return jnp.concatenate([block, second[0], second[1]], axis=0)


def heavy(kernel, outs, scratch, weights, operands):
    return pl.pallas_call(
        kernel,
        in_specs=[pl.BlockSpec(memory_space=pl.ANY)] * len(weights)
        + [pl.BlockSpec(memory_space=pltpu.VMEM)] * len(operands),
        out_shape=tuple(jax.ShapeDtypeStruct(shape, dtype) for shape, dtype in outs),
        scratch_shapes=scratch,
        compiler_params=PARAMS,
        cost_estimate=LIGHT,
    )(*weights, *operands)


def dot_rows(left, right):
    return lax.dot_general(left, right, (((1,), (1,)), ((), ())), preferred_element_type=jnp.float32)


def dot_depth(left, right):
    return lax.dot_general(left, right, (((0,), (0,)), ((), ())), preferred_element_type=jnp.float32)


def store_upright(value, padded, mine, other):
    features = value.shape[1]
    padded[: value.shape[0]] = value
    turned = padded[...].T.astype(jnp.bfloat16)
    core = lax.axis_index("wide") & 1

    @pl.when(core == 0)
    def _():
        mine[...] = turned[: features // 2]
        other[...] = turned[features // 2 :]

    @pl.when(core == 1)
    def _():
        other[...] = turned[: features // 2]
        mine[...] = turned[features // 2 :]


def merge_forward(joined, weight, bias, gain, shift):
    length = joined.shape[0]

    def kernel(*refs):
        joined_ref, bias_ref, gain_ref, shift_ref = refs[6:10]
        stream, entry, up_mine, up_other, full, sems, padded = refs[10:]
        fetch(refs[:6], full, sems)
        padded[...] = jnp.zeros_like(padded)
        stream[...] = product(joined_ref[...], full[...]) + bias_ref[...]
        normed = normalize(stream[...])[0]
        value = (normed * gain_ref[...] + shift_ref[...]).astype(jnp.bfloat16)
        entry[...] = value
        store_upright(value.astype(jnp.float32), padded, up_mine, up_other)

    return heavy(
        kernel,
        [
            ((length, D), jnp.float32),
            ((length, D), jnp.bfloat16),
            ((D // 2, PAD), jnp.bfloat16),
            ((D // 2, PAD), jnp.bfloat16),
        ],
        weight_scratch(2 * D, D) + [pltpu.VMEM((PAD, D), jnp.float32)],
        weight,
        (joined, bias, gain, shift),
    )


def attend_head(heads, head, chances_ref, slot):
    at = head * HD
    queries = heads[:, at : at + HD]
    keys = heads[:, D + at : D + at + HD]
    values = heads[:, 2 * D + at : 2 * D + at + HD]
    logits = dot_rows(queries, keys) * HD ** (-0.5)
    powers = jnp.exp(logits - jnp.max(logits, axis=-1, keepdims=True))
    chances = powers / jnp.sum(powers, axis=-1, keepdims=True)
    chances_ref[slot] = chances
    return product(chances.astype(jnp.bfloat16), values).astype(jnp.bfloat16)


def attend_first(entry, weight):
    length = entry.shape[0]

    def kernel(*refs):
        entry_ref, heads, chances_ref, mix_ref, full, sems = refs[6:]
        fetch(refs[:6], full, sems, pl.ds(0, 3 * D))
        for part in range(3):
            columns = slice(part * D, (part + 1) * D)
            heads[:, columns] = product(entry_ref[...], full[:, columns]).astype(jnp.bfloat16)
        for head in range(H // 2):
            mix_ref[:, head * HD : (head + 1) * HD] = attend_head(heads, head, chances_ref, head)

    return heavy(
        kernel,
        [
            ((length, 3 * D), jnp.bfloat16),
            ((H // 2, length, length), jnp.float32),
            ((length, D // 2), jnp.bfloat16),
        ],
        weight_scratch(D, 3 * D),
        weight,
        (entry,),
    )


def attend_second(heads, mix_first, weight, stream_zero, bias, gain, shift):
    length = heads.shape[0]
    half = D // 2

    def kernel(*refs):
        heads_ref, first_ref, zero_ref, bias_ref, gain_ref, shift_ref = refs[6:12]
        chances_ref, stream, value_ref, up_mine, up_other, full, sems, mixed, padded = refs[12:]
        fetch(refs[:6], full, sems, pl.ds(3 * D, D))
        padded[...] = jnp.zeros_like(padded)
        mixed[:, :half] = first_ref[...]
        for head in range(H // 2, H):
            mixed[:, head * HD : (head + 1) * HD] = attend_head(
                heads_ref, head, chances_ref, head - H // 2
            )
        stream[...] = zero_ref[...] + product(mixed[...], full[...]) + bias_ref[...]
        store_upright(
            mixed[...].astype(jnp.float32), padded, up_mine.at[pl.ds(0, half)], up_other.at[pl.ds(0, half)]
        )
        normed = normalize(stream[...])[0]
        value = (normed * gain_ref[...] + shift_ref[...]).astype(jnp.bfloat16)
        value_ref[...] = value
        store_upright(
            value.astype(jnp.float32), padded, up_mine.at[pl.ds(half, half)], up_other.at[pl.ds(half, half)]
        )

    return heavy(
        kernel,
        [
            ((H // 2, length, length), jnp.float32),
            ((length, D), jnp.float32),
            ((length, D), jnp.bfloat16),
            ((D, PAD), jnp.bfloat16),
            ((D, PAD), jnp.bfloat16),
        ],
        weight_scratch(D, D)
        + [pltpu.VMEM((length, D), jnp.bfloat16), pltpu.VMEM((PAD, D), jnp.float32)],
        weight,
        (heads, mix_first, stream_zero, bias, gain, shift),
    )


def expand_forward(entry, weight, bias):
    length = entry.shape[0]

    def kernel(*refs):
        entry_ref, bias_ref = refs[6:8]
        active_ref, slope_ref, up_mine, up_other, full, sems, padded = refs[8:]
        core = lax.axis_index("wide") & 1
        fetch(refs[:6], full, sems)
        padded[...] = jnp.zeros_like(padded)
        for step in range(FF // D):
            columns = slice(step * D, (step + 1) * D)
            value = product(entry_ref[...], full[:, columns]) + bias_ref[:, columns]
            inside = 0.5 * (1.0 + lax.erf(value * (0.5**0.5)))
            bell = jnp.exp(-0.5 * value * value) * (2.0 * jnp.pi) ** -0.5
            active = (value * inside).astype(jnp.bfloat16)
            slope_ref[:, columns] = inside + value * bell
            active_ref[:, columns] = active
            padded[:length] = active.astype(jnp.float32)
            turned = padded[...].T.astype(jnp.bfloat16)
            rows = slice((step % 2) * D, (step % 2 + 1) * D)

            @pl.when(core == step // 2)
            def _():
                up_mine[rows] = turned

            @pl.when(core != step // 2)
            def _():
                up_other[rows] = turned

    return heavy(
        kernel,
        [
            ((length, FF), jnp.bfloat16),
            ((length, FF), jnp.float32),
            ((FF // 2, PAD), jnp.bfloat16),
            ((FF // 2, PAD), jnp.bfloat16),
        ],
        weight_scratch(D, FF) + [pltpu.VMEM((PAD, D), jnp.float32)],
        weight,
        (entry, bias),
    )


def hidden_backward(pulled, weight, slope):
    length = pulled.shape[0]

    def kernel(*refs):
        pulled_ref, slope_ref, low_ref, sum_ref, full, sems = refs[6:]
        fetch(refs[:6], full, sems)
        for step in range(FF // D):
            columns = slice(step * D, (step + 1) * D)
            delta = dot_rows(pulled_ref[...], full[columns]) * slope_ref[:, columns]
            low_ref[:, columns] = delta.astype(jnp.bfloat16)
            sum_ref[:, columns] = jnp.sum(delta, axis=0, keepdims=True)

    return heavy(
        kernel,
        [((length, FF), jnp.bfloat16), ((1, FF), jnp.float32)],
        weight_scratch(FF, D),
        weight,
        (pulled, slope),
    )


def expand_backward(hidden_low, weight, mixed_weight, pulled, stream_one, gain):
    length = pulled.shape[0]

    def kernel(*refs):
        hidden_ref, pulled_ref, stream_ref, gain_ref = refs[12:16]
        one_ref, low_ref, sums, mix_ref, full, sems, output, output_sems = refs[16:]
        fetch(refs[:6], full, sems)
        fetch(refs[6:12], output, output_sems, pl.ds(3 * D, D))
        value = dot_rows(hidden_ref[...], full[...])
        normed, inverse = normalize(stream_ref[...])
        upstream = pulled_ref[...].astype(jnp.float32)
        one = upstream + norm_back(value * gain_ref[...], normed, inverse)
        one_ref[...] = one
        low_value = one.astype(jnp.bfloat16)
        low_ref[...] = low_value
        sums[0:1] = jnp.sum(one, axis=0, keepdims=True)
        sums[1:2] = jnp.sum(value * normed, axis=0, keepdims=True)
        sums[2:3] = jnp.sum(value, axis=0, keepdims=True)
        sums[3:4] = jnp.sum(upstream, axis=0, keepdims=True)
        mix_ref[...] = dot_rows(low_value, output[...]).astype(jnp.bfloat16)

    return heavy(
        kernel,
        [
            ((length, D), jnp.float32),
            ((length, D), jnp.bfloat16),
            ((4, D), jnp.float32),
            ((length, D), jnp.bfloat16),
        ],
        weight_scratch(D, FF) + weight_scratch(D, D),
        (*weight, *mixed_weight),
        (hidden_low, pulled, stream_one, gain),
    )


def attend_backward(heads, chances_first, chances_second, delta_mixture):
    length = heads.shape[0]
    scale = HD ** (-0.5)

    def kernel(heads_ref, first_ref, second_ref, delta_ref, mixed):
        for head in range(H):
            at = head * HD
            queries = heads_ref[:, at : at + HD]
            keys = heads_ref[:, D + at : D + at + HD]
            values = heads_ref[:, 2 * D + at : 2 * D + at + HD]
            delta = delta_ref[:, at : at + HD]
            chances = (first_ref, second_ref)[head // (H // 2)][head % (H // 2)]
            pull = dot_rows(delta, values)
            inner_sum = jnp.sum(chances * pull, axis=-1, keepdims=True)
            scores = (scale * (chances * (pull - inner_sum))).astype(jnp.bfloat16)
            mixed[:, at : at + HD] = product(scores, keys).astype(jnp.bfloat16)
            mixed[:, D + at : D + at + HD] = dot_depth(scores, queries).astype(jnp.bfloat16)
            mixed[:, 2 * D + at : 2 * D + at + HD] = dot_depth(
                chances.astype(jnp.bfloat16), delta
            ).astype(jnp.bfloat16)

    return heavy(
        kernel,
        [((length, 3 * D), jnp.bfloat16)],
        [],
        (),
        (heads, chances_first, chances_second, delta_mixture),
    )[0]


def entry_backward(delta_mixed, weight, delta_one, stream_zero, gain):
    length = delta_mixed.shape[0]

    def kernel(*refs):
        mixed_ref, one_ref, stream_ref, gain_ref, low_ref, sums, full, sems = refs[6:]
        fetch(refs[:6], full, sems, pl.ds(0, 3 * D))
        value = dot_rows(mixed_ref[...], full[...])
        normed, inverse = normalize(stream_ref[...])
        zero = one_ref[...] + norm_back(value * gain_ref[...], normed, inverse)
        low_ref[...] = zero.astype(jnp.bfloat16)
        sums[0:1] = jnp.sum(zero, axis=0, keepdims=True)
        sums[1:2] = jnp.sum(value * normed, axis=0, keepdims=True)
        sums[2:3] = jnp.sum(value, axis=0, keepdims=True)

    return heavy(
        kernel,
        [((length, D), jnp.bfloat16), ((3, D), jnp.float32)],
        weight_scratch(D, 3 * D),
        weight,
        (delta_mixed, delta_one, stream_zero, gain),
    )


def joined_backward(zero_low, weight):
    length = zero_low.shape[0]
    width = 2 * D // 8

    def kernel(*refs):
        zero_ref, first_ref, second_ref, full, sems = refs[6:]
        fetch(refs[:6], full, sems)
        for parity in range(2):
            delta = dot_rows(zero_ref[...], full[parity * D : (parity + 1) * D])
            delta = delta.astype(jnp.bfloat16)
            for number in range(4):
                target = (first_ref, second_ref)[number // 2]
                column = (2 * (number % 2) + parity) * width
                target[:, column : column + width] = delta[:, number * width : (number + 1) * width]

    out = ((length, D), jnp.bfloat16)
    return heavy(kernel, [out, out], weight_scratch(2 * D, D), weight, (zero_low,))


def shrink_forward(active, weight, stream_one, bias):
    length = active.shape[0]
    width = D // 8

    def kernel(*refs):
        active_ref, stream_ref, bias_ref, out_ref, full, sems = refs[6:]
        fetch(refs[:6], full, sems)
        total = (
            stream_ref[...] + product(active_ref[...], full[...]) + bias_ref[...]
        ).astype(jnp.bfloat16)
        for parity in range(2):
            for number in range(4):
                column = (2 * number + parity) * width
                source = (4 * parity + number) * width
                out_ref[:, column : column + width] = total[:, source : source + width]

    return heavy(
        kernel,
        [((length, D), jnp.bfloat16)],
        weight_scratch(FF, D),
        weight,
        (active, stream_one, bias),
    )[0]


def on_device(
    inputs,
    skip_tokens,
    cotangent,
    merge_weight,
    merge_moment,
    merge_square,
    attend_weight,
    attend_moment,
    attend_square,
    output_weight,
    output_moment,
    output_square,
    expand_weight,
    expand_moment,
    expand_square,
    shrink_weight,
    shrink_moment,
    shrink_square,
    vectors,
    vector_moment,
    vector_square,
):
    high_bit, low_bit = spot()[4], spot()[3]
    core = spot()[0]
    low = jnp.bfloat16
    columns = attend_weight.shape[1]

    merge_low = fold(merge_weight.astype(low))
    width = merge_low.shape[1]
    count = vectors.shape[0]
    vector_rows = jnp.pad(vectors.astype(low), (0, 16 * width - count)).reshape(16, width)
    merge_low = jnp.concatenate([merge_low, vector_rows], axis=0)
    merge_others = across_narrow(merge_low)
    mixed_low = jnp.concatenate([attend_weight.astype(low), output_weight.astype(low)], axis=1)
    joined = inner(jnp.concatenate([inputs[0], skip_tokens[0]], axis=-1))
    joined_mine, joined_other = halves_of(joined, core)
    pulled = inner(cotangent[0])
    merge_others, mixed_low, joined, joined_mine, joined_other, pulled = together(
        merge_others, mixed_low, joined, joined_mine, joined_other, pulled
    )
    merge_block, vector_parts = arrange("merge", 2, merge_low, merge_others, 16)
    merge_first = gather_first(merge_block)
    mixed_far = swap_narrow(mixed_low, 2)
    mixed_near = swap_narrow(mixed_low, 1)
    expand_low = expand_weight.astype(low)
    merge_first, mixed_far, vector_parts, expand_low = together(
        merge_first, mixed_far, vector_parts, expand_low
    )
    merge_second = gather_second(merge_first)
    merge_sides = swap_sides(merge_first)
    mixed_last = swap_narrow(mixed_far, 1)
    shrink_low = fold(shrink_weight.astype(low))
    pieces = unpack(vector_parts.reshape(4, -1)[:, :count].reshape(-1).astype(jnp.float32))
    pieces = tuple(inner(piece)[None] for piece in pieces)
    merge_second, merge_sides, mixed_near, mixed_last, shrink_low, pieces = together(
        merge_second, merge_sides, mixed_near, mixed_last, shrink_low, pieces
    )
    skip_bias, gain_one, bias_one, output_bias, gain_two, bias_two, shrink_bias, expand_bias = pieces
    mixed_block = arrange("attend_output", 1, mixed_low, (mixed_near, mixed_far, mixed_last))[0]
    mixed_first = gather_first(mixed_block)
    expand_far = swap_narrow(expand_low, 2)
    expand_near = swap_narrow(expand_low, 1)
    merge_ends = ends_of(merge_block, merge_second)
    merge_pieces = (merge_ends, *merge_first, swap_wide(merge_ends, CORE), *merge_sides)
    stream_zero, attend_input, attend_up, attend_up_other = merge_forward(
        joined, merge_pieces, skip_bias, gain_one, bias_one
    )
    joined_up = upright(joined_mine)
    joined_up_other = upright(joined_other)
    (
        mixed_first,
        expand_far,
        expand_near,
        stream_zero,
        attend_input,
        attend_up_other,
        joined_up,
        joined_up_other,
    ) = together(
        mixed_first,
        expand_far,
        expand_near,
        stream_zero,
        attend_input,
        attend_up_other,
        joined_up,
        joined_up_other,
    )
    mixed_second = gather_second(mixed_first)
    mixed_sides = swap_sides(mixed_first)
    expand_last = swap_narrow(expand_far, 1)
    mixed_second, mixed_sides, expand_last = together(mixed_second, mixed_sides, expand_last)
    expand_block = arrange("expand", 1, expand_low, (expand_near, expand_far, expand_last))[0]
    expand_first = gather_first(expand_block)
    shrink_far = swap_narrow(shrink_low, 2)
    shrink_near = swap_narrow(shrink_low, 1)
    mixed_ends = ends_of(mixed_block, mixed_second)
    mixed_pieces = (mixed_ends, *mixed_first, swap_wide(mixed_ends, CORE), *mixed_sides)
    heads, chances_first, mix_first = attend_first(attend_input, mixed_pieces)
    expand_first, shrink_far, shrink_near, heads, mix_first = together(
        expand_first, shrink_far, shrink_near, heads, mix_first
    )
    expand_second = gather_second(expand_first)
    expand_sides = swap_sides(expand_first)
    shrink_last = swap_narrow(shrink_far, 1)
    chances_second, stream_one, expand_input, ups, ups_other = attend_second(
        heads, mix_first, mixed_pieces, stream_zero, output_bias, gain_two, bias_two
    )
    expand_second, expand_sides, shrink_last, expand_input, ups_other = together(
        expand_second, expand_sides, shrink_last, expand_input, ups_other
    )
    shrink_block = arrange("shrink", 4, shrink_low, (shrink_near, shrink_far, shrink_last))[0]
    shrink_first = gather_first(shrink_block)
    expand_ends = ends_of(expand_block, expand_second)
    expand_pieces = (expand_ends, *expand_first, swap_wide(expand_ends, CORE), *expand_sides)
    pulled_sibling = swap_wide(pulled, CORE)
    active, slope, active_up, active_up_other = expand_forward(
        expand_input, expand_pieces, expand_bias
    )
    shrink_first, pulled_sibling, active, slope, active_up, active_up_other = together(
        shrink_first, pulled_sibling, active, slope, active_up, active_up_other
    )
    shrink_second = gather_second(shrink_first)
    shrink_sides = swap_sides(shrink_first)
    active_up_sibling = swap_wide(active_up_other, CORE)
    shrink_blocks = pair_gradient([(active_up, active_up_sibling)], [(pulled, pulled_sibling)])
    shrink_second, shrink_sides, shrink_blocks = together(
        shrink_second, shrink_sides, shrink_blocks
    )
    shrink_far_got = send(shrink_blocks, SEND_FAR)
    shrink_near_got = send(shrink_blocks, SEND_NEAR)
    shrink_ends = ends_of(shrink_block, shrink_second)
    shrink_pieces = (shrink_ends, *shrink_first, swap_wide(shrink_ends, CORE), *shrink_sides)
    hidden_low, hidden_sum = hidden_backward(pulled, shrink_pieces, slope)
    outputs = shrink_forward(active, shrink_pieces, stream_one, shrink_bias)[None]
    shrink_far_got, shrink_near_got, hidden_low, hidden_sum, outputs, attend_up_other = together(
        shrink_far_got, shrink_near_got, hidden_low, hidden_sum, outputs, attend_up_other
    )
    shrink_got_last = forward(shrink_blocks, shrink_far_got)
    hidden_sibling = swap_wide(hidden_low, CORE)
    ups_sibling = swap_wide(ups_other, CORE)
    attend_up_sibling = swap_wide(attend_up_other, CORE)
    half = D // 2
    expand_blocks = pair_gradient(
        [(ups[half:], ups_sibling[half:])], [(hidden_low, hidden_sibling)]
    )
    shrink_got_last, expand_blocks, hidden_low, attend_up_sibling, joined_up_other = together(
        shrink_got_last, expand_blocks, hidden_low, attend_up_sibling, joined_up_other
    )
    expand_far_got = send(expand_blocks, SEND_FAR)
    joined_sibling = swap_wide(joined_up_other, CORE)
    delta_one, stream_low, sums_two, delta_mixture = expand_backward(
        hidden_low, expand_pieces, mixed_pieces, pulled, stream_one, gain_two
    )
    expand_far_got, joined_sibling, stream_low, delta_mixture, expand_blocks = together(
        expand_far_got, joined_sibling, stream_low, delta_mixture, expand_blocks
    )
    expand_near_got = send(expand_blocks, SEND_NEAR)
    stream_sibling = swap_wide(stream_low, CORE)
    delta_mixed = attend_backward(heads, chances_first, chances_second, delta_mixture)
    expand_near_got, stream_sibling, delta_mixed = together(
        expand_near_got, stream_sibling, delta_mixed
    )
    expand_got_last = forward(expand_blocks, expand_far_got)
    mixed_sibling = swap_wide(delta_mixed, CORE)
    shrink_quarters = settle("shrink", 4, shrink_blocks, shrink_near_got, shrink_got_last)
    mixed_blocks = pair_gradient(
        [(attend_up, attend_up_sibling), (ups[:half], ups_sibling[:half])],
        [(delta_mixed, mixed_sibling), (stream_low, stream_sibling)],
    )
    expand_got_last, shrink_quarters, mixed_blocks, delta_mixed = together(
        expand_got_last, shrink_quarters, mixed_blocks, delta_mixed
    )
    mixed_far_got = send(mixed_blocks, SEND_FAR)
    shrink_got = narrow_first(shrink_quarters)
    zero_low, sums_one = entry_backward(
        delta_mixed, mixed_pieces, delta_one, stream_zero, gain_one
    )
    mixed_far_got, shrink_got, zero_low, sums_one, mixed_blocks = together(
        mixed_far_got, shrink_got, zero_low, sums_one, mixed_blocks
    )
    mixed_near_got = send(mixed_blocks, SEND_NEAR)
    shrink_end = narrow_second(shrink_quarters, shrink_got)
    zero_sibling = swap_wide(zero_low, CORE)
    expand_quarters = settle("expand", 1, expand_blocks, expand_near_got, expand_got_last)
    input_gradient, skip_gradient = joined_backward(zero_low, merge_pieces)
    (
        mixed_near_got,
        shrink_end,
        zero_sibling,
        expand_quarters,
        zero_low,
        input_gradient,
        skip_gradient,
    ) = together(
        mixed_near_got,
        shrink_end,
        zero_sibling,
        expand_quarters,
        zero_low,
        input_gradient,
        skip_gradient,
    )
    mixed_got_last = forward(mixed_blocks, mixed_far_got)
    expand_got = narrow_first(expand_quarters)
    merge_blocks = pair_gradient([(joined_up, joined_sibling)], [(zero_low, zero_sibling)])
    vector_total = jnp.concatenate(
        [
            outer(row)
            for row in (
                sums_one[0],
                sums_one[1],
                sums_one[2],
                sums_two[0],
                sums_two[1],
                sums_two[2],
                sums_two[3],
                hidden_sum[0],
            )
        ]
    )
    mixed_got_last, expand_got, vector_total, merge_blocks, shrink_end = together(
        mixed_got_last, expand_got, vector_total, merge_blocks, shrink_end
    )
    merge_far_got = send(merge_blocks, SEND_FAR)
    merge_near_got = send(merge_blocks, SEND_NEAR)
    expand_end = narrow_second(expand_quarters, expand_got)
    mixed_quarters = settle("attend_output", 1, mixed_blocks, mixed_near_got, mixed_got_last)
    shrink_new = adamw_update(
        shrink_weight,
        shrink_moment,
        shrink_square,
        unfold(finish(shrink_quarters, shrink_got, shrink_end), shrink_weight.shape[0]),
        rate_shrink,
    )
    merge_far_got, merge_near_got, expand_end, mixed_quarters, vector_total, shrink_new = together(
        merge_far_got, merge_near_got, expand_end, mixed_quarters, vector_total, shrink_new
    )
    merge_got_last = forward(merge_blocks, merge_far_got)
    mixed_got = narrow_first(mixed_quarters)
    vector_total = vector_total + swap_wide(vector_total, CORE)
    vector_total = vector_total + swap_wide(vector_total, ACROSS)
    merge_got_last, mixed_got, vector_total, expand_end = together(
        merge_got_last, mixed_got, vector_total, expand_end
    )
    merge_quarters = settle("merge", 2, merge_blocks, merge_near_got, merge_got_last)
    merge_got = narrow_first(merge_quarters)
    mixed_end = narrow_second(mixed_quarters, mixed_got)
    vector_total = vector_total + swap_wide(vector_total, ALONG)
    expand_new = adamw_update(
        expand_weight,
        expand_moment,
        expand_square,
        finish(expand_quarters, expand_got, expand_end),
        rate_expand,
    )
    merge_got, mixed_end, vector_total, expand_new = together(
        merge_got, mixed_end, vector_total, expand_new
    )
    merge_end = narrow_second(merge_quarters, merge_got)
    halves = vector_total.reshape(2, -1)
    vector_total = pick(halves, high_bit) + swap_narrow(pick(halves, 1 - high_bit), 2)
    halves = vector_total.reshape(2, -1)
    vector_total = pick(halves, low_bit) + swap_narrow(pick(halves, 1 - low_bit), 1)
    mixed_total = finish(mixed_quarters, mixed_got, mixed_end)
    attend_new = adamw_update(
        attend_weight, attend_moment, attend_square, mixed_total[:, :columns], rate_attend
    )
    output_new = adamw_update(
        output_weight, output_moment, output_square, mixed_total[:, columns:], rate_output
    )
    merge_new = adamw_update(
        merge_weight,
        merge_moment,
        merge_square,
        unfold(finish(merge_quarters, merge_got, merge_end), merge_weight.shape[0]),
        rate_merge,
    )
    vector_new = adamw_update(vectors, vector_moment, vector_square, vector_total, rate_vector)
    return (
        outputs,
        input_gradient[None],
        skip_gradient[None],
        *merge_new,
        *attend_new,
        *output_new,
        *expand_new,
        *shrink_new,
        *vector_new,
    )


def solution(mesh):
    in_specs = (
        P(("wide", "narrow"), None, None),
        P(("wide", "narrow"), None, None),
        P(("wide", "narrow"), None, None),
        P("wide", "narrow"),
        P("wide", "narrow"),
        P("wide", "narrow"),
        P("wide", "narrow"),
        P("wide", "narrow"),
        P("wide", "narrow"),
        P("wide", "narrow"),
        P("wide", "narrow"),
        P("wide", "narrow"),
        P("wide", "narrow"),
        P("wide", "narrow"),
        P("wide", "narrow"),
        P("wide", "narrow"),
        P("wide", "narrow"),
        P("wide", "narrow"),
        P("narrow"),
        P("narrow"),
        P("narrow"),
    )
    out_specs = (
        P(("wide", "narrow"), None, None),
        P(("wide", "narrow"), None, None),
        P(("wide", "narrow"), None, None),
        P("wide", "narrow"),
        P("wide", "narrow"),
        P("wide", "narrow"),
        P("wide", "narrow"),
        P("wide", "narrow"),
        P("wide", "narrow"),
        P("wide", "narrow"),
        P("wide", "narrow"),
        P("wide", "narrow"),
        P("wide", "narrow"),
        P("wide", "narrow"),
        P("wide", "narrow"),
        P("wide", "narrow"),
        P("wide", "narrow"),
        P("wide", "narrow"),
        P("narrow"),
        P("narrow"),
        P("narrow"),
    )
    tuned = mesh.shape["wide"] == 8 and mesh.shape["narrow"] == 4
    return jax.shard_map(
        on_device if tuned else general_device, mesh=mesh, in_specs=in_specs, out_specs=out_specs, check_vma=False
    )
```

```python
import jax
import jax.numpy as jnp
from jax import lax
from jax.experimental import pallas as pl
from jax.experimental.pallas import tpu as pltpu
from jax.sharding import PartitionSpec as P

D = 1152
FF = 4608
H = 16
HD = 72
STEP = 5


norm_epsilon = 1e-05
adam_epsilon = 1e-08
beta_moment = 0.5
weight_decay = 0.01
rate_merge = 0.04
rate_attend = 0.08
rate_output = 0.6
rate_expand = 0.06
rate_shrink = 0.03
rate_vector = 0.6


def product(left_side, right_side):
    return jnp.dot(left_side, right_side, preferred_element_type=jnp.float32)


def transposed(gradient, matrix):
    return lax.dot_general(
        gradient,
        matrix,
        (((gradient.ndim - 1,), (1,)), ((), ())),
        preferred_element_type=jnp.float32,
    )


def weight_gradient(activations, gradient):
    flat_left = activations.reshape(-1, activations.shape[-1])
    flat_right = gradient.reshape(-1, gradient.shape[-1])
    return lax.dot_general(
        flat_left, flat_right, (((0,), (0,)), ((), ())), preferred_element_type=jnp.float32
    )


def normalize(values):
    centered = values - jnp.mean(values, axis=-1, keepdims=True)
    spread = jnp.mean(centered * centered, axis=-1, keepdims=True)
    inverse = lax.rsqrt(spread + norm_epsilon)
    return (centered * inverse, inverse)


def norm_back(gradient, normed, inverse):
    return inverse * (
        gradient
        - jnp.mean(gradient, axis=-1, keepdims=True)
        - normed * jnp.mean(gradient * normed, axis=-1, keepdims=True)
    )


def row_sum(values):
    return jnp.sum(values, axis=(0, 1))


def unpack(packed):
    return tuple((packed[position * D : (position + 1) * D] for position in range(7))) + (
        packed[7 * D : 7 * D + FF],
    )


def gaussian_unit(values):
    return jax.nn.gelu(values, approximate=False)


def adamw_update(weight, moment, square, gradient, step_rate):
    moment_new = beta_moment * moment + (1.0 - beta_moment) * gradient
    square_new = beta_moment * square + (1.0 - beta_moment) * gradient * gradient
    correct = 1.0 - beta_moment**STEP
    direction = moment_new / correct / (jnp.sqrt(square_new / correct) + adam_epsilon)
    return (weight - step_rate * (direction + weight_decay * weight), moment_new, square_new)


def general_device(
    inputs,
    skip_tokens,
    cotangent,
    merge_weight,
    merge_moment,
    merge_square,
    attend_weight,
    attend_moment,
    attend_square,
    output_weight,
    output_moment,
    output_square,
    expand_weight,
    expand_moment,
    expand_square,
    shrink_weight,
    shrink_moment,
    shrink_square,
    vectors,
    vector_moment,
    vector_square,
):
    merge_low = merge_weight.astype(jnp.bfloat16)
    attend_low = attend_weight.astype(jnp.bfloat16)
    output_low = output_weight.astype(jnp.bfloat16)
    expand_low = expand_weight.astype(jnp.bfloat16)
    shrink_low = shrink_weight.astype(jnp.bfloat16)
    vector_low = vectors.astype(jnp.bfloat16)
    columns = (
        lax.all_gather(merge_low, "narrow", axis=1, tiled=True),
        lax.all_gather(attend_low, "narrow", axis=1, tiled=True),
        lax.all_gather(output_low, "narrow", axis=1, tiled=True),
        lax.all_gather(expand_low, "narrow", axis=1, tiled=True),
        lax.all_gather(shrink_low, "narrow", axis=1, tiled=True),
        lax.all_gather(vector_low, "narrow", axis=0, tiled=True),
    )
    matrices = (
        lax.all_gather(columns[0], "wide", axis=0, tiled=True),
        lax.all_gather(columns[1], "wide", axis=0, tiled=True),
        lax.all_gather(columns[2], "wide", axis=0, tiled=True),
        lax.all_gather(columns[3], "wide", axis=0, tiled=True),
        lax.all_gather(columns[4], "wide", axis=0, tiled=True),
    )
    skip_bias, gain_one, bias_one, output_bias, gain_two, bias_two, shrink_bias, expand_bias = (
        unpack(columns[5].astype(jnp.float32))
    )
    images = inputs.shape[0]
    length = inputs.shape[1]
    softmax_scale = HD ** (-0.5)
    joined = jnp.concatenate([inputs, skip_tokens], axis=-1)
    stream_zero = product(joined, matrices[0]) + skip_bias
    normed_one, inverse_one = normalize(stream_zero)
    attend_input = (normed_one * gain_one + bias_one).astype(jnp.bfloat16)
    mixed_heads = product(attend_input, matrices[1]).astype(jnp.bfloat16)
    query_heads = mixed_heads[..., 0:D].reshape(images, length, H, HD)
    key_heads = mixed_heads[..., D : 2 * D].reshape(images, length, H, HD)
    value_heads = mixed_heads[..., 2 * D : 3 * D].reshape(images, length, H, HD)
    logits = (
        jnp.einsum("blhe,bmhe->bhlm", query_heads, key_heads, preferred_element_type=jnp.float32)
        * softmax_scale
    )
    maxima = jnp.max(logits, axis=-1, keepdims=True)
    log_total = maxima + jnp.log(jnp.sum(jnp.exp(logits - maxima), axis=-1, keepdims=True))
    softmax_low = jnp.exp(logits - log_total).astype(jnp.bfloat16)
    mixture = jnp.einsum(
        "bhlm,bmhe->blhe", softmax_low, value_heads, preferred_element_type=jnp.float32
    )
    mixture = mixture.astype(jnp.bfloat16).reshape(images, length, D)
    stream_one = stream_zero + product(mixture, matrices[2]) + output_bias
    normed_two, inverse_two = normalize(stream_one)
    expand_input = (normed_two * gain_two + bias_two).astype(jnp.bfloat16)
    hidden = product(expand_input, matrices[3]) + expand_bias
    active, pullback = jax.vjp(gaussian_unit, hidden)
    active_low = active.astype(jnp.bfloat16)
    outputs = (stream_one + product(active_low, matrices[4]) + shrink_bias).astype(jnp.bfloat16)
    columns_back = (
        lax.all_gather(merge_low, "narrow", axis=1, tiled=True),
        lax.all_gather(attend_low, "narrow", axis=1, tiled=True),
        lax.all_gather(output_low, "narrow", axis=1, tiled=True),
        lax.all_gather(expand_low, "narrow", axis=1, tiled=True),
        lax.all_gather(shrink_low, "narrow", axis=1, tiled=True),
        lax.all_gather(vector_low, "narrow", axis=0, tiled=True),
    )
    matrices_back = (
        lax.all_gather(columns_back[0], "wide", axis=0, tiled=True),
        lax.all_gather(columns_back[1], "wide", axis=0, tiled=True),
        lax.all_gather(columns_back[2], "wide", axis=0, tiled=True),
        lax.all_gather(columns_back[3], "wide", axis=0, tiled=True),
        lax.all_gather(columns_back[4], "wide", axis=0, tiled=True),
    )
    packed_back = columns_back[5].astype(jnp.float32)
    unpacked = unpack(packed_back)
    gain_first = unpacked[1]
    gain_second = unpacked[4]
    upstream = cotangent.astype(jnp.float32)
    shrink_gradient = weight_gradient(active_low, cotangent)
    delta_active = transposed(cotangent, matrices_back[4])
    delta_hidden = pullback(delta_active)[0]
    hidden_low = delta_hidden.astype(jnp.bfloat16)
    expand_gradient = weight_gradient(expand_input, hidden_low)
    delta_expand = transposed(hidden_low, matrices_back[3])
    delta_one = upstream + norm_back(delta_expand * gain_second, normed_two, inverse_two)
    stream_low = delta_one.astype(jnp.bfloat16)
    output_gradient = weight_gradient(mixture, stream_low)
    delta_mixture = (
        transposed(stream_low, matrices_back[2]).astype(jnp.bfloat16).reshape(images, length, H, HD)
    )
    logits_again = (
        jnp.einsum("blhe,bmhe->bhlm", query_heads, key_heads, preferred_element_type=jnp.float32)
        * softmax_scale
    )
    softmax_again = jnp.exp(logits_again - log_total)
    delta_softmax = jnp.einsum(
        "blhe,bmhe->bhlm", delta_mixture, value_heads, preferred_element_type=jnp.float32
    )
    delta_values = jnp.einsum(
        "bhlm,blhe->bmhe",
        softmax_again.astype(jnp.bfloat16),
        delta_mixture,
        preferred_element_type=jnp.float32,
    )
    delta_logits = softmax_again * (
        delta_softmax - jnp.sum(softmax_again * delta_softmax, axis=-1, keepdims=True)
    )
    delta_scores = (softmax_scale * delta_logits).astype(jnp.bfloat16)
    delta_queries = jnp.einsum(
        "bhlm,bmhe->blhe", delta_scores, key_heads, preferred_element_type=jnp.float32
    )
    delta_keys = jnp.einsum(
        "bhlm,blhe->bmhe", delta_scores, query_heads, preferred_element_type=jnp.float32
    )
    delta_mixed = jnp.concatenate(
        [
            delta_queries.reshape(images, length, D),
            delta_keys.reshape(images, length, D),
            delta_values.reshape(images, length, D),
        ],
        axis=-1,
    ).astype(jnp.bfloat16)
    attend_gradient = weight_gradient(attend_input, delta_mixed)
    delta_attend = transposed(delta_mixed, matrices_back[1])
    delta_zero = delta_one + norm_back(delta_attend * gain_first, normed_one, inverse_one)
    zero_low = delta_zero.astype(jnp.bfloat16)
    merge_gradient = weight_gradient(joined, zero_low)
    delta_joined = transposed(zero_low, matrices_back[0])
    input_gradient = delta_joined[..., 0:D].astype(jnp.bfloat16)
    skip_gradient = delta_joined[..., D : 2 * D].astype(jnp.bfloat16)
    vector_gradient = jnp.concatenate(
        [
            row_sum(delta_zero),
            row_sum(delta_attend * normed_one),
            row_sum(delta_attend),
            row_sum(delta_one),
            row_sum(delta_expand * normed_two),
            row_sum(delta_expand),
            row_sum(upstream),
            row_sum(delta_hidden),
        ]
    )
    owned_rows = (
        lax.psum_scatter(merge_gradient, "wide", scatter_dimension=0, tiled=True),
        lax.psum_scatter(attend_gradient, "wide", scatter_dimension=0, tiled=True),
        lax.psum_scatter(output_gradient, "wide", scatter_dimension=0, tiled=True),
        lax.psum_scatter(expand_gradient, "wide", scatter_dimension=0, tiled=True),
        lax.psum_scatter(shrink_gradient, "wide", scatter_dimension=0, tiled=True),
    )
    vector_total = lax.psum(vector_gradient, "wide")
    parted = (
        lax.psum_scatter(owned_rows[0], "narrow", scatter_dimension=1, tiled=True),
        lax.psum_scatter(owned_rows[1], "narrow", scatter_dimension=1, tiled=True),
        lax.psum_scatter(owned_rows[2], "narrow", scatter_dimension=1, tiled=True),
        lax.psum_scatter(owned_rows[3], "narrow", scatter_dimension=1, tiled=True),
        lax.psum_scatter(owned_rows[4], "narrow", scatter_dimension=1, tiled=True),
        lax.psum_scatter(vector_total, "narrow", scatter_dimension=0, tiled=True),
    )
    merge_new = adamw_update(merge_weight, merge_moment, merge_square, parted[0], rate_merge)
    attend_new = adamw_update(attend_weight, attend_moment, attend_square, parted[1], rate_attend)
    output_new = adamw_update(output_weight, output_moment, output_square, parted[2], rate_output)
    expand_new = adamw_update(expand_weight, expand_moment, expand_square, parted[3], rate_expand)
    shrink_new = adamw_update(shrink_weight, shrink_moment, shrink_square, parted[4], rate_shrink)
    vector_new = adamw_update(vectors, vector_moment, vector_square, parted[5], rate_vector)
    return (
        outputs,
        input_gradient,
        skip_gradient,
        merge_new[0],
        merge_new[1],
        merge_new[2],
        attend_new[0],
        attend_new[1],
        attend_new[2],
        output_new[0],
        output_new[1],
        output_new[2],
        expand_new[0],
        expand_new[1],
        expand_new[2],
        shrink_new[0],
        shrink_new[1],
        shrink_new[2],
        vector_new[0],
        vector_new[1],
        vector_new[2],
    )


CORE = 1
ACROSS = 2
ALONG = 4
PAD = 384
VMEM_BYTES = 56 * 1024 * 1024
LIGHT = pl.CostEstimate(flops=0, bytes_accessed=1024, transcendentals=0)
PARAMS = pltpu.CompilerParams(vmem_limit_bytes=VMEM_BYTES)


def swap_wide(value, bit):
    return lax.ppermute(value, "wide", [(i, i ^ bit) for i in range(8)])


def swap_narrow(value, bit):
    return lax.ppermute(value, "narrow", [(i, i ^ bit) for i in range(4)])


def together(*values):
    return lax.optimization_barrier(values)


def spot():
    wide = lax.axis_index("wide")
    narrow = lax.axis_index("narrow")
    return (wide & 1, (wide >> 1) & 1, (wide >> 2) & 1, narrow & 1, narrow >> 1)


def split_rows(rows):
    return -(-rows // 32) * 16


def column_blocks(kind, quarter):
    if kind == "attend_output":
        width = quarter // 8
        order = [8 * part + 2 * n + p for part in range(3) for p in range(2) for n in range(4)]
        blocks = [(block // 6, (block % 6) * width) for block in order]
        return width, blocks + [(n, (6 + p) * width) for p in range(2) for n in range(4)]
    width = quarter // 2
    return width, [(n, p * width) for p in range(2) for n in range(4)]


def fold(shard):
    parts = max(1, shard.shape[0] // (D // 8))
    height = shard.shape[0] // parts
    return jnp.concatenate(
        [shard[part * height : (part + 1) * height] for part in range(parts)], axis=1
    )


def unfold(value, rows):
    parts = rows // value.shape[0]
    quarter = value.shape[1] // parts
    return jnp.concatenate(
        [value[:, part * quarter : (part + 1) * quarter] for part in range(parts)], axis=0
    )


def arrange(kind, parts, shard, others, extra=0):
    height = shard.shape[0] - extra
    rows, quarter = parts * height, shard.shape[1] // parts
    width, blocks = column_blocks(kind, quarter)

    def kernel(*refs):
        full, apart, held = refs[4], refs[5], refs[-1]
        narrow = lax.axis_index("narrow")
        for relative in range(4):
            held[relative] = refs[relative][...]
        for number in range(4):
            value = held[narrow ^ number]
            if extra:
                apart[number] = value[height:]
            for position, (owner, offset) in enumerate(blocks):
                if owner == number:
                    column = slice(position * width, (position + 1) * width)
                    for part in range(parts):
                        start = part * quarter + offset
                        full[part * height : (part + 1) * height, column] = value[
                            :height, start : start + width
                        ]

    outs = [jax.ShapeDtypeStruct((rows, 4 * quarter), jnp.bfloat16)]
    if extra:
        outs.append(jax.ShapeDtypeStruct((4, extra, shard.shape[1]), jnp.bfloat16))
    return pl.pallas_call(
        kernel,
        out_shape=tuple(outs),
        scratch_shapes=[pltpu.VMEM((4,) + shard.shape, jnp.bfloat16)],
        compiler_params=PARAMS,
        cost_estimate=LIGHT,
    )(shard, *others)


def weight_scratch(rows, columns, chunks=1):
    return [pltpu.VMEM((rows, columns), jnp.bfloat16), pltpu.SemaphoreType.DMA((chunks, 8))]


class Fetch:
    def __init__(self, refs, full, sems, first=0):
        wide = lax.axis_index("wide")
        core, chip = wide & 1, wide >> 1
        rows = full.shape[0] // 8
        chunks = sems.shape[0]
        width = full.shape[1] // chunks
        self.copies = []
        for chunk in range(chunks):
            group = []
            for number, (ends, from_x, from_y) in enumerate((refs[:3], refs[3:])):
                parity = core if number == 0 else 1 - core
                own, far = ends.at[pl.ds(0, rows)], ends.at[pl.ds(rows, rows)]
                for relative, piece in enumerate((own, from_x, from_y, far)):
                    start = pl.multiple_of((4 * parity + (chip ^ relative)) * rows, 16)
                    group.append(
                        pltpu.make_async_copy(
                            piece.at[:, pl.ds(first + chunk * width, width)],
                            full.at[pl.ds(start, rows), pl.ds(chunk * width, width)],
                            sems.at[chunk, 4 * number + relative],
                        )
                    )
            self.copies.append(group)
        for group in self.copies:
            for copy in group:
                copy.start()

    def wait(self, chunk=0):
        for copy in self.copies[chunk]:
            copy.wait()


def pair_gradient(lefts, right):
    height = lefts[0][0].shape[0]
    rows = height // 4
    split = split_rows(rows)
    tokens, columns = right[0].shape
    tile = 384 if height > 576 else 1152
    count = len(lefts)
    ends = [sum(width for _, _, width in lefts[: number + 1]) // tile for number in range(count)]
    starts = [0] + ends[:-1]

    def kernel(*refs):
        left_refs = refs[: 2 * count]
        right_ref, sibling_ref = refs[2 * count : 2 * count + 2]
        outs = refs[2 * count + 2 : 2 * count + 6]
        joint, beside, total = refs[2 * count + 6 :]
        step = pl.program_id(0)

        @pl.when(step == 0)
        def _():
            joint[...] = jnp.zeros_like(joint)

        for number in range(count):

            @pl.when(step == starts[number])
            def _():
                beside[:, :PAD] = left_refs[2 * number][...]
                beside[:, PAD:] = left_refs[2 * number + 1][...]

        joint[:tokens] = right_ref[...]
        joint[PAD : PAD + tokens] = sibling_ref[...]
        total[...] = jnp.dot(
            beside[...], joint[...], preferred_element_type=jnp.float32
        ).astype(jnp.bfloat16)
        part_blocks(total, rows, outs)

    whole = pl.BlockSpec((height, PAD), lambda i: (0, 0))
    part = lambda size: pl.BlockSpec((size, tile), lambda i: (0, i))
    pair = lambda size: pl.BlockSpec((2, size, tile), lambda i: (0, 0, i))
    outs = pl.pallas_call(
        kernel,
        grid=(columns // tile,),
        in_specs=[whole] * (2 * count) + [part(tokens)] * 2,
        out_specs=(pair(split), pair(split), pair(rows - split), pair(rows - split)),
        out_shape=block_shapes(rows, columns),
        scratch_shapes=[
            pltpu.VMEM((2 * PAD, tile), jnp.bfloat16),
            pltpu.VMEM((height, 2 * PAD), jnp.bfloat16),
            pltpu.VMEM((height, tile), jnp.bfloat16),
        ],
        compiler_params=PARAMS,
        cost_estimate=LIGHT,
    )(*[left for pair_of in lefts for left in pair_of[:2]], *right)
    return outs


def block_shapes(rows, columns):
    split = split_rows(rows)
    top = jax.ShapeDtypeStruct((2, split, columns), jnp.bfloat16)
    bottom = jax.ShapeDtypeStruct((2, rows - split, columns), jnp.bfloat16)
    return top, top, bottom, bottom


def part_blocks(total, rows, outs):
    wide = lax.axis_index("wide")
    across, along = (wide >> 1) & 1, (wide >> 2) & 1
    split = split_rows(rows)
    for kept_x in range(2):
        for kept_y in range(2):
            x = across if kept_x else 1 - across
            y = along if kept_y else 1 - along
            start = pl.multiple_of((2 * y + x) * rows, 16)
            outs[1 - kept_x][1 - kept_y] = total[pl.ds(start, split)]
            outs[3 - kept_y][1 - kept_x] = total[
                pl.ds(pl.multiple_of(start + split, 16), rows - split)
            ]


def unarrange(kind, parts, blocks, got, got_last):
    split, columns = got_last[0].shape
    rest = got_last[1].shape[0]
    rows = split + rest
    quarter = columns // 4
    height = rows // parts
    width, column_parts = column_blocks(kind, quarter)

    def kernel(*refs):
        tops, bottoms = refs[:3], refs[3:6]
        outs, held = refs[6:10], refs[10]
        narrow = lax.axis_index("narrow")
        low_bit, high_bit = narrow & 1, narrow >> 1
        held[:split] = add_low(tops[0][...], tops[1][...], tops[2][...])
        held[split:] = add_low(bottoms[0][...], bottoms[1][...], bottoms[2][...])
        for owner in range(4):
            for which in range(4):
                low_same, high_same = 1 - which // 2, 1 - which % 2

                @pl.when(
                    ((low_bit == (owner & 1)) == (low_same == 1))
                    & ((high_bit == (owner >> 1)) == (high_same == 1))
                )
                def _():
                    for position, (quarter_of, offset) in enumerate(column_parts):
                        if quarter_of == owner:
                            piece = held[:, position * width : (position + 1) * width]
                            for part in range(parts):
                                start = part * quarter + offset
                                outs[which][:, start : start + width] = piece[
                                    part * height : (part + 1) * height
                                ]

    near = lambda size: pl.BlockSpec((None, size, columns), lambda i: (0, 0, 0))
    full = lambda size, width: pl.BlockSpec((size, width), lambda i: (0, 0))
    shape = jax.ShapeDtypeStruct((height, parts * quarter), jnp.bfloat16)
    return pl.pallas_call(
        kernel,
        grid=(1,),
        in_specs=[near(split), near(split), full(split, columns)]
        + [near(rest), near(rest), full(rest, columns)],
        out_specs=(full(height, parts * quarter),) * 4,
        out_shape=(shape,) * 4,
        scratch_shapes=[pltpu.VMEM((rows, columns), jnp.bfloat16)],
        compiler_params=PARAMS,
        cost_estimate=LIGHT,
    )(blocks[0], got[0], got_last[0], blocks[2], got[1], got_last[1])


def add_low(*terms):
    return sum(term.astype(jnp.float32) for term in terms).astype(jnp.bfloat16)


def pick(value, index, dim=0):
    return lax.dynamic_index_in_dim(value, index, dim, keepdims=False)


def halves_of(value, core):
    middle = value.shape[-1] // 2
    first, second = value[..., :middle], value[..., middle:]
    return jnp.where(core == 0, first, second), jnp.where(core == 0, second, first)


def inner(value):
    width = value.shape[-1] // 8
    return jnp.concatenate(
        [
            value[..., (2 * n + p) * width : (2 * n + p + 1) * width]
            for p in range(2)
            for n in range(4)
        ],
        axis=-1,
    )


def outer(value):
    width = value.shape[-1] // 8
    return jnp.concatenate(
        [
            value[..., (4 * p + n) * width : (4 * p + n + 1) * width]
            for n in range(4)
            for p in range(2)
        ],
        axis=-1,
    )


def upright(value):
    return jnp.pad(value, ((0, PAD - value.shape[0]), (0, 0))).T


KEEP_NEAR, KEEP_FAR, SEND_NEAR, SEND_FAR = range(4)


def send(blocks):
    return swap_wide(blocks[1], ACROSS), swap_wide(blocks[3], ALONG)


def forward(blocks, got):
    return (
        swap_wide(add_low(blocks[0][1], got[0][1]), ALONG),
        swap_wide(add_low(blocks[2][1], got[1][1]), ACROSS),
    )


def narrow_first(quarters):
    return swap_narrow(quarters[SEND_FAR], 1), swap_narrow(quarters[SEND_NEAR], 1)


def narrow_second(quarters, got):
    return swap_narrow(add_low(quarters[KEEP_FAR], got[0]), 2)


def finish(quarters, got, got_last):
    return (
        quarters[KEEP_NEAR].astype(jnp.float32)
        + got[1].astype(jnp.float32)
        + got_last.astype(jnp.float32)
    )


def across_narrow(shard):
    return tuple(swap_narrow(shard, bit) for bit in (1, 2, 3))


def gather_first(block):
    return swap_wide(block, ACROSS), swap_wide(block, ALONG)


def gather_second(first):
    split = split_rows(first[0].shape[0])
    return swap_wide(first[0][:split], ALONG), swap_wide(first[1][split:], ACROSS)


def swap_sides(first):
    return swap_wide(first[0], CORE), swap_wide(first[1], CORE)


def ends_of(block, second):
    return jnp.concatenate([block, second[0], second[1]], axis=0)


def direct_narrow(quarters):
    return (
        swap_narrow(quarters[KEEP_FAR], 2),
        swap_narrow(quarters[SEND_NEAR], 1),
        swap_narrow(quarters[SEND_FAR], 3),
    )


def direct_sum(quarters, got):
    return sum(term.astype(jnp.float32) for term in (quarters[KEEP_NEAR], *got))


def heavy(kernel, outs, scratch, weights, operands):
    return pl.pallas_call(
        kernel,
        in_specs=[pl.BlockSpec(memory_space=pl.ANY)] * len(weights)
        + [pl.BlockSpec(memory_space=pltpu.VMEM)] * len(operands),
        out_shape=tuple(jax.ShapeDtypeStruct(shape, dtype) for shape, dtype in outs),
        scratch_shapes=scratch,
        compiler_params=PARAMS,
        cost_estimate=LIGHT,
    )(*weights, *operands)


def dot_rows(left, right):
    return lax.dot_general(left, right, (((1,), (1,)), ((), ())), preferred_element_type=jnp.float32)


def dot_depth(left, right):
    return lax.dot_general(left, right, (((0,), (0,)), ((), ())), preferred_element_type=jnp.float32)


def store_upright(value, padded, mine, other):
    features = value.shape[1]
    padded[: value.shape[0]] = value
    turned = padded[...].T.astype(jnp.bfloat16)
    core = lax.axis_index("wide") & 1

    @pl.when(core == 0)
    def _():
        mine[...] = turned[: features // 2]
        other[...] = turned[features // 2 :]

    @pl.when(core == 1)
    def _():
        other[...] = turned[: features // 2]
        mine[...] = turned[features // 2 :]


def merge_forward(joined, weight, bias, gain, shift):
    length = joined.shape[0]

    def kernel(*refs):
        joined_ref, bias_ref, gain_ref, shift_ref = refs[6:10]
        stream, entry, up_mine, up_other, full, sems, padded = refs[10:]
        weight_in = Fetch(refs[:6], full, sems)
        padded[...] = jnp.zeros_like(padded)
        weight_in.wait()
        stream[...] = product(joined_ref[...], full[...]) + bias_ref[...]
        normed = normalize(stream[...])[0]
        value = (normed * gain_ref[...] + shift_ref[...]).astype(jnp.bfloat16)
        entry[...] = value
        store_upright(value.astype(jnp.float32), padded, up_mine, up_other)

    return heavy(
        kernel,
        [
            ((length, D), jnp.float32),
            ((length, D), jnp.bfloat16),
            ((D // 2, PAD), jnp.bfloat16),
            ((D // 2, PAD), jnp.bfloat16),
        ],
        weight_scratch(2 * D, D) + [pltpu.VMEM((PAD, D), jnp.float32)],
        weight,
        (joined, bias, gain, shift),
    )


def attend_head(heads, head, chances_ref, slot):
    at = head * HD
    queries = heads[:, at : at + HD]
    keys = heads[:, D + at : D + at + HD]
    values = heads[:, 2 * D + at : 2 * D + at + HD]
    logits = dot_rows(queries, keys) * HD ** (-0.5)
    powers = jnp.exp(logits - jnp.max(logits, axis=-1, keepdims=True))
    chances = powers / jnp.sum(powers, axis=-1, keepdims=True)
    chances_ref[slot] = chances
    return product(chances.astype(jnp.bfloat16), values).astype(jnp.bfloat16)


FIRST = 12


def attend_first(entry, weight):
    length = entry.shape[0]

    def kernel(*refs):
        entry_ref, heads, chances_ref, mix_ref, full, sems = refs[6:]
        weight_in = Fetch(refs[:6], full, sems)
        for part in range(3):
            weight_in.wait(part)
            columns = slice(part * D, (part + 1) * D)
            heads[:, columns] = product(entry_ref[...], full[:, columns]).astype(jnp.bfloat16)
        for head in range(FIRST):
            mix_ref[:, head * HD : (head + 1) * HD] = attend_head(heads, head, chances_ref, head)

    return heavy(
        kernel,
        [
            ((length, 3 * D), jnp.bfloat16),
            ((FIRST, length, length), jnp.float32),
            ((length, FIRST * HD), jnp.bfloat16),
        ],
        weight_scratch(D, 3 * D, 3),
        weight,
        (entry,),
    )


def attend_second(heads, mix_first, weight, stream_zero, bias, gain, shift):
    length = heads.shape[0]
    half = D // 2

    def kernel(*refs):
        heads_ref, first_ref, zero_ref, bias_ref, gain_ref, shift_ref = refs[6:12]
        chances_ref, stream, value_ref, up_mine, up_other, full, sems, mixed, padded = refs[12:]
        weight_in = Fetch(refs[:6], full, sems, 3 * D)
        padded[...] = jnp.zeros_like(padded)
        mixed[:, : FIRST * HD] = first_ref[...]
        for head in range(FIRST, H):
            mixed[:, head * HD : (head + 1) * HD] = attend_head(
                heads_ref, head, chances_ref, head - FIRST
            )
        weight_in.wait()
        stream[...] = zero_ref[...] + product(mixed[...], full[...]) + bias_ref[...]
        store_upright(
            mixed[...].astype(jnp.float32), padded, up_mine.at[pl.ds(0, half)], up_other.at[pl.ds(0, half)]
        )
        normed = normalize(stream[...])[0]
        value = (normed * gain_ref[...] + shift_ref[...]).astype(jnp.bfloat16)
        value_ref[...] = value
        store_upright(
            value.astype(jnp.float32), padded, up_mine.at[pl.ds(half, half)], up_other.at[pl.ds(half, half)]
        )

    return heavy(
        kernel,
        [
            ((H - FIRST, length, length), jnp.float32),
            ((length, D), jnp.float32),
            ((length, D), jnp.bfloat16),
            ((D, PAD), jnp.bfloat16),
            ((D, PAD), jnp.bfloat16),
        ],
        weight_scratch(D, D)
        + [pltpu.VMEM((length, D), jnp.bfloat16), pltpu.VMEM((PAD, D), jnp.float32)],
        weight,
        (heads, mix_first, stream_zero, bias, gain, shift),
    )


def expand_forward(entry, weight, bias):
    length = entry.shape[0]

    def kernel(*refs):
        entry_ref, bias_ref = refs[6:8]
        active_ref, slope_ref, up_mine, up_other, full, sems, padded = refs[8:]
        core = lax.axis_index("wide") & 1
        weight_in = Fetch(refs[:6], full, sems)
        padded[...] = jnp.zeros_like(padded)
        for step in range(FF // D):
            columns = slice(step * D, (step + 1) * D)
            weight_in.wait(step)
            value = product(entry_ref[...], full[:, columns]) + bias_ref[:, columns]
            inside = 0.5 * (1.0 + lax.erf(value * (0.5**0.5)))
            bell = jnp.exp(-0.5 * value * value) * (2.0 * jnp.pi) ** -0.5
            active = (value * inside).astype(jnp.bfloat16)
            slope_ref[:, columns] = inside + value * bell
            active_ref[:, columns] = active
            padded[:length] = active.astype(jnp.float32)
            turned = padded[...].T.astype(jnp.bfloat16)
            rows = slice((step % 2) * D, (step % 2 + 1) * D)

            @pl.when(core == step // 2)
            def _():
                up_mine[rows] = turned

            @pl.when(core != step // 2)
            def _():
                up_other[rows] = turned

    return heavy(
        kernel,
        [
            ((length, FF), jnp.bfloat16),
            ((length, FF), jnp.float32),
            ((FF // 2, PAD), jnp.bfloat16),
            ((FF // 2, PAD), jnp.bfloat16),
        ],
        weight_scratch(D, FF, FF // D) + [pltpu.VMEM((PAD, D), jnp.float32)],
        weight,
        (entry, bias),
    )


def hidden_backward(pulled, weight, slope):
    length = pulled.shape[0]

    def kernel(*refs):
        pulled_ref, slope_ref, low_ref, sum_ref, full, sems = refs[6:]
        Fetch(refs[:6], full, sems).wait()
        for step in range(FF // D):
            columns = slice(step * D, (step + 1) * D)
            delta = dot_rows(pulled_ref[...], full[columns]) * slope_ref[:, columns]
            low_ref[:, columns] = delta.astype(jnp.bfloat16)
            sum_ref[:, columns] = jnp.sum(delta, axis=0, keepdims=True)

    return heavy(
        kernel,
        [((length, FF), jnp.bfloat16), ((1, FF), jnp.float32)],
        weight_scratch(FF, D),
        weight,
        (pulled, slope),
    )


def expand_backward(hidden_low, weight, mixed_weight, pulled, stream_one, gain):
    length = pulled.shape[0]

    def kernel(*refs):
        hidden_ref, pulled_ref, stream_ref, gain_ref = refs[12:16]
        one_ref, low_ref, sums, mix_ref, full, sems, output, output_sems, delta = refs[16:]
        weight_in = Fetch(refs[:6], full, sems)
        output_in = Fetch(refs[6:12], output, output_sems, 3 * D)
        for step in range(FF // D):
            columns = slice(step * D, (step + 1) * D)
            weight_in.wait(step)
            part = dot_rows(hidden_ref[:, columns], full[:, columns])
            delta[...] = part if step == 0 else delta[...] + part
        value = delta[...]
        normed, inverse = normalize(stream_ref[...])
        upstream = pulled_ref[...].astype(jnp.float32)
        one = upstream + norm_back(value * gain_ref[...], normed, inverse)
        one_ref[...] = one
        low_value = one.astype(jnp.bfloat16)
        low_ref[...] = low_value
        sums[0:1] = jnp.sum(one, axis=0, keepdims=True)
        sums[1:2] = jnp.sum(value * normed, axis=0, keepdims=True)
        sums[2:3] = jnp.sum(value, axis=0, keepdims=True)
        sums[3:4] = jnp.sum(upstream, axis=0, keepdims=True)
        output_in.wait()
        mix_ref[...] = dot_rows(low_value, output[...]).astype(jnp.bfloat16)

    return heavy(
        kernel,
        [
            ((length, D), jnp.float32),
            ((length, D), jnp.bfloat16),
            ((4, D), jnp.float32),
            ((length, D), jnp.bfloat16),
        ],
        weight_scratch(D, FF, FF // D)
        + weight_scratch(D, D)
        + [pltpu.VMEM((length, D), jnp.float32)],
        (*weight, *mixed_weight),
        (hidden_low, pulled, stream_one, gain),
    )


def attend_backward(heads, chances_first, chances_second, delta_mixture, stream_low):
    length = heads.shape[0]
    scale = HD ** (-0.5)

    def kernel(heads_ref, first_ref, second_ref, delta_ref, stream_ref, mixed):
        mixed[:, 3 * D :] = stream_ref[...]
        for head in range(H):
            at = head * HD
            queries = heads_ref[:, at : at + HD]
            keys = heads_ref[:, D + at : D + at + HD]
            values = heads_ref[:, 2 * D + at : 2 * D + at + HD]
            delta = delta_ref[:, at : at + HD]
            chances = first_ref[head] if head < FIRST else second_ref[head - FIRST]
            pull = dot_rows(delta, values)
            inner_sum = jnp.sum(chances * pull, axis=-1, keepdims=True)
            scores = (scale * (chances * (pull - inner_sum))).astype(jnp.bfloat16)
            mixed[:, at : at + HD] = product(scores, keys).astype(jnp.bfloat16)
            mixed[:, D + at : D + at + HD] = dot_depth(scores, queries).astype(jnp.bfloat16)
            mixed[:, 2 * D + at : 2 * D + at + HD] = dot_depth(
                chances.astype(jnp.bfloat16), delta
            ).astype(jnp.bfloat16)

    return heavy(
        kernel,
        [((length, 4 * D), jnp.bfloat16)],
        [],
        (),
        (heads, chances_first, chances_second, delta_mixture, stream_low),
    )[0]


def entry_backward(delta_mixed, weight, delta_one, stream_zero, gain):
    length = delta_mixed.shape[0]

    def kernel(*refs):
        mixed_ref, one_ref, stream_ref, gain_ref, low_ref, sums, full, sems, delta = refs[6:]
        weight_in = Fetch(refs[:6], full, sems)
        for step in range(3):
            columns = slice(step * D, (step + 1) * D)
            weight_in.wait(step)
            part = dot_rows(mixed_ref[:, columns], full[:, columns])
            delta[...] = part if step == 0 else delta[...] + part
        value = delta[...]
        normed, inverse = normalize(stream_ref[...])
        zero = one_ref[...] + norm_back(value * gain_ref[...], normed, inverse)
        low_ref[...] = zero.astype(jnp.bfloat16)
        sums[0:1] = jnp.sum(zero, axis=0, keepdims=True)
        sums[1:2] = jnp.sum(value * normed, axis=0, keepdims=True)
        sums[2:3] = jnp.sum(value, axis=0, keepdims=True)

    return heavy(
        kernel,
        [((length, D), jnp.bfloat16), ((3, D), jnp.float32)],
        weight_scratch(D, 3 * D, 3) + [pltpu.VMEM((length, D), jnp.float32)],
        weight,
        (delta_mixed, delta_one, stream_zero, gain),
    )


def joined_backward(zero_low, weight):
    length = zero_low.shape[0]
    width = 2 * D // 8

    def kernel(*refs):
        zero_ref, first_ref, second_ref, full, sems = refs[6:]
        Fetch(refs[:6], full, sems).wait()
        for parity in range(2):
            delta = dot_rows(zero_ref[...], full[parity * D : (parity + 1) * D])
            delta = delta.astype(jnp.bfloat16)
            for number in range(4):
                target = (first_ref, second_ref)[number // 2]
                column = (2 * (number % 2) + parity) * width
                target[:, column : column + width] = delta[:, number * width : (number + 1) * width]

    out = ((length, D), jnp.bfloat16)
    return heavy(kernel, [out, out], weight_scratch(2 * D, D), weight, (zero_low,))


def shrink_forward(active, weight, stream_one, bias):
    length = active.shape[0]
    width = D // 8

    def kernel(*refs):
        active_ref, stream_ref, bias_ref, out_ref, full, sems = refs[6:]
        Fetch(refs[:6], full, sems).wait()
        total = (
            stream_ref[...] + product(active_ref[...], full[...]) + bias_ref[...]
        ).astype(jnp.bfloat16)
        for parity in range(2):
            for number in range(4):
                column = (2 * number + parity) * width
                source = (4 * parity + number) * width
                out_ref[:, column : column + width] = total[:, source : source + width]

    return heavy(
        kernel,
        [((length, D), jnp.bfloat16)],
        weight_scratch(FF, D),
        weight,
        (active, stream_one, bias),
    )[0]


def on_device(
    inputs,
    skip_tokens,
    cotangent,
    merge_weight,
    merge_moment,
    merge_square,
    attend_weight,
    attend_moment,
    attend_square,
    output_weight,
    output_moment,
    output_square,
    expand_weight,
    expand_moment,
    expand_square,
    shrink_weight,
    shrink_moment,
    shrink_square,
    vectors,
    vector_moment,
    vector_square,
):
    high_bit, low_bit = spot()[4], spot()[3]
    core = spot()[0]
    low = jnp.bfloat16
    columns = attend_weight.shape[1]

    merge_low = fold(merge_weight.astype(low))
    width = merge_low.shape[1]
    count = vectors.shape[0]
    vector_rows = jnp.pad(vectors.astype(low), (0, 16 * width - count)).reshape(16, width)
    merge_low = jnp.concatenate([merge_low, vector_rows], axis=0)
    merge_others = across_narrow(merge_low)
    mixed_low = jnp.concatenate([attend_weight.astype(low), output_weight.astype(low)], axis=1)
    joined = inner(jnp.concatenate([inputs[0], skip_tokens[0]], axis=-1))
    joined_mine, joined_other = halves_of(joined, core)
    pulled = inner(cotangent[0])
    merge_others, mixed_low, joined, joined_mine, joined_other, pulled = together(
        merge_others, mixed_low, joined, joined_mine, joined_other, pulled
    )
    merge_block, vector_parts = arrange("merge", 2, merge_low, merge_others, 16)
    merge_first = gather_first(merge_block)
    mixed_far = swap_narrow(mixed_low, 2)
    mixed_near = swap_narrow(mixed_low, 1)
    expand_low = expand_weight.astype(low)
    merge_first, mixed_far, vector_parts, expand_low = together(
        merge_first, mixed_far, vector_parts, expand_low
    )
    merge_second = gather_second(merge_first)
    merge_sides = swap_sides(merge_first)
    mixed_last = swap_narrow(mixed_far, 1)
    shrink_low = fold(shrink_weight.astype(low))
    pieces = unpack(vector_parts.reshape(4, -1)[:, :count].reshape(-1).astype(jnp.float32))
    pieces = tuple(inner(piece)[None] for piece in pieces)
    merge_second, merge_sides, mixed_near, mixed_last, shrink_low, pieces = together(
        merge_second, merge_sides, mixed_near, mixed_last, shrink_low, pieces
    )
    skip_bias, gain_one, bias_one, output_bias, gain_two, bias_two, shrink_bias, expand_bias = pieces
    mixed_block = arrange("attend_output", 1, mixed_low, (mixed_near, mixed_far, mixed_last))[0]
    mixed_first = gather_first(mixed_block)
    expand_far = swap_narrow(expand_low, 2)
    expand_near = swap_narrow(expand_low, 1)
    merge_ends = ends_of(merge_block, merge_second)
    merge_pieces = (merge_ends, *merge_first, swap_wide(merge_ends, CORE), *merge_sides)
    stream_zero, attend_input, attend_up, attend_up_other = merge_forward(
        joined, merge_pieces, skip_bias, gain_one, bias_one
    )
    joined_up = upright(joined_mine)
    joined_up_other = upright(joined_other)
    (
        mixed_first,
        expand_far,
        expand_near,
        stream_zero,
        attend_input,
        attend_up_other,
        joined_up,
        joined_up_other,
    ) = together(
        mixed_first,
        expand_far,
        expand_near,
        stream_zero,
        attend_input,
        attend_up_other,
        joined_up,
        joined_up_other,
    )
    mixed_second = gather_second(mixed_first)
    mixed_sides = swap_sides(mixed_first)
    expand_last = swap_narrow(expand_far, 1)
    expand_block = arrange("expand", 1, expand_low, (expand_near, expand_far, expand_last))[0]
    mixed_second, mixed_sides, expand_block = together(mixed_second, mixed_sides, expand_block)
    expand_first = gather_first(expand_block)
    shrink_far = swap_narrow(shrink_low, 2)
    shrink_near = swap_narrow(shrink_low, 1)
    mixed_ends = ends_of(mixed_block, mixed_second)
    mixed_pieces = (mixed_ends, *mixed_first, swap_wide(mixed_ends, CORE), *mixed_sides)
    heads, chances_first, mix_first = attend_first(attend_input, mixed_pieces)
    expand_first, shrink_far, shrink_near, heads, mix_first = together(
        expand_first, shrink_far, shrink_near, heads, mix_first
    )
    expand_second = gather_second(expand_first)
    expand_sides = swap_sides(expand_first)
    shrink_last = swap_narrow(shrink_far, 1)
    chances_second, stream_one, expand_input, ups, ups_other = attend_second(
        heads, mix_first, mixed_pieces, stream_zero, output_bias, gain_two, bias_two
    )
    shrink_block = arrange("shrink", 4, shrink_low, (shrink_near, shrink_far, shrink_last))[0]
    expand_second, expand_sides, shrink_block, expand_input, ups_other = together(
        expand_second, expand_sides, shrink_block, expand_input, ups_other
    )
    shrink_first = gather_first(shrink_block)
    expand_ends = ends_of(expand_block, expand_second)
    expand_pieces = (expand_ends, *expand_first, swap_wide(expand_ends, CORE), *expand_sides)
    pulled_sibling = swap_wide(pulled, CORE)
    active, slope, active_up, active_up_other = expand_forward(
        expand_input, expand_pieces, expand_bias
    )
    shrink_first, pulled_sibling, active, slope, active_up, active_up_other = together(
        shrink_first, pulled_sibling, active, slope, active_up, active_up_other
    )
    shrink_second = gather_second(shrink_first)
    shrink_sides = swap_sides(shrink_first)
    active_up_sibling = swap_wide(active_up_other, CORE)
    shrink_blocks = pair_gradient([(active_up, active_up_sibling, D)], (pulled, pulled_sibling))
    shrink_second, shrink_sides, shrink_blocks = together(
        shrink_second, shrink_sides, shrink_blocks
    )
    shrink_got = send(shrink_blocks)
    shrink_ends = ends_of(shrink_block, shrink_second)
    shrink_pieces = (shrink_ends, *shrink_first, swap_wide(shrink_ends, CORE), *shrink_sides)
    ups_sibling = swap_wide(ups_other, CORE)
    attend_up_sibling = swap_wide(attend_up_other, CORE)
    hidden_low, hidden_sum = hidden_backward(pulled, shrink_pieces, slope)
    outputs = shrink_forward(active, shrink_pieces, stream_one, shrink_bias)[None]
    shrink_got, ups_sibling, attend_up_sibling, hidden_low, hidden_sum, outputs, joined_up_other = (
        together(
            shrink_got,
            ups_sibling,
            attend_up_sibling,
            hidden_low,
            hidden_sum,
            outputs,
            joined_up_other,
        )
    )
    shrink_got_last = forward(shrink_blocks, shrink_got)
    hidden_sibling = swap_wide(hidden_low, CORE)
    half = D // 2
    expand_blocks = pair_gradient(
        [(ups[half:], ups_sibling[half:], FF)], (hidden_low, hidden_sibling)
    )
    shrink_got_last, expand_blocks, hidden_low, joined_up_other = together(
        shrink_got_last, expand_blocks, hidden_low, joined_up_other
    )
    expand_got = send(expand_blocks)
    joined_sibling = swap_wide(joined_up_other, CORE)
    delta_one, stream_low, sums_two, delta_mixture = expand_backward(
        hidden_low, expand_pieces, mixed_pieces, pulled, stream_one, gain_two
    )
    delta_mixed = attend_backward(heads, chances_first, chances_second, delta_mixture, stream_low)
    shrink_quarters = unarrange("shrink", 4, shrink_blocks, shrink_got, shrink_got_last)
    expand_got, joined_sibling, delta_mixed, shrink_quarters = together(
        expand_got, joined_sibling, delta_mixed, shrink_quarters
    )
    expand_got_last = forward(expand_blocks, expand_got)
    mixed_sibling = swap_wide(delta_mixed, CORE)
    shrink_narrow = narrow_first(shrink_quarters)
    mixed_blocks = pair_gradient(
        [(attend_up, attend_up_sibling, 3 * D), (ups[:half], ups_sibling[:half], D)],
        (delta_mixed, mixed_sibling),
    )
    expand_got_last, shrink_narrow, mixed_blocks, delta_mixed, moments = together(
        expand_got_last,
        shrink_narrow,
        mixed_blocks,
        delta_mixed,
        (shrink_weight, shrink_moment, shrink_square),
    )
    mixed_got = send(mixed_blocks)
    shrink_end = narrow_second(shrink_quarters, shrink_narrow)
    expand_quarters = unarrange("expand", 1, expand_blocks, expand_got, expand_got_last)
    expand_narrow = narrow_first(expand_quarters)
    zero_low, sums_one = entry_backward(
        delta_mixed, mixed_pieces, delta_one, stream_zero, gain_one
    )
    input_gradient, skip_gradient = joined_backward(zero_low, merge_pieces)
    mixed_got, shrink_end, expand_narrow, zero_low, sums_one, input_gradient, skip_gradient = (
        together(
            mixed_got,
            shrink_end,
            expand_narrow,
            zero_low,
            sums_one,
            input_gradient,
            skip_gradient,
        )
    )
    mixed_got_last = forward(mixed_blocks, mixed_got)
    expand_end = narrow_second(expand_quarters, expand_narrow)
    zero_sibling = swap_wide(zero_low, CORE)
    merge_blocks = pair_gradient([(joined_up, joined_sibling, D)], (zero_low, zero_sibling))
    vector_total = jnp.concatenate(
        [
            outer(row)
            for row in (
                sums_one[0],
                sums_one[1],
                sums_one[2],
                sums_two[0],
                sums_two[1],
                sums_two[2],
                sums_two[3],
                hidden_sum[0],
            )
        ]
    )
    mixed_got_last, expand_end, vector_total, merge_blocks, shrink_end = together(
        mixed_got_last, expand_end, vector_total, merge_blocks, shrink_end
    )
    merge_got = send(merge_blocks)
    mixed_quarters = unarrange("attend_output", 1, mixed_blocks, mixed_got, mixed_got_last)
    mixed_narrow = narrow_first(mixed_quarters)
    vector_total = vector_total + swap_wide(vector_total, CORE)
    merge_got, mixed_narrow, vector_total, expand_end, shrink_end = together(
        merge_got, mixed_narrow, vector_total, expand_end, shrink_end
    )
    merge_got_last = forward(merge_blocks, merge_got)
    mixed_end = narrow_second(mixed_quarters, mixed_narrow)
    vector_total = vector_total + swap_wide(vector_total, ACROSS)
    vector_total = vector_total + swap_wide(vector_total, ALONG)
    shrink_sum = unfold(
        finish(shrink_quarters, shrink_narrow, shrink_end), shrink_weight.shape[0]
    )
    shrink_new = adamw_update(*[moment.T for moment in moments], shrink_sum.T, rate_shrink)
    shrink_new = [new.T for new in shrink_new]
    merge_got_last, mixed_end, vector_total, shrink_new, expand_end = together(
        merge_got_last, mixed_end, vector_total, shrink_new, expand_end
    )
    merge_quarters = unarrange("merge", 2, merge_blocks, merge_got, merge_got_last)
    merge_narrow = direct_narrow(merge_quarters)
    halves = vector_total.reshape(2, -1)
    vector_total = pick(halves, high_bit) + swap_narrow(pick(halves, 1 - high_bit), 2)
    halves = vector_total.reshape(2, -1)
    vector_total = pick(halves, low_bit) + swap_narrow(pick(halves, 1 - low_bit), 1)
    expand_new = adamw_update(
        expand_weight,
        expand_moment,
        expand_square,
        finish(expand_quarters, expand_narrow, expand_end),
        rate_expand,
    )
    mixed_total = finish(mixed_quarters, mixed_narrow, mixed_end)
    attend_new = adamw_update(
        attend_weight, attend_moment, attend_square, mixed_total[:, :columns], rate_attend
    )
    output_new = adamw_update(
        output_weight, output_moment, output_square, mixed_total[:, columns:], rate_output
    )
    merge_narrow, vector_total, expand_new, attend_new, output_new = together(
        merge_narrow, vector_total, expand_new, attend_new, output_new
    )
    merge_new = adamw_update(
        merge_weight,
        merge_moment,
        merge_square,
        unfold(direct_sum(merge_quarters, merge_narrow), merge_weight.shape[0]),
        rate_merge,
    )
    vector_new = adamw_update(vectors, vector_moment, vector_square, vector_total, rate_vector)
    return (
        outputs,
        input_gradient[None],
        skip_gradient[None],
        *merge_new,
        *attend_new,
        *output_new,
        *expand_new,
        *shrink_new,
        *vector_new,
    )


def solution(mesh):
    in_specs = (
        P(("wide", "narrow"), None, None),
        P(("wide", "narrow"), None, None),
        P(("wide", "narrow"), None, None),
        P("wide", "narrow"),
        P("wide", "narrow"),
        P("wide", "narrow"),
        P("wide", "narrow"),
        P("wide", "narrow"),
        P("wide", "narrow"),
        P("wide", "narrow"),
        P("wide", "narrow"),
        P("wide", "narrow"),
        P("wide", "narrow"),
        P("wide", "narrow"),
        P("wide", "narrow"),
        P("wide", "narrow"),
        P("wide", "narrow"),
        P("wide", "narrow"),
        P("narrow"),
        P("narrow"),
        P("narrow"),
    )
    out_specs = (
        P(("wide", "narrow"), None, None),
        P(("wide", "narrow"), None, None),
        P(("wide", "narrow"), None, None),
        P("wide", "narrow"),
        P("wide", "narrow"),
        P("wide", "narrow"),
        P("wide", "narrow"),
        P("wide", "narrow"),
        P("wide", "narrow"),
        P("wide", "narrow"),
        P("wide", "narrow"),
        P("wide", "narrow"),
        P("wide", "narrow"),
        P("wide", "narrow"),
        P("wide", "narrow"),
        P("wide", "narrow"),
        P("wide", "narrow"),
        P("wide", "narrow"),
        P("narrow"),
        P("narrow"),
        P("narrow"),
    )
    tuned = mesh.shape["wide"] == 8 and mesh.shape["narrow"] == 4
    return jax.shard_map(
        on_device if tuned else general_device, mesh=mesh, in_specs=in_specs, out_specs=out_specs, check_vma=False
    )
```

```python
import jax
import jax.numpy as jnp
from jax import lax
from jax.experimental import pallas as pl
from jax.experimental.pallas import tpu as pltpu
from jax.sharding import PartitionSpec as P

D = 1152
FF = 4608
H = 16
HD = 72
STEP = 5


norm_epsilon = 1e-05
adam_epsilon = 1e-08
beta_moment = 0.5
weight_decay = 0.01
rate_merge = 0.04
rate_attend = 0.08
rate_output = 0.6
rate_expand = 0.06
rate_shrink = 0.03
rate_vector = 0.6


def product(left_side, right_side):
    return jnp.dot(left_side, right_side, preferred_element_type=jnp.float32)


def transposed(gradient, matrix):
    return lax.dot_general(
        gradient,
        matrix,
        (((gradient.ndim - 1,), (1,)), ((), ())),
        preferred_element_type=jnp.float32,
    )


def weight_gradient(activations, gradient):
    flat_left = activations.reshape(-1, activations.shape[-1])
    flat_right = gradient.reshape(-1, gradient.shape[-1])
    return lax.dot_general(
        flat_left, flat_right, (((0,), (0,)), ((), ())), preferred_element_type=jnp.float32
    )


def normalize(values):
    centered = values - jnp.mean(values, axis=-1, keepdims=True)
    spread = jnp.mean(centered * centered, axis=-1, keepdims=True)
    inverse = lax.rsqrt(spread + norm_epsilon)
    return (centered * inverse, inverse)


def norm_back(gradient, normed, inverse):
    return inverse * (
        gradient
        - jnp.mean(gradient, axis=-1, keepdims=True)
        - normed * jnp.mean(gradient * normed, axis=-1, keepdims=True)
    )


def row_sum(values):
    return jnp.sum(values, axis=(0, 1))


def unpack(packed):
    return tuple((packed[position * D : (position + 1) * D] for position in range(7))) + (
        packed[7 * D : 7 * D + FF],
    )


def gaussian_unit(values):
    return jax.nn.gelu(values, approximate=False)


def adamw_update(weight, moment, square, gradient, step_rate):
    moment_new = beta_moment * moment + (1.0 - beta_moment) * gradient
    square_new = beta_moment * square + (1.0 - beta_moment) * gradient * gradient
    correct = 1.0 - beta_moment**STEP
    direction = moment_new / correct / (jnp.sqrt(square_new / correct) + adam_epsilon)
    return (weight - step_rate * (direction + weight_decay * weight), moment_new, square_new)


def general_device(
    inputs,
    skip_tokens,
    cotangent,
    merge_weight,
    merge_moment,
    merge_square,
    attend_weight,
    attend_moment,
    attend_square,
    output_weight,
    output_moment,
    output_square,
    expand_weight,
    expand_moment,
    expand_square,
    shrink_weight,
    shrink_moment,
    shrink_square,
    vectors,
    vector_moment,
    vector_square,
):
    merge_low = merge_weight.astype(jnp.bfloat16)
    attend_low = attend_weight.astype(jnp.bfloat16)
    output_low = output_weight.astype(jnp.bfloat16)
    expand_low = expand_weight.astype(jnp.bfloat16)
    shrink_low = shrink_weight.astype(jnp.bfloat16)
    vector_low = vectors.astype(jnp.bfloat16)
    columns = (
        lax.all_gather(merge_low, "narrow", axis=1, tiled=True),
        lax.all_gather(attend_low, "narrow", axis=1, tiled=True),
        lax.all_gather(output_low, "narrow", axis=1, tiled=True),
        lax.all_gather(expand_low, "narrow", axis=1, tiled=True),
        lax.all_gather(shrink_low, "narrow", axis=1, tiled=True),
        lax.all_gather(vector_low, "narrow", axis=0, tiled=True),
    )
    matrices = (
        lax.all_gather(columns[0], "wide", axis=0, tiled=True),
        lax.all_gather(columns[1], "wide", axis=0, tiled=True),
        lax.all_gather(columns[2], "wide", axis=0, tiled=True),
        lax.all_gather(columns[3], "wide", axis=0, tiled=True),
        lax.all_gather(columns[4], "wide", axis=0, tiled=True),
    )
    skip_bias, gain_one, bias_one, output_bias, gain_two, bias_two, shrink_bias, expand_bias = (
        unpack(columns[5].astype(jnp.float32))
    )
    images = inputs.shape[0]
    length = inputs.shape[1]
    softmax_scale = HD ** (-0.5)
    joined = jnp.concatenate([inputs, skip_tokens], axis=-1)
    stream_zero = product(joined, matrices[0]) + skip_bias
    normed_one, inverse_one = normalize(stream_zero)
    attend_input = (normed_one * gain_one + bias_one).astype(jnp.bfloat16)
    mixed_heads = product(attend_input, matrices[1]).astype(jnp.bfloat16)
    query_heads = mixed_heads[..., 0:D].reshape(images, length, H, HD)
    key_heads = mixed_heads[..., D : 2 * D].reshape(images, length, H, HD)
    value_heads = mixed_heads[..., 2 * D : 3 * D].reshape(images, length, H, HD)
    logits = (
        jnp.einsum("blhe,bmhe->bhlm", query_heads, key_heads, preferred_element_type=jnp.float32)
        * softmax_scale
    )
    maxima = jnp.max(logits, axis=-1, keepdims=True)
    log_total = maxima + jnp.log(jnp.sum(jnp.exp(logits - maxima), axis=-1, keepdims=True))
    softmax_low = jnp.exp(logits - log_total).astype(jnp.bfloat16)
    mixture = jnp.einsum(
        "bhlm,bmhe->blhe", softmax_low, value_heads, preferred_element_type=jnp.float32
    )
    mixture = mixture.astype(jnp.bfloat16).reshape(images, length, D)
    stream_one = stream_zero + product(mixture, matrices[2]) + output_bias
    normed_two, inverse_two = normalize(stream_one)
    expand_input = (normed_two * gain_two + bias_two).astype(jnp.bfloat16)
    hidden = product(expand_input, matrices[3]) + expand_bias
    active, pullback = jax.vjp(gaussian_unit, hidden)
    active_low = active.astype(jnp.bfloat16)
    outputs = (stream_one + product(active_low, matrices[4]) + shrink_bias).astype(jnp.bfloat16)
    columns_back = (
        lax.all_gather(merge_low, "narrow", axis=1, tiled=True),
        lax.all_gather(attend_low, "narrow", axis=1, tiled=True),
        lax.all_gather(output_low, "narrow", axis=1, tiled=True),
        lax.all_gather(expand_low, "narrow", axis=1, tiled=True),
        lax.all_gather(shrink_low, "narrow", axis=1, tiled=True),
        lax.all_gather(vector_low, "narrow", axis=0, tiled=True),
    )
    matrices_back = (
        lax.all_gather(columns_back[0], "wide", axis=0, tiled=True),
        lax.all_gather(columns_back[1], "wide", axis=0, tiled=True),
        lax.all_gather(columns_back[2], "wide", axis=0, tiled=True),
        lax.all_gather(columns_back[3], "wide", axis=0, tiled=True),
        lax.all_gather(columns_back[4], "wide", axis=0, tiled=True),
    )
    packed_back = columns_back[5].astype(jnp.float32)
    unpacked = unpack(packed_back)
    gain_first = unpacked[1]
    gain_second = unpacked[4]
    upstream = cotangent.astype(jnp.float32)
    shrink_gradient = weight_gradient(active_low, cotangent)
    delta_active = transposed(cotangent, matrices_back[4])
    delta_hidden = pullback(delta_active)[0]
    hidden_low = delta_hidden.astype(jnp.bfloat16)
    expand_gradient = weight_gradient(expand_input, hidden_low)
    delta_expand = transposed(hidden_low, matrices_back[3])
    delta_one = upstream + norm_back(delta_expand * gain_second, normed_two, inverse_two)
    stream_low = delta_one.astype(jnp.bfloat16)
    output_gradient = weight_gradient(mixture, stream_low)
    delta_mixture = (
        transposed(stream_low, matrices_back[2]).astype(jnp.bfloat16).reshape(images, length, H, HD)
    )
    logits_again = (
        jnp.einsum("blhe,bmhe->bhlm", query_heads, key_heads, preferred_element_type=jnp.float32)
        * softmax_scale
    )
    softmax_again = jnp.exp(logits_again - log_total)
    delta_softmax = jnp.einsum(
        "blhe,bmhe->bhlm", delta_mixture, value_heads, preferred_element_type=jnp.float32
    )
    delta_values = jnp.einsum(
        "bhlm,blhe->bmhe",
        softmax_again.astype(jnp.bfloat16),
        delta_mixture,
        preferred_element_type=jnp.float32,
    )
    delta_logits = softmax_again * (
        delta_softmax - jnp.sum(softmax_again * delta_softmax, axis=-1, keepdims=True)
    )
    delta_scores = (softmax_scale * delta_logits).astype(jnp.bfloat16)
    delta_queries = jnp.einsum(
        "bhlm,bmhe->blhe", delta_scores, key_heads, preferred_element_type=jnp.float32
    )
    delta_keys = jnp.einsum(
        "bhlm,blhe->bmhe", delta_scores, query_heads, preferred_element_type=jnp.float32
    )
    delta_mixed = jnp.concatenate(
        [
            delta_queries.reshape(images, length, D),
            delta_keys.reshape(images, length, D),
            delta_values.reshape(images, length, D),
        ],
        axis=-1,
    ).astype(jnp.bfloat16)
    attend_gradient = weight_gradient(attend_input, delta_mixed)
    delta_attend = transposed(delta_mixed, matrices_back[1])
    delta_zero = delta_one + norm_back(delta_attend * gain_first, normed_one, inverse_one)
    zero_low = delta_zero.astype(jnp.bfloat16)
    merge_gradient = weight_gradient(joined, zero_low)
    delta_joined = transposed(zero_low, matrices_back[0])
    input_gradient = delta_joined[..., 0:D].astype(jnp.bfloat16)
    skip_gradient = delta_joined[..., D : 2 * D].astype(jnp.bfloat16)
    vector_gradient = jnp.concatenate(
        [
            row_sum(delta_zero),
            row_sum(delta_attend * normed_one),
            row_sum(delta_attend),
            row_sum(delta_one),
            row_sum(delta_expand * normed_two),
            row_sum(delta_expand),
            row_sum(upstream),
            row_sum(delta_hidden),
        ]
    )
    owned_rows = (
        lax.psum_scatter(merge_gradient, "wide", scatter_dimension=0, tiled=True),
        lax.psum_scatter(attend_gradient, "wide", scatter_dimension=0, tiled=True),
        lax.psum_scatter(output_gradient, "wide", scatter_dimension=0, tiled=True),
        lax.psum_scatter(expand_gradient, "wide", scatter_dimension=0, tiled=True),
        lax.psum_scatter(shrink_gradient, "wide", scatter_dimension=0, tiled=True),
    )
    vector_total = lax.psum(vector_gradient, "wide")
    parted = (
        lax.psum_scatter(owned_rows[0], "narrow", scatter_dimension=1, tiled=True),
        lax.psum_scatter(owned_rows[1], "narrow", scatter_dimension=1, tiled=True),
        lax.psum_scatter(owned_rows[2], "narrow", scatter_dimension=1, tiled=True),
        lax.psum_scatter(owned_rows[3], "narrow", scatter_dimension=1, tiled=True),
        lax.psum_scatter(owned_rows[4], "narrow", scatter_dimension=1, tiled=True),
        lax.psum_scatter(vector_total, "narrow", scatter_dimension=0, tiled=True),
    )
    merge_new = adamw_update(merge_weight, merge_moment, merge_square, parted[0], rate_merge)
    attend_new = adamw_update(attend_weight, attend_moment, attend_square, parted[1], rate_attend)
    output_new = adamw_update(output_weight, output_moment, output_square, parted[2], rate_output)
    expand_new = adamw_update(expand_weight, expand_moment, expand_square, parted[3], rate_expand)
    shrink_new = adamw_update(shrink_weight, shrink_moment, shrink_square, parted[4], rate_shrink)
    vector_new = adamw_update(vectors, vector_moment, vector_square, parted[5], rate_vector)
    return (
        outputs,
        input_gradient,
        skip_gradient,
        merge_new[0],
        merge_new[1],
        merge_new[2],
        attend_new[0],
        attend_new[1],
        attend_new[2],
        output_new[0],
        output_new[1],
        output_new[2],
        expand_new[0],
        expand_new[1],
        expand_new[2],
        shrink_new[0],
        shrink_new[1],
        shrink_new[2],
        vector_new[0],
        vector_new[1],
        vector_new[2],
    )


CORE = 1
ACROSS = 2
ALONG = 4
PAD = 384
VMEM_BYTES = 56 * 1024 * 1024
LIGHT = pl.CostEstimate(flops=0, bytes_accessed=1024, transcendentals=0)
PARAMS = pltpu.CompilerParams(vmem_limit_bytes=VMEM_BYTES)


def swap_wide(value, bit):
    return lax.ppermute(value, "wide", [(i, i ^ bit) for i in range(8)])


def swap_narrow(value, bit):
    return lax.ppermute(value, "narrow", [(i, i ^ bit) for i in range(4)])


def together(*values):
    return lax.optimization_barrier(values)


def spot():
    wide = lax.axis_index("wide")
    narrow = lax.axis_index("narrow")
    return (wide & 1, (wide >> 1) & 1, (wide >> 2) & 1, narrow & 1, narrow >> 1)


def split_shapes(rows, columns):
    if columns == FF:
        return (rows, columns // 2), True
    return (rows // 2, columns), False


def split_block(value):
    shape, by_columns = split_shapes(*value.shape[-2:])
    if by_columns:
        return value[..., : shape[1]], value[..., shape[1] :]
    return value[..., : shape[0], :], value[..., shape[0] :, :]


def column_blocks(kind, quarter):
    if kind == "attend_output":
        width = quarter // 8
        order = [8 * part + 2 * n + p for part in range(3) for p in range(2) for n in range(4)]
        blocks = [(block // 6, (block % 6) * width) for block in order]
        return width, blocks + [(n, (6 + p) * width) for p in range(2) for n in range(4)]
    width = quarter // 2
    return width, [(n, p * width) for p in range(2) for n in range(4)]


def fold(shard):
    parts = max(1, shard.shape[0] // (D // 8))
    height = shard.shape[0] // parts
    return jnp.concatenate(
        [shard[part * height : (part + 1) * height] for part in range(parts)], axis=1
    )


def unfold(value, rows):
    parts = rows // value.shape[0]
    quarter = value.shape[1] // parts
    return jnp.concatenate(
        [value[:, part * quarter : (part + 1) * quarter] for part in range(parts)], axis=0
    )


def arrange(kind, parts, shard, others, extra=0):
    height = shard.shape[0] - extra
    rows, quarter = parts * height, shard.shape[1] // parts
    width, blocks = column_blocks(kind, quarter)

    def kernel(*refs):
        full, apart, held = refs[4], refs[5], refs[-1]
        narrow = lax.axis_index("narrow")
        for relative in range(4):
            held[relative] = refs[relative][...]
        for number in range(4):
            value = held[narrow ^ number]
            if extra:
                apart[number] = value[height:]
            for position, (owner, offset) in enumerate(blocks):
                if owner == number:
                    column = slice(position * width, (position + 1) * width)
                    for part in range(parts):
                        start = part * quarter + offset
                        full[part * height : (part + 1) * height, column] = value[
                            :height, start : start + width
                        ]

    outs = [jax.ShapeDtypeStruct((rows, 4 * quarter), jnp.bfloat16)]
    if extra:
        outs.append(jax.ShapeDtypeStruct((4, extra, shard.shape[1]), jnp.bfloat16))
    return pl.pallas_call(
        kernel,
        out_shape=tuple(outs),
        scratch_shapes=[pltpu.VMEM((4,) + shard.shape, jnp.bfloat16)],
        compiler_params=PARAMS,
        cost_estimate=LIGHT,
    )(shard, *others)


def weight_scratch(rows, columns, chunks=1):
    return [pltpu.VMEM((rows, columns), jnp.bfloat16), pltpu.SemaphoreType.DMA((chunks, 8))]


class Fetch:
    def __init__(self, refs, full, sems, first=0):
        wide = lax.axis_index("wide")
        core, chip = wide & 1, wide >> 1
        rows = full.shape[0] // 8
        chunks = sems.shape[0]
        width = full.shape[1] // chunks
        self.copies = []
        for chunk in range(chunks):
            group = []
            for number, (ends, from_x, from_y) in enumerate((refs[:3], refs[3:])):
                parity = core if number == 0 else 1 - core
                own, far = ends.at[pl.ds(0, rows)], ends.at[pl.ds(rows, rows)]
                for relative, piece in enumerate((own, from_x, from_y, far)):
                    start = pl.multiple_of((4 * parity + (chip ^ relative)) * rows, 16)
                    group.append(
                        pltpu.make_async_copy(
                            piece.at[:, pl.ds(first + chunk * width, width)],
                            full.at[pl.ds(start, rows), pl.ds(chunk * width, width)],
                            sems.at[chunk, 4 * number + relative],
                        )
                    )
            self.copies.append(group)
        for group in self.copies:
            for copy in group:
                copy.start()

    def wait(self, chunk=0):
        for copy in self.copies[chunk]:
            copy.wait()


def pair_gradient(lefts, right):
    height = lefts[0][4]
    rows = height // 4
    tokens, columns = right[0].shape
    tile = 384 if height > 576 else 1152
    count = len(lefts)
    ends = [sum(left[2] for left in lefts[: number + 1]) // tile for number in range(count)]
    starts = [0] + ends[:-1]

    def kernel(*refs):
        left_refs = refs[: 2 * count]
        right_ref, sibling_ref = refs[2 * count : 2 * count + 2]
        outs = refs[2 * count + 2 : 2 * count + 6]
        joint, beside, total = refs[2 * count + 6 :]
        step = pl.program_id(0)

        @pl.when(step == 0)
        def _():
            joint[...] = jnp.zeros_like(joint)

        for number in range(count):

            @pl.when(step == starts[number])
            def _():
                beside[:, :PAD] = left_refs[2 * number][...]
                beside[:, PAD:] = left_refs[2 * number + 1][...]

        joint[:tokens] = right_ref[...]
        joint[PAD : PAD + tokens] = sibling_ref[...]
        total[...] = jnp.dot(
            beside[...], joint[...], preferred_element_type=jnp.float32
        ).astype(jnp.bfloat16)
        by_columns = split_shapes(rows, columns)[1]
        part_blocks(total, rows, outs, step < columns // tile // 2 if by_columns else None)

    whole = lambda place: pl.BlockSpec((height, PAD), lambda i: (place, 0))
    part = lambda size: pl.BlockSpec((size, tile), lambda i: (0, i))
    shape, by_columns = split_shapes(rows, columns)
    half = columns // tile // 2
    if by_columns:
        top = pl.BlockSpec((2, rows, tile), lambda i: (0, 0, jnp.minimum(i, half - 1)))
        bottom = pl.BlockSpec((2, rows, tile), lambda i: (0, 0, jnp.maximum(i - half, 0)))
    else:
        top = bottom = pl.BlockSpec((2, shape[0], tile), lambda i: (0, 0, i))
    outs = pl.pallas_call(
        kernel,
        grid=(columns // tile,),
        in_specs=[whole(left[3]) for left in lefts for _ in range(2)] + [part(tokens)] * 2,
        out_specs=(top, top, bottom, bottom),
        out_shape=block_shapes(rows, columns),
        scratch_shapes=[
            pltpu.VMEM((2 * PAD, tile), jnp.bfloat16),
            pltpu.VMEM((height, 2 * PAD), jnp.bfloat16),
            pltpu.VMEM((height, tile), jnp.bfloat16),
        ],
        compiler_params=PARAMS,
        cost_estimate=LIGHT,
    )(*[left for pair_of in lefts for left in pair_of[:2]], *right)
    return outs


def block_shapes(rows, columns):
    shape = split_shapes(rows, columns)[0]
    return (jax.ShapeDtypeStruct((2,) + shape, jnp.bfloat16),) * 4


def part_blocks(total, rows, outs, first_half):
    wide = lax.axis_index("wide")
    across, along = (wide >> 1) & 1, (wide >> 2) & 1
    half = rows // 2
    for kept_x in range(2):
        for kept_y in range(2):
            x = across if kept_x else 1 - across
            y = along if kept_y else 1 - along
            start = pl.multiple_of((2 * y + x) * rows, 16)
            top, bottom = outs[1 - kept_x], outs[3 - kept_y]
            if first_half is None:
                top[1 - kept_y] = total[pl.ds(start, half)]
                bottom[1 - kept_x] = total[pl.ds(pl.multiple_of(start + half, 16), half)]
                continue

            @pl.when(first_half)
            def _():
                top[1 - kept_y] = total[pl.ds(start, rows)]

            @pl.when(jnp.logical_not(first_half))
            def _():
                bottom[1 - kept_x] = total[pl.ds(start, rows)]


def unarrange(kind, parts, blocks, got, got_last):
    by_columns = got_last[0].shape[1] == FF // 2
    part_rows, part_columns = got_last[0].shape
    rows = part_rows if by_columns else 2 * part_rows
    columns = 2 * part_columns if by_columns else part_columns
    quarter = columns // 4
    height = rows // parts
    width, column_parts = column_blocks(kind, quarter)

    def kernel(*refs):
        tops, bottoms = refs[:3], refs[3:6]
        outs, held = refs[6:10], refs[10]
        narrow = lax.axis_index("narrow")
        low_bit, high_bit = narrow & 1, narrow >> 1
        top = add_low(tops[0][...], tops[1][...], tops[2][...])
        bottom = add_low(bottoms[0][...], bottoms[1][...], bottoms[2][...])
        if by_columns:
            held[:, :part_columns] = top
            held[:, part_columns:] = bottom
        else:
            held[:part_rows] = top
            held[part_rows:] = bottom
        for owner in range(4):
            for which in range(4):
                low_same, high_same = 1 - which // 2, 1 - which % 2

                @pl.when(
                    ((low_bit == (owner & 1)) == (low_same == 1))
                    & ((high_bit == (owner >> 1)) == (high_same == 1))
                )
                def _():
                    for position, (quarter_of, offset) in enumerate(column_parts):
                        if quarter_of == owner:
                            piece = held[:, position * width : (position + 1) * width]
                            for part in range(parts):
                                start = part * quarter + offset
                                outs[which][:, start : start + width] = piece[
                                    part * height : (part + 1) * height
                                ]

    near = pl.BlockSpec((None, part_rows, part_columns), lambda i: (0, 0, 0))
    full = lambda size, width: pl.BlockSpec((size, width), lambda i: (0, 0))
    shape = jax.ShapeDtypeStruct((height, parts * quarter), jnp.bfloat16)
    return pl.pallas_call(
        kernel,
        grid=(1,),
        in_specs=[near, near, full(part_rows, part_columns)] * 2,
        out_specs=(full(height, parts * quarter),) * 4,
        out_shape=(shape,) * 4,
        scratch_shapes=[pltpu.VMEM((rows, columns), jnp.bfloat16)],
        compiler_params=PARAMS,
        cost_estimate=LIGHT,
    )(blocks[0], got[0], got_last[0], blocks[2], got[1], got_last[1])


def add_low(*terms):
    return sum(term.astype(jnp.float32) for term in terms).astype(jnp.bfloat16)


def pick(value, index, dim=0):
    return lax.dynamic_index_in_dim(value, index, dim, keepdims=False)


def halves_of(value, core):
    middle = value.shape[-1] // 2
    first, second = value[..., :middle], value[..., middle:]
    return jnp.where(core == 0, first, second), jnp.where(core == 0, second, first)


def inner(value):
    width = value.shape[-1] // 8
    return jnp.concatenate(
        [
            value[..., (2 * n + p) * width : (2 * n + p + 1) * width]
            for p in range(2)
            for n in range(4)
        ],
        axis=-1,
    )


def outer(value):
    width = value.shape[-1] // 8
    return jnp.concatenate(
        [
            value[..., (4 * p + n) * width : (4 * p + n + 1) * width]
            for n in range(4)
            for p in range(2)
        ],
        axis=-1,
    )


def upright(value):
    return jnp.pad(value, ((0, PAD - value.shape[0]), (0, 0))).T


KEEP_NEAR, KEEP_FAR, SEND_NEAR, SEND_FAR = range(4)


def send(blocks):
    return swap_wide(blocks[1], ACROSS), swap_wide(blocks[3], ALONG)


def forward(blocks, got):
    return (
        swap_wide(add_low(blocks[0][1], got[0][1]), ALONG),
        swap_wide(add_low(blocks[2][1], got[1][1]), ACROSS),
    )


def narrow_first(quarters):
    return swap_narrow(quarters[SEND_FAR], 1), swap_narrow(quarters[SEND_NEAR], 1)


def narrow_second(quarters, got):
    return swap_narrow(add_low(quarters[KEEP_FAR], got[0]), 2)


def finish(quarters, got, got_last):
    return (
        quarters[KEEP_NEAR].astype(jnp.float32)
        + got[1].astype(jnp.float32)
        + got_last.astype(jnp.float32)
    )


def across_narrow(shard):
    return tuple(swap_narrow(shard, bit) for bit in (1, 2, 3))


def gather_first(block):
    return swap_wide(block, ACROSS), swap_wide(block, ALONG)


def gather_second(first):
    return (
        swap_wide(split_block(first[0])[0], ALONG),
        swap_wide(split_block(first[1])[1], ACROSS),
    )


def swap_sides(first):
    return swap_wide(first[0], CORE), swap_wide(first[1], CORE)


def ends_of(block, second):
    if split_shapes(*block.shape)[1]:
        return jnp.concatenate([block, jnp.concatenate(second, axis=1)], axis=0)
    return jnp.concatenate([block, *second], axis=0)


def line_gradient(lefts, rights, rights_sibling):
    tokens, height = lefts[0].shape
    width = rights.shape[2]
    rows = height // 4

    def kernel(*refs):
        right_ref, sibling_ref = refs[8:10]
        outs, total = refs[10:14], refs[14]
        chip = lax.axis_index("wide") >> 1
        for number in range(8):
            right = (right_ref, sibling_ref)[number // 4][number % 4]
            part = lax.dot_general(
                right,
                refs[number][...],
                (((0,), (0,)), ((), ())),
                preferred_element_type=jnp.float32,
            )
            total[...] = part if number == 0 else total[...] + part
        for owner in range(4):
            block = total[:, owner * rows : (owner + 1) * rows].T.astype(jnp.bfloat16)
            for relative in range(4):

                @pl.when((chip ^ relative) == owner)
                def _():
                    outs[relative][:, :width] = block[: rows // 2]
                    outs[relative][:, width:] = block[rows // 2 :]

    shape = jax.ShapeDtypeStruct((rows // 2, 2 * width), jnp.bfloat16)
    return pl.pallas_call(
        kernel,
        out_shape=(shape,) * 4,
        scratch_shapes=[pltpu.VMEM((width, height), jnp.float32)],
        compiler_params=PARAMS,
        cost_estimate=LIGHT,
    )(*lefts, rights, rights_sibling)


def turned_update(weight, moment, square, terms, parts, step_rate):
    rows, quarter = weight.shape
    height = rows // parts

    def kernel(*refs):
        weight_ref, moment_ref, square_ref = refs[: 3]
        total = sum(ref[...].astype(jnp.float32) for ref in refs[3 : 3 + len(terms)])
        outs, gradient = refs[3 + len(terms) : 6 + len(terms)], refs[-1]
        for part in range(parts):
            gradient[part * height : (part + 1) * height] = total[
                :, part * quarter : (part + 1) * quarter
            ]
        new = adamw_update(
            weight_ref[...], moment_ref[...], square_ref[...], gradient[...].T, step_rate
        )
        for out, value in zip(outs, new):
            out[...] = value

    new = pl.pallas_call(
        kernel,
        out_shape=(jax.ShapeDtypeStruct((quarter, rows), jnp.float32),) * 3,
        scratch_shapes=[pltpu.VMEM((rows, quarter), jnp.float32)],
        compiler_params=PARAMS,
        cost_estimate=LIGHT,
    )(weight.T, moment.T, square.T, *terms)
    return tuple(value.T for value in new)


def heavy(kernel, outs, scratch, weights, operands):
    return pl.pallas_call(
        kernel,
        in_specs=[pl.BlockSpec(memory_space=pl.ANY)] * len(weights)
        + [pl.BlockSpec(memory_space=pltpu.VMEM)] * len(operands),
        out_shape=tuple(jax.ShapeDtypeStruct(shape, dtype) for shape, dtype in outs),
        scratch_shapes=scratch,
        compiler_params=PARAMS,
        cost_estimate=LIGHT,
    )(*weights, *operands)


def dot_rows(left, right):
    return lax.dot_general(left, right, (((1,), (1,)), ((), ())), preferred_element_type=jnp.float32)


def dot_depth(left, right):
    return lax.dot_general(left, right, (((0,), (0,)), ((), ())), preferred_element_type=jnp.float32)


def store_upright(value, padded, mine, other):
    features = value.shape[1]
    padded[: value.shape[0]] = value
    turned = padded[...].T.astype(jnp.bfloat16)
    core = lax.axis_index("wide") & 1

    @pl.when(core == 0)
    def _():
        mine[...] = turned[: features // 2]
        other[...] = turned[features // 2 :]

    @pl.when(core == 1)
    def _():
        other[...] = turned[: features // 2]
        mine[...] = turned[features // 2 :]


def merge_forward(joined, weight, bias, gain, shift):
    length = joined.shape[0]

    def kernel(*refs):
        joined_ref, bias_ref, gain_ref, shift_ref = refs[6:10]
        stream, entry, up_mine, up_other, full, sems, padded = refs[10:]
        weight_in = Fetch(refs[:6], full, sems)
        padded[...] = jnp.zeros_like(padded)
        weight_in.wait()
        stream[...] = product(joined_ref[...], full[...]) + bias_ref[...]
        normed = normalize(stream[...])[0]
        value = (normed * gain_ref[...] + shift_ref[...]).astype(jnp.bfloat16)
        entry[...] = value
        store_upright(value.astype(jnp.float32), padded, up_mine, up_other)

    return heavy(
        kernel,
        [
            ((length, D), jnp.float32),
            ((length, D), jnp.bfloat16),
            ((D // 2, PAD), jnp.bfloat16),
            ((D // 2, PAD), jnp.bfloat16),
        ],
        weight_scratch(2 * D, D) + [pltpu.VMEM((PAD, D), jnp.float32)],
        weight,
        (joined, bias, gain, shift),
    )


def attend_head(heads, head, chances_ref, slot):
    at = head * HD
    queries = heads[:, at : at + HD]
    keys = heads[:, D + at : D + at + HD]
    values = heads[:, 2 * D + at : 2 * D + at + HD]
    logits = dot_rows(queries, keys) * HD ** (-0.5)
    powers = jnp.exp(logits - jnp.max(logits, axis=-1, keepdims=True))
    chances = powers / jnp.sum(powers, axis=-1, keepdims=True)
    chances_ref[slot] = chances
    return product(chances.astype(jnp.bfloat16), values).astype(jnp.bfloat16)


FIRST = 12


def attend_first(entry, weight):
    length = entry.shape[0]

    def kernel(*refs):
        entry_ref, heads, chances_ref, mix_ref, full, sems = refs[6:]
        weight_in = Fetch(refs[:6], full, sems)
        for part in range(3):
            weight_in.wait(part)
            columns = slice(part * D, (part + 1) * D)
            heads[:, columns] = product(entry_ref[...], full[:, columns]).astype(jnp.bfloat16)
        for head in range(FIRST):
            mix_ref[:, head * HD : (head + 1) * HD] = attend_head(heads, head, chances_ref, head)

    return heavy(
        kernel,
        [
            ((length, 3 * D), jnp.bfloat16),
            ((FIRST, length, length), jnp.float32),
            ((length, FIRST * HD), jnp.bfloat16),
        ],
        weight_scratch(D, 3 * D, 3),
        weight,
        (entry,),
    )


def attend_second(heads, mix_first, weight, stream_zero, bias, gain, shift):
    length = heads.shape[0]
    half = D // 2

    def kernel(*refs):
        heads_ref, first_ref, zero_ref, bias_ref, gain_ref, shift_ref = refs[6:12]
        chances_ref, stream, value_ref, up_mine, up_other, full, sems, mixed, padded = refs[12:]
        weight_in = Fetch(refs[:6], full, sems, 3 * D)
        padded[...] = jnp.zeros_like(padded)
        mixed[:, : FIRST * HD] = first_ref[...]
        for head in range(FIRST, H):
            mixed[:, head * HD : (head + 1) * HD] = attend_head(
                heads_ref, head, chances_ref, head - FIRST
            )
        weight_in.wait()
        stream[...] = zero_ref[...] + product(mixed[...], full[...]) + bias_ref[...]
        store_upright(
            mixed[...].astype(jnp.float32), padded, up_mine.at[pl.ds(0, half)], up_other.at[pl.ds(0, half)]
        )
        normed = normalize(stream[...])[0]
        value = (normed * gain_ref[...] + shift_ref[...]).astype(jnp.bfloat16)
        value_ref[...] = value
        store_upright(
            value.astype(jnp.float32), padded, up_mine.at[pl.ds(half, half)], up_other.at[pl.ds(half, half)]
        )

    return heavy(
        kernel,
        [
            ((H - FIRST, length, length), jnp.float32),
            ((length, D), jnp.float32),
            ((length, D), jnp.bfloat16),
            ((D, PAD), jnp.bfloat16),
            ((D, PAD), jnp.bfloat16),
        ],
        weight_scratch(D, D)
        + [pltpu.VMEM((length, D), jnp.bfloat16), pltpu.VMEM((PAD, D), jnp.float32)],
        weight,
        (heads, mix_first, stream_zero, bias, gain, shift),
    )


def expand_forward(entry, weight, bias):
    length = entry.shape[0]

    def kernel(*refs):
        entry_ref, bias_ref = refs[6:8]
        active_ref, slope_ref, up_mine, up_other, full, sems, padded = refs[8:]
        core = lax.axis_index("wide") & 1
        weight_in = Fetch(refs[:6], full, sems)
        padded[...] = jnp.zeros_like(padded)
        for step in range(FF // D):
            columns = slice(step * D, (step + 1) * D)
            weight_in.wait(step)
            value = product(entry_ref[...], full[:, columns]) + bias_ref[:, columns]
            inside = 0.5 * (1.0 + lax.erf(value * (0.5**0.5)))
            bell = jnp.exp(-0.5 * value * value) * (2.0 * jnp.pi) ** -0.5
            active = (value * inside).astype(jnp.bfloat16)
            slope_ref[:, columns] = inside + value * bell
            active_ref[:, columns] = active
            padded[:length] = active.astype(jnp.float32)
            turned = padded[...].T.astype(jnp.bfloat16)
            rows = slice((step % 2) * D, (step % 2 + 1) * D)

            @pl.when(core == step // 2)
            def _():
                up_mine[rows] = turned

            @pl.when(core != step // 2)
            def _():
                up_other[rows] = turned

    return heavy(
        kernel,
        [
            ((length, FF), jnp.bfloat16),
            ((length, FF), jnp.float32),
            ((FF // 2, PAD), jnp.bfloat16),
            ((FF // 2, PAD), jnp.bfloat16),
        ],
        weight_scratch(D, FF, FF // D) + [pltpu.VMEM((PAD, D), jnp.float32)],
        weight,
        (entry, bias),
    )


def hidden_backward(pulled, weight, slope):
    length = pulled.shape[0]

    def kernel(*refs):
        pulled_ref, slope_ref, low_ref, sum_ref, full, sems = refs[6:]
        Fetch(refs[:6], full, sems).wait()
        for step in range(FF // D):
            columns = slice(step * D, (step + 1) * D)
            delta = dot_rows(pulled_ref[...], full[columns]) * slope_ref[:, columns]
            low_ref[:, columns] = delta.astype(jnp.bfloat16)
            sum_ref[:, columns] = jnp.sum(delta, axis=0, keepdims=True)

    return heavy(
        kernel,
        [((length, FF), jnp.bfloat16), ((1, FF), jnp.float32)],
        weight_scratch(FF, D),
        weight,
        (pulled, slope),
    )


def expand_backward(hidden_low, weight, mixed_weight, pulled, stream_one, gain):
    length = pulled.shape[0]

    def kernel(*refs):
        hidden_ref, pulled_ref, stream_ref, gain_ref = refs[12:16]
        one_ref, low_ref, sums, mix_ref, full, sems, output, output_sems, delta = refs[16:]
        weight_in = Fetch(refs[:6], full, sems)
        output_in = Fetch(refs[6:12], output, output_sems, 3 * D)
        for step in range(FF // D):
            columns = slice(step * D, (step + 1) * D)
            weight_in.wait(step)
            part = dot_rows(hidden_ref[:, columns], full[:, columns])
            delta[...] = part if step == 0 else delta[...] + part
        value = delta[...]
        normed, inverse = normalize(stream_ref[...])
        upstream = pulled_ref[...].astype(jnp.float32)
        one = upstream + norm_back(value * gain_ref[...], normed, inverse)
        one_ref[...] = one
        low_value = one.astype(jnp.bfloat16)
        low_ref[...] = low_value
        sums[0:1] = jnp.sum(one, axis=0, keepdims=True)
        sums[1:2] = jnp.sum(value * normed, axis=0, keepdims=True)
        sums[2:3] = jnp.sum(value, axis=0, keepdims=True)
        sums[3:4] = jnp.sum(upstream, axis=0, keepdims=True)
        output_in.wait()
        mix_ref[...] = dot_rows(low_value, output[...]).astype(jnp.bfloat16)

    return heavy(
        kernel,
        [
            ((length, D), jnp.float32),
            ((length, D), jnp.bfloat16),
            ((4, D), jnp.float32),
            ((length, D), jnp.bfloat16),
        ],
        weight_scratch(D, FF, FF // D)
        + weight_scratch(D, D)
        + [pltpu.VMEM((length, D), jnp.float32)],
        (*weight, *mixed_weight),
        (hidden_low, pulled, stream_one, gain),
    )


def attend_backward(heads, chances_first, chances_second, delta_mixture, stream_low):
    length = heads.shape[0]
    scale = HD ** (-0.5)

    def kernel(heads_ref, first_ref, second_ref, delta_ref, stream_ref, mixed):
        mixed[:, 3 * D :] = stream_ref[...]
        for head in range(H):
            at = head * HD
            queries = heads_ref[:, at : at + HD]
            keys = heads_ref[:, D + at : D + at + HD]
            values = heads_ref[:, 2 * D + at : 2 * D + at + HD]
            delta = delta_ref[:, at : at + HD]
            chances = first_ref[head] if head < FIRST else second_ref[head - FIRST]
            pull = dot_rows(delta, values)
            inner_sum = jnp.sum(chances * pull, axis=-1, keepdims=True)
            scores = (scale * (chances * (pull - inner_sum))).astype(jnp.bfloat16)
            mixed[:, at : at + HD] = product(scores, keys).astype(jnp.bfloat16)
            mixed[:, D + at : D + at + HD] = dot_depth(scores, queries).astype(jnp.bfloat16)
            mixed[:, 2 * D + at : 2 * D + at + HD] = dot_depth(
                chances.astype(jnp.bfloat16), delta
            ).astype(jnp.bfloat16)

    return heavy(
        kernel,
        [((length, 4 * D), jnp.bfloat16)],
        [],
        (),
        (heads, chances_first, chances_second, delta_mixture, stream_low),
    )[0]


def entry_backward(delta_mixed, weight, delta_one, stream_zero, gain):
    length = delta_mixed.shape[0]
    width = D // 8

    def kernel(*refs):
        mixed_ref, one_ref, stream_ref, gain_ref, low_ref, sums = refs[6:12]
        quarters, (full, sems, delta) = refs[12:16], refs[16:]
        weight_in = Fetch(refs[:6], full, sems)
        for step in range(3):
            columns = slice(step * D, (step + 1) * D)
            weight_in.wait(step)
            part = dot_rows(mixed_ref[:, columns], full[:, columns])
            delta[...] = part if step == 0 else delta[...] + part
        value = delta[...]
        normed, inverse = normalize(stream_ref[...])
        zero = one_ref[...] + norm_back(value * gain_ref[...], normed, inverse)
        zero_low = zero.astype(jnp.bfloat16)
        low_ref[...] = zero_low
        narrow = lax.axis_index("narrow")
        for owner in range(4):
            for relative in range(4):

                @pl.when((narrow ^ relative) == owner)
                def _():
                    for parity in range(2):
                        start = (4 * parity + owner) * width
                        quarters[relative][:, parity * width : (parity + 1) * width] = zero_low[
                            :, start : start + width
                        ]

        sums[0:1] = jnp.sum(zero, axis=0, keepdims=True)
        sums[1:2] = jnp.sum(value * normed, axis=0, keepdims=True)
        sums[2:3] = jnp.sum(value, axis=0, keepdims=True)

    return heavy(
        kernel,
        [((length, D), jnp.bfloat16), ((3, D), jnp.float32)]
        + [((length, D // 4), jnp.bfloat16)] * 4,
        weight_scratch(D, 3 * D, 3) + [pltpu.VMEM((length, D), jnp.float32)],
        weight,
        (delta_mixed, delta_one, stream_zero, gain),
    )


def joined_backward(zero_low, weight):
    length = zero_low.shape[0]
    width = 2 * D // 8

    def kernel(*refs):
        zero_ref, first_ref, second_ref, full, sems = refs[6:]
        Fetch(refs[:6], full, sems).wait()
        for parity in range(2):
            delta = dot_rows(zero_ref[...], full[parity * D : (parity + 1) * D])
            delta = delta.astype(jnp.bfloat16)
            for number in range(4):
                target = (first_ref, second_ref)[number // 2]
                column = (2 * (number % 2) + parity) * width
                target[:, column : column + width] = delta[:, number * width : (number + 1) * width]

    out = ((length, D), jnp.bfloat16)
    return heavy(kernel, [out, out], weight_scratch(2 * D, D), weight, (zero_low,))


def shrink_forward(active, weight, stream_one, bias):
    length = active.shape[0]
    width = D // 8

    def kernel(*refs):
        active_ref, stream_ref, bias_ref, out_ref, full, sems = refs[6:]
        Fetch(refs[:6], full, sems).wait()
        total = (
            stream_ref[...] + product(active_ref[...], full[...]) + bias_ref[...]
        ).astype(jnp.bfloat16)
        for parity in range(2):
            for number in range(4):
                column = (2 * number + parity) * width
                source = (4 * parity + number) * width
                out_ref[:, column : column + width] = total[:, source : source + width]

    return heavy(
        kernel,
        [((length, D), jnp.bfloat16)],
        weight_scratch(FF, D),
        weight,
        (active, stream_one, bias),
    )[0]


def on_device(
    inputs,
    skip_tokens,
    cotangent,
    merge_weight,
    merge_moment,
    merge_square,
    attend_weight,
    attend_moment,
    attend_square,
    output_weight,
    output_moment,
    output_square,
    expand_weight,
    expand_moment,
    expand_square,
    shrink_weight,
    shrink_moment,
    shrink_square,
    vectors,
    vector_moment,
    vector_square,
):
    core = spot()[0]
    low = jnp.bfloat16
    columns = attend_weight.shape[1]

    merge_low = fold(merge_weight.astype(low))
    width = merge_low.shape[1]
    count = vectors.shape[0]
    vector_rows = jnp.pad(vectors.astype(low), (0, 16 * width - count)).reshape(16, width)
    merge_low = jnp.concatenate([merge_low, vector_rows], axis=0)
    merge_others = across_narrow(merge_low)
    mixed_low = jnp.concatenate([attend_weight.astype(low), output_weight.astype(low)], axis=1)
    joined = inner(jnp.concatenate([inputs[0], skip_tokens[0]], axis=-1))
    joined_mine, joined_other = halves_of(joined, core)
    pulled = inner(cotangent[0])
    merge_others, mixed_low, joined, joined_mine, joined_other, pulled = together(
        merge_others, mixed_low, joined, joined_mine, joined_other, pulled
    )
    merge_block, vector_parts = arrange("merge", 2, merge_low, merge_others, 16)
    merge_first = gather_first(merge_block)
    mixed_far = swap_narrow(mixed_low, 2)
    mixed_near = swap_narrow(mixed_low, 1)
    expand_low = expand_weight.astype(low)
    known_sibling = swap_wide(jnp.concatenate([joined_other, pulled], axis=1), CORE)
    merge_first, mixed_far, vector_parts, expand_low, known_sibling = together(
        merge_first, mixed_far, vector_parts, expand_low, known_sibling
    )
    joined_sibling, pulled_sibling = known_sibling[:, :D], known_sibling[:, D:]
    merge_second = gather_second(merge_first)
    merge_sides = swap_sides(merge_first)
    mixed_last = swap_narrow(mixed_far, 1)
    shrink_low = fold(shrink_weight.astype(low))
    pieces = unpack(vector_parts.reshape(4, -1)[:, :count].reshape(-1).astype(jnp.float32))
    pieces = tuple(inner(piece)[None] for piece in pieces)
    merge_second, merge_sides, mixed_near, mixed_last, shrink_low, pieces = together(
        merge_second, merge_sides, mixed_near, mixed_last, shrink_low, pieces
    )
    skip_bias, gain_one, bias_one, output_bias, gain_two, bias_two, shrink_bias, expand_bias = pieces
    mixed_block = arrange("attend_output", 1, mixed_low, (mixed_near, mixed_far, mixed_last))[0]
    mixed_first = gather_first(mixed_block)
    expand_far = swap_narrow(expand_low, 2)
    expand_near = swap_narrow(expand_low, 1)
    merge_ends = ends_of(merge_block, merge_second)
    merge_pieces = (merge_ends, *merge_first, swap_wide(merge_ends, CORE), *merge_sides)
    stream_zero, attend_input, attend_up, attend_up_other = merge_forward(
        joined, merge_pieces, skip_bias, gain_one, bias_one
    )
    mixed_first, expand_far, expand_near, stream_zero, attend_input, attend_up_other = together(
        mixed_first, expand_far, expand_near, stream_zero, attend_input, attend_up_other
    )
    mixed_second = gather_second(mixed_first)
    mixed_sides = swap_sides(mixed_first)
    expand_last = swap_narrow(expand_far, 1)
    expand_block = arrange("expand", 1, expand_low, (expand_near, expand_far, expand_last))[0]
    mixed_second, mixed_sides, expand_block = together(mixed_second, mixed_sides, expand_block)
    expand_first = gather_first(expand_block)
    shrink_far = swap_narrow(shrink_low, 2)
    shrink_near = swap_narrow(shrink_low, 1)
    mixed_ends = ends_of(mixed_block, mixed_second)
    mixed_pieces = (mixed_ends, *mixed_first, swap_wide(mixed_ends, CORE), *mixed_sides)
    heads, chances_first, mix_first = attend_first(attend_input, mixed_pieces)
    expand_first, shrink_far, shrink_near, heads, mix_first = together(
        expand_first, shrink_far, shrink_near, heads, mix_first
    )
    expand_second = gather_second(expand_first)
    expand_sides = swap_sides(expand_first)
    shrink_last = swap_narrow(shrink_far, 1)
    chances_second, stream_one, expand_input, ups, ups_other = attend_second(
        heads, mix_first, mixed_pieces, stream_zero, output_bias, gain_two, bias_two
    )
    shrink_block = arrange("shrink", 4, shrink_low, (shrink_near, shrink_far, shrink_last))[0]
    (
        expand_second,
        expand_sides,
        shrink_block,
        expand_input,
        ups_other,
        joined_mine,
        joined_sibling,
    ) = together(
        expand_second,
        expand_sides,
        shrink_block,
        expand_input,
        ups_other,
        joined_mine,
        joined_sibling,
    )
    shrink_first = gather_first(shrink_block)
    expand_ends = ends_of(expand_block, expand_second)
    expand_pieces = (expand_ends, *expand_first, swap_wide(expand_ends, CORE), *expand_sides)
    joined_far = swap_narrow(joined_mine, 2)
    joined_near = swap_narrow(joined_mine, 1)
    active, slope, active_up, active_up_other = expand_forward(
        expand_input, expand_pieces, expand_bias
    )
    shrink_first, joined_far, joined_near, active, slope, active_up, active_up_other = together(
        shrink_first, joined_far, joined_near, active, slope, active_up, active_up_other
    )
    shrink_second = gather_second(shrink_first)
    shrink_sides = swap_sides(shrink_first)
    active_up_sibling = swap_wide(active_up_other, CORE)
    shrink_blocks = pair_gradient([(active_up, active_up_sibling, D, 0, FF // 2)], (pulled, pulled_sibling))
    shrink_second, shrink_sides, shrink_blocks, joined_far, joined_sibling, ups_other = together(
        shrink_second, shrink_sides, shrink_blocks, joined_far, joined_sibling, ups_other
    )
    shrink_got = send(shrink_blocks)
    shrink_ends = ends_of(shrink_block, shrink_second)
    shrink_pieces = (shrink_ends, *shrink_first, swap_wide(shrink_ends, CORE), *shrink_sides)
    sibling_far = swap_narrow(joined_sibling, 2)
    joined_last = swap_narrow(joined_far, 1)
    hidden_low, hidden_sum = hidden_backward(pulled, shrink_pieces, slope)
    outputs = shrink_forward(active, shrink_pieces, stream_one, shrink_bias)[None]
    (
        shrink_got,
        sibling_far,
        joined_last,
        hidden_low,
        hidden_sum,
        outputs,
        joined_sibling,
        ups_other,
        attend_up_other,
    ) = together(
        shrink_got,
        sibling_far,
        joined_last,
        hidden_low,
        hidden_sum,
        outputs,
        joined_sibling,
        ups_other,
        attend_up_other,
    )
    shrink_got_last = forward(shrink_blocks, shrink_got)
    hidden_sibling = swap_wide(hidden_low, CORE)
    ups_sibling = swap_wide(ups_other, CORE)
    sibling_near = swap_narrow(joined_sibling, 1)
    half = D // 2
    expand_blocks = pair_gradient(
        [(ups, ups_sibling, FF, 1, half)], (hidden_low, hidden_sibling)
    )
    shrink_got_last, sibling_near, expand_blocks, hidden_low, sibling_far = together(
        shrink_got_last, sibling_near, expand_blocks, hidden_low, sibling_far
    )
    expand_got = send(expand_blocks)
    sibling_last = swap_narrow(sibling_far, 1)
    attend_up_sibling = swap_wide(attend_up_other, CORE)
    delta_one, stream_low, sums_two, delta_mixture = expand_backward(
        hidden_low, expand_pieces, mixed_pieces, pulled, stream_one, gain_two
    )
    delta_mixed = attend_backward(heads, chances_first, chances_second, delta_mixture, stream_low)
    expand_got, sibling_last, delta_mixed, attend_up_sibling = together(
        expand_got, sibling_last, delta_mixed, attend_up_sibling
    )
    expand_got_last = forward(expand_blocks, expand_got)
    mixed_sibling = swap_wide(delta_mixed, CORE)
    shrink_quarters = unarrange("shrink", 4, shrink_blocks, shrink_got, shrink_got_last)
    shrink_narrow = narrow_first(shrink_quarters)
    mixed_blocks = pair_gradient(
        [(attend_up, attend_up_sibling, 3 * D, 0, half), (ups, ups_sibling, D, 0, half)],
        (delta_mixed, mixed_sibling),
    )
    expand_got_last, shrink_narrow, mixed_blocks, delta_mixed = together(
        expand_got_last, shrink_narrow, mixed_blocks, delta_mixed
    )
    mixed_got = send(mixed_blocks)
    expand_quarters = unarrange("expand", 1, expand_blocks, expand_got, expand_got_last)
    expand_narrow = narrow_first(expand_quarters)
    shrink_end = narrow_second(shrink_quarters, shrink_narrow)
    zero_low, sums_one, *zero_quarters = entry_backward(
        delta_mixed, mixed_pieces, delta_one, stream_zero, gain_one
    )
    mixed_got, expand_narrow, zero_low, sums_one, zero_quarters, shrink_end = together(
        mixed_got, expand_narrow, zero_low, sums_one, zero_quarters, shrink_end
    )
    mixed_got_last = forward(mixed_blocks, mixed_got)
    zero_got = tuple(swap_narrow(zero_quarters[bit], bit) for bit in (1, 2, 3))
    input_gradient, skip_gradient = joined_backward(zero_low, merge_pieces)
    vector_total = jnp.concatenate(
        [
            outer(row)
            for row in (
                sums_one[0],
                sums_one[1],
                sums_one[2],
                sums_two[0],
                sums_two[1],
                sums_two[2],
                sums_two[3],
                hidden_sum[0],
            )
        ]
    )
    vector_total = vector_total + swap_wide(vector_total, CORE)
    mixed_got_last, zero_got, vector_total, input_gradient, skip_gradient, shrink_end = together(
        mixed_got_last, zero_got, vector_total, input_gradient, skip_gradient, shrink_end
    )
    mixed_quarters = unarrange("attend_output", 1, mixed_blocks, mixed_got, mixed_got_last)
    mixed_narrow = narrow_first(mixed_quarters)
    expand_end = narrow_second(expand_quarters, expand_narrow)
    zero_line = jnp.stack([zero_quarters[0], *zero_got])
    zero_line_sibling = swap_wide(zero_line, CORE)
    merge_blocks = line_gradient(
        (
            joined_mine,
            joined_near,
            joined_far,
            joined_last,
            joined_sibling,
            sibling_near,
            sibling_far,
            sibling_last,
        ),
        zero_line,
        zero_line_sibling,
    )
    vector_total = vector_total + swap_wide(vector_total, ACROSS)
    mixed_narrow, merge_blocks, vector_total, shrink_end, expand_end = together(
        mixed_narrow, merge_blocks, vector_total, shrink_end, expand_end
    )
    vector_total = vector_total + swap_wide(vector_total, ALONG)
    mixed_end = narrow_second(mixed_quarters, mixed_narrow)
    merge_got = (
        swap_wide(merge_blocks[1], ACROSS),
        swap_wide(merge_blocks[2], ALONG),
        swap_wide(merge_blocks[3], ACROSS + ALONG),
    )
    shrink_new = turned_update(
        shrink_weight,
        shrink_moment,
        shrink_square,
        (shrink_quarters[KEEP_NEAR], shrink_narrow[1], shrink_end),
        4,
        rate_shrink,
    )
    expand_new = adamw_update(
        expand_weight,
        expand_moment,
        expand_square,
        finish(expand_quarters, expand_narrow, expand_end),
        rate_expand,
    )
    merge_sum = sum(term.astype(jnp.float32) for term in (merge_blocks[0], *merge_got))
    merge_new = adamw_update(
        merge_weight,
        merge_moment,
        merge_square,
        unfold(merge_sum, merge_weight.shape[0]),
        rate_merge,
    )
    merge_new, mixed_end, vector_total, shrink_new, expand_new = together(
        merge_new, mixed_end, vector_total, shrink_new, expand_new
    )
    vector_parts = vector_total.reshape(4, -1)
    narrow = lax.axis_index("narrow")
    vector_total = pick(vector_parts, narrow)
    for bit in (1, 2, 3):
        vector_total = vector_total + swap_narrow(pick(vector_parts, narrow ^ bit), bit)
    mixed_total = finish(mixed_quarters, mixed_narrow, mixed_end)
    attend_new = adamw_update(
        attend_weight, attend_moment, attend_square, mixed_total[:, :columns], rate_attend
    )
    output_new = adamw_update(
        output_weight, output_moment, output_square, mixed_total[:, columns:], rate_output
    )
    vector_new = adamw_update(vectors, vector_moment, vector_square, vector_total, rate_vector)
    return (
        outputs,
        input_gradient[None],
        skip_gradient[None],
        *merge_new,
        *attend_new,
        *output_new,
        *expand_new,
        *shrink_new,
        *vector_new,
    )


def solution(mesh):
    in_specs = (
        P(("wide", "narrow"), None, None),
        P(("wide", "narrow"), None, None),
        P(("wide", "narrow"), None, None),
        P("wide", "narrow"),
        P("wide", "narrow"),
        P("wide", "narrow"),
        P("wide", "narrow"),
        P("wide", "narrow"),
        P("wide", "narrow"),
        P("wide", "narrow"),
        P("wide", "narrow"),
        P("wide", "narrow"),
        P("wide", "narrow"),
        P("wide", "narrow"),
        P("wide", "narrow"),
        P("wide", "narrow"),
        P("wide", "narrow"),
        P("wide", "narrow"),
        P("narrow"),
        P("narrow"),
        P("narrow"),
    )
    out_specs = (
        P(("wide", "narrow"), None, None),
        P(("wide", "narrow"), None, None),
        P(("wide", "narrow"), None, None),
        P("wide", "narrow"),
        P("wide", "narrow"),
        P("wide", "narrow"),
        P("wide", "narrow"),
        P("wide", "narrow"),
        P("wide", "narrow"),
        P("wide", "narrow"),
        P("wide", "narrow"),
        P("wide", "narrow"),
        P("wide", "narrow"),
        P("wide", "narrow"),
        P("wide", "narrow"),
        P("wide", "narrow"),
        P("wide", "narrow"),
        P("wide", "narrow"),
        P("narrow"),
        P("narrow"),
        P("narrow"),
    )
    tuned = mesh.shape["wide"] == 8 and mesh.shape["narrow"] == 4
    return jax.shard_map(
        on_device if tuned else general_device, mesh=mesh, in_specs=in_specs, out_specs=out_specs, check_vma=False
    )
```

```python
import jax
import jax.numpy as jnp
from jax import lax
from jax.experimental import pallas as pl
from jax.experimental.pallas import tpu as pltpu
from jax.sharding import PartitionSpec as P

D = 1152
FF = 4608
H = 16
HD = 72
STEP = 5


norm_epsilon = 1e-05
adam_epsilon = 1e-08
beta_moment = 0.5
weight_decay = 0.01
rate_merge = 0.04
rate_attend = 0.08
rate_output = 0.6
rate_expand = 0.06
rate_shrink = 0.03
rate_vector = 0.6


def product(left_side, right_side):
    return jnp.dot(left_side, right_side, preferred_element_type=jnp.float32)


def transposed(gradient, matrix):
    return lax.dot_general(
        gradient,
        matrix,
        (((gradient.ndim - 1,), (1,)), ((), ())),
        preferred_element_type=jnp.float32,
    )


def weight_gradient(activations, gradient):
    flat_left = activations.reshape(-1, activations.shape[-1])
    flat_right = gradient.reshape(-1, gradient.shape[-1])
    return lax.dot_general(
        flat_left, flat_right, (((0,), (0,)), ((), ())), preferred_element_type=jnp.float32
    )


def normalize(values):
    centered = values - jnp.mean(values, axis=-1, keepdims=True)
    spread = jnp.mean(centered * centered, axis=-1, keepdims=True)
    inverse = lax.rsqrt(spread + norm_epsilon)
    return (centered * inverse, inverse)


def norm_back(gradient, normed, inverse):
    return inverse * (
        gradient
        - jnp.mean(gradient, axis=-1, keepdims=True)
        - normed * jnp.mean(gradient * normed, axis=-1, keepdims=True)
    )


def row_sum(values):
    return jnp.sum(values, axis=(0, 1))


def unpack(packed):
    return tuple((packed[position * D : (position + 1) * D] for position in range(7))) + (
        packed[7 * D : 7 * D + FF],
    )


def gaussian_unit(values):
    return jax.nn.gelu(values, approximate=False)


def adamw_update(weight, moment, square, gradient, step_rate):
    moment_new = beta_moment * moment + (1.0 - beta_moment) * gradient
    square_new = beta_moment * square + (1.0 - beta_moment) * gradient * gradient
    correct = 1.0 - beta_moment**STEP
    direction = moment_new / correct / (jnp.sqrt(square_new / correct) + adam_epsilon)
    return (weight - step_rate * (direction + weight_decay * weight), moment_new, square_new)


def general_device(
    inputs,
    skip_tokens,
    cotangent,
    merge_weight,
    merge_moment,
    merge_square,
    attend_weight,
    attend_moment,
    attend_square,
    output_weight,
    output_moment,
    output_square,
    expand_weight,
    expand_moment,
    expand_square,
    shrink_weight,
    shrink_moment,
    shrink_square,
    vectors,
    vector_moment,
    vector_square,
):
    merge_low = merge_weight.astype(jnp.bfloat16)
    attend_low = attend_weight.astype(jnp.bfloat16)
    output_low = output_weight.astype(jnp.bfloat16)
    expand_low = expand_weight.astype(jnp.bfloat16)
    shrink_low = shrink_weight.astype(jnp.bfloat16)
    vector_low = vectors.astype(jnp.bfloat16)
    columns = (
        lax.all_gather(merge_low, "narrow", axis=1, tiled=True),
        lax.all_gather(attend_low, "narrow", axis=1, tiled=True),
        lax.all_gather(output_low, "narrow", axis=1, tiled=True),
        lax.all_gather(expand_low, "narrow", axis=1, tiled=True),
        lax.all_gather(shrink_low, "narrow", axis=1, tiled=True),
        lax.all_gather(vector_low, "narrow", axis=0, tiled=True),
    )
    matrices = (
        lax.all_gather(columns[0], "wide", axis=0, tiled=True),
        lax.all_gather(columns[1], "wide", axis=0, tiled=True),
        lax.all_gather(columns[2], "wide", axis=0, tiled=True),
        lax.all_gather(columns[3], "wide", axis=0, tiled=True),
        lax.all_gather(columns[4], "wide", axis=0, tiled=True),
    )
    skip_bias, gain_one, bias_one, output_bias, gain_two, bias_two, shrink_bias, expand_bias = (
        unpack(columns[5].astype(jnp.float32))
    )
    images = inputs.shape[0]
    length = inputs.shape[1]
    softmax_scale = HD ** (-0.5)
    joined = jnp.concatenate([inputs, skip_tokens], axis=-1)
    stream_zero = product(joined, matrices[0]) + skip_bias
    normed_one, inverse_one = normalize(stream_zero)
    attend_input = (normed_one * gain_one + bias_one).astype(jnp.bfloat16)
    mixed_heads = product(attend_input, matrices[1]).astype(jnp.bfloat16)
    query_heads = mixed_heads[..., 0:D].reshape(images, length, H, HD)
    key_heads = mixed_heads[..., D : 2 * D].reshape(images, length, H, HD)
    value_heads = mixed_heads[..., 2 * D : 3 * D].reshape(images, length, H, HD)
    logits = (
        jnp.einsum("blhe,bmhe->bhlm", query_heads, key_heads, preferred_element_type=jnp.float32)
        * softmax_scale
    )
    maxima = jnp.max(logits, axis=-1, keepdims=True)
    log_total = maxima + jnp.log(jnp.sum(jnp.exp(logits - maxima), axis=-1, keepdims=True))
    softmax_low = jnp.exp(logits - log_total).astype(jnp.bfloat16)
    mixture = jnp.einsum(
        "bhlm,bmhe->blhe", softmax_low, value_heads, preferred_element_type=jnp.float32
    )
    mixture = mixture.astype(jnp.bfloat16).reshape(images, length, D)
    stream_one = stream_zero + product(mixture, matrices[2]) + output_bias
    normed_two, inverse_two = normalize(stream_one)
    expand_input = (normed_two * gain_two + bias_two).astype(jnp.bfloat16)
    hidden = product(expand_input, matrices[3]) + expand_bias
    active, pullback = jax.vjp(gaussian_unit, hidden)
    active_low = active.astype(jnp.bfloat16)
    outputs = (stream_one + product(active_low, matrices[4]) + shrink_bias).astype(jnp.bfloat16)
    columns_back = (
        lax.all_gather(merge_low, "narrow", axis=1, tiled=True),
        lax.all_gather(attend_low, "narrow", axis=1, tiled=True),
        lax.all_gather(output_low, "narrow", axis=1, tiled=True),
        lax.all_gather(expand_low, "narrow", axis=1, tiled=True),
        lax.all_gather(shrink_low, "narrow", axis=1, tiled=True),
        lax.all_gather(vector_low, "narrow", axis=0, tiled=True),
    )
    matrices_back = (
        lax.all_gather(columns_back[0], "wide", axis=0, tiled=True),
        lax.all_gather(columns_back[1], "wide", axis=0, tiled=True),
        lax.all_gather(columns_back[2], "wide", axis=0, tiled=True),
        lax.all_gather(columns_back[3], "wide", axis=0, tiled=True),
        lax.all_gather(columns_back[4], "wide", axis=0, tiled=True),
    )
    packed_back = columns_back[5].astype(jnp.float32)
    unpacked = unpack(packed_back)
    gain_first = unpacked[1]
    gain_second = unpacked[4]
    upstream = cotangent.astype(jnp.float32)
    shrink_gradient = weight_gradient(active_low, cotangent)
    delta_active = transposed(cotangent, matrices_back[4])
    delta_hidden = pullback(delta_active)[0]
    hidden_low = delta_hidden.astype(jnp.bfloat16)
    expand_gradient = weight_gradient(expand_input, hidden_low)
    delta_expand = transposed(hidden_low, matrices_back[3])
    delta_one = upstream + norm_back(delta_expand * gain_second, normed_two, inverse_two)
    stream_low = delta_one.astype(jnp.bfloat16)
    output_gradient = weight_gradient(mixture, stream_low)
    delta_mixture = (
        transposed(stream_low, matrices_back[2]).astype(jnp.bfloat16).reshape(images, length, H, HD)
    )
    logits_again = (
        jnp.einsum("blhe,bmhe->bhlm", query_heads, key_heads, preferred_element_type=jnp.float32)
        * softmax_scale
    )
    softmax_again = jnp.exp(logits_again - log_total)
    delta_softmax = jnp.einsum(
        "blhe,bmhe->bhlm", delta_mixture, value_heads, preferred_element_type=jnp.float32
    )
    delta_values = jnp.einsum(
        "bhlm,blhe->bmhe",
        softmax_again.astype(jnp.bfloat16),
        delta_mixture,
        preferred_element_type=jnp.float32,
    )
    delta_logits = softmax_again * (
        delta_softmax - jnp.sum(softmax_again * delta_softmax, axis=-1, keepdims=True)
    )
    delta_scores = (softmax_scale * delta_logits).astype(jnp.bfloat16)
    delta_queries = jnp.einsum(
        "bhlm,bmhe->blhe", delta_scores, key_heads, preferred_element_type=jnp.float32
    )
    delta_keys = jnp.einsum(
        "bhlm,blhe->bmhe", delta_scores, query_heads, preferred_element_type=jnp.float32
    )
    delta_mixed = jnp.concatenate(
        [
            delta_queries.reshape(images, length, D),
            delta_keys.reshape(images, length, D),
            delta_values.reshape(images, length, D),
        ],
        axis=-1,
    ).astype(jnp.bfloat16)
    attend_gradient = weight_gradient(attend_input, delta_mixed)
    delta_attend = transposed(delta_mixed, matrices_back[1])
    delta_zero = delta_one + norm_back(delta_attend * gain_first, normed_one, inverse_one)
    zero_low = delta_zero.astype(jnp.bfloat16)
    merge_gradient = weight_gradient(joined, zero_low)
    delta_joined = transposed(zero_low, matrices_back[0])
    input_gradient = delta_joined[..., 0:D].astype(jnp.bfloat16)
    skip_gradient = delta_joined[..., D : 2 * D].astype(jnp.bfloat16)
    vector_gradient = jnp.concatenate(
        [
            row_sum(delta_zero),
            row_sum(delta_attend * normed_one),
            row_sum(delta_attend),
            row_sum(delta_one),
            row_sum(delta_expand * normed_two),
            row_sum(delta_expand),
            row_sum(upstream),
            row_sum(delta_hidden),
        ]
    )
    owned_rows = (
        lax.psum_scatter(merge_gradient, "wide", scatter_dimension=0, tiled=True),
        lax.psum_scatter(attend_gradient, "wide", scatter_dimension=0, tiled=True),
        lax.psum_scatter(output_gradient, "wide", scatter_dimension=0, tiled=True),
        lax.psum_scatter(expand_gradient, "wide", scatter_dimension=0, tiled=True),
        lax.psum_scatter(shrink_gradient, "wide", scatter_dimension=0, tiled=True),
    )
    vector_total = lax.psum(vector_gradient, "wide")
    parted = (
        lax.psum_scatter(owned_rows[0], "narrow", scatter_dimension=1, tiled=True),
        lax.psum_scatter(owned_rows[1], "narrow", scatter_dimension=1, tiled=True),
        lax.psum_scatter(owned_rows[2], "narrow", scatter_dimension=1, tiled=True),
        lax.psum_scatter(owned_rows[3], "narrow", scatter_dimension=1, tiled=True),
        lax.psum_scatter(owned_rows[4], "narrow", scatter_dimension=1, tiled=True),
        lax.psum_scatter(vector_total, "narrow", scatter_dimension=0, tiled=True),
    )
    merge_new = adamw_update(merge_weight, merge_moment, merge_square, parted[0], rate_merge)
    attend_new = adamw_update(attend_weight, attend_moment, attend_square, parted[1], rate_attend)
    output_new = adamw_update(output_weight, output_moment, output_square, parted[2], rate_output)
    expand_new = adamw_update(expand_weight, expand_moment, expand_square, parted[3], rate_expand)
    shrink_new = adamw_update(shrink_weight, shrink_moment, shrink_square, parted[4], rate_shrink)
    vector_new = adamw_update(vectors, vector_moment, vector_square, parted[5], rate_vector)
    return (
        outputs,
        input_gradient,
        skip_gradient,
        merge_new[0],
        merge_new[1],
        merge_new[2],
        attend_new[0],
        attend_new[1],
        attend_new[2],
        output_new[0],
        output_new[1],
        output_new[2],
        expand_new[0],
        expand_new[1],
        expand_new[2],
        shrink_new[0],
        shrink_new[1],
        shrink_new[2],
        vector_new[0],
        vector_new[1],
        vector_new[2],
    )


CORE = 1
ACROSS = 2
ALONG = 4
PAD = 384
VECTOR_ROWS = 11
VMEM_BYTES = 56 * 1024 * 1024
LIGHT = pl.CostEstimate(flops=0, bytes_accessed=1024, transcendentals=0)
PARAMS = pltpu.CompilerParams(vmem_limit_bytes=VMEM_BYTES)


def swap_wide(value, bit):
    return lax.ppermute(value, "wide", [(i, i ^ bit) for i in range(8)])


def swap_narrow(value, bit):
    return lax.ppermute(value, "narrow", [(i, i ^ bit) for i in range(4)])


def together(*values):
    return lax.optimization_barrier(values)


def spot():
    wide = lax.axis_index("wide")
    narrow = lax.axis_index("narrow")
    return (wide & 1, (wide >> 1) & 1, (wide >> 2) & 1, narrow & 1, narrow >> 1)


def split_shapes(rows, columns):
    if columns == FF:
        return (rows, columns // 2), True
    return (rows // 2, columns), False


def split_block(value):
    shape, by_columns = split_shapes(*value.shape[-2:])
    if by_columns:
        return value[..., : shape[1]], value[..., shape[1] :]
    return value[..., : shape[0], :], value[..., shape[0] :, :]


def column_blocks(kind, quarter):
    if kind == "attend_output":
        width = quarter // 8
        order = [8 * part + 2 * n + p for part in range(3) for p in range(2) for n in range(4)]
        blocks = [(block // 6, (block % 6) * width) for block in order]
        return width, blocks + [(n, (6 + p) * width) for p in range(2) for n in range(4)]
    width = quarter // 2
    return width, [(n, p * width) for p in range(2) for n in range(4)]


def fold(shard):
    parts = max(1, shard.shape[0] // (D // 8))
    height = shard.shape[0] // parts
    return jnp.concatenate(
        [shard[part * height : (part + 1) * height] for part in range(parts)], axis=1
    )


def unfold(value, rows):
    parts = rows // value.shape[0]
    quarter = value.shape[1] // parts
    return jnp.concatenate(
        [value[:, part * quarter : (part + 1) * quarter] for part in range(parts)], axis=0
    )


def arrange(kind, parts, shard, others, extra=0):
    height = shard.shape[0] - extra
    rows, quarter = parts * height, shard.shape[1] // parts
    width, blocks = column_blocks(kind, quarter)

    def kernel(*refs):
        full, apart, held = refs[4], refs[5], refs[-1]
        narrow = lax.axis_index("narrow")
        for relative in range(4):
            held[relative] = refs[relative][...]
        for number in range(4):
            value = held[narrow ^ number]
            if extra:
                apart[number] = value[height:]
            for position, (owner, offset) in enumerate(blocks):
                if owner == number:
                    column = slice(position * width, (position + 1) * width)
                    for part in range(parts):
                        start = part * quarter + offset
                        full[part * height : (part + 1) * height, column] = value[
                            :height, start : start + width
                        ]

    outs = [jax.ShapeDtypeStruct((rows, 4 * quarter), jnp.bfloat16)]
    if extra:
        outs.append(jax.ShapeDtypeStruct((4, extra, shard.shape[1]), jnp.bfloat16))
    return pl.pallas_call(
        kernel,
        out_shape=tuple(outs),
        scratch_shapes=[pltpu.VMEM((4,) + shard.shape, jnp.bfloat16)],
        compiler_params=PARAMS,
        cost_estimate=LIGHT,
    )(shard, *others)


def weight_scratch(rows, columns, chunks=1):
    return [pltpu.VMEM((rows, columns), jnp.bfloat16), pltpu.SemaphoreType.DMA((chunks, 8))]


class Fetch:
    def __init__(self, refs, full, sems, first=0):
        wide = lax.axis_index("wide")
        core, chip = wide & 1, wide >> 1
        rows = full.shape[0] // 8
        chunks = sems.shape[0]
        width = full.shape[1] // chunks
        self.copies = []
        for chunk in range(chunks):
            group = []
            for number, (ends, from_x, from_y) in enumerate((refs[:3], refs[3:])):
                parity = core if number == 0 else 1 - core
                own, far = ends.at[pl.ds(0, rows)], ends.at[pl.ds(rows, rows)]
                for relative, piece in enumerate((own, from_x, from_y, far)):
                    start = pl.multiple_of((4 * parity + (chip ^ relative)) * rows, 16)
                    group.append(
                        pltpu.make_async_copy(
                            piece.at[:, pl.ds(first + chunk * width, width)],
                            full.at[pl.ds(start, rows), pl.ds(chunk * width, width)],
                            sems.at[chunk, 4 * number + relative],
                        )
                    )
            self.copies.append(group)
        for group in self.copies:
            for copy in group:
                copy.start()

    def wait(self, chunk=0):
        for copy in self.copies[chunk]:
            copy.wait()


def pair_gradient(lefts, right):
    height = lefts[0][4]
    rows = height // 4
    tokens, columns = right[0].shape
    tile = 384 if height > 576 else 1152
    count = len(lefts)
    ends = [sum(left[2] for left in lefts[: number + 1]) // tile for number in range(count)]
    starts = [0] + ends[:-1]

    def kernel(*refs):
        left_refs = refs[: 2 * count]
        right_ref, sibling_ref = refs[2 * count : 2 * count + 2]
        outs = refs[2 * count + 2 : 2 * count + 6]
        joint, beside, total = refs[2 * count + 6 :]
        step = pl.program_id(0)

        @pl.when(step == 0)
        def _():
            joint[...] = jnp.zeros_like(joint)

        for number in range(count):

            @pl.when(step == starts[number])
            def _():
                beside[:, :PAD] = left_refs[2 * number][...]
                beside[:, PAD:] = left_refs[2 * number + 1][...]

        joint[:tokens] = right_ref[...]
        joint[PAD : PAD + tokens] = sibling_ref[...]
        total[...] = jnp.dot(
            beside[...], joint[...], preferred_element_type=jnp.float32
        ).astype(jnp.bfloat16)
        by_columns = split_shapes(rows, columns)[1]
        part_blocks(total, rows, outs, step < columns // tile // 2 if by_columns else None)

    whole = lambda place: pl.BlockSpec((height, PAD), lambda i: (place, 0))
    part = lambda size: pl.BlockSpec((size, tile), lambda i: (0, i))
    shape, by_columns = split_shapes(rows, columns)
    half = columns // tile // 2
    if by_columns:
        top = pl.BlockSpec((2, rows, tile), lambda i: (0, 0, jnp.minimum(i, half - 1)))
        bottom = pl.BlockSpec((2, rows, tile), lambda i: (0, 0, jnp.maximum(i - half, 0)))
    else:
        top = bottom = pl.BlockSpec((2, shape[0], tile), lambda i: (0, 0, i))
    outs = pl.pallas_call(
        kernel,
        grid=(columns // tile,),
        in_specs=[whole(left[3]) for left in lefts for _ in range(2)] + [part(tokens)] * 2,
        out_specs=(top, top, bottom, bottom),
        out_shape=block_shapes(rows, columns),
        scratch_shapes=[
            pltpu.VMEM((2 * PAD, tile), jnp.bfloat16),
            pltpu.VMEM((height, 2 * PAD), jnp.bfloat16),
            pltpu.VMEM((height, tile), jnp.bfloat16),
        ],
        compiler_params=PARAMS,
        cost_estimate=LIGHT,
    )(*[left for pair_of in lefts for left in pair_of[:2]], *right)
    return outs


def block_shapes(rows, columns):
    shape = split_shapes(rows, columns)[0]
    return (jax.ShapeDtypeStruct((2,) + shape, jnp.bfloat16),) * 4


def part_blocks(total, rows, outs, first_half):
    wide = lax.axis_index("wide")
    across, along = (wide >> 1) & 1, (wide >> 2) & 1
    half = rows // 2
    for kept_x in range(2):
        for kept_y in range(2):
            x = across if kept_x else 1 - across
            y = along if kept_y else 1 - along
            start = pl.multiple_of((2 * y + x) * rows, 16)
            top, bottom = outs[1 - kept_x], outs[3 - kept_y]
            if first_half is None:
                top[1 - kept_y] = total[pl.ds(start, half)]
                bottom[1 - kept_x] = total[pl.ds(pl.multiple_of(start + half, 16), half)]
                continue

            @pl.when(first_half)
            def _():
                top[1 - kept_y] = total[pl.ds(start, rows)]

            @pl.when(jnp.logical_not(first_half))
            def _():
                bottom[1 - kept_x] = total[pl.ds(start, rows)]


def unarrange(kind, parts, blocks, got, got_last):
    by_columns = got_last[0].shape[1] == FF // 2
    part_rows, part_columns = got_last[0].shape
    rows = part_rows if by_columns else 2 * part_rows
    columns = 2 * part_columns if by_columns else part_columns
    quarter = columns // 4
    height = rows // parts
    width, column_parts = column_blocks(kind, quarter)

    def kernel(*refs):
        tops, bottoms = refs[:3], refs[3:6]
        outs, held = refs[6:10], refs[10]
        narrow = lax.axis_index("narrow")
        low_bit, high_bit = narrow & 1, narrow >> 1
        top = add_low(tops[0][...], tops[1][...], tops[2][...])
        bottom = add_low(bottoms[0][...], bottoms[1][...], bottoms[2][...])
        if by_columns:
            held[:, :part_columns] = top
            held[:, part_columns:] = bottom
        else:
            held[:part_rows] = top
            held[part_rows:] = bottom
        for owner in range(4):
            for which in range(4):
                low_same, high_same = 1 - which // 2, 1 - which % 2

                @pl.when(
                    ((low_bit == (owner & 1)) == (low_same == 1))
                    & ((high_bit == (owner >> 1)) == (high_same == 1))
                )
                def _():
                    for position, (quarter_of, offset) in enumerate(column_parts):
                        if quarter_of == owner:
                            piece = held[:, position * width : (position + 1) * width]
                            for part in range(parts):
                                start = part * quarter + offset
                                outs[which][:, start : start + width] = piece[
                                    part * height : (part + 1) * height
                                ]

    near = pl.BlockSpec((None, part_rows, part_columns), lambda i: (0, 0, 0))
    full = lambda size, width: pl.BlockSpec((size, width), lambda i: (0, 0))
    shape = jax.ShapeDtypeStruct((height, parts * quarter), jnp.bfloat16)
    return pl.pallas_call(
        kernel,
        grid=(1,),
        in_specs=[near, near, full(part_rows, part_columns)] * 2,
        out_specs=(full(height, parts * quarter),) * 4,
        out_shape=(shape,) * 4,
        scratch_shapes=[pltpu.VMEM((rows, columns), jnp.bfloat16)],
        compiler_params=PARAMS,
        cost_estimate=LIGHT,
    )(blocks[0], got[0], got_last[0], blocks[2], got[1], got_last[1])


def add_low(*terms):
    return sum(term.astype(jnp.float32) for term in terms).astype(jnp.bfloat16)


def pick(value, index, dim=0):
    return lax.dynamic_index_in_dim(value, index, dim, keepdims=False)


def halves_of(value, core):
    middle = value.shape[-1] // 2
    first, second = value[..., :middle], value[..., middle:]
    return jnp.where(core == 0, first, second), jnp.where(core == 0, second, first)


def inner(value):
    width = value.shape[-1] // 8
    return jnp.concatenate(
        [
            value[..., (2 * n + p) * width : (2 * n + p + 1) * width]
            for p in range(2)
            for n in range(4)
        ],
        axis=-1,
    )


def outer(value):
    width = value.shape[-1] // 8
    return jnp.concatenate(
        [
            value[..., (4 * p + n) * width : (4 * p + n + 1) * width]
            for n in range(4)
            for p in range(2)
        ],
        axis=-1,
    )


def upright(value):
    return jnp.pad(value, ((0, PAD - value.shape[0]), (0, 0))).T


KEEP_NEAR, KEEP_FAR, SEND_NEAR, SEND_FAR = range(4)


def send(blocks):
    return swap_wide(blocks[1], ACROSS), swap_wide(blocks[3], ALONG)


def forward(blocks, got):
    return (
        swap_wide(add_low(blocks[0][1], got[0][1]), ALONG),
        swap_wide(add_low(blocks[2][1], got[1][1]), ACROSS),
    )


def narrow_first(quarters):
    return swap_narrow(quarters[SEND_FAR], 1), swap_narrow(quarters[SEND_NEAR], 1)


def narrow_second(quarters, got):
    return swap_narrow(add_low(quarters[KEEP_FAR], got[0]), 2)


def finish(quarters, got, got_last):
    return (
        quarters[KEEP_NEAR].astype(jnp.float32)
        + got[1].astype(jnp.float32)
        + got_last.astype(jnp.float32)
    )


def across_narrow(shard):
    return tuple(swap_narrow(shard, bit) for bit in (1, 2, 3))


def gather_first(block):
    return swap_wide(block, ACROSS), swap_wide(block, ALONG)


def gather_second(first):
    return (
        swap_wide(split_block(first[0])[0], ALONG),
        swap_wide(split_block(first[1])[1], ACROSS),
    )


def swap_sides(first):
    return swap_wide(first[0], CORE), swap_wide(first[1], CORE)


def ends_of(block, second):
    if split_shapes(*block.shape)[1]:
        return jnp.concatenate([block, jnp.concatenate(second, axis=1)], axis=0)
    return jnp.stack([block, jnp.concatenate(second, axis=0)]).reshape(-1, block.shape[1])


def line_gradient(lefts, rights, rights_sibling):
    tokens, height = lefts[0].shape
    width = rights.shape[2]
    rows = height // 4

    def kernel(*refs):
        right_ref, sibling_ref = refs[8:10]
        outs, total = refs[10:14], refs[14]
        chip = lax.axis_index("wide") >> 1
        for number in range(8):
            right = (right_ref, sibling_ref)[number // 4][number % 4, :tokens]
            part = lax.dot_general(
                right,
                refs[number][...],
                (((0,), (0,)), ((), ())),
                preferred_element_type=jnp.float32,
            )
            total[...] = part if number == 0 else total[...] + part
        sums = sum(
            ref[number, tokens:].astype(jnp.float32)
            for ref in (right_ref, sibling_ref)
            for number in range(4)
        )
        for ref in outs:
            for row in range(VECTOR_ROWS):
                ref[rows // 2 + row // 2, (row % 2) * width : (row % 2 + 1) * width] = sums[
                    row
                ].astype(jnp.bfloat16)
        for owner in range(4):
            block = total[:, owner * rows : (owner + 1) * rows].T.astype(jnp.bfloat16)
            for relative in range(4):

                @pl.when((chip ^ relative) == owner)
                def _():
                    outs[relative][: rows // 2, :width] = block[: rows // 2]
                    outs[relative][: rows // 2, width:] = block[rows // 2 :]

    shape = jax.ShapeDtypeStruct((rows // 2 + 16, 2 * width), jnp.bfloat16)
    return pl.pallas_call(
        kernel,
        out_shape=(shape,) * 4,
        scratch_shapes=[pltpu.VMEM((width, height), jnp.float32)],
        compiler_params=PARAMS,
        cost_estimate=LIGHT,
    )(*lefts, rights, rights_sibling)


def turned_update(weight, moment, square, terms, parts, step_rate):
    rows, quarter = weight.shape
    height = rows // parts

    def kernel(*refs):
        weight_ref, moment_ref, square_ref = refs[: 3]
        total = sum(ref[...].astype(jnp.float32) for ref in refs[3 : 3 + len(terms)])
        outs, gradient = refs[3 + len(terms) : 6 + len(terms)], refs[-1]
        for part in range(parts):
            gradient[part * height : (part + 1) * height] = total[
                :, part * quarter : (part + 1) * quarter
            ]
        new = adamw_update(
            weight_ref[...], moment_ref[...], square_ref[...], gradient[...].T, step_rate
        )
        for out, value in zip(outs, new):
            out[...] = value

    new = pl.pallas_call(
        kernel,
        out_shape=(jax.ShapeDtypeStruct((quarter, rows), jnp.float32),) * 3,
        scratch_shapes=[pltpu.VMEM((rows, quarter), jnp.float32)],
        compiler_params=PARAMS,
        cost_estimate=LIGHT,
    )(weight.T, moment.T, square.T, *terms)
    return tuple(value.T for value in new)


def heavy(kernel, outs, scratch, weights, operands):
    return pl.pallas_call(
        kernel,
        in_specs=[pl.BlockSpec(memory_space=pl.ANY)] * len(weights)
        + [pl.BlockSpec(memory_space=pltpu.VMEM)] * len(operands),
        out_shape=tuple(jax.ShapeDtypeStruct(shape, dtype) for shape, dtype in outs),
        scratch_shapes=scratch,
        compiler_params=PARAMS,
        cost_estimate=LIGHT,
    )(*weights, *operands)


def dot_rows(left, right):
    return lax.dot_general(left, right, (((1,), (1,)), ((), ())), preferred_element_type=jnp.float32)


def dot_depth(left, right):
    return lax.dot_general(left, right, (((0,), (0,)), ((), ())), preferred_element_type=jnp.float32)


def store_upright(value, padded, mine, other):
    features = value.shape[1]
    padded[: value.shape[0]] = value
    turned = padded[...].T.astype(jnp.bfloat16)
    core = lax.axis_index("wide") & 1

    @pl.when(core == 0)
    def _():
        mine[...] = turned[: features // 2]
        other[...] = turned[features // 2 :]

    @pl.when(core == 1)
    def _():
        other[...] = turned[: features // 2]
        mine[...] = turned[features // 2 :]


def merge_forward(joined, weight, bias, gain, shift):
    length = joined.shape[0]

    def kernel(*refs):
        joined_ref, bias_ref, gain_ref, shift_ref = refs[6:10]
        stream, entry, up_mine, up_other, full, sems, padded = refs[10:]
        weight_in = Fetch(refs[:6], full, sems)
        padded[...] = jnp.zeros_like(padded)
        weight_in.wait()
        stream[...] = product(joined_ref[...], full[...]) + bias_ref[...]
        normed = normalize(stream[...])[0]
        value = (normed * gain_ref[...] + shift_ref[...]).astype(jnp.bfloat16)
        entry[...] = value
        store_upright(value.astype(jnp.float32), padded, up_mine, up_other)

    return heavy(
        kernel,
        [
            ((length, D), jnp.float32),
            ((length, D), jnp.bfloat16),
            ((D // 2, PAD), jnp.bfloat16),
            ((D // 2, PAD), jnp.bfloat16),
        ],
        weight_scratch(2 * D, D) + [pltpu.VMEM((PAD, D), jnp.float32)],
        weight,
        (joined, bias, gain, shift),
    )


def attend_head(heads, head, chances_ref, slot):
    at = head * HD
    queries = heads[:, at : at + HD]
    keys = heads[:, D + at : D + at + HD]
    values = heads[:, 2 * D + at : 2 * D + at + HD]
    logits = dot_rows(queries, keys) * HD ** (-0.5)
    powers = jnp.exp(logits - jnp.max(logits, axis=-1, keepdims=True))
    chances = powers / jnp.sum(powers, axis=-1, keepdims=True)
    chances_ref[slot] = chances
    return product(chances.astype(jnp.bfloat16), values).astype(jnp.bfloat16)


FIRST = 12


def attend_first(entry, weight):
    length = entry.shape[0]

    def kernel(*refs):
        entry_ref, heads, chances_ref, mix_ref, full, sems = refs[6:]
        weight_in = Fetch(refs[:6], full, sems)
        for part in range(3):
            weight_in.wait(part)
            columns = slice(part * D, (part + 1) * D)
            heads[:, columns] = product(entry_ref[...], full[:, columns]).astype(jnp.bfloat16)
        for head in range(FIRST):
            mix_ref[:, head * HD : (head + 1) * HD] = attend_head(heads, head, chances_ref, head)

    return heavy(
        kernel,
        [
            ((length, 3 * D), jnp.bfloat16),
            ((FIRST, length, length), jnp.float32),
            ((length, FIRST * HD), jnp.bfloat16),
        ],
        weight_scratch(D, 3 * D, 3),
        weight,
        (entry,),
    )


def attend_second(heads, mix_first, weight, stream_zero, bias, gain, shift):
    length = heads.shape[0]
    half = D // 2

    def kernel(*refs):
        heads_ref, first_ref, zero_ref, bias_ref, gain_ref, shift_ref = refs[6:12]
        chances_ref, stream, value_ref, up_mine, up_other, full, sems, mixed, padded = refs[12:]
        weight_in = Fetch(refs[:6], full, sems, 3 * D)
        padded[...] = jnp.zeros_like(padded)
        mixed[:, : FIRST * HD] = first_ref[...]
        for head in range(FIRST, H):
            mixed[:, head * HD : (head + 1) * HD] = attend_head(
                heads_ref, head, chances_ref, head - FIRST
            )
        weight_in.wait()
        stream[...] = zero_ref[...] + product(mixed[...], full[...]) + bias_ref[...]
        store_upright(
            mixed[...].astype(jnp.float32), padded, up_mine.at[pl.ds(0, half)], up_other.at[pl.ds(0, half)]
        )
        normed = normalize(stream[...])[0]
        value = (normed * gain_ref[...] + shift_ref[...]).astype(jnp.bfloat16)
        value_ref[...] = value
        store_upright(
            value.astype(jnp.float32), padded, up_mine.at[pl.ds(half, half)], up_other.at[pl.ds(half, half)]
        )

    return heavy(
        kernel,
        [
            ((H - FIRST, length, length), jnp.float32),
            ((length, D), jnp.float32),
            ((length, D), jnp.bfloat16),
            ((D, PAD), jnp.bfloat16),
            ((D, PAD), jnp.bfloat16),
        ],
        weight_scratch(D, D)
        + [pltpu.VMEM((length, D), jnp.bfloat16), pltpu.VMEM((PAD, D), jnp.float32)],
        weight,
        (heads, mix_first, stream_zero, bias, gain, shift),
    )


def expand_forward(entry, weight, bias):
    length = entry.shape[0]

    def kernel(*refs):
        entry_ref, bias_ref = refs[6:8]
        active_ref, slope_ref, up_mine, up_other, full, sems, padded = refs[8:]
        core = lax.axis_index("wide") & 1
        weight_in = Fetch(refs[:6], full, sems)
        padded[...] = jnp.zeros_like(padded)
        for step in range(FF // D):
            columns = slice(step * D, (step + 1) * D)
            weight_in.wait(step)
            value = product(entry_ref[...], full[:, columns]) + bias_ref[:, columns]
            inside = 0.5 * (1.0 + lax.erf(value * (0.5**0.5)))
            bell = jnp.exp(-0.5 * value * value) * (2.0 * jnp.pi) ** -0.5
            active = (value * inside).astype(jnp.bfloat16)
            slope_ref[:, columns] = inside + value * bell
            active_ref[:, columns] = active
            padded[:length] = active.astype(jnp.float32)
            turned = padded[...].T.astype(jnp.bfloat16)
            rows = slice((step % 2) * D, (step % 2 + 1) * D)

            @pl.when(core == step // 2)
            def _():
                up_mine[rows] = turned

            @pl.when(core != step // 2)
            def _():
                up_other[rows] = turned

    return heavy(
        kernel,
        [
            ((length, FF), jnp.bfloat16),
            ((length, FF), jnp.float32),
            ((FF // 2, PAD), jnp.bfloat16),
            ((FF // 2, PAD), jnp.bfloat16),
        ],
        weight_scratch(D, FF, FF // D) + [pltpu.VMEM((PAD, D), jnp.float32)],
        weight,
        (entry, bias),
    )


def hidden_backward(pulled, weight, slope):
    length = pulled.shape[0]

    def kernel(*refs):
        pulled_ref, slope_ref, low_ref, sum_ref, full, sems = refs[6:]
        Fetch(refs[:6], full, sems).wait()
        for step in range(FF // D):
            columns = slice(step * D, (step + 1) * D)
            delta = dot_rows(pulled_ref[...], full[columns]) * slope_ref[:, columns]
            low_ref[:, columns] = delta.astype(jnp.bfloat16)
            sum_ref[:, columns] = jnp.sum(delta, axis=0, keepdims=True)

    return heavy(
        kernel,
        [((length, FF), jnp.bfloat16), ((1, FF), jnp.float32)],
        weight_scratch(FF, D),
        weight,
        (pulled, slope),
    )


def expand_backward(hidden_low, weight, mixed_weight, pulled, stream_one, gain):
    length = pulled.shape[0]

    def kernel(*refs):
        hidden_ref, pulled_ref, stream_ref, gain_ref = refs[12:16]
        one_ref, low_ref, sums, mix_ref, full, sems, output, output_sems, delta = refs[16:]
        weight_in = Fetch(refs[:6], full, sems)
        output_in = Fetch(refs[6:12], output, output_sems, 3 * D)
        for step in range(FF // D):
            columns = slice(step * D, (step + 1) * D)
            weight_in.wait(step)
            part = dot_rows(hidden_ref[:, columns], full[:, columns])
            delta[...] = part if step == 0 else delta[...] + part
        value = delta[...]
        normed, inverse = normalize(stream_ref[...])
        upstream = pulled_ref[...].astype(jnp.float32)
        one = upstream + norm_back(value * gain_ref[...], normed, inverse)
        one_ref[...] = one
        low_value = one.astype(jnp.bfloat16)
        low_ref[...] = low_value
        sums[0:1] = jnp.sum(one, axis=0, keepdims=True)
        sums[1:2] = jnp.sum(value * normed, axis=0, keepdims=True)
        sums[2:3] = jnp.sum(value, axis=0, keepdims=True)
        sums[3:4] = jnp.sum(upstream, axis=0, keepdims=True)
        output_in.wait()
        mix_ref[...] = dot_rows(low_value, output[...]).astype(jnp.bfloat16)

    return heavy(
        kernel,
        [
            ((length, D), jnp.float32),
            ((length, D), jnp.bfloat16),
            ((4, D), jnp.float32),
            ((length, D), jnp.bfloat16),
        ],
        weight_scratch(D, FF, FF // D)
        + weight_scratch(D, D)
        + [pltpu.VMEM((length, D), jnp.float32)],
        (*weight, *mixed_weight),
        (hidden_low, pulled, stream_one, gain),
    )


def attend_backward(heads, chances_first, chances_second, delta_mixture, stream_low):
    length = heads.shape[0]
    scale = HD ** (-0.5)

    def kernel(heads_ref, first_ref, second_ref, delta_ref, stream_ref, mixed):
        mixed[:, 3 * D :] = stream_ref[...]
        for head in range(H):
            at = head * HD
            queries = heads_ref[:, at : at + HD]
            keys = heads_ref[:, D + at : D + at + HD]
            values = heads_ref[:, 2 * D + at : 2 * D + at + HD]
            delta = delta_ref[:, at : at + HD]
            chances = first_ref[head] if head < FIRST else second_ref[head - FIRST]
            pull = dot_rows(delta, values)
            inner_sum = jnp.sum(chances * pull, axis=-1, keepdims=True)
            scores = (scale * (chances * (pull - inner_sum))).astype(jnp.bfloat16)
            mixed[:, at : at + HD] = product(scores, keys).astype(jnp.bfloat16)
            mixed[:, D + at : D + at + HD] = dot_depth(scores, queries).astype(jnp.bfloat16)
            mixed[:, 2 * D + at : 2 * D + at + HD] = dot_depth(
                chances.astype(jnp.bfloat16), delta
            ).astype(jnp.bfloat16)

    return heavy(
        kernel,
        [((length, 4 * D), jnp.bfloat16)],
        [],
        (),
        (heads, chances_first, chances_second, delta_mixture, stream_low),
    )[0]


def entry_backward(delta_mixed, weight, delta_one, stream_zero, gain, sums_two, hidden_sum):
    length = delta_mixed.shape[0]
    width = D // 8
    tall = -(-(length + VECTOR_ROWS) // 16) * 16

    def kernel(*refs):
        mixed_ref, one_ref, stream_ref, gain_ref, sums_ref, hidden_ref, low_ref = refs[6:13]
        quarters, (full, sems, delta, held) = refs[13:17], refs[17:]
        weight_in = Fetch(refs[:6], full, sems)
        for step in range(3):
            columns = slice(step * D, (step + 1) * D)
            weight_in.wait(step)
            part = dot_rows(mixed_ref[:, columns], full[:, columns])
            delta[...] = part if step == 0 else delta[...] + part
        value = delta[...]
        normed, inverse = normalize(stream_ref[...])
        zero = one_ref[...] + norm_back(value * gain_ref[...], normed, inverse)
        zero_low = zero.astype(jnp.bfloat16)
        low_ref[...] = zero_low
        sums = [jnp.sum(part, axis=0, keepdims=True) for part in (zero, value * normed, value)]
        sums += [sums_ref[row : row + 1] for row in range(4)]
        held[...] = jnp.zeros_like(held)
        for block in range(VECTOR_ROWS * 8):
            owner, place = block // (2 * VECTOR_ROWS), block % (2 * VECTOR_ROWS)
            if block < 56:
                source, wide = sums[block // 8], block % 8
                start = (4 * (wide % 2) + wide // 2) * width
            else:
                source, wide = hidden_ref, (block - 56) // 4
                start = (4 * (wide % 2) + wide // 2) * 4 * width + (block % 4) * width
            columns = slice((place % 2) * width, (place % 2 + 1) * width)
            held[owner, place // 2 : place // 2 + 1, columns] = source[:, start : start + width]
        narrow = lax.axis_index("narrow")
        for owner in range(4):
            for relative in range(4):

                @pl.when((narrow ^ relative) == owner)
                def _():
                    for parity in range(2):
                        start = (4 * parity + owner) * width
                        quarters[relative][:length, parity * width : (parity + 1) * width] = (
                            zero_low[:, start : start + width]
                        )
                    quarters[relative][length:] = held[owner, : tall - length].astype(jnp.bfloat16)

    return heavy(
        kernel,
        [((length, D), jnp.bfloat16)] + [((tall, D // 4), jnp.bfloat16)] * 4,
        weight_scratch(D, 3 * D, 3)
        + [pltpu.VMEM((length, D), jnp.float32), pltpu.VMEM((4, 16, D // 4), jnp.float32)],
        weight,
        (delta_mixed, delta_one, stream_zero, gain, sums_two, hidden_sum),
    )


def joined_backward(zero_low, weight):
    length = zero_low.shape[0]
    width = 2 * D // 8

    def kernel(*refs):
        zero_ref, first_ref, second_ref, full, sems = refs[6:]
        Fetch(refs[:6], full, sems).wait()
        for parity in range(2):
            delta = dot_rows(zero_ref[...], full[parity * D : (parity + 1) * D])
            delta = delta.astype(jnp.bfloat16)
            for number in range(4):
                target = (first_ref, second_ref)[number // 2]
                column = (2 * (number % 2) + parity) * width
                target[:, column : column + width] = delta[:, number * width : (number + 1) * width]

    out = ((length, D), jnp.bfloat16)
    return heavy(kernel, [out, out], weight_scratch(2 * D, D), weight, (zero_low,))


def shrink_forward(active, weight, stream_one, bias):
    length = active.shape[0]
    width = D // 8

    def kernel(*refs):
        active_ref, stream_ref, bias_ref, out_ref, full, sems = refs[6:]
        Fetch(refs[:6], full, sems).wait()
        total = (
            stream_ref[...] + product(active_ref[...], full[...]) + bias_ref[...]
        ).astype(jnp.bfloat16)
        for parity in range(2):
            for number in range(4):
                column = (2 * number + parity) * width
                source = (4 * parity + number) * width
                out_ref[:, column : column + width] = total[:, source : source + width]

    return heavy(
        kernel,
        [((length, D), jnp.bfloat16)],
        weight_scratch(FF, D),
        weight,
        (active, stream_one, bias),
    )[0]


def on_device(
    inputs,
    skip_tokens,
    cotangent,
    merge_weight,
    merge_moment,
    merge_square,
    attend_weight,
    attend_moment,
    attend_square,
    output_weight,
    output_moment,
    output_square,
    expand_weight,
    expand_moment,
    expand_square,
    shrink_weight,
    shrink_moment,
    shrink_square,
    vectors,
    vector_moment,
    vector_square,
):
    core = spot()[0]
    low = jnp.bfloat16
    columns = attend_weight.shape[1]

    merge_low = fold(merge_weight.astype(low))
    width = merge_low.shape[1]
    count = vectors.shape[0]
    vector_rows = jnp.pad(vectors.astype(low), (0, 16 * width - count)).reshape(16, width)
    merge_low = jnp.concatenate([merge_low, vector_rows], axis=0)
    merge_others = across_narrow(merge_low)
    mixed_low = jnp.concatenate([attend_weight.astype(low), output_weight.astype(low)], axis=1)
    joined = inner(jnp.concatenate([inputs[0], skip_tokens[0]], axis=-1))
    joined_mine, joined_other = halves_of(joined, core)
    pulled = inner(cotangent[0])
    merge_others, mixed_low, joined, joined_mine, joined_other, pulled = together(
        merge_others, mixed_low, joined, joined_mine, joined_other, pulled
    )
    merge_block, vector_parts = arrange("merge", 2, merge_low, merge_others, 16)
    merge_first = gather_first(merge_block)
    mixed_far = swap_narrow(mixed_low, 2)
    mixed_near = swap_narrow(mixed_low, 1)
    expand_low = expand_weight.astype(low)
    known_sibling = swap_wide(jnp.concatenate([joined_other, pulled], axis=1), CORE)
    merge_first, mixed_far, vector_parts, expand_low, known_sibling = together(
        merge_first, mixed_far, vector_parts, expand_low, known_sibling
    )
    joined_sibling, pulled_sibling = known_sibling[:, :D], known_sibling[:, D:]
    merge_second = gather_second(merge_first)
    merge_sides = swap_sides(merge_first)
    mixed_last = swap_narrow(mixed_far, 1)
    shrink_low = fold(shrink_weight.astype(low))
    pieces = unpack(vector_parts.reshape(4, -1)[:, :count].reshape(-1).astype(jnp.float32))
    pieces = tuple(inner(piece)[None] for piece in pieces)
    merge_second, merge_sides, mixed_near, mixed_last, shrink_low, pieces = together(
        merge_second, merge_sides, mixed_near, mixed_last, shrink_low, pieces
    )
    skip_bias, gain_one, bias_one, output_bias, gain_two, bias_two, shrink_bias, expand_bias = pieces
    mixed_block = arrange("attend_output", 1, mixed_low, (mixed_near, mixed_far, mixed_last))[0]
    mixed_first = gather_first(mixed_block)
    expand_far = swap_narrow(expand_low, 2)
    expand_near = swap_narrow(expand_low, 1)
    merge_ends = ends_of(merge_block, merge_second)
    merge_pieces = (merge_ends, *merge_first, swap_wide(merge_ends, CORE), *merge_sides)
    stream_zero, attend_input, attend_up, attend_up_other = merge_forward(
        joined, merge_pieces, skip_bias, gain_one, bias_one
    )
    mixed_first, expand_far, expand_near, stream_zero, attend_input, attend_up_other = together(
        mixed_first, expand_far, expand_near, stream_zero, attend_input, attend_up_other
    )
    mixed_second = gather_second(mixed_first)
    mixed_sides = swap_sides(mixed_first)
    expand_last = swap_narrow(expand_far, 1)
    expand_block = arrange("expand", 1, expand_low, (expand_near, expand_far, expand_last))[0]
    mixed_second, mixed_sides, expand_block = together(mixed_second, mixed_sides, expand_block)
    expand_first = gather_first(expand_block)
    shrink_far = swap_narrow(shrink_low, 2)
    shrink_near = swap_narrow(shrink_low, 1)
    mixed_ends = ends_of(mixed_block, mixed_second)
    mixed_pieces = (mixed_ends, *mixed_first, swap_wide(mixed_ends, CORE), *mixed_sides)
    heads, chances_first, mix_first = attend_first(attend_input, mixed_pieces)
    expand_first, shrink_far, shrink_near, heads, mix_first = together(
        expand_first, shrink_far, shrink_near, heads, mix_first
    )
    expand_second = gather_second(expand_first)
    expand_sides = swap_sides(expand_first)
    shrink_last = swap_narrow(shrink_far, 1)
    chances_second, stream_one, expand_input, ups, ups_other = attend_second(
        heads, mix_first, mixed_pieces, stream_zero, output_bias, gain_two, bias_two
    )
    shrink_block = arrange("shrink", 4, shrink_low, (shrink_near, shrink_far, shrink_last))[0]
    (
        expand_second,
        expand_sides,
        shrink_block,
        expand_input,
        ups_other,
        joined_mine,
        joined_sibling,
    ) = together(
        expand_second,
        expand_sides,
        shrink_block,
        expand_input,
        ups_other,
        joined_mine,
        joined_sibling,
    )
    shrink_first = gather_first(shrink_block)
    expand_ends = ends_of(expand_block, expand_second)
    expand_pieces = (expand_ends, *expand_first, swap_wide(expand_ends, CORE), *expand_sides)
    joined_far = swap_narrow(joined_mine, 2)
    joined_near = swap_narrow(joined_mine, 1)
    active, slope, active_up, active_up_other = expand_forward(
        expand_input, expand_pieces, expand_bias
    )
    shrink_first, joined_far, joined_near, active, slope, active_up, active_up_other = together(
        shrink_first, joined_far, joined_near, active, slope, active_up, active_up_other
    )
    shrink_second = gather_second(shrink_first)
    shrink_sides = swap_sides(shrink_first)
    active_up_sibling = swap_wide(active_up_other, CORE)
    shrink_blocks = pair_gradient([(active_up, active_up_sibling, D, 0, FF // 2)], (pulled, pulled_sibling))
    shrink_second, shrink_sides, shrink_blocks, joined_far, joined_sibling, ups_other = together(
        shrink_second, shrink_sides, shrink_blocks, joined_far, joined_sibling, ups_other
    )
    shrink_got = send(shrink_blocks)
    shrink_ends = ends_of(shrink_block, shrink_second)
    shrink_pieces = (shrink_ends, *shrink_first, swap_wide(shrink_ends, CORE), *shrink_sides)
    sibling_far = swap_narrow(joined_sibling, 2)
    joined_last = swap_narrow(joined_far, 1)
    hidden_low, hidden_sum = hidden_backward(pulled, shrink_pieces, slope)
    outputs = shrink_forward(active, shrink_pieces, stream_one, shrink_bias)[None]
    (
        shrink_got,
        sibling_far,
        joined_last,
        hidden_low,
        hidden_sum,
        outputs,
        joined_sibling,
        ups_other,
        attend_up_other,
    ) = together(
        shrink_got,
        sibling_far,
        joined_last,
        hidden_low,
        hidden_sum,
        outputs,
        joined_sibling,
        ups_other,
        attend_up_other,
    )
    shrink_got_last = forward(shrink_blocks, shrink_got)
    hidden_sibling = swap_wide(hidden_low, CORE)
    ups_sibling = swap_wide(ups_other, CORE)
    sibling_near = swap_narrow(joined_sibling, 1)
    half = D // 2
    expand_blocks = pair_gradient(
        [(ups, ups_sibling, FF, 1, half)], (hidden_low, hidden_sibling)
    )
    shrink_got_last, sibling_near, expand_blocks, hidden_low, sibling_far = together(
        shrink_got_last, sibling_near, expand_blocks, hidden_low, sibling_far
    )
    expand_got = send(expand_blocks)
    sibling_last = swap_narrow(sibling_far, 1)
    attend_up_sibling = swap_wide(attend_up_other, CORE)
    delta_one, stream_low, sums_two, delta_mixture = expand_backward(
        hidden_low, expand_pieces, mixed_pieces, pulled, stream_one, gain_two
    )
    delta_mixed = attend_backward(heads, chances_first, chances_second, delta_mixture, stream_low)
    expand_got, sibling_last, delta_mixed, attend_up_sibling = together(
        expand_got, sibling_last, delta_mixed, attend_up_sibling
    )
    expand_got_last = forward(expand_blocks, expand_got)
    mixed_sibling = swap_wide(delta_mixed, CORE)
    shrink_quarters = unarrange("shrink", 4, shrink_blocks, shrink_got, shrink_got_last)
    shrink_narrow = narrow_first(shrink_quarters)
    mixed_blocks = pair_gradient(
        [(attend_up, attend_up_sibling, 3 * D, 0, half), (ups, ups_sibling, D, 0, half)],
        (delta_mixed, mixed_sibling),
    )
    expand_got_last, shrink_narrow, mixed_blocks, delta_mixed = together(
        expand_got_last, shrink_narrow, mixed_blocks, delta_mixed
    )
    mixed_got = send(mixed_blocks)
    expand_quarters = unarrange("expand", 1, expand_blocks, expand_got, expand_got_last)
    expand_narrow = narrow_first(expand_quarters)
    shrink_end = narrow_second(shrink_quarters, shrink_narrow)
    zero_low, *zero_quarters = entry_backward(
        delta_mixed, mixed_pieces, delta_one, stream_zero, gain_one, sums_two, hidden_sum
    )
    mixed_got, expand_narrow, zero_low, zero_quarters, shrink_end = together(
        mixed_got, expand_narrow, zero_low, zero_quarters, shrink_end
    )
    mixed_got_last = forward(mixed_blocks, mixed_got)
    zero_got = tuple(swap_narrow(zero_quarters[bit], bit) for bit in (1, 2, 3))
    input_gradient, skip_gradient = joined_backward(zero_low, merge_pieces)
    mixed_got_last, zero_got, input_gradient, skip_gradient, shrink_end = together(
        mixed_got_last, zero_got, input_gradient, skip_gradient, shrink_end
    )
    mixed_quarters = unarrange("attend_output", 1, mixed_blocks, mixed_got, mixed_got_last)
    mixed_narrow = narrow_first(mixed_quarters)
    expand_end = narrow_second(expand_quarters, expand_narrow)
    zero_line = jnp.stack([zero_quarters[0], *zero_got])
    zero_line_sibling = swap_wide(zero_line, CORE)
    merge_blocks = line_gradient(
        (
            joined_mine,
            joined_near,
            joined_far,
            joined_last,
            joined_sibling,
            sibling_near,
            sibling_far,
            sibling_last,
        ),
        zero_line,
        zero_line_sibling,
    )
    mixed_narrow, merge_blocks, shrink_end, expand_end = together(
        mixed_narrow, merge_blocks, shrink_end, expand_end
    )
    mixed_end = narrow_second(mixed_quarters, mixed_narrow)
    merge_got = (
        swap_wide(merge_blocks[1], ACROSS),
        swap_wide(merge_blocks[2], ALONG),
        swap_wide(merge_blocks[3], ACROSS + ALONG),
    )
    shrink_new = turned_update(
        shrink_weight,
        shrink_moment,
        shrink_square,
        (shrink_quarters[KEEP_NEAR], shrink_narrow[1], shrink_end),
        4,
        rate_shrink,
    )
    expand_new = adamw_update(
        expand_weight,
        expand_moment,
        expand_square,
        finish(expand_quarters, expand_narrow, expand_end),
        rate_expand,
    )
    tall = merge_blocks[0].shape[0] - 16
    merge_sum = sum(term.astype(jnp.float32) for term in (merge_blocks[0], *merge_got))
    merge_new = adamw_update(
        merge_weight,
        merge_moment,
        merge_square,
        unfold(merge_sum[:tall], merge_weight.shape[0]),
        rate_merge,
    )
    vector_total = merge_sum[tall:].reshape(-1)[: vectors.shape[0]]
    vector_new = adamw_update(vectors, vector_moment, vector_square, vector_total, rate_vector)
    merge_new, mixed_end, vector_new, shrink_new, expand_new = together(
        merge_new, mixed_end, vector_new, shrink_new, expand_new
    )
    mixed_total = finish(mixed_quarters, mixed_narrow, mixed_end)
    attend_new = adamw_update(
        attend_weight, attend_moment, attend_square, mixed_total[:, :columns], rate_attend
    )
    output_new = adamw_update(
        output_weight, output_moment, output_square, mixed_total[:, columns:], rate_output
    )
    return (
        outputs,
        input_gradient[None],
        skip_gradient[None],
        *merge_new,
        *attend_new,
        *output_new,
        *expand_new,
        *shrink_new,
        *vector_new,
    )


def solution(mesh):
    in_specs = (
        P(("wide", "narrow"), None, None),
        P(("wide", "narrow"), None, None),
        P(("wide", "narrow"), None, None),
        P("wide", "narrow"),
        P("wide", "narrow"),
        P("wide", "narrow"),
        P("wide", "narrow"),
        P("wide", "narrow"),
        P("wide", "narrow"),
        P("wide", "narrow"),
        P("wide", "narrow"),
        P("wide", "narrow"),
        P("wide", "narrow"),
        P("wide", "narrow"),
        P("wide", "narrow"),
        P("wide", "narrow"),
        P("wide", "narrow"),
        P("wide", "narrow"),
        P("narrow"),
        P("narrow"),
        P("narrow"),
    )
    out_specs = (
        P(("wide", "narrow"), None, None),
        P(("wide", "narrow"), None, None),
        P(("wide", "narrow"), None, None),
        P("wide", "narrow"),
        P("wide", "narrow"),
        P("wide", "narrow"),
        P("wide", "narrow"),
        P("wide", "narrow"),
        P("wide", "narrow"),
        P("wide", "narrow"),
        P("wide", "narrow"),
        P("wide", "narrow"),
        P("wide", "narrow"),
        P("wide", "narrow"),
        P("wide", "narrow"),
        P("wide", "narrow"),
        P("wide", "narrow"),
        P("wide", "narrow"),
        P("narrow"),
        P("narrow"),
        P("narrow"),
    )
    tuned = mesh.shape["wide"] == 8 and mesh.shape["narrow"] == 4
    return jax.shard_map(
        on_device if tuned else general_device, mesh=mesh, in_specs=in_specs, out_specs=out_specs, check_vma=False
    )
```

```python
import jax
import jax.numpy as jnp
from jax import lax
from jax.experimental import pallas as pl
from jax.experimental.pallas import tpu as pltpu
from jax.sharding import PartitionSpec as P

D = 1152
FF = 4608
H = 16
HD = 72
STEP = 5


norm_epsilon = 1e-05
adam_epsilon = 1e-08
beta_moment = 0.5
weight_decay = 0.01
rate_merge = 0.04
rate_attend = 0.08
rate_output = 0.6
rate_expand = 0.06
rate_shrink = 0.03
rate_vector = 0.6


def product(left_side, right_side):
    return jnp.dot(left_side, right_side, preferred_element_type=jnp.float32)


def transposed(gradient, matrix):
    return lax.dot_general(
        gradient,
        matrix,
        (((gradient.ndim - 1,), (1,)), ((), ())),
        preferred_element_type=jnp.float32,
    )


def weight_gradient(activations, gradient):
    flat_left = activations.reshape(-1, activations.shape[-1])
    flat_right = gradient.reshape(-1, gradient.shape[-1])
    return lax.dot_general(
        flat_left, flat_right, (((0,), (0,)), ((), ())), preferred_element_type=jnp.float32
    )


def normalize(values):
    centered = values - jnp.mean(values, axis=-1, keepdims=True)
    spread = jnp.mean(centered * centered, axis=-1, keepdims=True)
    inverse = lax.rsqrt(spread + norm_epsilon)
    return (centered * inverse, inverse)


def norm_back(gradient, normed, inverse):
    return inverse * (
        gradient
        - jnp.mean(gradient, axis=-1, keepdims=True)
        - normed * jnp.mean(gradient * normed, axis=-1, keepdims=True)
    )


def row_sum(values):
    return jnp.sum(values, axis=(0, 1))


def unpack(packed):
    return tuple((packed[position * D : (position + 1) * D] for position in range(7))) + (
        packed[7 * D : 7 * D + FF],
    )


def gaussian_unit(values):
    return jax.nn.gelu(values, approximate=False)


def adamw_update(weight, moment, square, gradient, step_rate):
    moment_new = beta_moment * moment + (1.0 - beta_moment) * gradient
    square_new = beta_moment * square + (1.0 - beta_moment) * gradient * gradient
    correct = 1.0 - beta_moment**STEP
    direction = moment_new / correct / (jnp.sqrt(square_new / correct) + adam_epsilon)
    return (weight - step_rate * (direction + weight_decay * weight), moment_new, square_new)


def general_device(
    inputs,
    skip_tokens,
    cotangent,
    merge_weight,
    merge_moment,
    merge_square,
    attend_weight,
    attend_moment,
    attend_square,
    output_weight,
    output_moment,
    output_square,
    expand_weight,
    expand_moment,
    expand_square,
    shrink_weight,
    shrink_moment,
    shrink_square,
    vectors,
    vector_moment,
    vector_square,
):
    merge_low = merge_weight.astype(jnp.bfloat16)
    attend_low = attend_weight.astype(jnp.bfloat16)
    output_low = output_weight.astype(jnp.bfloat16)
    expand_low = expand_weight.astype(jnp.bfloat16)
    shrink_low = shrink_weight.astype(jnp.bfloat16)
    vector_low = vectors.astype(jnp.bfloat16)
    columns = (
        lax.all_gather(merge_low, "narrow", axis=1, tiled=True),
        lax.all_gather(attend_low, "narrow", axis=1, tiled=True),
        lax.all_gather(output_low, "narrow", axis=1, tiled=True),
        lax.all_gather(expand_low, "narrow", axis=1, tiled=True),
        lax.all_gather(shrink_low, "narrow", axis=1, tiled=True),
        lax.all_gather(vector_low, "narrow", axis=0, tiled=True),
    )
    matrices = (
        lax.all_gather(columns[0], "wide", axis=0, tiled=True),
        lax.all_gather(columns[1], "wide", axis=0, tiled=True),
        lax.all_gather(columns[2], "wide", axis=0, tiled=True),
        lax.all_gather(columns[3], "wide", axis=0, tiled=True),
        lax.all_gather(columns[4], "wide", axis=0, tiled=True),
    )
    skip_bias, gain_one, bias_one, output_bias, gain_two, bias_two, shrink_bias, expand_bias = (
        unpack(columns[5].astype(jnp.float32))
    )
    images = inputs.shape[0]
    length = inputs.shape[1]
    softmax_scale = HD ** (-0.5)
    joined = jnp.concatenate([inputs, skip_tokens], axis=-1)
    stream_zero = product(joined, matrices[0]) + skip_bias
    normed_one, inverse_one = normalize(stream_zero)
    attend_input = (normed_one * gain_one + bias_one).astype(jnp.bfloat16)
    mixed_heads = product(attend_input, matrices[1]).astype(jnp.bfloat16)
    query_heads = mixed_heads[..., 0:D].reshape(images, length, H, HD)
    key_heads = mixed_heads[..., D : 2 * D].reshape(images, length, H, HD)
    value_heads = mixed_heads[..., 2 * D : 3 * D].reshape(images, length, H, HD)
    logits = (
        jnp.einsum("blhe,bmhe->bhlm", query_heads, key_heads, preferred_element_type=jnp.float32)
        * softmax_scale
    )
    maxima = jnp.max(logits, axis=-1, keepdims=True)
    log_total = maxima + jnp.log(jnp.sum(jnp.exp(logits - maxima), axis=-1, keepdims=True))
    softmax_low = jnp.exp(logits - log_total).astype(jnp.bfloat16)
    mixture = jnp.einsum(
        "bhlm,bmhe->blhe", softmax_low, value_heads, preferred_element_type=jnp.float32
    )
    mixture = mixture.astype(jnp.bfloat16).reshape(images, length, D)
    stream_one = stream_zero + product(mixture, matrices[2]) + output_bias
    normed_two, inverse_two = normalize(stream_one)
    expand_input = (normed_two * gain_two + bias_two).astype(jnp.bfloat16)
    hidden = product(expand_input, matrices[3]) + expand_bias
    active, pullback = jax.vjp(gaussian_unit, hidden)
    active_low = active.astype(jnp.bfloat16)
    outputs = (stream_one + product(active_low, matrices[4]) + shrink_bias).astype(jnp.bfloat16)
    columns_back = (
        lax.all_gather(merge_low, "narrow", axis=1, tiled=True),
        lax.all_gather(attend_low, "narrow", axis=1, tiled=True),
        lax.all_gather(output_low, "narrow", axis=1, tiled=True),
        lax.all_gather(expand_low, "narrow", axis=1, tiled=True),
        lax.all_gather(shrink_low, "narrow", axis=1, tiled=True),
        lax.all_gather(vector_low, "narrow", axis=0, tiled=True),
    )
    matrices_back = (
        lax.all_gather(columns_back[0], "wide", axis=0, tiled=True),
        lax.all_gather(columns_back[1], "wide", axis=0, tiled=True),
        lax.all_gather(columns_back[2], "wide", axis=0, tiled=True),
        lax.all_gather(columns_back[3], "wide", axis=0, tiled=True),
        lax.all_gather(columns_back[4], "wide", axis=0, tiled=True),
    )
    packed_back = columns_back[5].astype(jnp.float32)
    unpacked = unpack(packed_back)
    gain_first = unpacked[1]
    gain_second = unpacked[4]
    upstream = cotangent.astype(jnp.float32)
    shrink_gradient = weight_gradient(active_low, cotangent)
    delta_active = transposed(cotangent, matrices_back[4])
    delta_hidden = pullback(delta_active)[0]
    hidden_low = delta_hidden.astype(jnp.bfloat16)
    expand_gradient = weight_gradient(expand_input, hidden_low)
    delta_expand = transposed(hidden_low, matrices_back[3])
    delta_one = upstream + norm_back(delta_expand * gain_second, normed_two, inverse_two)
    stream_low = delta_one.astype(jnp.bfloat16)
    output_gradient = weight_gradient(mixture, stream_low)
    delta_mixture = (
        transposed(stream_low, matrices_back[2]).astype(jnp.bfloat16).reshape(images, length, H, HD)
    )
    logits_again = (
        jnp.einsum("blhe,bmhe->bhlm", query_heads, key_heads, preferred_element_type=jnp.float32)
        * softmax_scale
    )
    softmax_again = jnp.exp(logits_again - log_total)
    delta_softmax = jnp.einsum(
        "blhe,bmhe->bhlm", delta_mixture, value_heads, preferred_element_type=jnp.float32
    )
    delta_values = jnp.einsum(
        "bhlm,blhe->bmhe",
        softmax_again.astype(jnp.bfloat16),
        delta_mixture,
        preferred_element_type=jnp.float32,
    )
    delta_logits = softmax_again * (
        delta_softmax - jnp.sum(softmax_again * delta_softmax, axis=-1, keepdims=True)
    )
    delta_scores = (softmax_scale * delta_logits).astype(jnp.bfloat16)
    delta_queries = jnp.einsum(
        "bhlm,bmhe->blhe", delta_scores, key_heads, preferred_element_type=jnp.float32
    )
    delta_keys = jnp.einsum(
        "bhlm,blhe->bmhe", delta_scores, query_heads, preferred_element_type=jnp.float32
    )
    delta_mixed = jnp.concatenate(
        [
            delta_queries.reshape(images, length, D),
            delta_keys.reshape(images, length, D),
            delta_values.reshape(images, length, D),
        ],
        axis=-1,
    ).astype(jnp.bfloat16)
    attend_gradient = weight_gradient(attend_input, delta_mixed)
    delta_attend = transposed(delta_mixed, matrices_back[1])
    delta_zero = delta_one + norm_back(delta_attend * gain_first, normed_one, inverse_one)
    zero_low = delta_zero.astype(jnp.bfloat16)
    merge_gradient = weight_gradient(joined, zero_low)
    delta_joined = transposed(zero_low, matrices_back[0])
    input_gradient = delta_joined[..., 0:D].astype(jnp.bfloat16)
    skip_gradient = delta_joined[..., D : 2 * D].astype(jnp.bfloat16)
    vector_gradient = jnp.concatenate(
        [
            row_sum(delta_zero),
            row_sum(delta_attend * normed_one),
            row_sum(delta_attend),
            row_sum(delta_one),
            row_sum(delta_expand * normed_two),
            row_sum(delta_expand),
            row_sum(upstream),
            row_sum(delta_hidden),
        ]
    )
    owned_rows = (
        lax.psum_scatter(merge_gradient, "wide", scatter_dimension=0, tiled=True),
        lax.psum_scatter(attend_gradient, "wide", scatter_dimension=0, tiled=True),
        lax.psum_scatter(output_gradient, "wide", scatter_dimension=0, tiled=True),
        lax.psum_scatter(expand_gradient, "wide", scatter_dimension=0, tiled=True),
        lax.psum_scatter(shrink_gradient, "wide", scatter_dimension=0, tiled=True),
    )
    vector_total = lax.psum(vector_gradient, "wide")
    parted = (
        lax.psum_scatter(owned_rows[0], "narrow", scatter_dimension=1, tiled=True),
        lax.psum_scatter(owned_rows[1], "narrow", scatter_dimension=1, tiled=True),
        lax.psum_scatter(owned_rows[2], "narrow", scatter_dimension=1, tiled=True),
        lax.psum_scatter(owned_rows[3], "narrow", scatter_dimension=1, tiled=True),
        lax.psum_scatter(owned_rows[4], "narrow", scatter_dimension=1, tiled=True),
        lax.psum_scatter(vector_total, "narrow", scatter_dimension=0, tiled=True),
    )
    merge_new = adamw_update(merge_weight, merge_moment, merge_square, parted[0], rate_merge)
    attend_new = adamw_update(attend_weight, attend_moment, attend_square, parted[1], rate_attend)
    output_new = adamw_update(output_weight, output_moment, output_square, parted[2], rate_output)
    expand_new = adamw_update(expand_weight, expand_moment, expand_square, parted[3], rate_expand)
    shrink_new = adamw_update(shrink_weight, shrink_moment, shrink_square, parted[4], rate_shrink)
    vector_new = adamw_update(vectors, vector_moment, vector_square, parted[5], rate_vector)
    return (
        outputs,
        input_gradient,
        skip_gradient,
        merge_new[0],
        merge_new[1],
        merge_new[2],
        attend_new[0],
        attend_new[1],
        attend_new[2],
        output_new[0],
        output_new[1],
        output_new[2],
        expand_new[0],
        expand_new[1],
        expand_new[2],
        shrink_new[0],
        shrink_new[1],
        shrink_new[2],
        vector_new[0],
        vector_new[1],
        vector_new[2],
    )


CORE = 1
ACROSS = 2
ALONG = 4
PAD = 384
VECTOR_ROWS = 11
VMEM_BYTES = 56 * 1024 * 1024
LIGHT = pl.CostEstimate(flops=0, bytes_accessed=1024, transcendentals=0)
PARAMS = pltpu.CompilerParams(vmem_limit_bytes=VMEM_BYTES)


def swap_wide(value, bit):
    return lax.ppermute(value, "wide", [(i, i ^ bit) for i in range(8)])


def swap_narrow(value, bit):
    return lax.ppermute(value, "narrow", [(i, i ^ bit) for i in range(4)])


def together(*values):
    return lax.optimization_barrier(values)


def spot():
    wide = lax.axis_index("wide")
    narrow = lax.axis_index("narrow")
    return (wide & 1, (wide >> 1) & 1, (wide >> 2) & 1, narrow & 1, narrow >> 1)


def split_shapes(rows, columns):
    if columns == FF:
        return (rows, columns // 2), True
    return (rows // 2, columns), False


def split_block(value):
    shape, by_columns = split_shapes(*value.shape[-2:])
    if by_columns:
        return value[..., : shape[1]], value[..., shape[1] :]
    return value[..., : shape[0], :], value[..., shape[0] :, :]


def column_blocks(kind, quarter):
    if kind == "attend_output":
        width = quarter // 8
        order = [8 * part + 2 * n + p for part in range(3) for p in range(2) for n in range(4)]
        blocks = [(block // 6, (block % 6) * width) for block in order]
        return width, blocks + [(n, (6 + p) * width) for p in range(2) for n in range(4)]
    width = quarter // 2
    return width, [(n, p * width) for p in range(2) for n in range(4)]


def fold(shard):
    parts = max(1, shard.shape[0] // (D // 8))
    height = shard.shape[0] // parts
    return jnp.concatenate(
        [shard[part * height : (part + 1) * height] for part in range(parts)], axis=1
    )


def unfold(value, rows):
    parts = rows // value.shape[0]
    quarter = value.shape[1] // parts
    return jnp.concatenate(
        [value[:, part * quarter : (part + 1) * quarter] for part in range(parts)], axis=0
    )


def arrange(kind, parts, shard, others, extra=0):
    height = shard.shape[0] - extra
    rows, quarter = parts * height, shard.shape[1] // parts
    width, blocks = column_blocks(kind, quarter)

    def kernel(*refs):
        full, apart = refs[4], refs[-1]
        narrow = lax.axis_index("narrow")
        for number in range(4):
            for relative in range(4):

                @pl.when((narrow ^ relative) == number)
                def _():
                    value = refs[relative]
                    if extra:
                        apart[number] = value[height:]
                    for position, (owner, offset) in enumerate(blocks):
                        if owner == number:
                            column = slice(position * width, (position + 1) * width)
                            for part in range(parts):
                                start = part * quarter + offset
                                full[part * height : (part + 1) * height, column] = value[
                                    :height, start : start + width
                                ]

    outs = [jax.ShapeDtypeStruct((rows, 4 * quarter), jnp.bfloat16)]
    if extra:
        outs.append(jax.ShapeDtypeStruct((4, extra, shard.shape[1]), jnp.bfloat16))
    return pl.pallas_call(
        kernel,
        out_shape=tuple(outs),
        compiler_params=PARAMS,
        cost_estimate=LIGHT,
    )(shard, *others)


def weight_scratch(rows, columns, chunks=1):
    return [pltpu.VMEM((rows, columns), jnp.bfloat16), pltpu.SemaphoreType.DMA((chunks, 8))]


class Fetch:
    def __init__(self, refs, full, sems, first=0):
        wide = lax.axis_index("wide")
        core, chip = wide & 1, wide >> 1
        rows = full.shape[0] // 8
        chunks = sems.shape[0]
        width = full.shape[1] // chunks
        self.copies = []
        for chunk in range(chunks):
            group = []
            for number, (ends, from_x, from_y) in enumerate((refs[:3], refs[3:])):
                parity = core if number == 0 else 1 - core
                own, far = ends.at[pl.ds(0, rows)], ends.at[pl.ds(rows, rows)]
                for relative, piece in enumerate((own, from_x, from_y, far)):
                    start = pl.multiple_of((4 * parity + (chip ^ relative)) * rows, 16)
                    group.append(
                        pltpu.make_async_copy(
                            piece.at[:, pl.ds(first + chunk * width, width)],
                            full.at[pl.ds(start, rows), pl.ds(chunk * width, width)],
                            sems.at[chunk, 4 * number + relative],
                        )
                    )
            self.copies.append(group)
        for group in self.copies:
            for copy in group:
                copy.start()

    def wait(self, chunk=0):
        for copy in self.copies[chunk]:
            copy.wait()


def pair_gradient(lefts, right):
    height = lefts[0][4]
    rows = height // 4
    tokens, columns = right[0].shape
    tile = 384 if height > 576 else 1152
    count = len(lefts)
    ends = [sum(left[2] for left in lefts[: number + 1]) // tile for number in range(count)]
    starts = [0] + ends[:-1]

    def kernel(*refs):
        left_refs = refs[: 2 * count]
        right_ref, sibling_ref = refs[2 * count : 2 * count + 2]
        outs = refs[2 * count + 2 : 2 * count + 6]
        joint, beside, total = refs[2 * count + 6 :]
        step = pl.program_id(0)

        @pl.when(step == 0)
        def _():
            joint[...] = jnp.zeros_like(joint)

        for number in range(count):

            @pl.when(step == starts[number])
            def _():
                beside[:, :PAD] = left_refs[2 * number][...]
                beside[:, PAD:] = left_refs[2 * number + 1][...]

        joint[:tokens] = right_ref[...]
        joint[PAD : PAD + tokens] = sibling_ref[...]
        total[...] = jnp.dot(
            beside[...], joint[...], preferred_element_type=jnp.float32
        ).astype(jnp.bfloat16)
        by_columns = split_shapes(rows, columns)[1]
        part_blocks(total, rows, outs, step < columns // tile // 2 if by_columns else None)

    whole = lambda place: pl.BlockSpec((height, PAD), lambda i: (place, 0))
    part = lambda size: pl.BlockSpec((size, tile), lambda i: (0, i))
    shape, by_columns = split_shapes(rows, columns)
    half = columns // tile // 2
    if by_columns:
        top = pl.BlockSpec((2, rows, tile), lambda i: (0, 0, jnp.minimum(i, half - 1)))
        bottom = pl.BlockSpec((2, rows, tile), lambda i: (0, 0, jnp.maximum(i - half, 0)))
    else:
        top = bottom = pl.BlockSpec((2, shape[0], tile), lambda i: (0, 0, i))
    outs = pl.pallas_call(
        kernel,
        grid=(columns // tile,),
        in_specs=[whole(left[3]) for left in lefts for _ in range(2)] + [part(tokens)] * 2,
        out_specs=(top, top, bottom, bottom),
        out_shape=block_shapes(rows, columns),
        scratch_shapes=[
            pltpu.VMEM((2 * PAD, tile), jnp.bfloat16),
            pltpu.VMEM((height, 2 * PAD), jnp.bfloat16),
            pltpu.VMEM((height, tile), jnp.bfloat16),
        ],
        compiler_params=PARAMS,
        cost_estimate=LIGHT,
    )(*[left for pair_of in lefts for left in pair_of[:2]], *right)
    return outs


def block_shapes(rows, columns):
    shape = split_shapes(rows, columns)[0]
    return (jax.ShapeDtypeStruct((2,) + shape, jnp.bfloat16),) * 4


def part_blocks(total, rows, outs, first_half):
    wide = lax.axis_index("wide")
    across, along = (wide >> 1) & 1, (wide >> 2) & 1
    half = rows // 2
    for kept_x in range(2):
        for kept_y in range(2):
            x = across if kept_x else 1 - across
            y = along if kept_y else 1 - along
            start = pl.multiple_of((2 * y + x) * rows, 16)
            top, bottom = outs[1 - kept_x], outs[3 - kept_y]
            if first_half is None:
                top[1 - kept_y] = total[pl.ds(start, half)]
                bottom[1 - kept_x] = total[pl.ds(pl.multiple_of(start + half, 16), half)]
                continue

            @pl.when(first_half)
            def _():
                top[1 - kept_y] = total[pl.ds(start, rows)]

            @pl.when(jnp.logical_not(first_half))
            def _():
                bottom[1 - kept_x] = total[pl.ds(start, rows)]


def unarrange(kind, parts, blocks, got, got_last):
    by_columns = got_last[0].shape[1] == FF // 2
    part_rows, part_columns = got_last[0].shape
    rows = part_rows if by_columns else 2 * part_rows
    columns = 2 * part_columns if by_columns else part_columns
    quarter = columns // 4
    height = rows // parts
    width, column_parts = column_blocks(kind, quarter)

    def kernel(*refs):
        tops, bottoms = refs[:3], refs[3:6]
        outs, held = refs[6:10], refs[10]
        narrow = lax.axis_index("narrow")
        low_bit, high_bit = narrow & 1, narrow >> 1
        top = add_low(tops[0][...], tops[1][...], tops[2][...])
        bottom = add_low(bottoms[0][...], bottoms[1][...], bottoms[2][...])
        if by_columns:
            held[:, :part_columns] = top
            held[:, part_columns:] = bottom
        else:
            held[:part_rows] = top
            held[part_rows:] = bottom
        for owner in range(4):
            for which in range(4):
                low_same, high_same = 1 - which // 2, 1 - which % 2

                @pl.when(
                    ((low_bit == (owner & 1)) == (low_same == 1))
                    & ((high_bit == (owner >> 1)) == (high_same == 1))
                )
                def _():
                    for position, (quarter_of, offset) in enumerate(column_parts):
                        if quarter_of == owner:
                            piece = held[:, position * width : (position + 1) * width]
                            for part in range(parts):
                                start = part * quarter + offset
                                outs[which][:, start : start + width] = piece[
                                    part * height : (part + 1) * height
                                ]

    near = pl.BlockSpec((None, part_rows, part_columns), lambda i: (0, 0, 0))
    full = lambda size, width: pl.BlockSpec((size, width), lambda i: (0, 0))
    shape = jax.ShapeDtypeStruct((height, parts * quarter), jnp.bfloat16)
    return pl.pallas_call(
        kernel,
        grid=(1,),
        in_specs=[near, near, full(part_rows, part_columns)] * 2,
        out_specs=(full(height, parts * quarter),) * 4,
        out_shape=(shape,) * 4,
        scratch_shapes=[pltpu.VMEM((rows, columns), jnp.bfloat16)],
        compiler_params=PARAMS,
        cost_estimate=LIGHT,
    )(blocks[0], got[0], got_last[0], blocks[2], got[1], got_last[1])


def add_low(*terms):
    return sum(term.astype(jnp.float32) for term in terms).astype(jnp.bfloat16)


def pick(value, index, dim=0):
    return lax.dynamic_index_in_dim(value, index, dim, keepdims=False)


def halves_of(value, core):
    middle = value.shape[-1] // 2
    first, second = value[..., :middle], value[..., middle:]
    return jnp.where(core == 0, first, second), jnp.where(core == 0, second, first)


def inner(value):
    width = value.shape[-1] // 8
    return jnp.concatenate(
        [
            value[..., (2 * n + p) * width : (2 * n + p + 1) * width]
            for p in range(2)
            for n in range(4)
        ],
        axis=-1,
    )


def outer(value):
    width = value.shape[-1] // 8
    return jnp.concatenate(
        [
            value[..., (4 * p + n) * width : (4 * p + n + 1) * width]
            for n in range(4)
            for p in range(2)
        ],
        axis=-1,
    )


def upright(value):
    return jnp.pad(value, ((0, PAD - value.shape[0]), (0, 0))).T


KEEP_NEAR, KEEP_FAR, SEND_NEAR, SEND_FAR = range(4)


def send(blocks):
    return swap_wide(blocks[1], ACROSS), swap_wide(blocks[3], ALONG)


def forward(blocks, got):
    return (
        swap_wide(add_low(blocks[0][1], got[0][1]), ALONG),
        swap_wide(add_low(blocks[2][1], got[1][1]), ACROSS),
    )


def narrow_first(quarters):
    return swap_narrow(quarters[SEND_FAR], 1), swap_narrow(quarters[SEND_NEAR], 1)


def narrow_second(quarters, got):
    return swap_narrow(add_low(quarters[KEEP_FAR], got[0]), 2)


def finish(quarters, got, got_last):
    return (
        quarters[KEEP_NEAR].astype(jnp.float32)
        + got[1].astype(jnp.float32)
        + got_last.astype(jnp.float32)
    )


def across_narrow(shard):
    return tuple(swap_narrow(shard, bit) for bit in (1, 2, 3))


def gather_first(block):
    return swap_wide(block, ACROSS), swap_wide(block, ALONG)


def gather_second(first):
    return (
        swap_wide(split_block(first[0])[0], ALONG),
        swap_wide(split_block(first[1])[1], ACROSS),
    )


def swap_sides(first):
    return swap_wide(first[0], CORE), swap_wide(first[1], CORE)


def ends_of(block, second):
    if split_shapes(*block.shape)[1]:
        return jnp.concatenate([block, jnp.concatenate(second, axis=1)], axis=0)
    if block.shape[0] > 2 * D // 8:
        return jnp.concatenate([block, *second], axis=0)
    return jnp.stack([block, jnp.concatenate(second, axis=0)]).reshape(-1, block.shape[1])


def line_gradient(lefts, rights, rights_sibling):
    tokens, height = lefts[0].shape
    width = rights.shape[2]
    rows = height // 4

    def kernel(*refs):
        right_ref, sibling_ref = refs[8:10]
        outs, total = refs[10:14], refs[14]
        chip = lax.axis_index("wide") >> 1
        for number in range(8):
            right = (right_ref, sibling_ref)[number // 4][number % 4, :tokens]
            part = lax.dot_general(
                right,
                refs[number][...],
                (((0,), (0,)), ((), ())),
                preferred_element_type=jnp.float32,
            )
            total[...] = part if number == 0 else total[...] + part
        sums = sum(
            ref[number, tokens:].astype(jnp.float32)
            for ref in (right_ref, sibling_ref)
            for number in range(4)
        )
        for ref in outs:
            for row in range(VECTOR_ROWS):
                ref[rows // 2 + row // 2, (row % 2) * width : (row % 2 + 1) * width] = sums[
                    row
                ].astype(jnp.bfloat16)
        for owner in range(4):
            block = total[:, owner * rows : (owner + 1) * rows].T.astype(jnp.bfloat16)
            for relative in range(4):

                @pl.when((chip ^ relative) == owner)
                def _():
                    outs[relative][: rows // 2, :width] = block[: rows // 2]
                    outs[relative][: rows // 2, width:] = block[rows // 2 :]

    shape = jax.ShapeDtypeStruct((rows // 2 + 16, 2 * width), jnp.bfloat16)
    return pl.pallas_call(
        kernel,
        out_shape=(shape,) * 4,
        scratch_shapes=[pltpu.VMEM((width, height), jnp.float32)],
        compiler_params=PARAMS,
        cost_estimate=LIGHT,
    )(*lefts, rights, rights_sibling)


def turned_update(weight, moment, square, terms, parts, step_rate):
    rows, quarter = weight.shape
    height = rows // parts

    def kernel(*refs):
        weight_ref, moment_ref, square_ref = refs[: 3]
        total = sum(ref[...].astype(jnp.float32) for ref in refs[3 : 3 + len(terms)])
        outs, gradient = refs[3 + len(terms) : 6 + len(terms)], refs[-1]
        for part in range(parts):
            gradient[part * height : (part + 1) * height] = total[
                :, part * quarter : (part + 1) * quarter
            ]
        new = adamw_update(
            weight_ref[...], moment_ref[...], square_ref[...], gradient[...].T, step_rate
        )
        for out, value in zip(outs, new):
            out[...] = value

    new = pl.pallas_call(
        kernel,
        out_shape=(jax.ShapeDtypeStruct((quarter, rows), jnp.float32),) * 3,
        scratch_shapes=[pltpu.VMEM((rows, quarter), jnp.float32)],
        compiler_params=PARAMS,
        cost_estimate=LIGHT,
    )(weight.T, moment.T, square.T, *terms)
    return tuple(value.T for value in new)


def heavy(kernel, outs, scratch, weights, operands):
    return pl.pallas_call(
        kernel,
        in_specs=[pl.BlockSpec(memory_space=pl.ANY)] * len(weights)
        + [pl.BlockSpec(memory_space=pltpu.VMEM)] * len(operands),
        out_shape=tuple(jax.ShapeDtypeStruct(shape, dtype) for shape, dtype in outs),
        scratch_shapes=scratch,
        compiler_params=PARAMS,
        cost_estimate=LIGHT,
    )(*weights, *operands)


def dot_rows(left, right):
    return lax.dot_general(left, right, (((1,), (1,)), ((), ())), preferred_element_type=jnp.float32)


def dot_depth(left, right):
    return lax.dot_general(left, right, (((0,), (0,)), ((), ())), preferred_element_type=jnp.float32)


def store_upright(value, padded, mine, other):
    features = value.shape[1]
    padded[: value.shape[0]] = value
    turned = padded[...].T.astype(jnp.bfloat16)
    core = lax.axis_index("wide") & 1

    @pl.when(core == 0)
    def _():
        mine[...] = turned[: features // 2]
        other[...] = turned[features // 2 :]

    @pl.when(core == 1)
    def _():
        other[...] = turned[: features // 2]
        mine[...] = turned[features // 2 :]


def merge_forward(joined, weight, bias, gain, shift):
    length = joined.shape[0]

    def kernel(*refs):
        joined_ref, bias_ref, gain_ref, shift_ref = refs[6:10]
        stream, entry, up_mine, up_other, full, sems, padded = refs[10:]
        weight_in = Fetch(refs[:6], full, sems)
        padded[...] = jnp.zeros_like(padded)
        weight_in.wait()
        stream[...] = product(joined_ref[...], full[...]) + bias_ref[...]
        normed = normalize(stream[...])[0]
        value = (normed * gain_ref[...] + shift_ref[...]).astype(jnp.bfloat16)
        entry[...] = value
        store_upright(value.astype(jnp.float32), padded, up_mine, up_other)

    return heavy(
        kernel,
        [
            ((length, D), jnp.float32),
            ((length, D), jnp.bfloat16),
            ((D // 2, PAD), jnp.bfloat16),
            ((D // 2, PAD), jnp.bfloat16),
        ],
        weight_scratch(2 * D, D) + [pltpu.VMEM((PAD, D), jnp.float32)],
        weight,
        (joined, bias, gain, shift),
    )


def attend_head(heads, head, chances_ref, slot):
    at = head * HD
    queries = heads[:, at : at + HD]
    keys = heads[:, D + at : D + at + HD]
    values = heads[:, 2 * D + at : 2 * D + at + HD]
    logits = dot_rows(queries, keys) * HD ** (-0.5)
    powers = jnp.exp(logits - jnp.max(logits, axis=-1, keepdims=True))
    chances = powers / jnp.sum(powers, axis=-1, keepdims=True)
    chances_ref[slot] = chances
    return product(chances.astype(jnp.bfloat16), values).astype(jnp.bfloat16)


FIRST = 15


def attend_first(entry, weight):
    length = entry.shape[0]

    def kernel(*refs):
        entry_ref, heads, chances_ref, mix_ref, full, sems = refs[6:]
        weight_in = Fetch(refs[:6], full, sems)
        for part in range(3):
            weight_in.wait(part)
            columns = slice(part * D, (part + 1) * D)
            heads[:, columns] = product(entry_ref[...], full[:, columns]).astype(jnp.bfloat16)
        for head in range(FIRST):
            mix_ref[:, head * HD : (head + 1) * HD] = attend_head(heads, head, chances_ref, head)

    return heavy(
        kernel,
        [
            ((length, 3 * D), jnp.bfloat16),
            ((FIRST, length, length), jnp.float32),
            ((length, FIRST * HD), jnp.bfloat16),
        ],
        weight_scratch(D, 3 * D, 3),
        weight,
        (entry,),
    )


def attend_second(heads, mix_first, weight, stream_zero, bias, gain, shift):
    length = heads.shape[0]
    half = D // 2

    def kernel(*refs):
        heads_ref, first_ref, zero_ref, bias_ref, gain_ref, shift_ref = refs[6:12]
        chances_ref, stream, value_ref, up_mine, up_other, full, sems, mixed, padded = refs[12:]
        weight_in = Fetch(refs[:6], full, sems, 3 * D)
        padded[...] = jnp.zeros_like(padded)
        mixed[:, : FIRST * HD] = first_ref[...]
        for head in range(FIRST, H):
            mixed[:, head * HD : (head + 1) * HD] = attend_head(
                heads_ref, head, chances_ref, head - FIRST
            )
        weight_in.wait()
        stream[...] = zero_ref[...] + product(mixed[...], full[...]) + bias_ref[...]
        store_upright(
            mixed[...].astype(jnp.float32), padded, up_mine.at[pl.ds(0, half)], up_other.at[pl.ds(0, half)]
        )
        normed = normalize(stream[...])[0]
        value = (normed * gain_ref[...] + shift_ref[...]).astype(jnp.bfloat16)
        value_ref[...] = value
        store_upright(
            value.astype(jnp.float32), padded, up_mine.at[pl.ds(half, half)], up_other.at[pl.ds(half, half)]
        )

    return heavy(
        kernel,
        [
            ((H - FIRST, length, length), jnp.float32),
            ((length, D), jnp.float32),
            ((length, D), jnp.bfloat16),
            ((D, PAD), jnp.bfloat16),
            ((D, PAD), jnp.bfloat16),
        ],
        weight_scratch(D, D)
        + [pltpu.VMEM((length, D), jnp.bfloat16), pltpu.VMEM((PAD, D), jnp.float32)],
        weight,
        (heads, mix_first, stream_zero, bias, gain, shift),
    )


def expand_forward(entry, weight, bias):
    length = entry.shape[0]

    def kernel(*refs):
        entry_ref, bias_ref = refs[6:8]
        active_ref, slope_ref, up_mine, up_other, full, sems, padded = refs[8:]
        core = lax.axis_index("wide") & 1
        weight_in = Fetch(refs[:6], full, sems)
        padded[...] = jnp.zeros_like(padded)
        for step in range(FF // D):
            columns = slice(step * D, (step + 1) * D)
            weight_in.wait(step)
            value = product(entry_ref[...], full[:, columns]) + bias_ref[:, columns]
            inside = 0.5 * (1.0 + lax.erf(value * (0.5**0.5)))
            bell = jnp.exp(-0.5 * value * value) * (2.0 * jnp.pi) ** -0.5
            active = (value * inside).astype(jnp.bfloat16)
            slope_ref[:, columns] = inside + value * bell
            active_ref[:, columns] = active
            padded[:length] = active.astype(jnp.float32)
            turned = padded[...].T.astype(jnp.bfloat16)
            rows = slice((step % 2) * D, (step % 2 + 1) * D)

            @pl.when(core == step // 2)
            def _():
                up_mine[rows] = turned

            @pl.when(core != step // 2)
            def _():
                up_other[rows] = turned

    return heavy(
        kernel,
        [
            ((length, FF), jnp.bfloat16),
            ((length, FF), jnp.float32),
            ((FF // 2, PAD), jnp.bfloat16),
            ((FF // 2, PAD), jnp.bfloat16),
        ],
        weight_scratch(D, FF, FF // D) + [pltpu.VMEM((PAD, D), jnp.float32)],
        weight,
        (entry, bias),
    )


def hidden_backward(pulled, weight, slope):
    length = pulled.shape[0]

    def kernel(*refs):
        pulled_ref, slope_ref, low_ref, sum_ref, full, sems = refs[6:]
        Fetch(refs[:6], full, sems).wait()
        for step in range(FF // D):
            columns = slice(step * D, (step + 1) * D)
            delta = dot_rows(pulled_ref[...], full[columns]) * slope_ref[:, columns]
            low_ref[:, columns] = delta.astype(jnp.bfloat16)
            sum_ref[:, columns] = jnp.sum(delta, axis=0, keepdims=True)

    return heavy(
        kernel,
        [((length, FF), jnp.bfloat16), ((1, FF), jnp.float32)],
        weight_scratch(FF, D),
        weight,
        (pulled, slope),
    )


def expand_backward(hidden_low, weight, mixed_weight, pulled, stream_one, gain):
    length = pulled.shape[0]

    def kernel(*refs):
        hidden_ref, pulled_ref, stream_ref, gain_ref = refs[12:16]
        one_ref, low_ref, sums, mix_ref, full, sems, output, output_sems, delta = refs[16:]
        weight_in = Fetch(refs[:6], full, sems)
        output_in = Fetch(refs[6:12], output, output_sems, 3 * D)
        for step in range(FF // D):
            columns = slice(step * D, (step + 1) * D)
            weight_in.wait(step)
            part = dot_rows(hidden_ref[:, columns], full[:, columns])
            delta[...] = part if step == 0 else delta[...] + part
        value = delta[...]
        normed, inverse = normalize(stream_ref[...])
        upstream = pulled_ref[...].astype(jnp.float32)
        one = upstream + norm_back(value * gain_ref[...], normed, inverse)
        one_ref[...] = one
        low_value = one.astype(jnp.bfloat16)
        low_ref[...] = low_value
        sums[0:1] = jnp.sum(one, axis=0, keepdims=True)
        sums[1:2] = jnp.sum(value * normed, axis=0, keepdims=True)
        sums[2:3] = jnp.sum(value, axis=0, keepdims=True)
        sums[3:4] = jnp.sum(upstream, axis=0, keepdims=True)
        output_in.wait()
        mix_ref[...] = dot_rows(low_value, output[...]).astype(jnp.bfloat16)

    return heavy(
        kernel,
        [
            ((length, D), jnp.float32),
            ((length, D), jnp.bfloat16),
            ((4, D), jnp.float32),
            ((length, D), jnp.bfloat16),
        ],
        weight_scratch(D, FF, FF // D)
        + weight_scratch(D, D)
        + [pltpu.VMEM((length, D), jnp.float32)],
        (*weight, *mixed_weight),
        (hidden_low, pulled, stream_one, gain),
    )


def attend_backward(heads, chances_first, chances_second, delta_mixture, stream_low):
    length = heads.shape[0]
    scale = HD ** (-0.5)

    def kernel(heads_ref, first_ref, second_ref, delta_ref, stream_ref, mixed):
        mixed[:, 3 * D :] = stream_ref[...]
        for head in range(H):
            at = head * HD
            queries = heads_ref[:, at : at + HD]
            keys = heads_ref[:, D + at : D + at + HD]
            values = heads_ref[:, 2 * D + at : 2 * D + at + HD]
            delta = delta_ref[:, at : at + HD]
            chances = first_ref[head] if head < FIRST else second_ref[head - FIRST]
            pull = dot_rows(delta, values)
            inner_sum = jnp.sum(chances * pull, axis=-1, keepdims=True)
            scores = (scale * (chances * (pull - inner_sum))).astype(jnp.bfloat16)
            mixed[:, at : at + HD] = product(scores, keys).astype(jnp.bfloat16)
            mixed[:, D + at : D + at + HD] = dot_depth(scores, queries).astype(jnp.bfloat16)
            mixed[:, 2 * D + at : 2 * D + at + HD] = dot_depth(
                chances.astype(jnp.bfloat16), delta
            ).astype(jnp.bfloat16)

    return heavy(
        kernel,
        [((length, 4 * D), jnp.bfloat16)],
        [],
        (),
        (heads, chances_first, chances_second, delta_mixture, stream_low),
    )[0]


def entry_backward(delta_mixed, weight, delta_one, stream_zero, gain, sums_two, hidden_sum):
    length = delta_mixed.shape[0]
    width = D // 8
    tall = -(-(length + VECTOR_ROWS) // 16) * 16

    def kernel(*refs):
        mixed_ref, one_ref, stream_ref, gain_ref, sums_ref, hidden_ref, low_ref = refs[6:13]
        quarters, (full, sems, delta, held) = refs[13:17], refs[17:]
        weight_in = Fetch(refs[:6], full, sems)
        for step in range(3):
            columns = slice(step * D, (step + 1) * D)
            weight_in.wait(step)
            part = dot_rows(mixed_ref[:, columns], full[:, columns])
            delta[...] = part if step == 0 else delta[...] + part
        value = delta[...]
        normed, inverse = normalize(stream_ref[...])
        zero = one_ref[...] + norm_back(value * gain_ref[...], normed, inverse)
        zero_low = zero.astype(jnp.bfloat16)
        low_ref[...] = zero_low
        sums = [jnp.sum(part, axis=0, keepdims=True) for part in (zero, value * normed, value)]
        sums += [sums_ref[row : row + 1] for row in range(4)]
        held[...] = jnp.zeros_like(held)
        for block in range(VECTOR_ROWS * 8):
            owner, place = block // (2 * VECTOR_ROWS), block % (2 * VECTOR_ROWS)
            if block < 56:
                source, wide = sums[block // 8], block % 8
                start = (4 * (wide % 2) + wide // 2) * width
            else:
                source, wide = hidden_ref, (block - 56) // 4
                start = (4 * (wide % 2) + wide // 2) * 4 * width + (block % 4) * width
            columns = slice((place % 2) * width, (place % 2 + 1) * width)
            held[owner, place // 2 : place // 2 + 1, columns] = source[:, start : start + width]
        narrow = lax.axis_index("narrow")
        for owner in range(4):
            for relative in range(4):

                @pl.when((narrow ^ relative) == owner)
                def _():
                    for parity in range(2):
                        start = (4 * parity + owner) * width
                        quarters[relative][:length, parity * width : (parity + 1) * width] = (
                            zero_low[:, start : start + width]
                        )
                    quarters[relative][length:] = held[owner, : tall - length].astype(jnp.bfloat16)

    return heavy(
        kernel,
        [((length, D), jnp.bfloat16)] + [((tall, D // 4), jnp.bfloat16)] * 4,
        weight_scratch(D, 3 * D, 3)
        + [pltpu.VMEM((length, D), jnp.float32), pltpu.VMEM((4, 16, D // 4), jnp.float32)],
        weight,
        (delta_mixed, delta_one, stream_zero, gain, sums_two, hidden_sum),
    )


def joined_backward(zero_low, weight):
    length = zero_low.shape[0]
    width = 2 * D // 8

    def kernel(*refs):
        zero_ref, first_ref, second_ref, full, sems = refs[6:]
        Fetch(refs[:6], full, sems).wait()
        for parity in range(2):
            delta = dot_rows(zero_ref[...], full[parity * D : (parity + 1) * D])
            delta = delta.astype(jnp.bfloat16)
            for number in range(4):
                target = (first_ref, second_ref)[number // 2]
                column = (2 * (number % 2) + parity) * width
                target[:, column : column + width] = delta[:, number * width : (number + 1) * width]

    out = ((length, D), jnp.bfloat16)
    return heavy(kernel, [out, out], weight_scratch(2 * D, D), weight, (zero_low,))


def shrink_forward(active, weight, stream_one, bias):
    length = active.shape[0]
    width = D // 8

    def kernel(*refs):
        active_ref, stream_ref, bias_ref, out_ref, full, sems = refs[6:]
        Fetch(refs[:6], full, sems).wait()
        total = (
            stream_ref[...] + product(active_ref[...], full[...]) + bias_ref[...]
        ).astype(jnp.bfloat16)
        for parity in range(2):
            for number in range(4):
                column = (2 * number + parity) * width
                source = (4 * parity + number) * width
                out_ref[:, column : column + width] = total[:, source : source + width]

    return heavy(
        kernel,
        [((length, D), jnp.bfloat16)],
        weight_scratch(FF, D),
        weight,
        (active, stream_one, bias),
    )[0]


def on_device(
    inputs,
    skip_tokens,
    cotangent,
    merge_weight,
    merge_moment,
    merge_square,
    attend_weight,
    attend_moment,
    attend_square,
    output_weight,
    output_moment,
    output_square,
    expand_weight,
    expand_moment,
    expand_square,
    shrink_weight,
    shrink_moment,
    shrink_square,
    vectors,
    vector_moment,
    vector_square,
):
    core = spot()[0]
    low = jnp.bfloat16
    columns = attend_weight.shape[1]

    merge_low = fold(merge_weight.astype(low))
    width = merge_low.shape[1]
    count = vectors.shape[0]
    vector_rows = jnp.pad(vectors.astype(low), (0, 16 * width - count)).reshape(16, width)
    merge_low = jnp.concatenate([merge_low, vector_rows], axis=0)
    merge_others = across_narrow(merge_low)
    mixed_low = jnp.concatenate([attend_weight.astype(low), output_weight.astype(low)], axis=1)
    joined = inner(jnp.concatenate([inputs[0], skip_tokens[0]], axis=-1))
    joined_mine, joined_other = halves_of(joined, core)
    pulled = inner(cotangent[0])
    merge_others, mixed_low, joined, joined_mine, joined_other, pulled = together(
        merge_others, mixed_low, joined, joined_mine, joined_other, pulled
    )
    merge_block, vector_parts = arrange("merge", 2, merge_low, merge_others, 16)
    merge_first = gather_first(merge_block)
    mixed_far = swap_narrow(mixed_low, 2)
    mixed_near = swap_narrow(mixed_low, 1)
    expand_low = expand_weight.astype(low)
    known_sibling = swap_wide(jnp.concatenate([joined_other, pulled], axis=1), CORE)
    merge_first, mixed_far, vector_parts, expand_low, known_sibling = together(
        merge_first, mixed_far, vector_parts, expand_low, known_sibling
    )
    joined_sibling, pulled_sibling = known_sibling[:, :D], known_sibling[:, D:]
    merge_second = gather_second(merge_first)
    merge_sides = swap_sides(merge_first)
    mixed_last = swap_narrow(mixed_far, 1)
    shrink_low = fold(shrink_weight.astype(low))
    pieces = unpack(vector_parts.reshape(4, -1)[:, :count].reshape(-1).astype(jnp.float32))
    pieces = tuple(inner(piece)[None] for piece in pieces)
    merge_second, merge_sides, mixed_near, mixed_last, shrink_low, pieces = together(
        merge_second, merge_sides, mixed_near, mixed_last, shrink_low, pieces
    )
    skip_bias, gain_one, bias_one, output_bias, gain_two, bias_two, shrink_bias, expand_bias = pieces
    mixed_block = arrange("attend_output", 1, mixed_low, (mixed_near, mixed_far, mixed_last))[0]
    mixed_first = gather_first(mixed_block)
    expand_far = swap_narrow(expand_low, 2)
    expand_near = swap_narrow(expand_low, 1)
    merge_ends = ends_of(merge_block, merge_second)
    merge_pieces = (merge_ends, *merge_first, swap_wide(merge_ends, CORE), *merge_sides)
    stream_zero, attend_input, attend_up, attend_up_other = merge_forward(
        joined, merge_pieces, skip_bias, gain_one, bias_one
    )
    mixed_first, expand_far, expand_near, stream_zero, attend_input, attend_up_other = together(
        mixed_first, expand_far, expand_near, stream_zero, attend_input, attend_up_other
    )
    mixed_second = gather_second(mixed_first)
    mixed_sides = swap_sides(mixed_first)
    expand_last = swap_narrow(expand_far, 1)
    expand_block = arrange("expand", 1, expand_low, (expand_near, expand_far, expand_last))[0]
    mixed_second, mixed_sides, expand_block = together(mixed_second, mixed_sides, expand_block)
    expand_first = gather_first(expand_block)
    shrink_far = swap_narrow(shrink_low, 2)
    shrink_near = swap_narrow(shrink_low, 1)
    mixed_ends = ends_of(mixed_block, mixed_second)
    mixed_pieces = (mixed_ends, *mixed_first, swap_wide(mixed_ends, CORE), *mixed_sides)
    heads, chances_first, mix_first = attend_first(attend_input, mixed_pieces)
    expand_first, shrink_far, shrink_near, heads, mix_first = together(
        expand_first, shrink_far, shrink_near, heads, mix_first
    )
    expand_second = gather_second(expand_first)
    expand_sides = swap_sides(expand_first)
    shrink_last = swap_narrow(shrink_far, 1)
    chances_second, stream_one, expand_input, ups, ups_other = attend_second(
        heads, mix_first, mixed_pieces, stream_zero, output_bias, gain_two, bias_two
    )
    shrink_block = arrange("shrink", 4, shrink_low, (shrink_near, shrink_far, shrink_last))[0]
    (
        expand_second,
        expand_sides,
        shrink_block,
        expand_input,
        ups_other,
        joined_mine,
        joined_sibling,
    ) = together(
        expand_second,
        expand_sides,
        shrink_block,
        expand_input,
        ups_other,
        joined_mine,
        joined_sibling,
    )
    shrink_first = gather_first(shrink_block)
    expand_ends = ends_of(expand_block, expand_second)
    expand_pieces = (expand_ends, *expand_first, swap_wide(expand_ends, CORE), *expand_sides)
    joined_far = swap_narrow(joined_mine, 2)
    joined_near = swap_narrow(joined_mine, 1)
    active, slope, active_up, active_up_other = expand_forward(
        expand_input, expand_pieces, expand_bias
    )
    shrink_first, joined_far, joined_near, active, slope, active_up, active_up_other = together(
        shrink_first, joined_far, joined_near, active, slope, active_up, active_up_other
    )
    shrink_second = gather_second(shrink_first)
    shrink_sides = swap_sides(shrink_first)
    active_up_sibling = swap_wide(active_up_other, CORE)
    shrink_blocks = pair_gradient([(active_up, active_up_sibling, D, 0, FF // 2)], (pulled, pulled_sibling))
    shrink_second, shrink_sides, shrink_blocks, joined_far, joined_sibling, ups_other = together(
        shrink_second, shrink_sides, shrink_blocks, joined_far, joined_sibling, ups_other
    )
    shrink_got = send(shrink_blocks)
    shrink_ends = ends_of(shrink_block, shrink_second)
    shrink_pieces = (shrink_ends, *shrink_first, swap_wide(shrink_ends, CORE), *shrink_sides)
    sibling_far = swap_narrow(joined_sibling, 2)
    joined_last = swap_narrow(joined_far, 1)
    hidden_low, hidden_sum = hidden_backward(pulled, shrink_pieces, slope)
    outputs = shrink_forward(active, shrink_pieces, stream_one, shrink_bias)[None]
    (
        shrink_got,
        sibling_far,
        joined_last,
        hidden_low,
        hidden_sum,
        outputs,
        joined_sibling,
        ups_other,
        attend_up_other,
    ) = together(
        shrink_got,
        sibling_far,
        joined_last,
        hidden_low,
        hidden_sum,
        outputs,
        joined_sibling,
        ups_other,
        attend_up_other,
    )
    shrink_got_last = forward(shrink_blocks, shrink_got)
    hidden_sibling = swap_wide(hidden_low, CORE)
    ups_sibling = swap_wide(ups_other, CORE)
    sibling_near = swap_narrow(joined_sibling, 1)
    half = D // 2
    expand_blocks = pair_gradient(
        [(ups, ups_sibling, FF, 1, half)], (hidden_low, hidden_sibling)
    )
    shrink_got_last, sibling_near, expand_blocks, hidden_low, sibling_far = together(
        shrink_got_last, sibling_near, expand_blocks, hidden_low, sibling_far
    )
    expand_got = send(expand_blocks)
    sibling_last = swap_narrow(sibling_far, 1)
    attend_up_sibling = swap_wide(attend_up_other, CORE)
    delta_one, stream_low, sums_two, delta_mixture = expand_backward(
        hidden_low, expand_pieces, mixed_pieces, pulled, stream_one, gain_two
    )
    delta_mixed = attend_backward(heads, chances_first, chances_second, delta_mixture, stream_low)
    expand_got, sibling_last, delta_mixed, attend_up_sibling = together(
        expand_got, sibling_last, delta_mixed, attend_up_sibling
    )
    expand_got_last = forward(expand_blocks, expand_got)
    mixed_sibling = swap_wide(delta_mixed, CORE)
    shrink_quarters = unarrange("shrink", 4, shrink_blocks, shrink_got, shrink_got_last)
    shrink_narrow = narrow_first(shrink_quarters)
    mixed_blocks = pair_gradient(
        [(attend_up, attend_up_sibling, 3 * D, 0, half), (ups, ups_sibling, D, 0, half)],
        (delta_mixed, mixed_sibling),
    )
    expand_got_last, shrink_narrow, mixed_blocks, delta_mixed = together(
        expand_got_last, shrink_narrow, mixed_blocks, delta_mixed
    )
    mixed_got = send(mixed_blocks)
    expand_quarters = unarrange("expand", 1, expand_blocks, expand_got, expand_got_last)
    expand_narrow = narrow_first(expand_quarters)
    shrink_end = narrow_second(shrink_quarters, shrink_narrow)
    zero_low, *zero_quarters = entry_backward(
        delta_mixed, mixed_pieces, delta_one, stream_zero, gain_one, sums_two, hidden_sum
    )
    mixed_got, expand_narrow, zero_low, zero_quarters, shrink_end = together(
        mixed_got, expand_narrow, zero_low, zero_quarters, shrink_end
    )
    mixed_got_last = forward(mixed_blocks, mixed_got)
    zero_got = tuple(swap_narrow(zero_quarters[bit], bit) for bit in (1, 2, 3))
    input_gradient, skip_gradient = joined_backward(zero_low, merge_pieces)
    mixed_got_last, zero_got, input_gradient, skip_gradient, shrink_end = together(
        mixed_got_last, zero_got, input_gradient, skip_gradient, shrink_end
    )
    mixed_quarters = unarrange("attend_output", 1, mixed_blocks, mixed_got, mixed_got_last)
    mixed_far_got = swap_narrow(mixed_quarters[SEND_FAR], 1)
    expand_end = narrow_second(expand_quarters, expand_narrow)
    zero_line = jnp.stack([zero_quarters[0], *zero_got])
    zero_line_sibling = swap_wide(zero_line, CORE)
    merge_blocks = line_gradient(
        (
            joined_mine,
            joined_near,
            joined_far,
            joined_last,
            joined_sibling,
            sibling_near,
            sibling_far,
            sibling_last,
        ),
        zero_line,
        zero_line_sibling,
    )
    mixed_far_got, mixed_quarters, merge_blocks, shrink_end, expand_end = together(
        mixed_far_got, mixed_quarters, merge_blocks, shrink_end, expand_end
    )
    mixed_end = narrow_second(mixed_quarters, (mixed_far_got,))
    mixed_near_got = swap_narrow(mixed_quarters[SEND_NEAR], 1)
    merge_got = (
        swap_wide(merge_blocks[1], ACROSS),
        swap_wide(merge_blocks[2], ALONG),
        swap_wide(merge_blocks[3], ACROSS + ALONG),
    )
    shrink_new = turned_update(
        shrink_weight,
        shrink_moment,
        shrink_square,
        (shrink_quarters[KEEP_NEAR], shrink_narrow[1], shrink_end),
        4,
        rate_shrink,
    )
    expand_new = adamw_update(
        expand_weight,
        expand_moment,
        expand_square,
        finish(expand_quarters, expand_narrow, expand_end),
        rate_expand,
    )
    tall = merge_blocks[0].shape[0] - 16
    merge_sum = sum(term.astype(jnp.float32) for term in (merge_blocks[0], *merge_got))
    merge_new = adamw_update(
        merge_weight,
        merge_moment,
        merge_square,
        unfold(merge_sum[:tall], merge_weight.shape[0]),
        rate_merge,
    )
    vector_total = merge_sum[tall:].reshape(-1)[: vectors.shape[0]]
    vector_new = adamw_update(vectors, vector_moment, vector_square, vector_total, rate_vector)
    merge_new, mixed_end, mixed_near_got, vector_new, shrink_new, expand_new = together(
        merge_new, mixed_end, mixed_near_got, vector_new, shrink_new, expand_new
    )
    mixed_total = finish(mixed_quarters, (mixed_far_got, mixed_near_got), mixed_end)
    attend_new = adamw_update(
        attend_weight, attend_moment, attend_square, mixed_total[:, :columns], rate_attend
    )
    output_new = adamw_update(
        output_weight, output_moment, output_square, mixed_total[:, columns:], rate_output
    )
    return (
        outputs,
        input_gradient[None],
        skip_gradient[None],
        *merge_new,
        *attend_new,
        *output_new,
        *expand_new,
        *shrink_new,
        *vector_new,
    )


def solution(mesh):
    in_specs = (
        P(("wide", "narrow"), None, None),
        P(("wide", "narrow"), None, None),
        P(("wide", "narrow"), None, None),
        P("wide", "narrow"),
        P("wide", "narrow"),
        P("wide", "narrow"),
        P("wide", "narrow"),
        P("wide", "narrow"),
        P("wide", "narrow"),
        P("wide", "narrow"),
        P("wide", "narrow"),
        P("wide", "narrow"),
        P("wide", "narrow"),
        P("wide", "narrow"),
        P("wide", "narrow"),
        P("wide", "narrow"),
        P("wide", "narrow"),
        P("wide", "narrow"),
        P("narrow"),
        P("narrow"),
        P("narrow"),
    )
    out_specs = (
        P(("wide", "narrow"), None, None),
        P(("wide", "narrow"), None, None),
        P(("wide", "narrow"), None, None),
        P("wide", "narrow"),
        P("wide", "narrow"),
        P("wide", "narrow"),
        P("wide", "narrow"),
        P("wide", "narrow"),
        P("wide", "narrow"),
        P("wide", "narrow"),
        P("wide", "narrow"),
        P("wide", "narrow"),
        P("wide", "narrow"),
        P("wide", "narrow"),
        P("wide", "narrow"),
        P("wide", "narrow"),
        P("wide", "narrow"),
        P("wide", "narrow"),
        P("narrow"),
        P("narrow"),
        P("narrow"),
    )
    tuned = mesh.shape["wide"] == 8 and mesh.shape["narrow"] == 4
    return jax.shard_map(
        on_device if tuned else general_device, mesh=mesh, in_specs=in_specs, out_specs=out_specs, check_vma=False
    )
```

```python
import jax
import jax.numpy as jnp
from jax import lax
from jax.experimental import pallas as pl
from jax.experimental.pallas import tpu as pltpu
from jax.sharding import PartitionSpec as P

D = 1152
FF = 4608
H = 16
HD = 72
STEP = 5


norm_epsilon = 1e-05
adam_epsilon = 1e-08
beta_moment = 0.5
weight_decay = 0.01
rate_merge = 0.04
rate_attend = 0.08
rate_output = 0.6
rate_expand = 0.06
rate_shrink = 0.03
rate_vector = 0.6


def product(left_side, right_side):
    return jnp.dot(left_side, right_side, preferred_element_type=jnp.float32)


def transposed(gradient, matrix):
    return lax.dot_general(
        gradient,
        matrix,
        (((gradient.ndim - 1,), (1,)), ((), ())),
        preferred_element_type=jnp.float32,
    )


def weight_gradient(activations, gradient):
    flat_left = activations.reshape(-1, activations.shape[-1])
    flat_right = gradient.reshape(-1, gradient.shape[-1])
    return lax.dot_general(
        flat_left, flat_right, (((0,), (0,)), ((), ())), preferred_element_type=jnp.float32
    )


def normalize(values):
    centered = values - jnp.mean(values, axis=-1, keepdims=True)
    spread = jnp.mean(centered * centered, axis=-1, keepdims=True)
    inverse = lax.rsqrt(spread + norm_epsilon)
    return (centered * inverse, inverse)


def norm_back(gradient, normed, inverse):
    return inverse * (
        gradient
        - jnp.mean(gradient, axis=-1, keepdims=True)
        - normed * jnp.mean(gradient * normed, axis=-1, keepdims=True)
    )


def row_sum(values):
    return jnp.sum(values, axis=(0, 1))


def unpack(packed):
    return tuple((packed[position * D : (position + 1) * D] for position in range(7))) + (
        packed[7 * D : 7 * D + FF],
    )


def gaussian_unit(values):
    return jax.nn.gelu(values, approximate=False)


def adamw_update(weight, moment, square, gradient, step_rate):
    moment_new = beta_moment * moment + (1.0 - beta_moment) * gradient
    square_new = beta_moment * square + (1.0 - beta_moment) * gradient * gradient
    correct = 1.0 - beta_moment**STEP
    direction = moment_new / correct / (jnp.sqrt(square_new / correct) + adam_epsilon)
    return (weight - step_rate * (direction + weight_decay * weight), moment_new, square_new)


def general_device(
    inputs,
    skip_tokens,
    cotangent,
    merge_weight,
    merge_moment,
    merge_square,
    attend_weight,
    attend_moment,
    attend_square,
    output_weight,
    output_moment,
    output_square,
    expand_weight,
    expand_moment,
    expand_square,
    shrink_weight,
    shrink_moment,
    shrink_square,
    vectors,
    vector_moment,
    vector_square,
):
    merge_low = merge_weight.astype(jnp.bfloat16)
    attend_low = attend_weight.astype(jnp.bfloat16)
    output_low = output_weight.astype(jnp.bfloat16)
    expand_low = expand_weight.astype(jnp.bfloat16)
    shrink_low = shrink_weight.astype(jnp.bfloat16)
    vector_low = vectors.astype(jnp.bfloat16)
    columns = (
        lax.all_gather(merge_low, "narrow", axis=1, tiled=True),
        lax.all_gather(attend_low, "narrow", axis=1, tiled=True),
        lax.all_gather(output_low, "narrow", axis=1, tiled=True),
        lax.all_gather(expand_low, "narrow", axis=1, tiled=True),
        lax.all_gather(shrink_low, "narrow", axis=1, tiled=True),
        lax.all_gather(vector_low, "narrow", axis=0, tiled=True),
    )
    matrices = (
        lax.all_gather(columns[0], "wide", axis=0, tiled=True),
        lax.all_gather(columns[1], "wide", axis=0, tiled=True),
        lax.all_gather(columns[2], "wide", axis=0, tiled=True),
        lax.all_gather(columns[3], "wide", axis=0, tiled=True),
        lax.all_gather(columns[4], "wide", axis=0, tiled=True),
    )
    skip_bias, gain_one, bias_one, output_bias, gain_two, bias_two, shrink_bias, expand_bias = (
        unpack(columns[5].astype(jnp.float32))
    )
    images = inputs.shape[0]
    length = inputs.shape[1]
    softmax_scale = HD ** (-0.5)
    joined = jnp.concatenate([inputs, skip_tokens], axis=-1)
    stream_zero = product(joined, matrices[0]) + skip_bias
    normed_one, inverse_one = normalize(stream_zero)
    attend_input = (normed_one * gain_one + bias_one).astype(jnp.bfloat16)
    mixed_heads = product(attend_input, matrices[1]).astype(jnp.bfloat16)
    query_heads = mixed_heads[..., 0:D].reshape(images, length, H, HD)
    key_heads = mixed_heads[..., D : 2 * D].reshape(images, length, H, HD)
    value_heads = mixed_heads[..., 2 * D : 3 * D].reshape(images, length, H, HD)
    logits = (
        jnp.einsum("blhe,bmhe->bhlm", query_heads, key_heads, preferred_element_type=jnp.float32)
        * softmax_scale
    )
    maxima = jnp.max(logits, axis=-1, keepdims=True)
    log_total = maxima + jnp.log(jnp.sum(jnp.exp(logits - maxima), axis=-1, keepdims=True))
    softmax_low = jnp.exp(logits - log_total).astype(jnp.bfloat16)
    mixture = jnp.einsum(
        "bhlm,bmhe->blhe", softmax_low, value_heads, preferred_element_type=jnp.float32
    )
    mixture = mixture.astype(jnp.bfloat16).reshape(images, length, D)
    stream_one = stream_zero + product(mixture, matrices[2]) + output_bias
    normed_two, inverse_two = normalize(stream_one)
    expand_input = (normed_two * gain_two + bias_two).astype(jnp.bfloat16)
    hidden = product(expand_input, matrices[3]) + expand_bias
    active, pullback = jax.vjp(gaussian_unit, hidden)
    active_low = active.astype(jnp.bfloat16)
    outputs = (stream_one + product(active_low, matrices[4]) + shrink_bias).astype(jnp.bfloat16)
    columns_back = (
        lax.all_gather(merge_low, "narrow", axis=1, tiled=True),
        lax.all_gather(attend_low, "narrow", axis=1, tiled=True),
        lax.all_gather(output_low, "narrow", axis=1, tiled=True),
        lax.all_gather(expand_low, "narrow", axis=1, tiled=True),
        lax.all_gather(shrink_low, "narrow", axis=1, tiled=True),
        lax.all_gather(vector_low, "narrow", axis=0, tiled=True),
    )
    matrices_back = (
        lax.all_gather(columns_back[0], "wide", axis=0, tiled=True),
        lax.all_gather(columns_back[1], "wide", axis=0, tiled=True),
        lax.all_gather(columns_back[2], "wide", axis=0, tiled=True),
        lax.all_gather(columns_back[3], "wide", axis=0, tiled=True),
        lax.all_gather(columns_back[4], "wide", axis=0, tiled=True),
    )
    packed_back = columns_back[5].astype(jnp.float32)
    unpacked = unpack(packed_back)
    gain_first = unpacked[1]
    gain_second = unpacked[4]
    upstream = cotangent.astype(jnp.float32)
    shrink_gradient = weight_gradient(active_low, cotangent)
    delta_active = transposed(cotangent, matrices_back[4])
    delta_hidden = pullback(delta_active)[0]
    hidden_low = delta_hidden.astype(jnp.bfloat16)
    expand_gradient = weight_gradient(expand_input, hidden_low)
    delta_expand = transposed(hidden_low, matrices_back[3])
    delta_one = upstream + norm_back(delta_expand * gain_second, normed_two, inverse_two)
    stream_low = delta_one.astype(jnp.bfloat16)
    output_gradient = weight_gradient(mixture, stream_low)
    delta_mixture = (
        transposed(stream_low, matrices_back[2]).astype(jnp.bfloat16).reshape(images, length, H, HD)
    )
    logits_again = (
        jnp.einsum("blhe,bmhe->bhlm", query_heads, key_heads, preferred_element_type=jnp.float32)
        * softmax_scale
    )
    softmax_again = jnp.exp(logits_again - log_total)
    delta_softmax = jnp.einsum(
        "blhe,bmhe->bhlm", delta_mixture, value_heads, preferred_element_type=jnp.float32
    )
    delta_values = jnp.einsum(
        "bhlm,blhe->bmhe",
        softmax_again.astype(jnp.bfloat16),
        delta_mixture,
        preferred_element_type=jnp.float32,
    )
    delta_logits = softmax_again * (
        delta_softmax - jnp.sum(softmax_again * delta_softmax, axis=-1, keepdims=True)
    )
    delta_scores = (softmax_scale * delta_logits).astype(jnp.bfloat16)
    delta_queries = jnp.einsum(
        "bhlm,bmhe->blhe", delta_scores, key_heads, preferred_element_type=jnp.float32
    )
    delta_keys = jnp.einsum(
        "bhlm,blhe->bmhe", delta_scores, query_heads, preferred_element_type=jnp.float32
    )
    delta_mixed = jnp.concatenate(
        [
            delta_queries.reshape(images, length, D),
            delta_keys.reshape(images, length, D),
            delta_values.reshape(images, length, D),
        ],
        axis=-1,
    ).astype(jnp.bfloat16)
    attend_gradient = weight_gradient(attend_input, delta_mixed)
    delta_attend = transposed(delta_mixed, matrices_back[1])
    delta_zero = delta_one + norm_back(delta_attend * gain_first, normed_one, inverse_one)
    zero_low = delta_zero.astype(jnp.bfloat16)
    merge_gradient = weight_gradient(joined, zero_low)
    delta_joined = transposed(zero_low, matrices_back[0])
    input_gradient = delta_joined[..., 0:D].astype(jnp.bfloat16)
    skip_gradient = delta_joined[..., D : 2 * D].astype(jnp.bfloat16)
    vector_gradient = jnp.concatenate(
        [
            row_sum(delta_zero),
            row_sum(delta_attend * normed_one),
            row_sum(delta_attend),
            row_sum(delta_one),
            row_sum(delta_expand * normed_two),
            row_sum(delta_expand),
            row_sum(upstream),
            row_sum(delta_hidden),
        ]
    )
    owned_rows = (
        lax.psum_scatter(merge_gradient, "wide", scatter_dimension=0, tiled=True),
        lax.psum_scatter(attend_gradient, "wide", scatter_dimension=0, tiled=True),
        lax.psum_scatter(output_gradient, "wide", scatter_dimension=0, tiled=True),
        lax.psum_scatter(expand_gradient, "wide", scatter_dimension=0, tiled=True),
        lax.psum_scatter(shrink_gradient, "wide", scatter_dimension=0, tiled=True),
    )
    vector_total = lax.psum(vector_gradient, "wide")
    parted = (
        lax.psum_scatter(owned_rows[0], "narrow", scatter_dimension=1, tiled=True),
        lax.psum_scatter(owned_rows[1], "narrow", scatter_dimension=1, tiled=True),
        lax.psum_scatter(owned_rows[2], "narrow", scatter_dimension=1, tiled=True),
        lax.psum_scatter(owned_rows[3], "narrow", scatter_dimension=1, tiled=True),
        lax.psum_scatter(owned_rows[4], "narrow", scatter_dimension=1, tiled=True),
        lax.psum_scatter(vector_total, "narrow", scatter_dimension=0, tiled=True),
    )
    merge_new = adamw_update(merge_weight, merge_moment, merge_square, parted[0], rate_merge)
    attend_new = adamw_update(attend_weight, attend_moment, attend_square, parted[1], rate_attend)
    output_new = adamw_update(output_weight, output_moment, output_square, parted[2], rate_output)
    expand_new = adamw_update(expand_weight, expand_moment, expand_square, parted[3], rate_expand)
    shrink_new = adamw_update(shrink_weight, shrink_moment, shrink_square, parted[4], rate_shrink)
    vector_new = adamw_update(vectors, vector_moment, vector_square, parted[5], rate_vector)
    return (
        outputs,
        input_gradient,
        skip_gradient,
        merge_new[0],
        merge_new[1],
        merge_new[2],
        attend_new[0],
        attend_new[1],
        attend_new[2],
        output_new[0],
        output_new[1],
        output_new[2],
        expand_new[0],
        expand_new[1],
        expand_new[2],
        shrink_new[0],
        shrink_new[1],
        shrink_new[2],
        vector_new[0],
        vector_new[1],
        vector_new[2],
    )


CORE = 1
ACROSS = 2
ALONG = 4
PAD = 384
VECTOR_ROWS = 11
VMEM_BYTES = 56 * 1024 * 1024
LIGHT = pl.CostEstimate(flops=0, bytes_accessed=1024, transcendentals=0)
PARAMS = pltpu.CompilerParams(vmem_limit_bytes=VMEM_BYTES)


def swap_wide(value, bit):
    return lax.ppermute(value, "wide", [(i, i ^ bit) for i in range(8)])


def swap_narrow(value, bit):
    return lax.ppermute(value, "narrow", [(i, i ^ bit) for i in range(4)])


def together(*values):
    return lax.optimization_barrier(values)


def spot():
    wide = lax.axis_index("wide")
    narrow = lax.axis_index("narrow")
    return (wide & 1, (wide >> 1) & 1, (wide >> 2) & 1, narrow & 1, narrow >> 1)


def split_shapes(rows, columns):
    if columns == FF:
        return (rows, columns // 2), True
    return (rows // 2, columns), False


def split_block(value):
    shape, by_columns = split_shapes(*value.shape[-2:])
    if by_columns:
        return value[..., : shape[1]], value[..., shape[1] :]
    return value[..., : shape[0], :], value[..., shape[0] :, :]


def column_blocks(kind, quarter):
    if kind == "attend_output":
        width = quarter // 8
        order = [8 * part + 2 * n + p for part in range(3) for p in range(2) for n in range(4)]
        blocks = [(block // 6, (block % 6) * width) for block in order]
        return width, blocks + [(n, (6 + p) * width) for p in range(2) for n in range(4)]
    width = quarter // 2
    return width, [(n, p * width) for p in range(2) for n in range(4)]


def fold(shard):
    parts = max(1, shard.shape[0] // (D // 8))
    height = shard.shape[0] // parts
    return jnp.concatenate(
        [shard[part * height : (part + 1) * height] for part in range(parts)], axis=1
    )


def unfold(value, rows):
    parts = rows // value.shape[0]
    quarter = value.shape[1] // parts
    return jnp.concatenate(
        [value[:, part * quarter : (part + 1) * quarter] for part in range(parts)], axis=0
    )


def arrange(kind, parts, shard, others, extra=0):
    height = shard.shape[0]
    rows, quarter = parts * height, (shard.shape[1] - extra) // parts
    width, blocks = column_blocks(kind, quarter)

    def kernel(*refs):
        full, apart = refs[4], refs[-1]
        narrow = lax.axis_index("narrow")
        for number in range(4):
            for relative in range(4):

                @pl.when((narrow ^ relative) == number)
                def _():
                    value = refs[relative]
                    if extra:
                        apart[number] = value[:, parts * quarter :]
                    for position, (owner, offset) in enumerate(blocks):
                        if owner == number:
                            column = slice(position * width, (position + 1) * width)
                            for part in range(parts):
                                start = part * quarter + offset
                                full[part * height : (part + 1) * height, column] = value[
                                    :, start : start + width
                                ]

    outs = [jax.ShapeDtypeStruct((rows, 4 * quarter), jnp.bfloat16)]
    if extra:
        outs.append(jax.ShapeDtypeStruct((4, height, extra), jnp.bfloat16))
    return pl.pallas_call(
        kernel,
        out_shape=tuple(outs),
        compiler_params=PARAMS,
        cost_estimate=LIGHT,
    )(shard, *others)


def weight_scratch(rows, columns, chunks=1):
    return [pltpu.VMEM((rows, columns), jnp.bfloat16), pltpu.SemaphoreType.DMA((chunks, 8))]


class Fetch:
    def __init__(self, refs, full, sems, first=0):
        wide = lax.axis_index("wide")
        core, chip = wide & 1, wide >> 1
        rows = full.shape[0] // 8
        chunks = sems.shape[0]
        width = full.shape[1] // chunks
        self.copies = []
        for chunk in range(chunks):
            group = []
            for number, (ends, from_x, from_y) in enumerate((refs[:3], refs[3:])):
                parity = core if number == 0 else 1 - core
                own, far = ends.at[pl.ds(0, rows)], ends.at[pl.ds(rows, rows)]
                for relative, piece in enumerate((own, from_x, from_y, far)):
                    start = pl.multiple_of((4 * parity + (chip ^ relative)) * rows, 16)
                    group.append(
                        pltpu.make_async_copy(
                            piece.at[:, pl.ds(first + chunk * width, width)],
                            full.at[pl.ds(start, rows), pl.ds(chunk * width, width)],
                            sems.at[chunk, 4 * number + relative],
                        )
                    )
            self.copies.append(group)
        for group in self.copies:
            for copy in group:
                copy.start()

    def wait(self, chunk=0):
        for copy in self.copies[chunk]:
            copy.wait()


def pair_gradient(lefts, right):
    height = lefts[0][4]
    rows = height // 4
    tokens, columns = right[0].shape
    tile = 384 if height > 576 else 1152
    count = len(lefts)
    ends = [sum(left[2] for left in lefts[: number + 1]) // tile for number in range(count)]
    starts = [0] + ends[:-1]

    def kernel(*refs):
        left_refs = refs[: 2 * count]
        right_ref, sibling_ref = refs[2 * count : 2 * count + 2]
        outs = refs[2 * count + 2 : 2 * count + 6]
        joint, beside, total = refs[2 * count + 6 :]
        step = pl.program_id(0)

        @pl.when(step == 0)
        def _():
            joint[...] = jnp.zeros_like(joint)

        for number in range(count):

            @pl.when(step == starts[number])
            def _():
                beside[:, :PAD] = left_refs[2 * number][...]
                beside[:, PAD:] = left_refs[2 * number + 1][...]

        joint[:tokens] = right_ref[...]
        joint[PAD : PAD + tokens] = sibling_ref[...]
        total[...] = jnp.dot(
            beside[...], joint[...], preferred_element_type=jnp.float32
        ).astype(jnp.bfloat16)
        by_columns = split_shapes(rows, columns)[1]
        part_blocks(total, rows, outs, step < columns // tile // 2 if by_columns else None)

    whole = lambda place: pl.BlockSpec((height, PAD), lambda i: (place, 0))
    part = lambda size: pl.BlockSpec((size, tile), lambda i: (0, i))
    shape, by_columns = split_shapes(rows, columns)
    half = columns // tile // 2
    if by_columns:
        top = pl.BlockSpec((2, rows, tile), lambda i: (0, 0, jnp.minimum(i, half - 1)))
        bottom = pl.BlockSpec((2, rows, tile), lambda i: (0, 0, jnp.maximum(i - half, 0)))
    else:
        top = bottom = pl.BlockSpec((2, shape[0], tile), lambda i: (0, 0, i))
    outs = pl.pallas_call(
        kernel,
        grid=(columns // tile,),
        in_specs=[whole(left[3]) for left in lefts for _ in range(2)] + [part(tokens)] * 2,
        out_specs=(top, top, bottom, bottom),
        out_shape=block_shapes(rows, columns),
        scratch_shapes=[
            pltpu.VMEM((2 * PAD, tile), jnp.bfloat16),
            pltpu.VMEM((height, 2 * PAD), jnp.bfloat16),
            pltpu.VMEM((height, tile), jnp.bfloat16),
        ],
        compiler_params=PARAMS,
        cost_estimate=LIGHT,
    )(*[left for pair_of in lefts for left in pair_of[:2]], *right)
    return outs


def block_shapes(rows, columns):
    shape = split_shapes(rows, columns)[0]
    return (jax.ShapeDtypeStruct((2,) + shape, jnp.bfloat16),) * 4


def part_blocks(total, rows, outs, first_half):
    wide = lax.axis_index("wide")
    across, along = (wide >> 1) & 1, (wide >> 2) & 1
    half = rows // 2
    for kept_x in range(2):
        for kept_y in range(2):
            x = across if kept_x else 1 - across
            y = along if kept_y else 1 - along
            start = pl.multiple_of((2 * y + x) * rows, 16)
            top, bottom = outs[1 - kept_x], outs[3 - kept_y]
            if first_half is None:
                top[1 - kept_y] = total[pl.ds(start, half)]
                bottom[1 - kept_x] = total[pl.ds(pl.multiple_of(start + half, 16), half)]
                continue

            @pl.when(first_half)
            def _():
                top[1 - kept_y] = total[pl.ds(start, rows)]

            @pl.when(jnp.logical_not(first_half))
            def _():
                bottom[1 - kept_x] = total[pl.ds(start, rows)]


def unarrange(kind, parts, blocks, got, got_last):
    by_columns = got_last[0].shape[1] == FF // 2
    part_rows, part_columns = got_last[0].shape
    rows = part_rows if by_columns else 2 * part_rows
    columns = 2 * part_columns if by_columns else part_columns
    quarter = columns // 4
    height = rows // parts
    width, column_parts = column_blocks(kind, quarter)

    def kernel(*refs):
        tops, bottoms = refs[:3], refs[3:6]
        outs, held = refs[6:10], refs[10]
        narrow = lax.axis_index("narrow")
        low_bit, high_bit = narrow & 1, narrow >> 1
        top = add_low(tops[0][...], tops[1][...], tops[2][...])
        bottom = add_low(bottoms[0][...], bottoms[1][...], bottoms[2][...])
        if by_columns:
            held[:, :part_columns] = top
            held[:, part_columns:] = bottom
        else:
            held[:part_rows] = top
            held[part_rows:] = bottom
        for owner in range(4):
            for which in range(4):
                low_same, high_same = 1 - which // 2, 1 - which % 2

                @pl.when(
                    ((low_bit == (owner & 1)) == (low_same == 1))
                    & ((high_bit == (owner >> 1)) == (high_same == 1))
                )
                def _():
                    for position, (quarter_of, offset) in enumerate(column_parts):
                        if quarter_of == owner:
                            piece = held[:, position * width : (position + 1) * width]
                            for part in range(parts):
                                start = part * quarter + offset
                                outs[which][:, start : start + width] = piece[
                                    part * height : (part + 1) * height
                                ]

    near = pl.BlockSpec((None, part_rows, part_columns), lambda i: (0, 0, 0))
    full = lambda size, width: pl.BlockSpec((size, width), lambda i: (0, 0))
    shape = jax.ShapeDtypeStruct((height, parts * quarter), jnp.bfloat16)
    return pl.pallas_call(
        kernel,
        grid=(1,),
        in_specs=[near, near, full(part_rows, part_columns)] * 2,
        out_specs=(full(height, parts * quarter),) * 4,
        out_shape=(shape,) * 4,
        scratch_shapes=[pltpu.VMEM((rows, columns), jnp.bfloat16)],
        compiler_params=PARAMS,
        cost_estimate=LIGHT,
    )(blocks[0], got[0], got_last[0], blocks[2], got[1], got_last[1])


def add_low(*terms):
    return sum(term.astype(jnp.float32) for term in terms).astype(jnp.bfloat16)


def pick(value, index, dim=0):
    return lax.dynamic_index_in_dim(value, index, dim, keepdims=False)


def halves_of(value, core):
    middle = value.shape[-1] // 2
    first, second = value[..., :middle], value[..., middle:]
    return jnp.where(core == 0, first, second), jnp.where(core == 0, second, first)


def inner(value):
    width = value.shape[-1] // 8
    return jnp.concatenate(
        [
            value[..., (2 * n + p) * width : (2 * n + p + 1) * width]
            for p in range(2)
            for n in range(4)
        ],
        axis=-1,
    )


def outer(value):
    width = value.shape[-1] // 8
    return jnp.concatenate(
        [
            value[..., (4 * p + n) * width : (4 * p + n + 1) * width]
            for n in range(4)
            for p in range(2)
        ],
        axis=-1,
    )


def upright(value):
    return jnp.pad(value, ((0, PAD - value.shape[0]), (0, 0))).T


KEEP_NEAR, KEEP_FAR, SEND_NEAR, SEND_FAR = range(4)


def send(blocks):
    return swap_wide(blocks[1], ACROSS), swap_wide(blocks[3], ALONG)


def forward(blocks, got):
    return (
        swap_wide(add_low(blocks[0][1], got[0][1]), ALONG),
        swap_wide(add_low(blocks[2][1], got[1][1]), ACROSS),
    )


def narrow_first(quarters):
    return swap_narrow(quarters[SEND_FAR], 1), swap_narrow(quarters[SEND_NEAR], 1)


def narrow_second(quarters, got):
    return swap_narrow(add_low(quarters[KEEP_FAR], got[0]), 2)


def finish(quarters, got, got_last):
    return (
        quarters[KEEP_NEAR].astype(jnp.float32)
        + got[1].astype(jnp.float32)
        + got_last.astype(jnp.float32)
    )


def across_narrow(shard):
    return tuple(swap_narrow(shard, bit) for bit in (1, 2, 3))


def gather_first(block):
    return swap_wide(block, ACROSS), swap_wide(block, ALONG)


def gather_second(first):
    return (
        swap_wide(split_block(first[0])[0], ALONG),
        swap_wide(split_block(first[1])[1], ACROSS),
    )


def swap_sides(first):
    return swap_wide(first[0], CORE), swap_wide(first[1], CORE)


def ends_of(block, second):
    if split_shapes(*block.shape)[1]:
        return jnp.concatenate([block, jnp.concatenate(second, axis=1)], axis=0)
    if block.shape[0] > 2 * D // 8:
        return jnp.concatenate([block, *second], axis=0)
    return jnp.stack([block, jnp.concatenate(second, axis=0)]).reshape(-1, block.shape[1])


def line_gradient(lefts, rights, rights_sibling):
    tokens, height = lefts[0].shape
    width = rights.shape[2]
    rows = height // 4

    def kernel(*refs):
        right_ref, sibling_ref = refs[8:10]
        outs, total = refs[10:14], refs[14]
        chip = lax.axis_index("wide") >> 1
        for number in range(8):
            right = (right_ref, sibling_ref)[number // 4][number % 4, :tokens]
            part = lax.dot_general(
                right,
                refs[number][...],
                (((0,), (0,)), ((), ())),
                preferred_element_type=jnp.float32,
            )
            total[...] = part if number == 0 else total[...] + part
        sums = sum(
            ref[number, tokens:].astype(jnp.float32)
            for ref in (right_ref, sibling_ref)
            for number in range(4)
        )
        for ref in outs:
            for row in range(VECTOR_ROWS):
                ref[rows // 2 + row // 2, (row % 2) * width : (row % 2 + 1) * width] = sums[
                    row
                ].astype(jnp.bfloat16)
        for owner in range(4):
            block = total[:, owner * rows : (owner + 1) * rows].T.astype(jnp.bfloat16)
            for relative in range(4):

                @pl.when((chip ^ relative) == owner)
                def _():
                    outs[relative][: rows // 2, :width] = block[: rows // 2]
                    outs[relative][: rows // 2, width:] = block[rows // 2 :]

    shape = jax.ShapeDtypeStruct((rows // 2 + 16, 2 * width), jnp.bfloat16)
    return pl.pallas_call(
        kernel,
        out_shape=(shape,) * 4,
        scratch_shapes=[pltpu.VMEM((width, height), jnp.float32)],
        compiler_params=PARAMS,
        cost_estimate=LIGHT,
    )(*lefts, rights, rights_sibling)


def turned_update(weight, moment, square, terms, parts, step_rate):
    rows, quarter = weight.shape
    height = rows // parts

    def kernel(*refs):
        weight_ref, moment_ref, square_ref = refs[: 3]
        total = sum(ref[...].astype(jnp.float32) for ref in refs[3 : 3 + len(terms)])
        outs, gradient = refs[3 + len(terms) : 6 + len(terms)], refs[-1]
        for part in range(parts):
            gradient[part * height : (part + 1) * height] = total[
                :, part * quarter : (part + 1) * quarter
            ]
        new = adamw_update(
            weight_ref[...], moment_ref[...], square_ref[...], gradient[...].T, step_rate
        )
        for out, value in zip(outs, new):
            out[...] = value

    new = pl.pallas_call(
        kernel,
        out_shape=(jax.ShapeDtypeStruct((quarter, rows), jnp.float32),) * 3,
        scratch_shapes=[pltpu.VMEM((rows, quarter), jnp.float32)],
        compiler_params=PARAMS,
        cost_estimate=LIGHT,
    )(weight.T, moment.T, square.T, *terms)
    return tuple(value.T for value in new)


def heavy(kernel, outs, scratch, weights, operands):
    return pl.pallas_call(
        kernel,
        in_specs=[pl.BlockSpec(memory_space=pl.ANY)] * len(weights)
        + [pl.BlockSpec(memory_space=pltpu.VMEM)] * len(operands),
        out_shape=tuple(jax.ShapeDtypeStruct(shape, dtype) for shape, dtype in outs),
        scratch_shapes=scratch,
        compiler_params=PARAMS,
        cost_estimate=LIGHT,
    )(*weights, *operands)


def dot_rows(left, right):
    return lax.dot_general(left, right, (((1,), (1,)), ((), ())), preferred_element_type=jnp.float32)


def dot_depth(left, right):
    return lax.dot_general(left, right, (((0,), (0,)), ((), ())), preferred_element_type=jnp.float32)


def store_upright(value, padded, mine, other):
    features = value.shape[1]
    padded[: value.shape[0]] = value
    turned = padded[...].T.astype(jnp.bfloat16)
    core = lax.axis_index("wide") & 1

    @pl.when(core == 0)
    def _():
        mine[...] = turned[: features // 2]
        other[...] = turned[features // 2 :]

    @pl.when(core == 1)
    def _():
        other[...] = turned[: features // 2]
        mine[...] = turned[features // 2 :]


def merge_forward(joined, weight, bias, gain, shift):
    length = joined.shape[0]

    def kernel(*refs):
        joined_ref, bias_ref, gain_ref, shift_ref = refs[6:10]
        stream, entry, up_mine, up_other, full, sems, padded = refs[10:]
        weight_in = Fetch(refs[:6], full, sems)
        padded[...] = jnp.zeros_like(padded)
        weight_in.wait()
        stream[...] = product(joined_ref[...], full[...]) + bias_ref[...]
        normed = normalize(stream[...])[0]
        value = (normed * gain_ref[...] + shift_ref[...]).astype(jnp.bfloat16)
        entry[...] = value
        store_upright(value.astype(jnp.float32), padded, up_mine, up_other)

    return heavy(
        kernel,
        [
            ((length, D), jnp.float32),
            ((length, D), jnp.bfloat16),
            ((D // 2, PAD), jnp.bfloat16),
            ((D // 2, PAD), jnp.bfloat16),
        ],
        weight_scratch(2 * D, D) + [pltpu.VMEM((PAD, D), jnp.float32)],
        weight,
        (joined, bias, gain, shift),
    )


def attend_head(heads, head, chances_ref, slot):
    at = head * HD
    queries = heads[:, at : at + HD]
    keys = heads[:, D + at : D + at + HD]
    values = heads[:, 2 * D + at : 2 * D + at + HD]
    logits = dot_rows(queries, keys) * HD ** (-0.5)
    powers = jnp.exp(logits - jnp.max(logits, axis=-1, keepdims=True))
    chances = powers / jnp.sum(powers, axis=-1, keepdims=True)
    chances_ref[slot] = chances
    return product(chances.astype(jnp.bfloat16), values).astype(jnp.bfloat16)


FIRST = 15


def attend_first(entry, weight):
    length = entry.shape[0]

    def kernel(*refs):
        entry_ref, heads, chances_ref, mix_ref, full, sems = refs[6:]
        weight_in = Fetch(refs[:6], full, sems)
        for part in range(3):
            weight_in.wait(part)
            columns = slice(part * D, (part + 1) * D)
            heads[:, columns] = product(entry_ref[...], full[:, columns]).astype(jnp.bfloat16)
        for head in range(FIRST):
            mix_ref[:, head * HD : (head + 1) * HD] = attend_head(heads, head, chances_ref, head)

    return heavy(
        kernel,
        [
            ((length, 3 * D), jnp.bfloat16),
            ((FIRST, length, length), jnp.float32),
            ((length, FIRST * HD), jnp.bfloat16),
        ],
        weight_scratch(D, 3 * D, 3),
        weight,
        (entry,),
    )


def attend_second(heads, mix_first, weight, stream_zero, bias, gain, shift):
    length = heads.shape[0]
    half = D // 2

    def kernel(*refs):
        heads_ref, first_ref, zero_ref, bias_ref, gain_ref, shift_ref = refs[6:12]
        chances_ref, stream, value_ref, up_mine, up_other, full, sems, mixed, padded = refs[12:]
        weight_in = Fetch(refs[:6], full, sems, 3 * D)
        padded[...] = jnp.zeros_like(padded)
        mixed[:, : FIRST * HD] = first_ref[...]
        for head in range(FIRST, H):
            mixed[:, head * HD : (head + 1) * HD] = attend_head(
                heads_ref, head, chances_ref, head - FIRST
            )
        weight_in.wait()
        stream[...] = zero_ref[...] + product(mixed[...], full[...]) + bias_ref[...]
        store_upright(
            mixed[...].astype(jnp.float32), padded, up_mine.at[pl.ds(0, half)], up_other.at[pl.ds(0, half)]
        )
        normed = normalize(stream[...])[0]
        value = (normed * gain_ref[...] + shift_ref[...]).astype(jnp.bfloat16)
        value_ref[...] = value
        store_upright(
            value.astype(jnp.float32), padded, up_mine.at[pl.ds(half, half)], up_other.at[pl.ds(half, half)]
        )

    return heavy(
        kernel,
        [
            ((H - FIRST, length, length), jnp.float32),
            ((length, D), jnp.float32),
            ((length, D), jnp.bfloat16),
            ((D, PAD), jnp.bfloat16),
            ((D, PAD), jnp.bfloat16),
        ],
        weight_scratch(D, D)
        + [pltpu.VMEM((length, D), jnp.bfloat16), pltpu.VMEM((PAD, D), jnp.float32)],
        weight,
        (heads, mix_first, stream_zero, bias, gain, shift),
    )


def expand_forward(entry, weight, bias):
    length = entry.shape[0]

    def kernel(*refs):
        entry_ref, bias_ref = refs[6:8]
        active_ref, slope_ref, up_mine, up_other, full, sems, padded = refs[8:]
        core = lax.axis_index("wide") & 1
        weight_in = Fetch(refs[:6], full, sems)
        padded[...] = jnp.zeros_like(padded)
        for step in range(FF // D):
            columns = slice(step * D, (step + 1) * D)
            weight_in.wait(step)
            value = product(entry_ref[...], full[:, columns]) + bias_ref[:, columns]
            inside = 0.5 * (1.0 + lax.erf(value * (0.5**0.5)))
            bell = jnp.exp(-0.5 * value * value) * (2.0 * jnp.pi) ** -0.5
            active = (value * inside).astype(jnp.bfloat16)
            slope_ref[:, columns] = inside + value * bell
            active_ref[:, columns] = active
            padded[:length] = active.astype(jnp.float32)
            turned = padded[...].T.astype(jnp.bfloat16)
            rows = slice((step % 2) * D, (step % 2 + 1) * D)

            @pl.when(core == step // 2)
            def _():
                up_mine[rows] = turned

            @pl.when(core != step // 2)
            def _():
                up_other[rows] = turned

    return heavy(
        kernel,
        [
            ((length, FF), jnp.bfloat16),
            ((length, FF), jnp.float32),
            ((FF // 2, PAD), jnp.bfloat16),
            ((FF // 2, PAD), jnp.bfloat16),
        ],
        weight_scratch(D, FF, FF // D) + [pltpu.VMEM((PAD, D), jnp.float32)],
        weight,
        (entry, bias),
    )


def hidden_backward(pulled, weight, slope):
    length = pulled.shape[0]

    def kernel(*refs):
        pulled_ref, slope_ref, low_ref, sum_ref, full, sems = refs[6:]
        Fetch(refs[:6], full, sems).wait()
        for step in range(FF // D):
            columns = slice(step * D, (step + 1) * D)
            delta = dot_rows(pulled_ref[...], full[columns]) * slope_ref[:, columns]
            low_ref[:, columns] = delta.astype(jnp.bfloat16)
            sum_ref[:, columns] = jnp.sum(delta, axis=0, keepdims=True)

    return heavy(
        kernel,
        [((length, FF), jnp.bfloat16), ((1, FF), jnp.float32)],
        weight_scratch(FF, D),
        weight,
        (pulled, slope),
    )


def expand_backward(hidden_low, weight, mixed_weight, pulled, stream_one, gain):
    length = pulled.shape[0]

    def kernel(*refs):
        hidden_ref, pulled_ref, stream_ref, gain_ref = refs[12:16]
        one_ref, low_ref, sums, mix_ref, full, sems, output, output_sems, delta = refs[16:]
        weight_in = Fetch(refs[:6], full, sems)
        output_in = Fetch(refs[6:12], output, output_sems, 3 * D)
        for step in range(FF // D):
            columns = slice(step * D, (step + 1) * D)
            weight_in.wait(step)
            part = dot_rows(hidden_ref[:, columns], full[:, columns])
            delta[...] = part if step == 0 else delta[...] + part
        value = delta[...]
        normed, inverse = normalize(stream_ref[...])
        upstream = pulled_ref[...].astype(jnp.float32)
        one = upstream + norm_back(value * gain_ref[...], normed, inverse)
        one_ref[...] = one
        low_value = one.astype(jnp.bfloat16)
        low_ref[...] = low_value
        sums[0:1] = jnp.sum(one, axis=0, keepdims=True)
        sums[1:2] = jnp.sum(value * normed, axis=0, keepdims=True)
        sums[2:3] = jnp.sum(value, axis=0, keepdims=True)
        sums[3:4] = jnp.sum(upstream, axis=0, keepdims=True)
        output_in.wait()
        mix_ref[...] = dot_rows(low_value, output[...]).astype(jnp.bfloat16)

    return heavy(
        kernel,
        [
            ((length, D), jnp.float32),
            ((length, D), jnp.bfloat16),
            ((4, D), jnp.float32),
            ((length, D), jnp.bfloat16),
        ],
        weight_scratch(D, FF, FF // D)
        + weight_scratch(D, D)
        + [pltpu.VMEM((length, D), jnp.float32)],
        (*weight, *mixed_weight),
        (hidden_low, pulled, stream_one, gain),
    )


def attend_backward(heads, chances_first, chances_second, delta_mixture, stream_low):
    length = heads.shape[0]
    scale = HD ** (-0.5)

    def kernel(heads_ref, first_ref, second_ref, delta_ref, stream_ref, mixed):
        mixed[:, 3 * D :] = stream_ref[...]
        for head in range(H):
            at = head * HD
            queries = heads_ref[:, at : at + HD]
            keys = heads_ref[:, D + at : D + at + HD]
            values = heads_ref[:, 2 * D + at : 2 * D + at + HD]
            delta = delta_ref[:, at : at + HD]
            chances = first_ref[head] if head < FIRST else second_ref[head - FIRST]
            pull = dot_rows(delta, values)
            inner_sum = jnp.sum(chances * pull, axis=-1, keepdims=True)
            scores = (scale * (chances * (pull - inner_sum))).astype(jnp.bfloat16)
            mixed[:, at : at + HD] = product(scores, keys).astype(jnp.bfloat16)
            mixed[:, D + at : D + at + HD] = dot_depth(scores, queries).astype(jnp.bfloat16)
            mixed[:, 2 * D + at : 2 * D + at + HD] = dot_depth(
                chances.astype(jnp.bfloat16), delta
            ).astype(jnp.bfloat16)

    return heavy(
        kernel,
        [((length, 4 * D), jnp.bfloat16)],
        [],
        (),
        (heads, chances_first, chances_second, delta_mixture, stream_low),
    )[0]


def entry_backward(delta_mixed, weight, delta_one, stream_zero, gain, sums_two, hidden_sum):
    length = delta_mixed.shape[0]
    width = D // 8
    tall = -(-(length + VECTOR_ROWS) // 16) * 16

    def kernel(*refs):
        mixed_ref, one_ref, stream_ref, gain_ref, sums_ref, hidden_ref, low_ref = refs[6:13]
        quarters, (full, sems, delta, held) = refs[13:17], refs[17:]
        weight_in = Fetch(refs[:6], full, sems)
        for step in range(3):
            columns = slice(step * D, (step + 1) * D)
            weight_in.wait(step)
            part = dot_rows(mixed_ref[:, columns], full[:, columns])
            delta[...] = part if step == 0 else delta[...] + part
        value = delta[...]
        normed, inverse = normalize(stream_ref[...])
        zero = one_ref[...] + norm_back(value * gain_ref[...], normed, inverse)
        zero_low = zero.astype(jnp.bfloat16)
        low_ref[...] = zero_low
        sums = [jnp.sum(part, axis=0, keepdims=True) for part in (zero, value * normed, value)]
        sums += [sums_ref[row : row + 1] for row in range(4)]
        held[...] = jnp.zeros_like(held)
        for block in range(VECTOR_ROWS * 8):
            owner, place = block // (2 * VECTOR_ROWS), block % (2 * VECTOR_ROWS)
            if block < 56:
                source, wide = sums[block // 8], block % 8
                start = (4 * (wide % 2) + wide // 2) * width
            else:
                source, wide = hidden_ref, (block - 56) // 4
                start = (4 * (wide % 2) + wide // 2) * 4 * width + (block % 4) * width
            columns = slice((place % 2) * width, (place % 2 + 1) * width)
            held[owner, place // 2 : place // 2 + 1, columns] = source[:, start : start + width]
        narrow = lax.axis_index("narrow")
        for owner in range(4):
            for relative in range(4):

                @pl.when((narrow ^ relative) == owner)
                def _():
                    for parity in range(2):
                        start = (4 * parity + owner) * width
                        quarters[relative][:length, parity * width : (parity + 1) * width] = (
                            zero_low[:, start : start + width]
                        )
                    quarters[relative][length:] = held[owner, : tall - length].astype(jnp.bfloat16)

    return heavy(
        kernel,
        [((length, D), jnp.bfloat16)] + [((tall, D // 4), jnp.bfloat16)] * 4,
        weight_scratch(D, 3 * D, 3)
        + [pltpu.VMEM((length, D), jnp.float32), pltpu.VMEM((4, 16, D // 4), jnp.float32)],
        weight,
        (delta_mixed, delta_one, stream_zero, gain, sums_two, hidden_sum),
    )


def joined_backward(zero_low, weight):
    length = zero_low.shape[0]
    width = 2 * D // 8

    def kernel(*refs):
        zero_ref, first_ref, second_ref, full, sems = refs[6:]
        Fetch(refs[:6], full, sems).wait()
        for parity in range(2):
            delta = dot_rows(zero_ref[...], full[parity * D : (parity + 1) * D])
            delta = delta.astype(jnp.bfloat16)
            for number in range(4):
                target = (first_ref, second_ref)[number // 2]
                column = (2 * (number % 2) + parity) * width
                target[:, column : column + width] = delta[:, number * width : (number + 1) * width]

    out = ((length, D), jnp.bfloat16)
    return heavy(kernel, [out, out], weight_scratch(2 * D, D), weight, (zero_low,))


def shrink_forward(active, weight, stream_one, bias):
    length = active.shape[0]
    width = D // 8

    def kernel(*refs):
        active_ref, stream_ref, bias_ref, out_ref, full, sems = refs[6:]
        Fetch(refs[:6], full, sems).wait()
        total = (
            stream_ref[...] + product(active_ref[...], full[...]) + bias_ref[...]
        ).astype(jnp.bfloat16)
        for parity in range(2):
            for number in range(4):
                column = (2 * number + parity) * width
                source = (4 * parity + number) * width
                out_ref[:, column : column + width] = total[:, source : source + width]

    return heavy(
        kernel,
        [((length, D), jnp.bfloat16)],
        weight_scratch(FF, D),
        weight,
        (active, stream_one, bias),
    )[0]


def on_device(
    inputs,
    skip_tokens,
    cotangent,
    merge_weight,
    merge_moment,
    merge_square,
    attend_weight,
    attend_moment,
    attend_square,
    output_weight,
    output_moment,
    output_square,
    expand_weight,
    expand_moment,
    expand_square,
    shrink_weight,
    shrink_moment,
    shrink_square,
    vectors,
    vector_moment,
    vector_square,
):
    core = spot()[0]
    low = jnp.bfloat16
    columns = attend_weight.shape[1]

    merge_low = fold(merge_weight.astype(low))
    rows = merge_low.shape[0]
    count = vectors.shape[0]
    vector_rows = jnp.pad(vectors.astype(low), (0, 64 * rows - count)).reshape(rows, 64)
    merge_low = jnp.concatenate([merge_low, vector_rows], axis=1)
    merge_others = across_narrow(merge_low)
    mixed_low = jnp.concatenate([attend_weight.astype(low), output_weight.astype(low)], axis=1)
    joined = inner(jnp.concatenate([inputs[0], skip_tokens[0]], axis=-1))
    joined_mine, joined_other = halves_of(joined, core)
    pulled = inner(cotangent[0])
    merge_others, mixed_low, joined, joined_mine, joined_other, pulled = together(
        merge_others, mixed_low, joined, joined_mine, joined_other, pulled
    )
    merge_block, vector_parts = arrange("merge", 2, merge_low, merge_others, 64)
    merge_first = gather_first(merge_block)
    mixed_far = swap_narrow(mixed_low, 2)
    mixed_near = swap_narrow(mixed_low, 1)
    expand_low = expand_weight.astype(low)
    known_sibling = swap_wide(jnp.concatenate([joined_other, pulled], axis=1), CORE)
    merge_first, mixed_far, vector_parts, expand_low, known_sibling = together(
        merge_first, mixed_far, vector_parts, expand_low, known_sibling
    )
    joined_sibling, pulled_sibling = known_sibling[:, :D], known_sibling[:, D:]
    merge_second = gather_second(merge_first)
    merge_sides = swap_sides(merge_first)
    mixed_last = swap_narrow(mixed_far, 1)
    shrink_low = fold(shrink_weight.astype(low))
    pieces = unpack(vector_parts.reshape(4, -1)[:, :count].reshape(-1).astype(jnp.float32))
    pieces = tuple(inner(piece)[None] for piece in pieces)
    merge_second, merge_sides, mixed_near, mixed_last, shrink_low, pieces = together(
        merge_second, merge_sides, mixed_near, mixed_last, shrink_low, pieces
    )
    skip_bias, gain_one, bias_one, output_bias, gain_two, bias_two, shrink_bias, expand_bias = pieces
    mixed_block = arrange("attend_output", 1, mixed_low, (mixed_near, mixed_far, mixed_last))[0]
    mixed_first = gather_first(mixed_block)
    expand_far = swap_narrow(expand_low, 2)
    expand_near = swap_narrow(expand_low, 1)
    merge_ends = ends_of(merge_block, merge_second)
    merge_pieces = (merge_ends, *merge_first, swap_wide(merge_ends, CORE), *merge_sides)
    stream_zero, attend_input, attend_up, attend_up_other = merge_forward(
        joined, merge_pieces, skip_bias, gain_one, bias_one
    )
    mixed_first, expand_far, expand_near, stream_zero, attend_input, attend_up_other = together(
        mixed_first, expand_far, expand_near, stream_zero, attend_input, attend_up_other
    )
    mixed_second = gather_second(mixed_first)
    mixed_sides = swap_sides(mixed_first)
    expand_last = swap_narrow(expand_far, 1)
    expand_block = arrange("expand", 1, expand_low, (expand_near, expand_far, expand_last))[0]
    mixed_second, mixed_sides, expand_block = together(mixed_second, mixed_sides, expand_block)
    expand_first = gather_first(expand_block)
    shrink_far = swap_narrow(shrink_low, 2)
    shrink_near = swap_narrow(shrink_low, 1)
    mixed_ends = ends_of(mixed_block, mixed_second)
    mixed_pieces = (mixed_ends, *mixed_first, swap_wide(mixed_ends, CORE), *mixed_sides)
    heads, chances_first, mix_first = attend_first(attend_input, mixed_pieces)
    expand_first, shrink_far, shrink_near, heads, mix_first = together(
        expand_first, shrink_far, shrink_near, heads, mix_first
    )
    expand_second = gather_second(expand_first)
    expand_sides = swap_sides(expand_first)
    shrink_last = swap_narrow(shrink_far, 1)
    chances_second, stream_one, expand_input, ups, ups_other = attend_second(
        heads, mix_first, mixed_pieces, stream_zero, output_bias, gain_two, bias_two
    )
    shrink_block = arrange("shrink", 4, shrink_low, (shrink_near, shrink_far, shrink_last))[0]
    (
        expand_second,
        expand_sides,
        shrink_block,
        expand_input,
        ups_other,
        joined_mine,
        joined_sibling,
    ) = together(
        expand_second,
        expand_sides,
        shrink_block,
        expand_input,
        ups_other,
        joined_mine,
        joined_sibling,
    )
    shrink_first = gather_first(shrink_block)
    expand_ends = ends_of(expand_block, expand_second)
    expand_pieces = (expand_ends, *expand_first, swap_wide(expand_ends, CORE), *expand_sides)
    joined_far = swap_narrow(joined_mine, 2)
    joined_near = swap_narrow(joined_mine, 1)
    active, slope, active_up, active_up_other = expand_forward(
        expand_input, expand_pieces, expand_bias
    )
    shrink_first, joined_far, joined_near, active, slope, active_up, active_up_other = together(
        shrink_first, joined_far, joined_near, active, slope, active_up, active_up_other
    )
    shrink_second = gather_second(shrink_first)
    shrink_sides = swap_sides(shrink_first)
    active_up_sibling = swap_wide(active_up_other, CORE)
    shrink_blocks = pair_gradient([(active_up, active_up_sibling, D, 0, FF // 2)], (pulled, pulled_sibling))
    shrink_second, shrink_sides, shrink_blocks, joined_far, joined_sibling, ups_other = together(
        shrink_second, shrink_sides, shrink_blocks, joined_far, joined_sibling, ups_other
    )
    shrink_got = send(shrink_blocks)
    shrink_ends = ends_of(shrink_block, shrink_second)
    shrink_pieces = (shrink_ends, *shrink_first, swap_wide(shrink_ends, CORE), *shrink_sides)
    sibling_far = swap_narrow(joined_sibling, 2)
    joined_last = swap_narrow(joined_far, 1)
    hidden_low, hidden_sum = hidden_backward(pulled, shrink_pieces, slope)
    outputs = shrink_forward(active, shrink_pieces, stream_one, shrink_bias)[None]
    (
        shrink_got,
        sibling_far,
        joined_last,
        hidden_low,
        hidden_sum,
        outputs,
        joined_sibling,
        ups_other,
        attend_up_other,
    ) = together(
        shrink_got,
        sibling_far,
        joined_last,
        hidden_low,
        hidden_sum,
        outputs,
        joined_sibling,
        ups_other,
        attend_up_other,
    )
    shrink_got_last = forward(shrink_blocks, shrink_got)
    hidden_sibling = swap_wide(hidden_low, CORE)
    ups_sibling = swap_wide(ups_other, CORE)
    sibling_near = swap_narrow(joined_sibling, 1)
    half = D // 2
    expand_blocks = pair_gradient(
        [(ups, ups_sibling, FF, 1, half)], (hidden_low, hidden_sibling)
    )
    shrink_got_last, sibling_near, expand_blocks, hidden_low, sibling_far = together(
        shrink_got_last, sibling_near, expand_blocks, hidden_low, sibling_far
    )
    expand_got = send(expand_blocks)
    sibling_last = swap_narrow(sibling_far, 1)
    attend_up_sibling = swap_wide(attend_up_other, CORE)
    shrink_quarters = unarrange("shrink", 4, shrink_blocks, shrink_got, shrink_got_last)
    shrink_hop = swap_narrow(shrink_quarters[SEND_FAR], 1)
    delta_one, stream_low, sums_two, delta_mixture = expand_backward(
        hidden_low, expand_pieces, mixed_pieces, pulled, stream_one, gain_two
    )
    delta_mixed = attend_backward(heads, chances_first, chances_second, delta_mixture, stream_low)
    expand_got, sibling_last, delta_mixed, attend_up_sibling, shrink_hop, shrink_quarters = together(
        expand_got, sibling_last, delta_mixed, attend_up_sibling, shrink_hop, shrink_quarters
    )
    expand_got_last = forward(expand_blocks, expand_got)
    mixed_sibling = swap_wide(delta_mixed, CORE)
    shrink_end = narrow_second(shrink_quarters, (shrink_hop,))
    shrink_near_hop = swap_narrow(shrink_quarters[SEND_NEAR], 1)
    mixed_blocks = pair_gradient(
        [(attend_up, attend_up_sibling, 3 * D, 0, half), (ups, ups_sibling, D, 0, half)],
        (delta_mixed, mixed_sibling),
    )
    expand_got_last, shrink_end, shrink_near_hop, mixed_blocks, delta_mixed = together(
        expand_got_last, shrink_end, shrink_near_hop, mixed_blocks, delta_mixed
    )
    mixed_got = send(mixed_blocks)
    expand_quarters = unarrange("expand", 1, expand_blocks, expand_got, expand_got_last)
    expand_hop = swap_narrow(expand_quarters[SEND_FAR], 1)
    expand_end = narrow_second(expand_quarters, (expand_hop,))
    expand_near_hop = swap_narrow(expand_quarters[SEND_NEAR], 1)
    zero_low, *zero_quarters = entry_backward(
        delta_mixed, mixed_pieces, delta_one, stream_zero, gain_one, sums_two, hidden_sum
    )
    mixed_got, expand_end, expand_near_hop, zero_low, zero_quarters, shrink_end = together(
        mixed_got, expand_end, expand_near_hop, zero_low, zero_quarters, shrink_end
    )
    mixed_got_last = forward(mixed_blocks, mixed_got)
    zero_got = tuple(swap_narrow(zero_quarters[bit], bit) for bit in (1, 2, 3))
    input_gradient, skip_gradient = joined_backward(zero_low, merge_pieces)
    mixed_got_last, zero_got, input_gradient, skip_gradient, shrink_end, expand_end = together(
        mixed_got_last, zero_got, input_gradient, skip_gradient, shrink_end, expand_end
    )
    mixed_quarters = unarrange("attend_output", 1, mixed_blocks, mixed_got, mixed_got_last)
    mixed_far_got = swap_narrow(mixed_quarters[SEND_FAR], 1)
    zero_line = jnp.stack([zero_quarters[0], *zero_got])
    zero_line_sibling = swap_wide(zero_line, CORE)
    merge_blocks = line_gradient(
        (
            joined_mine,
            joined_near,
            joined_far,
            joined_last,
            joined_sibling,
            sibling_near,
            sibling_far,
            sibling_last,
        ),
        zero_line,
        zero_line_sibling,
    )
    mixed_far_got, mixed_quarters, merge_blocks, shrink_end, expand_end = together(
        mixed_far_got, mixed_quarters, merge_blocks, shrink_end, expand_end
    )
    mixed_end = narrow_second(mixed_quarters, (mixed_far_got,))
    mixed_near_got = swap_narrow(mixed_quarters[SEND_NEAR], 1)
    merge_got = (
        swap_wide(merge_blocks[1], ACROSS),
        swap_wide(merge_blocks[2], ALONG),
        swap_wide(merge_blocks[3], ACROSS + ALONG),
    )
    shrink_new = turned_update(
        shrink_weight,
        shrink_moment,
        shrink_square,
        (shrink_quarters[KEEP_NEAR], shrink_near_hop, shrink_end),
        4,
        rate_shrink,
    )
    expand_new = adamw_update(
        expand_weight,
        expand_moment,
        expand_square,
        finish(expand_quarters, (expand_hop, expand_near_hop), expand_end),
        rate_expand,
    )
    tall = merge_blocks[0].shape[0] - 16
    merge_sum = sum(term.astype(jnp.float32) for term in (merge_blocks[0], *merge_got))
    merge_new = adamw_update(
        merge_weight,
        merge_moment,
        merge_square,
        unfold(merge_sum[:tall], merge_weight.shape[0]),
        rate_merge,
    )
    vector_total = merge_sum[tall:].reshape(-1)[: vectors.shape[0]]
    vector_new = adamw_update(vectors, vector_moment, vector_square, vector_total, rate_vector)
    merge_new, mixed_end, mixed_near_got, vector_new, shrink_new, expand_new = together(
        merge_new, mixed_end, mixed_near_got, vector_new, shrink_new, expand_new
    )
    mixed_total = finish(mixed_quarters, (mixed_far_got, mixed_near_got), mixed_end)
    attend_new = adamw_update(
        attend_weight, attend_moment, attend_square, mixed_total[:, :columns], rate_attend
    )
    output_new = adamw_update(
        output_weight, output_moment, output_square, mixed_total[:, columns:], rate_output
    )
    return (
        outputs,
        input_gradient[None],
        skip_gradient[None],
        *merge_new,
        *attend_new,
        *output_new,
        *expand_new,
        *shrink_new,
        *vector_new,
    )


def solution(mesh):
    in_specs = (
        P(("wide", "narrow"), None, None),
        P(("wide", "narrow"), None, None),
        P(("wide", "narrow"), None, None),
        P("wide", "narrow"),
        P("wide", "narrow"),
        P("wide", "narrow"),
        P("wide", "narrow"),
        P("wide", "narrow"),
        P("wide", "narrow"),
        P("wide", "narrow"),
        P("wide", "narrow"),
        P("wide", "narrow"),
        P("wide", "narrow"),
        P("wide", "narrow"),
        P("wide", "narrow"),
        P("wide", "narrow"),
        P("wide", "narrow"),
        P("wide", "narrow"),
        P("narrow"),
        P("narrow"),
        P("narrow"),
    )
    out_specs = (
        P(("wide", "narrow"), None, None),
        P(("wide", "narrow"), None, None),
        P(("wide", "narrow"), None, None),
        P("wide", "narrow"),
        P("wide", "narrow"),
        P("wide", "narrow"),
        P("wide", "narrow"),
        P("wide", "narrow"),
        P("wide", "narrow"),
        P("wide", "narrow"),
        P("wide", "narrow"),
        P("wide", "narrow"),
        P("wide", "narrow"),
        P("wide", "narrow"),
        P("wide", "narrow"),
        P("wide", "narrow"),
        P("wide", "narrow"),
        P("wide", "narrow"),
        P("narrow"),
        P("narrow"),
        P("narrow"),
    )
    tuned = mesh.shape["wide"] == 8 and mesh.shape["narrow"] == 4
    return jax.shard_map(
        on_device if tuned else general_device, mesh=mesh, in_specs=in_specs, out_specs=out_specs, check_vma=False
    )
```

```python
import jax
import jax.numpy as jnp
from jax import lax
from jax.experimental import pallas as pl
from jax.experimental.pallas import tpu as pltpu
from jax.sharding import PartitionSpec as P

D = 1152
FF = 4608
H = 16
HD = 72
STEP = 5


norm_epsilon = 1e-05
adam_epsilon = 1e-08
beta_moment = 0.5
weight_decay = 0.01
rate_merge = 0.04
rate_attend = 0.08
rate_output = 0.6
rate_expand = 0.06
rate_shrink = 0.03
rate_vector = 0.6


def product(left_side, right_side):
    return jnp.dot(left_side, right_side, preferred_element_type=jnp.float32)


def transposed(gradient, matrix):
    return lax.dot_general(
        gradient,
        matrix,
        (((gradient.ndim - 1,), (1,)), ((), ())),
        preferred_element_type=jnp.float32,
    )


def weight_gradient(activations, gradient):
    flat_left = activations.reshape(-1, activations.shape[-1])
    flat_right = gradient.reshape(-1, gradient.shape[-1])
    return lax.dot_general(
        flat_left, flat_right, (((0,), (0,)), ((), ())), preferred_element_type=jnp.float32
    )


def normalize(values):
    centered = values - jnp.mean(values, axis=-1, keepdims=True)
    spread = jnp.mean(centered * centered, axis=-1, keepdims=True)
    inverse = lax.rsqrt(spread + norm_epsilon)
    return (centered * inverse, inverse)


def norm_back(gradient, normed, inverse):
    return inverse * (
        gradient
        - jnp.mean(gradient, axis=-1, keepdims=True)
        - normed * jnp.mean(gradient * normed, axis=-1, keepdims=True)
    )


def row_sum(values):
    return jnp.sum(values, axis=(0, 1))


def unpack(packed):
    return tuple((packed[position * D : (position + 1) * D] for position in range(7))) + (
        packed[7 * D : 7 * D + FF],
    )


def gaussian_unit(values):
    return jax.nn.gelu(values, approximate=False)


def adamw_update(weight, moment, square, gradient, step_rate):
    moment_new = beta_moment * moment + (1.0 - beta_moment) * gradient
    square_new = beta_moment * square + (1.0 - beta_moment) * gradient * gradient
    correct = 1.0 - beta_moment**STEP
    direction = moment_new / correct / (jnp.sqrt(square_new / correct) + adam_epsilon)
    return (weight - step_rate * (direction + weight_decay * weight), moment_new, square_new)


def general_device(
    inputs,
    skip_tokens,
    cotangent,
    merge_weight,
    merge_moment,
    merge_square,
    attend_weight,
    attend_moment,
    attend_square,
    output_weight,
    output_moment,
    output_square,
    expand_weight,
    expand_moment,
    expand_square,
    shrink_weight,
    shrink_moment,
    shrink_square,
    vectors,
    vector_moment,
    vector_square,
):
    merge_low = merge_weight.astype(jnp.bfloat16)
    attend_low = attend_weight.astype(jnp.bfloat16)
    output_low = output_weight.astype(jnp.bfloat16)
    expand_low = expand_weight.astype(jnp.bfloat16)
    shrink_low = shrink_weight.astype(jnp.bfloat16)
    vector_low = vectors.astype(jnp.bfloat16)
    columns = (
        lax.all_gather(merge_low, "narrow", axis=1, tiled=True),
        lax.all_gather(attend_low, "narrow", axis=1, tiled=True),
        lax.all_gather(output_low, "narrow", axis=1, tiled=True),
        lax.all_gather(expand_low, "narrow", axis=1, tiled=True),
        lax.all_gather(shrink_low, "narrow", axis=1, tiled=True),
        lax.all_gather(vector_low, "narrow", axis=0, tiled=True),
    )
    matrices = (
        lax.all_gather(columns[0], "wide", axis=0, tiled=True),
        lax.all_gather(columns[1], "wide", axis=0, tiled=True),
        lax.all_gather(columns[2], "wide", axis=0, tiled=True),
        lax.all_gather(columns[3], "wide", axis=0, tiled=True),
        lax.all_gather(columns[4], "wide", axis=0, tiled=True),
    )
    skip_bias, gain_one, bias_one, output_bias, gain_two, bias_two, shrink_bias, expand_bias = (
        unpack(columns[5].astype(jnp.float32))
    )
    images = inputs.shape[0]
    length = inputs.shape[1]
    softmax_scale = HD ** (-0.5)
    joined = jnp.concatenate([inputs, skip_tokens], axis=-1)
    stream_zero = product(joined, matrices[0]) + skip_bias
    normed_one, inverse_one = normalize(stream_zero)
    attend_input = (normed_one * gain_one + bias_one).astype(jnp.bfloat16)
    mixed_heads = product(attend_input, matrices[1]).astype(jnp.bfloat16)
    query_heads = mixed_heads[..., 0:D].reshape(images, length, H, HD)
    key_heads = mixed_heads[..., D : 2 * D].reshape(images, length, H, HD)
    value_heads = mixed_heads[..., 2 * D : 3 * D].reshape(images, length, H, HD)
    logits = (
        jnp.einsum("blhe,bmhe->bhlm", query_heads, key_heads, preferred_element_type=jnp.float32)
        * softmax_scale
    )
    maxima = jnp.max(logits, axis=-1, keepdims=True)
    log_total = maxima + jnp.log(jnp.sum(jnp.exp(logits - maxima), axis=-1, keepdims=True))
    softmax_low = jnp.exp(logits - log_total).astype(jnp.bfloat16)
    mixture = jnp.einsum(
        "bhlm,bmhe->blhe", softmax_low, value_heads, preferred_element_type=jnp.float32
    )
    mixture = mixture.astype(jnp.bfloat16).reshape(images, length, D)
    stream_one = stream_zero + product(mixture, matrices[2]) + output_bias
    normed_two, inverse_two = normalize(stream_one)
    expand_input = (normed_two * gain_two + bias_two).astype(jnp.bfloat16)
    hidden = product(expand_input, matrices[3]) + expand_bias
    active, pullback = jax.vjp(gaussian_unit, hidden)
    active_low = active.astype(jnp.bfloat16)
    outputs = (stream_one + product(active_low, matrices[4]) + shrink_bias).astype(jnp.bfloat16)
    columns_back = (
        lax.all_gather(merge_low, "narrow", axis=1, tiled=True),
        lax.all_gather(attend_low, "narrow", axis=1, tiled=True),
        lax.all_gather(output_low, "narrow", axis=1, tiled=True),
        lax.all_gather(expand_low, "narrow", axis=1, tiled=True),
        lax.all_gather(shrink_low, "narrow", axis=1, tiled=True),
        lax.all_gather(vector_low, "narrow", axis=0, tiled=True),
    )
    matrices_back = (
        lax.all_gather(columns_back[0], "wide", axis=0, tiled=True),
        lax.all_gather(columns_back[1], "wide", axis=0, tiled=True),
        lax.all_gather(columns_back[2], "wide", axis=0, tiled=True),
        lax.all_gather(columns_back[3], "wide", axis=0, tiled=True),
        lax.all_gather(columns_back[4], "wide", axis=0, tiled=True),
    )
    packed_back = columns_back[5].astype(jnp.float32)
    unpacked = unpack(packed_back)
    gain_first = unpacked[1]
    gain_second = unpacked[4]
    upstream = cotangent.astype(jnp.float32)
    shrink_gradient = weight_gradient(active_low, cotangent)
    delta_active = transposed(cotangent, matrices_back[4])
    delta_hidden = pullback(delta_active)[0]
    hidden_low = delta_hidden.astype(jnp.bfloat16)
    expand_gradient = weight_gradient(expand_input, hidden_low)
    delta_expand = transposed(hidden_low, matrices_back[3])
    delta_one = upstream + norm_back(delta_expand * gain_second, normed_two, inverse_two)
    stream_low = delta_one.astype(jnp.bfloat16)
    output_gradient = weight_gradient(mixture, stream_low)
    delta_mixture = (
        transposed(stream_low, matrices_back[2]).astype(jnp.bfloat16).reshape(images, length, H, HD)
    )
    logits_again = (
        jnp.einsum("blhe,bmhe->bhlm", query_heads, key_heads, preferred_element_type=jnp.float32)
        * softmax_scale
    )
    softmax_again = jnp.exp(logits_again - log_total)
    delta_softmax = jnp.einsum(
        "blhe,bmhe->bhlm", delta_mixture, value_heads, preferred_element_type=jnp.float32
    )
    delta_values = jnp.einsum(
        "bhlm,blhe->bmhe",
        softmax_again.astype(jnp.bfloat16),
        delta_mixture,
        preferred_element_type=jnp.float32,
    )
    delta_logits = softmax_again * (
        delta_softmax - jnp.sum(softmax_again * delta_softmax, axis=-1, keepdims=True)
    )
    delta_scores = (softmax_scale * delta_logits).astype(jnp.bfloat16)
    delta_queries = jnp.einsum(
        "bhlm,bmhe->blhe", delta_scores, key_heads, preferred_element_type=jnp.float32
    )
    delta_keys = jnp.einsum(
        "bhlm,blhe->bmhe", delta_scores, query_heads, preferred_element_type=jnp.float32
    )
    delta_mixed = jnp.concatenate(
        [
            delta_queries.reshape(images, length, D),
            delta_keys.reshape(images, length, D),
            delta_values.reshape(images, length, D),
        ],
        axis=-1,
    ).astype(jnp.bfloat16)
    attend_gradient = weight_gradient(attend_input, delta_mixed)
    delta_attend = transposed(delta_mixed, matrices_back[1])
    delta_zero = delta_one + norm_back(delta_attend * gain_first, normed_one, inverse_one)
    zero_low = delta_zero.astype(jnp.bfloat16)
    merge_gradient = weight_gradient(joined, zero_low)
    delta_joined = transposed(zero_low, matrices_back[0])
    input_gradient = delta_joined[..., 0:D].astype(jnp.bfloat16)
    skip_gradient = delta_joined[..., D : 2 * D].astype(jnp.bfloat16)
    vector_gradient = jnp.concatenate(
        [
            row_sum(delta_zero),
            row_sum(delta_attend * normed_one),
            row_sum(delta_attend),
            row_sum(delta_one),
            row_sum(delta_expand * normed_two),
            row_sum(delta_expand),
            row_sum(upstream),
            row_sum(delta_hidden),
        ]
    )
    owned_rows = (
        lax.psum_scatter(merge_gradient, "wide", scatter_dimension=0, tiled=True),
        lax.psum_scatter(attend_gradient, "wide", scatter_dimension=0, tiled=True),
        lax.psum_scatter(output_gradient, "wide", scatter_dimension=0, tiled=True),
        lax.psum_scatter(expand_gradient, "wide", scatter_dimension=0, tiled=True),
        lax.psum_scatter(shrink_gradient, "wide", scatter_dimension=0, tiled=True),
    )
    vector_total = lax.psum(vector_gradient, "wide")
    parted = (
        lax.psum_scatter(owned_rows[0], "narrow", scatter_dimension=1, tiled=True),
        lax.psum_scatter(owned_rows[1], "narrow", scatter_dimension=1, tiled=True),
        lax.psum_scatter(owned_rows[2], "narrow", scatter_dimension=1, tiled=True),
        lax.psum_scatter(owned_rows[3], "narrow", scatter_dimension=1, tiled=True),
        lax.psum_scatter(owned_rows[4], "narrow", scatter_dimension=1, tiled=True),
        lax.psum_scatter(vector_total, "narrow", scatter_dimension=0, tiled=True),
    )
    merge_new = adamw_update(merge_weight, merge_moment, merge_square, parted[0], rate_merge)
    attend_new = adamw_update(attend_weight, attend_moment, attend_square, parted[1], rate_attend)
    output_new = adamw_update(output_weight, output_moment, output_square, parted[2], rate_output)
    expand_new = adamw_update(expand_weight, expand_moment, expand_square, parted[3], rate_expand)
    shrink_new = adamw_update(shrink_weight, shrink_moment, shrink_square, parted[4], rate_shrink)
    vector_new = adamw_update(vectors, vector_moment, vector_square, parted[5], rate_vector)
    return (
        outputs,
        input_gradient,
        skip_gradient,
        merge_new[0],
        merge_new[1],
        merge_new[2],
        attend_new[0],
        attend_new[1],
        attend_new[2],
        output_new[0],
        output_new[1],
        output_new[2],
        expand_new[0],
        expand_new[1],
        expand_new[2],
        shrink_new[0],
        shrink_new[1],
        shrink_new[2],
        vector_new[0],
        vector_new[1],
        vector_new[2],
    )


CORE = 1
ACROSS = 2
ALONG = 4
PAD = 384
VECTOR_ROWS = 11
VMEM_BYTES = 56 * 1024 * 1024
LIGHT = pl.CostEstimate(flops=0, bytes_accessed=1024, transcendentals=0)
PARAMS = pltpu.CompilerParams(vmem_limit_bytes=VMEM_BYTES)


def swap_wide(value, bit):
    return lax.ppermute(value, "wide", [(i, i ^ bit) for i in range(8)])


def swap_narrow(value, bit):
    return lax.ppermute(value, "narrow", [(i, i ^ bit) for i in range(4)])


def together(*values):
    return lax.optimization_barrier(values)


def spot():
    wide = lax.axis_index("wide")
    narrow = lax.axis_index("narrow")
    return (wide & 1, (wide >> 1) & 1, (wide >> 2) & 1, narrow & 1, narrow >> 1)


def split_shapes(rows, columns):
    if columns == FF:
        return (rows, columns // 2), True
    return (rows // 2, columns), False


def split_block(value):
    shape, by_columns = split_shapes(*value.shape[-2:])
    if by_columns:
        return value[..., : shape[1]], value[..., shape[1] :]
    return value[..., : shape[0], :], value[..., shape[0] :, :]


def column_blocks(kind, quarter):
    if kind == "attend_output":
        width = quarter // 8
        order = [8 * part + 2 * n + p for part in range(3) for p in range(2) for n in range(4)]
        blocks = [(block // 6, (block % 6) * width) for block in order]
        return width, blocks + [(n, (6 + p) * width) for p in range(2) for n in range(4)]
    width = quarter // 2
    return width, [(n, p * width) for p in range(2) for n in range(4)]


def fold(shard):
    parts = max(1, shard.shape[0] // (D // 8))
    height = shard.shape[0] // parts
    return jnp.concatenate(
        [shard[part * height : (part + 1) * height] for part in range(parts)], axis=1
    )


def unfold(value, rows):
    parts = rows // value.shape[0]
    quarter = value.shape[1] // parts
    return jnp.concatenate(
        [value[:, part * quarter : (part + 1) * quarter] for part in range(parts)], axis=0
    )


def arrange(kind, parts, shard, others, extra=0):
    height = shard.shape[0]
    rows, quarter = parts * height, (shard.shape[1] - extra) // parts
    width, blocks = column_blocks(kind, quarter)

    def kernel(*refs):
        full, apart = refs[4], refs[-1]
        narrow = lax.axis_index("narrow")
        for number in range(4):
            for relative in range(4):

                @pl.when((narrow ^ relative) == number)
                def _():
                    value = refs[relative]
                    if extra:
                        apart[number] = value[:, parts * quarter :]
                    for position, (owner, offset) in enumerate(blocks):
                        if owner == number:
                            column = slice(position * width, (position + 1) * width)
                            for part in range(parts):
                                start = part * quarter + offset
                                full[part * height : (part + 1) * height, column] = value[
                                    :, start : start + width
                                ]

    outs = [jax.ShapeDtypeStruct((rows, 4 * quarter), jnp.bfloat16)]
    if extra:
        outs.append(jax.ShapeDtypeStruct((4, height, extra), jnp.bfloat16))
    return pl.pallas_call(
        kernel,
        out_shape=tuple(outs),
        compiler_params=PARAMS,
        cost_estimate=LIGHT,
    )(shard, *others)


def weight_scratch(rows, columns, chunks=1):
    return [pltpu.VMEM((rows, columns), jnp.bfloat16), pltpu.SemaphoreType.DMA((chunks, 8))]


class Fetch:
    def __init__(self, refs, full, sems, first=0):
        wide = lax.axis_index("wide")
        core, chip = wide & 1, wide >> 1
        rows = full.shape[0] // 8
        chunks = sems.shape[0]
        width = full.shape[1] // chunks
        self.copies = []
        for chunk in range(chunks):
            group = []
            for number, (ends, from_x, from_y) in enumerate((refs[:3], refs[3:])):
                parity = core if number == 0 else 1 - core
                own, far = ends.at[pl.ds(0, rows)], ends.at[pl.ds(rows, rows)]
                for relative, piece in enumerate((own, from_x, from_y, far)):
                    start = pl.multiple_of((4 * parity + (chip ^ relative)) * rows, 16)
                    group.append(
                        pltpu.make_async_copy(
                            piece.at[:, pl.ds(first + chunk * width, width)],
                            full.at[pl.ds(start, rows), pl.ds(chunk * width, width)],
                            sems.at[chunk, 4 * number + relative],
                        )
                    )
            self.copies.append(group)
        for group in self.copies:
            for copy in group:
                copy.start()

    def wait(self, chunk=0):
        for copy in self.copies[chunk]:
            copy.wait()


def pair_gradient(lefts, right):
    height = lefts[0][4]
    rows = height // 4
    tokens, columns = right[0].shape
    tile = 384 if height > 576 else 1152
    count = len(lefts)
    ends = [sum(left[2] for left in lefts[: number + 1]) // tile for number in range(count)]
    starts = [0] + ends[:-1]

    def kernel(*refs):
        left_refs = refs[: 2 * count]
        right_ref, sibling_ref = refs[2 * count : 2 * count + 2]
        outs = refs[2 * count + 2 : 2 * count + 6]
        joint, beside, total = refs[2 * count + 6 :]
        step = pl.program_id(0)

        @pl.when(step == 0)
        def _():
            joint[...] = jnp.zeros_like(joint)

        for number in range(count):

            @pl.when(step == starts[number])
            def _():
                beside[:, :PAD] = left_refs[2 * number][...]
                beside[:, PAD:] = left_refs[2 * number + 1][...]

        joint[:tokens] = right_ref[...]
        joint[PAD : PAD + tokens] = sibling_ref[...]
        total[...] = jnp.dot(
            beside[...], joint[...], preferred_element_type=jnp.float32
        ).astype(jnp.bfloat16)
        by_columns = split_shapes(rows, columns)[1]
        part_blocks(total, rows, outs, step < columns // tile // 2 if by_columns else None)

    whole = lambda place: pl.BlockSpec((height, PAD), lambda i: (place, 0))
    part = lambda size: pl.BlockSpec((size, tile), lambda i: (0, i))
    shape, by_columns = split_shapes(rows, columns)
    half = columns // tile // 2
    if by_columns:
        top = pl.BlockSpec((2, rows, tile), lambda i: (0, 0, jnp.minimum(i, half - 1)))
        bottom = pl.BlockSpec((2, rows, tile), lambda i: (0, 0, jnp.maximum(i - half, 0)))
    else:
        top = bottom = pl.BlockSpec((2, shape[0], tile), lambda i: (0, 0, i))
    outs = pl.pallas_call(
        kernel,
        grid=(columns // tile,),
        in_specs=[whole(left[3]) for left in lefts for _ in range(2)] + [part(tokens)] * 2,
        out_specs=(top, top, bottom, bottom),
        out_shape=block_shapes(rows, columns),
        scratch_shapes=[
            pltpu.VMEM((2 * PAD, tile), jnp.bfloat16),
            pltpu.VMEM((height, 2 * PAD), jnp.bfloat16),
            pltpu.VMEM((height, tile), jnp.bfloat16),
        ],
        compiler_params=PARAMS,
        cost_estimate=LIGHT,
    )(*[left for pair_of in lefts for left in pair_of[:2]], *right)
    return outs


def block_shapes(rows, columns):
    shape = split_shapes(rows, columns)[0]
    return (jax.ShapeDtypeStruct((2,) + shape, jnp.bfloat16),) * 4


def part_blocks(total, rows, outs, first_half):
    wide = lax.axis_index("wide")
    across, along = (wide >> 1) & 1, (wide >> 2) & 1
    half = rows // 2
    for kept_x in range(2):
        for kept_y in range(2):
            x = across if kept_x else 1 - across
            y = along if kept_y else 1 - along
            start = pl.multiple_of((2 * y + x) * rows, 16)
            top, bottom = outs[1 - kept_x], outs[3 - kept_y]
            if first_half is None:
                top[1 - kept_y] = total[pl.ds(start, half)]
                bottom[1 - kept_x] = total[pl.ds(pl.multiple_of(start + half, 16), half)]
                continue

            @pl.when(first_half)
            def _():
                top[1 - kept_y] = total[pl.ds(start, rows)]

            @pl.when(jnp.logical_not(first_half))
            def _():
                bottom[1 - kept_x] = total[pl.ds(start, rows)]


def unarrange(kind, parts, blocks, got, got_last):
    by_columns = got_last[0].shape[1] == FF // 2
    part_rows, part_columns = got_last[0].shape
    rows = part_rows if by_columns else 2 * part_rows
    columns = 2 * part_columns if by_columns else part_columns
    quarter = columns // 4
    height = rows // parts
    width, column_parts = column_blocks(kind, quarter)

    def kernel(*refs):
        tops, bottoms = refs[:3], refs[3:6]
        outs, held = refs[6:10], refs[10]
        narrow = lax.axis_index("narrow")
        low_bit, high_bit = narrow & 1, narrow >> 1
        top = add_low(tops[0][...], tops[1][...], tops[2][...])
        bottom = add_low(bottoms[0][...], bottoms[1][...], bottoms[2][...])
        if by_columns:
            held[:, :part_columns] = top
            held[:, part_columns:] = bottom
        else:
            held[:part_rows] = top
            held[part_rows:] = bottom
        for owner in range(4):
            for which in range(4):
                low_same, high_same = 1 - which // 2, 1 - which % 2

                @pl.when(
                    ((low_bit == (owner & 1)) == (low_same == 1))
                    & ((high_bit == (owner >> 1)) == (high_same == 1))
                )
                def _():
                    for position, (quarter_of, offset) in enumerate(column_parts):
                        if quarter_of == owner:
                            piece = held[:, position * width : (position + 1) * width]
                            for part in range(parts):
                                start = part * quarter + offset
                                outs[which][:, start : start + width] = piece[
                                    part * height : (part + 1) * height
                                ]

    near = pl.BlockSpec((None, part_rows, part_columns), lambda i: (0, 0, 0))
    full = lambda size, width: pl.BlockSpec((size, width), lambda i: (0, 0))
    shape = jax.ShapeDtypeStruct((height, parts * quarter), jnp.bfloat16)
    return pl.pallas_call(
        kernel,
        grid=(1,),
        in_specs=[near, near, full(part_rows, part_columns)] * 2,
        out_specs=(full(height, parts * quarter),) * 4,
        out_shape=(shape,) * 4,
        scratch_shapes=[pltpu.VMEM((rows, columns), jnp.bfloat16)],
        compiler_params=PARAMS,
        cost_estimate=LIGHT,
    )(blocks[0], got[0], got_last[0], blocks[2], got[1], got_last[1])


def add_low(*terms):
    return sum(term.astype(jnp.float32) for term in terms).astype(jnp.bfloat16)


def pick(value, index, dim=0):
    return lax.dynamic_index_in_dim(value, index, dim, keepdims=False)


def halves_of(value, core):
    middle = value.shape[-1] // 2
    first, second = value[..., :middle], value[..., middle:]
    return jnp.where(core == 0, first, second), jnp.where(core == 0, second, first)


def inner(value):
    width = value.shape[-1] // 8
    return jnp.concatenate(
        [
            value[..., (2 * n + p) * width : (2 * n + p + 1) * width]
            for p in range(2)
            for n in range(4)
        ],
        axis=-1,
    )


def outer(value):
    width = value.shape[-1] // 8
    return jnp.concatenate(
        [
            value[..., (4 * p + n) * width : (4 * p + n + 1) * width]
            for n in range(4)
            for p in range(2)
        ],
        axis=-1,
    )


def upright(value):
    return jnp.pad(value, ((0, PAD - value.shape[0]), (0, 0))).T


KEEP_NEAR, KEEP_FAR, SEND_NEAR, SEND_FAR = range(4)


def send(blocks):
    return swap_wide(blocks[1], ACROSS), swap_wide(blocks[3], ALONG)


def forward(blocks, got):
    return (
        swap_wide(add_low(blocks[0][1], got[0][1]), ALONG),
        swap_wide(add_low(blocks[2][1], got[1][1]), ACROSS),
    )


def narrow_first(quarters):
    return swap_narrow(quarters[SEND_FAR], 1), swap_narrow(quarters[SEND_NEAR], 1)


def narrow_second(quarters, got):
    return swap_narrow(add_low(quarters[KEEP_FAR], got[0]), 2)


def finish(quarters, got, got_last):
    return (
        quarters[KEEP_NEAR].astype(jnp.float32)
        + got[1].astype(jnp.float32)
        + got_last.astype(jnp.float32)
    )


def across_narrow(shard):
    return tuple(swap_narrow(shard, bit) for bit in (1, 2, 3))


def gather_first(block):
    return swap_wide(block, ACROSS), swap_wide(block, ALONG)


def gather_second(first):
    return (
        swap_wide(split_block(first[0])[0], ALONG),
        swap_wide(split_block(first[1])[1], ACROSS),
    )


def swap_sides(first):
    return swap_wide(first[0], CORE), swap_wide(first[1], CORE)


def ends_of(block, second):
    if split_shapes(*block.shape)[1]:
        return jnp.concatenate([block, jnp.concatenate(second, axis=1)], axis=0)
    if block.shape[0] > 2 * D // 8:
        return jnp.concatenate([block, *second], axis=0)
    return jnp.stack([block, jnp.concatenate(second, axis=0)]).reshape(-1, block.shape[1])


def line_gradient(lefts, rights, rights_sibling):
    tokens, height = lefts[0].shape
    width = rights.shape[2]
    rows = height // 4

    def kernel(*refs):
        right_ref, sibling_ref = refs[8:10]
        outs, (total, joined) = refs[10:14], refs[14:]
        chip = lax.axis_index("wide") >> 1
        for number in range(8):
            right = (right_ref, sibling_ref)[number // 4][number % 4, :tokens]
            part = lax.dot_general(
                right,
                refs[number][...],
                (((0,), (0,)), ((), ())),
                preferred_element_type=jnp.float32,
            )
            total[...] = part if number == 0 else total[...] + part
        sums = sum(
            ref[number, rights.shape[1] - 16 :].astype(jnp.float32)
            for ref in (right_ref, sibling_ref)
            for number in range(4)
        )
        joined[...] = jnp.zeros_like(joined)
        for row in range(VECTOR_ROWS):
            columns = slice((row % 2) * width, (row % 2 + 1) * width)
            joined[row // 2 : row // 2 + 1, columns] = sums[row : row + 1]
        for ref in outs:
            ref[rows // 2 :] = joined[...].astype(jnp.bfloat16)
        for owner in range(4):
            block = total[:, owner * rows : (owner + 1) * rows].T.astype(jnp.bfloat16)
            for relative in range(4):

                @pl.when((chip ^ relative) == owner)
                def _():
                    outs[relative][: rows // 2, :width] = block[: rows // 2]
                    outs[relative][: rows // 2, width:] = block[rows // 2 :]

    shape = jax.ShapeDtypeStruct((rows // 2 + 16, 2 * width), jnp.bfloat16)
    return pl.pallas_call(
        kernel,
        out_shape=(shape,) * 4,
        scratch_shapes=[
            pltpu.VMEM((width, height), jnp.float32),
            pltpu.VMEM((16, 2 * width), jnp.float32),
        ],
        compiler_params=PARAMS,
        cost_estimate=LIGHT,
    )(*lefts, rights, rights_sibling)


def turned_update(weight, moment, square, terms, parts, step_rate):
    rows, quarter = weight.shape
    height = rows // parts

    def kernel(*refs):
        weight_ref, moment_ref, square_ref = refs[: 3]
        total = sum(ref[...].astype(jnp.float32) for ref in refs[3 : 3 + len(terms)])
        outs, gradient = refs[3 + len(terms) : 6 + len(terms)], refs[-1]
        for part in range(parts):
            gradient[part * height : (part + 1) * height] = total[
                :, part * quarter : (part + 1) * quarter
            ]
        new = adamw_update(
            weight_ref[...], moment_ref[...], square_ref[...], gradient[...].T, step_rate
        )
        for out, value in zip(outs, new):
            out[...] = value

    new = pl.pallas_call(
        kernel,
        out_shape=(jax.ShapeDtypeStruct((quarter, rows), jnp.float32),) * 3,
        scratch_shapes=[pltpu.VMEM((rows, quarter), jnp.float32)],
        compiler_params=PARAMS,
        cost_estimate=LIGHT,
    )(weight.T, moment.T, square.T, *terms)
    return tuple(value.T for value in new)


def heavy(kernel, outs, scratch, weights, operands):
    return pl.pallas_call(
        kernel,
        in_specs=[pl.BlockSpec(memory_space=pl.ANY)] * len(weights)
        + [pl.BlockSpec(memory_space=pltpu.VMEM)] * len(operands),
        out_shape=tuple(jax.ShapeDtypeStruct(shape, dtype) for shape, dtype in outs),
        scratch_shapes=scratch,
        compiler_params=PARAMS,
        cost_estimate=LIGHT,
    )(*weights, *operands)


def dot_rows(left, right):
    return lax.dot_general(left, right, (((1,), (1,)), ((), ())), preferred_element_type=jnp.float32)


def dot_depth(left, right):
    return lax.dot_general(left, right, (((0,), (0,)), ((), ())), preferred_element_type=jnp.float32)


def store_upright(value, padded, mine, other):
    features = value.shape[1]
    padded[: value.shape[0]] = value
    turned = padded[...].T.astype(jnp.bfloat16)
    core = lax.axis_index("wide") & 1

    @pl.when(core == 0)
    def _():
        mine[...] = turned[: features // 2]
        other[...] = turned[features // 2 :]

    @pl.when(core == 1)
    def _():
        other[...] = turned[: features // 2]
        mine[...] = turned[features // 2 :]


def merge_forward(joined, weight, bias, gain, shift):
    length = joined.shape[0]

    def kernel(*refs):
        joined_ref, bias_ref, gain_ref, shift_ref = refs[6:10]
        stream, entry, up_mine, up_other, full, sems, padded = refs[10:]
        weight_in = Fetch(refs[:6], full, sems)
        padded[...] = jnp.zeros_like(padded)
        weight_in.wait()
        stream[...] = product(joined_ref[...], full[...]) + bias_ref[...]
        normed = normalize(stream[...])[0]
        value = (normed * gain_ref[...] + shift_ref[...]).astype(jnp.bfloat16)
        entry[...] = value
        store_upright(value.astype(jnp.float32), padded, up_mine, up_other)

    return heavy(
        kernel,
        [
            ((length, D), jnp.float32),
            ((length, D), jnp.bfloat16),
            ((D // 2, PAD), jnp.bfloat16),
            ((D // 2, PAD), jnp.bfloat16),
        ],
        weight_scratch(2 * D, D) + [pltpu.VMEM((PAD, D), jnp.float32)],
        weight,
        (joined, bias, gain, shift),
    )


def attend_head(heads, head, chances_ref, slot):
    at = head * HD
    queries = heads[:, at : at + HD]
    keys = heads[:, D + at : D + at + HD]
    values = heads[:, 2 * D + at : 2 * D + at + HD]
    logits = dot_rows(queries, keys) * HD ** (-0.5)
    powers = jnp.exp(logits - jnp.max(logits, axis=-1, keepdims=True))
    chances = powers / jnp.sum(powers, axis=-1, keepdims=True)
    chances_ref[slot] = chances
    return product(chances.astype(jnp.bfloat16), values).astype(jnp.bfloat16)


FIRST = 15


def attend_first(entry, weight):
    length = entry.shape[0]

    def kernel(*refs):
        entry_ref, heads, chances_ref, mix_ref, full, sems = refs[6:]
        weight_in = Fetch(refs[:6], full, sems)
        for part in range(3):
            weight_in.wait(part)
            columns = slice(part * D, (part + 1) * D)
            heads[:, columns] = product(entry_ref[...], full[:, columns]).astype(jnp.bfloat16)
        for head in range(FIRST):
            mix_ref[:, head * HD : (head + 1) * HD] = attend_head(heads, head, chances_ref, head)

    return heavy(
        kernel,
        [
            ((length, 3 * D), jnp.bfloat16),
            ((FIRST, length, length), jnp.float32),
            ((length, FIRST * HD), jnp.bfloat16),
        ],
        weight_scratch(D, 3 * D, 3),
        weight,
        (entry,),
    )


def attend_second(heads, mix_first, weight, stream_zero, bias, gain, shift):
    length = heads.shape[0]
    half = D // 2

    def kernel(*refs):
        heads_ref, first_ref, zero_ref, bias_ref, gain_ref, shift_ref = refs[6:12]
        chances_ref, stream, value_ref, up_mine, up_other, full, sems, mixed, padded = refs[12:]
        weight_in = Fetch(refs[:6], full, sems, 3 * D)
        padded[...] = jnp.zeros_like(padded)
        mixed[:, : FIRST * HD] = first_ref[...]
        for head in range(FIRST, H):
            mixed[:, head * HD : (head + 1) * HD] = attend_head(
                heads_ref, head, chances_ref, head - FIRST
            )
        weight_in.wait()
        stream[...] = zero_ref[...] + product(mixed[...], full[...]) + bias_ref[...]
        store_upright(
            mixed[...].astype(jnp.float32), padded, up_mine.at[pl.ds(0, half)], up_other.at[pl.ds(0, half)]
        )
        normed = normalize(stream[...])[0]
        value = (normed * gain_ref[...] + shift_ref[...]).astype(jnp.bfloat16)
        value_ref[...] = value
        store_upright(
            value.astype(jnp.float32), padded, up_mine.at[pl.ds(half, half)], up_other.at[pl.ds(half, half)]
        )

    return heavy(
        kernel,
        [
            ((H - FIRST, length, length), jnp.float32),
            ((length, D), jnp.float32),
            ((length, D), jnp.bfloat16),
            ((D, PAD), jnp.bfloat16),
            ((D, PAD), jnp.bfloat16),
        ],
        weight_scratch(D, D)
        + [pltpu.VMEM((length, D), jnp.bfloat16), pltpu.VMEM((PAD, D), jnp.float32)],
        weight,
        (heads, mix_first, stream_zero, bias, gain, shift),
    )


def expand_forward(entry, weight, bias):
    length = entry.shape[0]

    def kernel(*refs):
        entry_ref, bias_ref = refs[6:8]
        active_ref, slope_ref, up_mine, up_other, full, sems, padded = refs[8:]
        core = lax.axis_index("wide") & 1
        weight_in = Fetch(refs[:6], full, sems)
        padded[...] = jnp.zeros_like(padded)
        for step in range(FF // D):
            columns = slice(step * D, (step + 1) * D)
            weight_in.wait(step)
            value = product(entry_ref[...], full[:, columns]) + bias_ref[:, columns]
            inside = 0.5 * (1.0 + lax.erf(value * (0.5**0.5)))
            bell = jnp.exp(-0.5 * value * value) * (2.0 * jnp.pi) ** -0.5
            active = (value * inside).astype(jnp.bfloat16)
            slope_ref[:, columns] = inside + value * bell
            active_ref[:, columns] = active
            padded[:length] = active.astype(jnp.float32)
            turned = padded[...].T.astype(jnp.bfloat16)
            rows = slice((step % 2) * D, (step % 2 + 1) * D)

            @pl.when(core == step // 2)
            def _():
                up_mine[rows] = turned

            @pl.when(core != step // 2)
            def _():
                up_other[rows] = turned

    return heavy(
        kernel,
        [
            ((length, FF), jnp.bfloat16),
            ((length, FF), jnp.float32),
            ((FF // 2, PAD), jnp.bfloat16),
            ((FF // 2, PAD), jnp.bfloat16),
        ],
        weight_scratch(D, FF, FF // D) + [pltpu.VMEM((PAD, D), jnp.float32)],
        weight,
        (entry, bias),
    )


def hidden_backward(pulled, weight, slope):
    length = pulled.shape[0]

    def kernel(*refs):
        pulled_ref, slope_ref, low_ref, sum_ref, full, sems = refs[6:]
        Fetch(refs[:6], full, sems).wait()
        for step in range(FF // D):
            columns = slice(step * D, (step + 1) * D)
            delta = dot_rows(pulled_ref[...], full[columns]) * slope_ref[:, columns]
            low_ref[:, columns] = delta.astype(jnp.bfloat16)
            sum_ref[:, columns] = jnp.sum(delta, axis=0, keepdims=True)

    return heavy(
        kernel,
        [((length, FF), jnp.bfloat16), ((1, FF), jnp.float32)],
        weight_scratch(FF, D),
        weight,
        (pulled, slope),
    )


def expand_backward(hidden_low, weight, mixed_weight, pulled, stream_one, gain):
    length = pulled.shape[0]

    def kernel(*refs):
        hidden_ref, pulled_ref, stream_ref, gain_ref = refs[12:16]
        one_ref, low_ref, sums, mix_ref, full, sems, output, output_sems, delta = refs[16:]
        weight_in = Fetch(refs[:6], full, sems)
        output_in = Fetch(refs[6:12], output, output_sems, 3 * D)
        for step in range(FF // D):
            columns = slice(step * D, (step + 1) * D)
            weight_in.wait(step)
            part = dot_rows(hidden_ref[:, columns], full[:, columns])
            delta[...] = part if step == 0 else delta[...] + part
        value = delta[...]
        normed, inverse = normalize(stream_ref[...])
        upstream = pulled_ref[...].astype(jnp.float32)
        one = upstream + norm_back(value * gain_ref[...], normed, inverse)
        one_ref[...] = one
        low_value = one.astype(jnp.bfloat16)
        low_ref[...] = low_value
        sums[0:1] = jnp.sum(one, axis=0, keepdims=True)
        sums[1:2] = jnp.sum(value * normed, axis=0, keepdims=True)
        sums[2:3] = jnp.sum(value, axis=0, keepdims=True)
        sums[3:4] = jnp.sum(upstream, axis=0, keepdims=True)
        output_in.wait()
        mix_ref[...] = dot_rows(low_value, output[...]).astype(jnp.bfloat16)

    return heavy(
        kernel,
        [
            ((length, D), jnp.float32),
            ((length, D), jnp.bfloat16),
            ((4, D), jnp.float32),
            ((length, D), jnp.bfloat16),
        ],
        weight_scratch(D, FF, FF // D)
        + weight_scratch(D, D)
        + [pltpu.VMEM((length, D), jnp.float32)],
        (*weight, *mixed_weight),
        (hidden_low, pulled, stream_one, gain),
    )


def attend_backward(heads, chances_first, chances_second, delta_mixture, stream_low):
    length = heads.shape[0]
    scale = HD ** (-0.5)

    def kernel(heads_ref, first_ref, second_ref, delta_ref, stream_ref, mixed):
        mixed[:, 3 * D :] = stream_ref[...]
        for head in range(H):
            at = head * HD
            queries = heads_ref[:, at : at + HD]
            keys = heads_ref[:, D + at : D + at + HD]
            values = heads_ref[:, 2 * D + at : 2 * D + at + HD]
            delta = delta_ref[:, at : at + HD]
            chances = first_ref[head] if head < FIRST else second_ref[head - FIRST]
            pull = dot_rows(delta, values)
            inner_sum = jnp.sum(chances * pull, axis=-1, keepdims=True)
            scores = (scale * (chances * (pull - inner_sum))).astype(jnp.bfloat16)
            mixed[:, at : at + HD] = product(scores, keys).astype(jnp.bfloat16)
            mixed[:, D + at : D + at + HD] = dot_depth(scores, queries).astype(jnp.bfloat16)
            mixed[:, 2 * D + at : 2 * D + at + HD] = dot_depth(
                chances.astype(jnp.bfloat16), delta
            ).astype(jnp.bfloat16)

    return heavy(
        kernel,
        [((length, 4 * D), jnp.bfloat16)],
        [],
        (),
        (heads, chances_first, chances_second, delta_mixture, stream_low),
    )[0]


def entry_backward(delta_mixed, weight, delta_one, stream_zero, gain, sums_two, hidden_sum):
    length = delta_mixed.shape[0]
    width = D // 8
    tall = -(-length // 16) * 16 + 16

    def kernel(*refs):
        mixed_ref, one_ref, stream_ref, gain_ref, sums_ref, hidden_ref, low_ref = refs[6:13]
        quarters, (full, sems, delta, held) = refs[13:17], refs[17:]
        weight_in = Fetch(refs[:6], full, sems)
        for step in range(3):
            columns = slice(step * D, (step + 1) * D)
            weight_in.wait(step)
            part = dot_rows(mixed_ref[:, columns], full[:, columns])
            delta[...] = part if step == 0 else delta[...] + part
        value = delta[...]
        normed, inverse = normalize(stream_ref[...])
        zero = one_ref[...] + norm_back(value * gain_ref[...], normed, inverse)
        zero_low = zero.astype(jnp.bfloat16)
        low_ref[...] = zero_low
        sums = [jnp.sum(part, axis=0, keepdims=True) for part in (zero, value * normed, value)]
        sums += [sums_ref[row : row + 1] for row in range(4)]
        held[...] = jnp.zeros_like(held)
        for block in range(VECTOR_ROWS * 8):
            owner, place = block // (2 * VECTOR_ROWS), block % (2 * VECTOR_ROWS)
            if block < 56:
                source, wide = sums[block // 8], block % 8
                start = (4 * (wide % 2) + wide // 2) * width
            else:
                source, wide = hidden_ref, (block - 56) // 4
                start = (4 * (wide % 2) + wide // 2) * 4 * width + (block % 4) * width
            columns = slice((place % 2) * width, (place % 2 + 1) * width)
            held[owner, place // 2 : place // 2 + 1, columns] = source[:, start : start + width]
        narrow = lax.axis_index("narrow")
        for owner in range(4):
            for relative in range(4):

                @pl.when((narrow ^ relative) == owner)
                def _():
                    for parity in range(2):
                        start = (4 * parity + owner) * width
                        quarters[relative][:length, parity * width : (parity + 1) * width] = (
                            zero_low[:, start : start + width]
                        )
                    quarters[relative][tall - 16 :] = held[owner].astype(jnp.bfloat16)

    return heavy(
        kernel,
        [((length, D), jnp.bfloat16)] + [((tall, D // 4), jnp.bfloat16)] * 4,
        weight_scratch(D, 3 * D, 3)
        + [pltpu.VMEM((length, D), jnp.float32), pltpu.VMEM((4, 16, D // 4), jnp.float32)],
        weight,
        (delta_mixed, delta_one, stream_zero, gain, sums_two, hidden_sum),
    )


def joined_backward(zero_low, weight):
    length = zero_low.shape[0]
    width = 2 * D // 8

    def kernel(*refs):
        zero_ref, first_ref, second_ref, full, sems = refs[6:]
        Fetch(refs[:6], full, sems).wait()
        for parity in range(2):
            delta = dot_rows(zero_ref[...], full[parity * D : (parity + 1) * D])
            delta = delta.astype(jnp.bfloat16)
            for number in range(4):
                target = (first_ref, second_ref)[number // 2]
                column = (2 * (number % 2) + parity) * width
                target[:, column : column + width] = delta[:, number * width : (number + 1) * width]

    out = ((length, D), jnp.bfloat16)
    return heavy(kernel, [out, out], weight_scratch(2 * D, D), weight, (zero_low,))


def shrink_forward(active, weight, stream_one, bias):
    length = active.shape[0]
    width = D // 8

    def kernel(*refs):
        active_ref, stream_ref, bias_ref, out_ref, full, sems = refs[6:]
        Fetch(refs[:6], full, sems).wait()
        total = (
            stream_ref[...] + product(active_ref[...], full[...]) + bias_ref[...]
        ).astype(jnp.bfloat16)
        for parity in range(2):
            for number in range(4):
                column = (2 * number + parity) * width
                source = (4 * parity + number) * width
                out_ref[:, column : column + width] = total[:, source : source + width]

    return heavy(
        kernel,
        [((length, D), jnp.bfloat16)],
        weight_scratch(FF, D),
        weight,
        (active, stream_one, bias),
    )[0]


def on_device(
    inputs,
    skip_tokens,
    cotangent,
    merge_weight,
    merge_moment,
    merge_square,
    attend_weight,
    attend_moment,
    attend_square,
    output_weight,
    output_moment,
    output_square,
    expand_weight,
    expand_moment,
    expand_square,
    shrink_weight,
    shrink_moment,
    shrink_square,
    vectors,
    vector_moment,
    vector_square,
):
    core = spot()[0]
    low = jnp.bfloat16
    columns = attend_weight.shape[1]

    merge_low = fold(merge_weight.astype(low))
    rows = merge_low.shape[0]
    count = vectors.shape[0]
    vector_rows = jnp.pad(vectors.astype(low), (0, 64 * rows - count)).reshape(rows, 64)
    merge_low = jnp.concatenate([merge_low, vector_rows], axis=1)
    merge_others = across_narrow(merge_low)
    mixed_low = jnp.concatenate([attend_weight.astype(low), output_weight.astype(low)], axis=1)
    joined = inner(jnp.concatenate([inputs[0], skip_tokens[0]], axis=-1))
    joined_mine, joined_other = halves_of(joined, core)
    pulled = inner(cotangent[0])
    merge_others, mixed_low, joined, joined_mine, joined_other, pulled = together(
        merge_others, mixed_low, joined, joined_mine, joined_other, pulled
    )
    merge_block, vector_parts = arrange("merge", 2, merge_low, merge_others, 64)
    merge_first = gather_first(merge_block)
    mixed_far = swap_narrow(mixed_low, 2)
    mixed_near = swap_narrow(mixed_low, 1)
    expand_low = expand_weight.astype(low)
    known_sibling = swap_wide(jnp.concatenate([joined_other, pulled], axis=1), CORE)
    merge_first, mixed_far, vector_parts, expand_low, known_sibling = together(
        merge_first, mixed_far, vector_parts, expand_low, known_sibling
    )
    joined_sibling, pulled_sibling = known_sibling[:, :D], known_sibling[:, D:]
    merge_second = gather_second(merge_first)
    merge_sides = swap_sides(merge_first)
    mixed_last = swap_narrow(mixed_far, 1)
    shrink_low = fold(shrink_weight.astype(low))
    pieces = unpack(vector_parts.reshape(4, -1)[:, :count].reshape(-1).astype(jnp.float32))
    pieces = tuple(inner(piece)[None] for piece in pieces)
    merge_second, merge_sides, mixed_near, mixed_last, shrink_low, pieces = together(
        merge_second, merge_sides, mixed_near, mixed_last, shrink_low, pieces
    )
    skip_bias, gain_one, bias_one, output_bias, gain_two, bias_two, shrink_bias, expand_bias = pieces
    mixed_block = arrange("attend_output", 1, mixed_low, (mixed_near, mixed_far, mixed_last))[0]
    mixed_first = gather_first(mixed_block)
    expand_far = swap_narrow(expand_low, 2)
    expand_near = swap_narrow(expand_low, 1)
    merge_ends = ends_of(merge_block, merge_second)
    merge_pieces = (merge_ends, *merge_first, swap_wide(merge_ends, CORE), *merge_sides)
    stream_zero, attend_input, attend_up, attend_up_other = merge_forward(
        joined, merge_pieces, skip_bias, gain_one, bias_one
    )
    mixed_first, expand_far, expand_near, stream_zero, attend_input, attend_up_other = together(
        mixed_first, expand_far, expand_near, stream_zero, attend_input, attend_up_other
    )
    mixed_second = gather_second(mixed_first)
    mixed_sides = swap_sides(mixed_first)
    expand_last = swap_narrow(expand_far, 1)
    expand_block = arrange("expand", 1, expand_low, (expand_near, expand_far, expand_last))[0]
    mixed_second, mixed_sides, expand_block = together(mixed_second, mixed_sides, expand_block)
    expand_first = gather_first(expand_block)
    shrink_far = swap_narrow(shrink_low, 2)
    shrink_near = swap_narrow(shrink_low, 1)
    mixed_ends = ends_of(mixed_block, mixed_second)
    mixed_pieces = (mixed_ends, *mixed_first, swap_wide(mixed_ends, CORE), *mixed_sides)
    heads, chances_first, mix_first = attend_first(attend_input, mixed_pieces)
    expand_first, shrink_far, shrink_near, heads, mix_first = together(
        expand_first, shrink_far, shrink_near, heads, mix_first
    )
    expand_second = gather_second(expand_first)
    expand_sides = swap_sides(expand_first)
    shrink_last = swap_narrow(shrink_far, 1)
    chances_second, stream_one, expand_input, ups, ups_other = attend_second(
        heads, mix_first, mixed_pieces, stream_zero, output_bias, gain_two, bias_two
    )
    shrink_block = arrange("shrink", 4, shrink_low, (shrink_near, shrink_far, shrink_last))[0]
    (
        expand_second,
        expand_sides,
        shrink_block,
        expand_input,
        ups_other,
        joined_mine,
        joined_sibling,
    ) = together(
        expand_second,
        expand_sides,
        shrink_block,
        expand_input,
        ups_other,
        joined_mine,
        joined_sibling,
    )
    shrink_first = gather_first(shrink_block)
    expand_ends = ends_of(expand_block, expand_second)
    expand_pieces = (expand_ends, *expand_first, swap_wide(expand_ends, CORE), *expand_sides)
    joined_far = swap_narrow(joined_mine, 2)
    joined_near = swap_narrow(joined_mine, 1)
    active, slope, active_up, active_up_other = expand_forward(
        expand_input, expand_pieces, expand_bias
    )
    shrink_first, joined_far, joined_near, active, slope, active_up, active_up_other = together(
        shrink_first, joined_far, joined_near, active, slope, active_up, active_up_other
    )
    shrink_second = gather_second(shrink_first)
    shrink_sides = swap_sides(shrink_first)
    active_up_sibling = swap_wide(active_up_other, CORE)
    shrink_blocks = pair_gradient([(active_up, active_up_sibling, D, 0, FF // 2)], (pulled, pulled_sibling))
    shrink_second, shrink_sides, shrink_blocks, joined_far, joined_sibling, ups_other = together(
        shrink_second, shrink_sides, shrink_blocks, joined_far, joined_sibling, ups_other
    )
    shrink_got = send(shrink_blocks)
    shrink_ends = ends_of(shrink_block, shrink_second)
    shrink_pieces = (shrink_ends, *shrink_first, swap_wide(shrink_ends, CORE), *shrink_sides)
    sibling_far = swap_narrow(joined_sibling, 2)
    joined_last = swap_narrow(joined_far, 1)
    hidden_low, hidden_sum = hidden_backward(pulled, shrink_pieces, slope)
    outputs = shrink_forward(active, shrink_pieces, stream_one, shrink_bias)[None]
    (
        shrink_got,
        sibling_far,
        joined_last,
        hidden_low,
        hidden_sum,
        outputs,
        joined_sibling,
        ups_other,
        attend_up_other,
    ) = together(
        shrink_got,
        sibling_far,
        joined_last,
        hidden_low,
        hidden_sum,
        outputs,
        joined_sibling,
        ups_other,
        attend_up_other,
    )
    shrink_got_last = forward(shrink_blocks, shrink_got)
    hidden_sibling = swap_wide(hidden_low, CORE)
    ups_sibling = swap_wide(ups_other, CORE)
    sibling_near = swap_narrow(joined_sibling, 1)
    half = D // 2
    expand_blocks = pair_gradient(
        [(ups, ups_sibling, FF, 1, half)], (hidden_low, hidden_sibling)
    )
    shrink_got_last, sibling_near, expand_blocks, hidden_low, sibling_far = together(
        shrink_got_last, sibling_near, expand_blocks, hidden_low, sibling_far
    )
    expand_got = send(expand_blocks)
    sibling_last = swap_narrow(sibling_far, 1)
    attend_up_sibling = swap_wide(attend_up_other, CORE)
    shrink_quarters = unarrange("shrink", 4, shrink_blocks, shrink_got, shrink_got_last)
    shrink_hop = swap_narrow(shrink_quarters[SEND_FAR], 1)
    delta_one, stream_low, sums_two, delta_mixture = expand_backward(
        hidden_low, expand_pieces, mixed_pieces, pulled, stream_one, gain_two
    )
    delta_mixed = attend_backward(heads, chances_first, chances_second, delta_mixture, stream_low)
    expand_got, sibling_last, delta_mixed, attend_up_sibling, shrink_hop, shrink_quarters = together(
        expand_got, sibling_last, delta_mixed, attend_up_sibling, shrink_hop, shrink_quarters
    )
    expand_got_last = forward(expand_blocks, expand_got)
    mixed_sibling = swap_wide(delta_mixed, CORE)
    shrink_end = narrow_second(shrink_quarters, (shrink_hop,))
    shrink_near_hop = swap_narrow(shrink_quarters[SEND_NEAR], 1)
    mixed_blocks = pair_gradient(
        [(attend_up, attend_up_sibling, 3 * D, 0, half), (ups, ups_sibling, D, 0, half)],
        (delta_mixed, mixed_sibling),
    )
    expand_got_last, shrink_end, shrink_near_hop, mixed_blocks, delta_mixed = together(
        expand_got_last, shrink_end, shrink_near_hop, mixed_blocks, delta_mixed
    )
    mixed_got = send(mixed_blocks)
    expand_quarters = unarrange("expand", 1, expand_blocks, expand_got, expand_got_last)
    expand_hop = swap_narrow(expand_quarters[SEND_FAR], 1)
    expand_end = narrow_second(expand_quarters, (expand_hop,))
    expand_near_hop = swap_narrow(expand_quarters[SEND_NEAR], 1)
    zero_low, *zero_quarters = entry_backward(
        delta_mixed, mixed_pieces, delta_one, stream_zero, gain_one, sums_two, hidden_sum
    )
    mixed_got, expand_end, expand_near_hop, zero_low, zero_quarters, shrink_end = together(
        mixed_got, expand_end, expand_near_hop, zero_low, zero_quarters, shrink_end
    )
    mixed_got_last = forward(mixed_blocks, mixed_got)
    zero_got = tuple(swap_narrow(zero_quarters[bit], bit) for bit in (1, 2, 3))
    input_gradient, skip_gradient = joined_backward(zero_low, merge_pieces)
    mixed_got_last, zero_got, input_gradient, skip_gradient, shrink_end, expand_end = together(
        mixed_got_last, zero_got, input_gradient, skip_gradient, shrink_end, expand_end
    )
    mixed_quarters = unarrange("attend_output", 1, mixed_blocks, mixed_got, mixed_got_last)
    mixed_far_got = swap_narrow(mixed_quarters[SEND_FAR], 1)
    zero_line = jnp.stack([zero_quarters[0], *zero_got])
    zero_line_sibling = swap_wide(zero_line, CORE)
    merge_blocks = line_gradient(
        (
            joined_mine,
            joined_near,
            joined_far,
            joined_last,
            joined_sibling,
            sibling_near,
            sibling_far,
            sibling_last,
        ),
        zero_line,
        zero_line_sibling,
    )
    mixed_far_got, mixed_quarters, merge_blocks, shrink_end, expand_end = together(
        mixed_far_got, mixed_quarters, merge_blocks, shrink_end, expand_end
    )
    mixed_end = narrow_second(mixed_quarters, (mixed_far_got,))
    mixed_near_got = swap_narrow(mixed_quarters[SEND_NEAR], 1)
    merge_got = (
        swap_wide(merge_blocks[1], ACROSS),
        swap_wide(merge_blocks[2], ALONG),
        swap_wide(merge_blocks[3], ACROSS + ALONG),
    )
    shrink_new = turned_update(
        shrink_weight,
        shrink_moment,
        shrink_square,
        (shrink_quarters[KEEP_NEAR], shrink_near_hop, shrink_end),
        4,
        rate_shrink,
    )
    expand_new = adamw_update(
        expand_weight,
        expand_moment,
        expand_square,
        finish(expand_quarters, (expand_hop, expand_near_hop), expand_end),
        rate_expand,
    )
    tall = merge_blocks[0].shape[0] - 16
    merge_sum = sum(term.astype(jnp.float32) for term in (merge_blocks[0], *merge_got))
    merge_new = adamw_update(
        merge_weight,
        merge_moment,
        merge_square,
        unfold(merge_sum[:tall], merge_weight.shape[0]),
        rate_merge,
    )
    vector_total = merge_sum[tall:].reshape(-1)[: vectors.shape[0]]
    vector_new = adamw_update(vectors, vector_moment, vector_square, vector_total, rate_vector)
    merge_new, mixed_end, mixed_near_got, vector_new, shrink_new, expand_new = together(
        merge_new, mixed_end, mixed_near_got, vector_new, shrink_new, expand_new
    )
    mixed_total = finish(mixed_quarters, (mixed_far_got, mixed_near_got), mixed_end)
    attend_new = adamw_update(
        attend_weight, attend_moment, attend_square, mixed_total[:, :columns], rate_attend
    )
    output_new = adamw_update(
        output_weight, output_moment, output_square, mixed_total[:, columns:], rate_output
    )
    return (
        outputs,
        input_gradient[None],
        skip_gradient[None],
        *merge_new,
        *attend_new,
        *output_new,
        *expand_new,
        *shrink_new,
        *vector_new,
    )


def solution(mesh):
    in_specs = (
        P(("wide", "narrow"), None, None),
        P(("wide", "narrow"), None, None),
        P(("wide", "narrow"), None, None),
        P("wide", "narrow"),
        P("wide", "narrow"),
        P("wide", "narrow"),
        P("wide", "narrow"),
        P("wide", "narrow"),
        P("wide", "narrow"),
        P("wide", "narrow"),
        P("wide", "narrow"),
        P("wide", "narrow"),
        P("wide", "narrow"),
        P("wide", "narrow"),
        P("wide", "narrow"),
        P("wide", "narrow"),
        P("wide", "narrow"),
        P("wide", "narrow"),
        P("narrow"),
        P("narrow"),
        P("narrow"),
    )
    out_specs = (
        P(("wide", "narrow"), None, None),
        P(("wide", "narrow"), None, None),
        P(("wide", "narrow"), None, None),
        P("wide", "narrow"),
        P("wide", "narrow"),
        P("wide", "narrow"),
        P("wide", "narrow"),
        P("wide", "narrow"),
        P("wide", "narrow"),
        P("wide", "narrow"),
        P("wide", "narrow"),
        P("wide", "narrow"),
        P("wide", "narrow"),
        P("wide", "narrow"),
        P("wide", "narrow"),
        P("wide", "narrow"),
        P("wide", "narrow"),
        P("wide", "narrow"),
        P("narrow"),
        P("narrow"),
        P("narrow"),
    )
    tuned = mesh.shape["wide"] == 8 and mesh.shape["narrow"] == 4
    return jax.shard_map(
        on_device if tuned else general_device, mesh=mesh, in_specs=in_specs, out_specs=out_specs, check_vma=False
    )
```
